128 devices in a mesh: dp: 4 (over x), row: 4 (over y_lo, core), col: 8 (over y_hi, z).
Axes of the slice: x: 4, y: 4 (y_hi: 2, y_lo: 2; y = y_hi * 2 + y_lo), z: 4, core: 2. Of those that a mesh axis runs over, the one named last changes fastest.
Arguments:
- tokens: bfloat16 [16400, 1024], P(('dp', 'row'), 'col'), may hold values from -6 to 6
- cotangent: float32 [16400, 1024], P(('dp', 'row'), 'col'), may hold values from -6 to 6
- attend_weight: bfloat16 [2, 1024, 3, 1024], P(None, 'row', None, 'col'), may hold values from -0.1875 to 0.1875
- output_weight: bfloat16 [2, 1024, 1024], P(None, 'col', 'row'), may hold values from -1.5 to 1.5
- up_weight: bfloat16 [2, 1024, 4096], P(None, 'row', 'col'), may hold values from -0.1875 to 0.1875
- down_weight: bfloat16 [2, 4096, 1024], P(None, 'col', 'row'), may hold values from -0.09375 to 0.09375
- norm_gain: float32 [2, 2, 1024], P(None, None, 'col'), may hold values from 0.1 to 1.9
- norm_shift: float32 [2, 2, 1024], P(None, None, 'col'), may hold values from -2 to 2
- attend_bias: float32 [2, 2, 1024], P(None, None, 'col'), may hold values from -3 to 3
- branch_bias: float32 [2, 2, 1024], P(None, None, 'col'), may hold values from -2 to 2
- layer_scale: float32 [2, 2, 1024], P(None, None, 'col'), may hold values from 0.3 to 1.5
- hidden_bias: float32 [2, 4096], P(None, 'col'), may hold values from -3 to 3
Outputs:
- block_output: float32 [16400, 1024], P(('dp', 'row'), 'col')
- tokens_grad: float32 [16400, 1024], P(('dp', 'row'), 'col')
- attend_grad: float32 [2, 1024, 3, 1024], P(None, 'row', None, 'col')
- output_grad: float32 [2, 1024, 1024], P(None, 'col', 'row')
- up_grad: float32 [2, 1024, 4096], P(None, 'row', 'col')
- down_grad: float32 [2, 4096, 1024], P(None, 'col', 'row')
- gain_grad: float32 [2, 2, 1024], P(None, None, 'col')
- shift_grad: float32 [2, 2, 1024], P(None, None, 'col')
- bias_grad: float32 [2, 2, 1024], P(None, None, 'col')
- branch_grad: float32 [2, 2, 1024], P(None, None, 'col')
- scale_grad: float32 [2, 2, 1024], P(None, None, 'col')
- hidden_grad: float32 [2, 4096], P(None, 'col')
The draws below stay inside these ranges and needn't reach their ends.
All inputs are finite; a program needn't handle non-finite values.
Results may differ from the reference program's by a relative error of at most 0.035.
Values may be sent and summed in bfloat16 or wider, within the bound.
A program may use at most 192 MiB of HBM per device.

```python
import math
import jax
import jax.numpy as jnp
from jax import lax

MODEL_WIDTH = 1024
FF = 4096
HEAD_DIM = 64
SEQ = 1025
LAYERS = 2
TOKENS = 16400


def level_of(rng, extent, cuts, low, high):
    level = 1.0
    for dim, parts in cuts:
        steps = jax.random.uniform(jax.random.fold_in(jax.random.fold_in(rng, 6), dim), (parts,), jnp.float32, low / len(cuts), high / len(cuts))
        level = level * jnp.repeat(jnp.exp(steps), extent[dim] // parts).reshape((-1,) + (1,) * (len(extent) - 1 - dim))
    return level


def scatter_about(stream_key, shape, scale, limit, shards=(), kind=jnp.bfloat16):
    values = jax.random.normal(stream_key, shape, jnp.float32) * scale
    if len(shards) > 0:
        values = level_of(stream_key, shape, shards, -0.22, 0.18) * values
    return jnp.clip(values, min=-limit, max=limit).astype(kind)


def setup_inputs(seed: int = 0) -> dict:
    seeds = jax.random.split(jax.random.key(seed), 13)
    tokens = scatter_about(seeds[0], (TOKENS, MODEL_WIDTH), 1.0, 6.0, ((0, 16), (1, 8)))
    cotangent = scatter_about(seeds[1], (TOKENS, MODEL_WIDTH), 1.0, 6.0, ((0, 16), (1, 8)), jnp.float32)
    attend_weight = scatter_about(seeds[2], (LAYERS, MODEL_WIDTH, 3, MODEL_WIDTH), MODEL_WIDTH ** -0.5, 0.1875, ((1, 4), (3, 8)))
    output_weight = scatter_about(seeds[3], (LAYERS, MODEL_WIDTH, MODEL_WIDTH), (max(MODEL_WIDTH * 16 // SEQ, 1)) ** -0.5, 1.5, ((1, 8), (2, 4)))
    up_weight = scatter_about(seeds[4], (LAYERS, MODEL_WIDTH, FF), MODEL_WIDTH ** -0.5, 0.1875, ((1, 4), (2, 8)))
    down_weight = scatter_about(seeds[5], (LAYERS, FF, MODEL_WIDTH), FF ** -0.5, 0.09375, ((1, 8), (2, 4)))
    norm_gain = jnp.clip(1.0 + 0.18 * jax.random.normal(seeds[6], (LAYERS, 2, MODEL_WIDTH), jnp.float32), 0.1, 1.9)
    norm_shift = scatter_about(seeds[7], (LAYERS, 2, MODEL_WIDTH), 0.3, 2.0, ((2, 8),), jnp.float32)
    attend_bias = scatter_about(seeds[8], (LAYERS, 2, MODEL_WIDTH), 0.5, 3.0, ((2, 8),), jnp.float32)
    branch_bias = scatter_about(seeds[9], (LAYERS, 2, MODEL_WIDTH), 0.3, 2.0, ((2, 8),), jnp.float32)
    layer_scale = jnp.clip(jnp.exp(math.log(1.5) - 1.60943787 * jax.random.uniform(seeds[10], (LAYERS, 2, MODEL_WIDTH), jnp.float32) ** level_of(seeds[10], (LAYERS, 2, MODEL_WIDTH), ((2, 8),), -0.2, 0.2)), 0.3, 1.5)
    hidden_bias = scatter_about(seeds[11], (LAYERS, FF), 0.5, 3.0, ((1, 8),), jnp.float32)
    return dict(tokens=tokens, cotangent=cotangent, attend_weight=attend_weight, output_weight=output_weight, up_weight=up_weight, down_weight=down_weight, norm_gain=norm_gain, norm_shift=norm_shift, attend_bias=attend_bias, branch_bias=branch_bias, layer_scale=layer_scale, hidden_bias=hidden_bias)


EPS = 1e-06
ROOT_HALF = 0.7071067811865476
HIGHEST = lax.Precision.HIGHEST

@jax.custom_vjp
def low(v):
    return lax.optimization_barrier(v.astype(jnp.bfloat16)).astype(jnp.float32)

@jax.custom_vjp
def low_back(v):
    return v

def low_keep(v):
    return (low(v), None)

def low_pass(kept, gradient_value):
    return (gradient_value,)

def back_keep(v):
    return (v, None)

def back_low(kept, gradient_value):
    return (low(gradient_value),)
low.defvjp(low_keep, low_pass)
low_back.defvjp(back_keep, back_low)

def gelu_value(value):
    return 0.5 * value * (1.0 + lax.erf(value * ROOT_HALF))

def layer_norm(residual_input, gain, shift):
    row_mean = lax.optimization_barrier(jnp.mean(residual_input, axis=1, keepdims=True))
    meansq = lax.optimization_barrier(jnp.mean(residual_input * residual_input, axis=1, keepdims=True))
    return (residual_input - row_mean) * lax.rsqrt(meansq - row_mean * row_mean + EPS) * gain + shift

def attend_image(packed):
    scale = HEAD_DIM ** (-0.5)
    query, key, value = (packed[:, 0], packed[:, 1], packed[:, 2])
    scores = low_back(jnp.einsum('qhd,khd->hqk', query, key, precision=HIGHEST) * scale)
    top = lax.optimization_barrier(jnp.max(scores, axis=-1, keepdims=True))
    expd = jnp.exp(scores - top)
    probs = expd / lax.optimization_barrier(jnp.sum(expd, axis=-1, keepdims=True))
    return jnp.einsum('hqk,khd->qhd', low(probs), value, precision=HIGHEST)

def one_layer(residual_input, attend_w, output_w, up_w, down_w, gain, shift, abias, bbias, scales, hbias):
    rows = residual_input.shape[0]
    normed = low(layer_norm(residual_input, gain[0], shift[0]))
    packed = jnp.einsum('nd,dkc->nkc', normed, attend_w, precision=HIGHEST)
    bias = jnp.stack([abias[0], jnp.zeros_like(abias[0]), abias[1]])
    packed = low_back(low(packed + bias))
    heads = MODEL_WIDTH // HEAD_DIM
    blocks = packed.reshape(rows // SEQ, SEQ, 3, heads, HEAD_DIM)
    att = lax.map(jax.checkpoint(attend_image), blocks).reshape(rows, MODEL_WIDTH)
    att = low_back(low(att))
    branch = low_back(jnp.dot(att, output_w, precision=HIGHEST) + bbias[0])
    middle = residual_input + scales[0] * branch
    normed = low(layer_norm(middle, gain[1], shift[1]))
    hidden = low_back(jnp.dot(normed, up_w, precision=HIGHEST) + hbias)
    active = low(gelu_value(hidden))
    branch = low_back(jnp.dot(active, down_w, precision=HIGHEST) + bbias[1])
    return middle + scales[1] * branch

def reference(tokens, cotangent, attend_weight, output_weight, up_weight, down_weight, norm_gain, norm_shift, attend_bias, branch_bias, layer_scale, hidden_bias):
    floats = tuple((item.astype(jnp.float32) for item in (tokens, attend_weight, output_weight, up_weight, down_weight, norm_gain, norm_shift, attend_bias, branch_bias, layer_scale, hidden_bias)))

    def forward(residual_input, attend_w, output_w, up_w, down_w, gain, shift, abias, bbias, scales, hbias):
        for layer in range(LAYERS):
            residual_input = one_layer(residual_input, attend_w[layer], output_w[layer], up_w[layer], down_w[layer], gain[layer], shift[layer], abias[layer], bbias[layer], scales[layer], hbias[layer])
        return residual_input
    result, pullback = jax.vjp(forward, *floats)
    grads = pullback(cotangent.astype(jnp.float32))
    return (result, grads[0], grads[1], grads[2], grads[3], grads[4], grads[5], grads[6], grads[7], grads[8], grads[9], grads[10])
```

```python
import functools

import jax
import jax.numpy as jnp
from jax import lax
from jax.experimental import pallas as pl
from jax.experimental.pallas import tpu as pltpu
from jax.sharding import Mesh, PartitionSpec as P

WIDTH = 1024
HALF = WIDTH // 2
SEQ = 1025
LAYERS = 2
REAL = 128
ROWS = 144
OWN = 4 * ROWS
KEYS = 2 * OWN
QROWS = 640
CHUNKS = ((0, 256), (256, 256), (512, 128))
EPS = 1e-06
ROOT_HALF = 0.7071067811865476
INV_ROOT_TWO_PI = 0.3989422804014327
MESH = pl.DeviceIdType.MESH
AXES = ("x", "yl", "co", "yh", "z")
VM = pl.BlockSpec(memory_space=pltpu.VMEM)
F32 = jnp.float32
BF16 = jnp.bfloat16


def gelu_value(value):
    return 0.5 * value * (1.0 + lax.erf(value * ROOT_HALF))


def gelu_slope(value):
    return 0.5 * (1.0 + lax.erf(value * ROOT_HALF)) + value * INV_ROOT_TWO_PI * jnp.exp(
        -0.5 * value * value
    )


def dot_nt(left, right):
    return lax.dot_general(left, right, (((1,), (1,)), ((), ())), preferred_element_type=F32)


def dot_tn(left, right):
    return lax.dot_general(left, right, (((0,), (0,)), ((), ())), preferred_element_type=F32)


def dot_nn(left, right):
    return jnp.dot(left, right, preferred_element_type=F32)


def device(**moved):
    return tuple(moved[a] if a in moved else lax.axis_index(a) for a in AXES)


def remote(src, dst, send, recv, to):
    return pltpu.make_async_remote_copy(
        src_ref=src, dst_ref=dst, send_sem=send, recv_sem=recv, device_id=to, device_id_type=MESH
    )


def signal(to):
    pl.semaphore_signal(
        pltpu.get_barrier_semaphore(), inc=1, device_id=to, device_id_type=MESH
    )


def ring():
    z = lax.axis_index("z")
    right, left, across = lax.rem(z + 1, 4), lax.rem(z + 3, 4), lax.rem(z + 2, 4)
    return z, right, left, across, device(z=right), device(z=left)


def greet_ring():
    _, _, _, _, to_right, to_left = ring()
    signal(to_right)
    signal(to_left)
    pl.semaphore_wait(pltpu.get_barrier_semaphore(), 2)


A = pl.ds(0, HALF)
B = pl.ds(HALF, HALF)


def ring_reduce(part, fin, relay, stage, send, recv):
    z, right, left, across, to_right, to_left = ring()

    def copy(i, src, dst, to):
        return remote(src, dst, send.at[i], recv.at[i], to)

    far_r = copy(0, part.at[across, :, A], relay.at[0], to_right)
    far_l = copy(1, part.at[across, :, B], relay.at[1], to_left)
    near_r = copy(2, part.at[right, :, B], fin.at[0, :, B], to_right)
    near_l = copy(3, part.at[left, :, A], fin.at[1, :, A], to_left)
    for c in (far_r, far_l, near_r, near_l):
        c.start()
    far_r.wait_recv()
    stage[0] = (part[right, :, A].astype(F32) + relay[0].astype(F32)).astype(BF16)
    sum_r = copy(4, stage.at[0], fin.at[0, :, A], to_right)
    sum_r.start()
    far_l.wait_recv()
    stage[1] = (part[left, :, B].astype(F32) + relay[1].astype(F32)).astype(BF16)
    sum_l = copy(5, stage.at[1], fin.at[1, :, B], to_left)
    sum_l.start()
    for c in (near_r, near_l, sum_r, sum_l):
        c.wait_recv()
    total = part[z].astype(F32) + fin[0].astype(F32) + fin[1].astype(F32)
    return total, (far_r, far_l, near_r, near_l, sum_r, sum_l)


def ring_gather(out, send, recv, base):
    z, right, left, across, to_right, to_left = ring()

    def copy(i, owner, cols, to):
        ref = out.at[owner, :, cols]
        return remote(ref, ref, send.at[base + i], recv.at[base + i], to)

    def lands(i, owner, cols):
        copy(i, owner, cols, to_right).wait_recv()

    first = (
        copy(0, z, A, to_right),
        copy(1, z, B, to_left),
        copy(2, z, B, to_right),
        copy(3, z, A, to_left),
    )
    for c in first:
        c.start()
    lands(0, left, A)
    on_r = copy(4, left, A, to_right)
    on_r.start()
    lands(1, right, B)
    on_l = copy(5, right, B, to_left)
    on_l.start()
    lands(2, left, B)
    lands(3, right, A)
    lands(4, across, A)
    lands(5, across, B)
    return first + (on_r, on_l)


def norm_of(value):
    mean = jnp.mean(value, axis=1, keepdims=True)
    meansq = jnp.mean(value * value, axis=1, keepdims=True)
    rstd = lax.rsqrt(meansq - mean * mean + EPS)
    return (value - mean) * rstd, rstd


def norm_back(grad, value, gain):
    hat, rstd = norm_of(value)
    e = grad * gain
    return (
        rstd
        * (
            e
            - jnp.mean(e, axis=1, keepdims=True)
            - hat * jnp.mean(e * hat, axis=1, keepdims=True)
        ),
        jnp.sum(grad * hat, axis=0, keepdims=True),
        jnp.sum(grad, axis=0, keepdims=True),
    )


RING_SCRATCH = [
    pltpu.VMEM((2, ROWS, WIDTH), BF16),
    pltpu.VMEM((2, ROWS, HALF), BF16),
    pltpu.VMEM((2, ROWS, HALF), BF16),
    pltpu.SemaphoreType.DMA((12,)),
    pltpu.SemaphoreType.DMA((12,)),
]
GAIN, SHIFT, BRANCH, SCALE = 0, 4, 8, 12


def call(kernel, outs, scratch, ident, inputs, **more):
    return pl.pallas_call(
        kernel,
        out_shape=[jax.ShapeDtypeStruct(s, d) for s, d in outs],
        in_specs=[VM] * len(inputs),
        out_specs=[VM] * len(outs),
        scratch_shapes=scratch,
        compiler_params=pltpu.CompilerParams(
            collective_id=ident, has_side_effects=True, vmem_limit_bytes=24 * 2**20
        ),
        **more,
    )(*inputs)


SHARD = (ROWS, WIDTH)
ALL = (4, ROWS, WIDTH)


def forward_kernel(
    at, part, x, table, branch_out, x_out, n_out, fin, relay, stage, send, recv
):
    greet_ring()
    total, sent = ring_reduce(part, fin, relay, stage, send, recv)
    bias, scale, gain, shift = (table[r : r + 1, :] for r in at)
    branch = total + bias
    x_new = x[...] + scale * branch
    branch_out[...] = branch
    x_out[...] = x_new
    hat, _ = norm_of(x_new)
    n_out[lax.axis_index("z")] = (hat * gain + shift).astype(BF16)
    for c in sent + ring_gather(n_out, send, recv, 6):
        c.wait_send()


def forward_step(part, x, table, at, ident):
    return call(
        functools.partial(forward_kernel, at),
        [(SHARD, F32), (SHARD, F32), (ALL, BF16)],
        RING_SCRATCH,
        ident,
        (part, x, table),
    )


def turn_kernel(at, part, x, cot, table, x_out, sums, d_out, fin, relay, stage, send, recv):
    greet_ring()
    bias, scale = (table[r : r + 1, :] for r in at)
    df = (cot[...] * scale).astype(BF16)
    d_out[lax.axis_index("z")] = df
    total, sent = ring_reduce(part, fin, relay, stage, send, recv)
    branch = total + bias
    x_out[...] = x[...] + scale * branch
    sums[...] = jnp.zeros_like(sums)
    sums[2:3, :] = jnp.sum(cot[...] * branch, axis=0, keepdims=True)
    sums[3:4, :] = jnp.sum(df.astype(F32), axis=0, keepdims=True)
    for c in sent + ring_gather(d_out, send, recv, 6):
        c.wait_send()


def turn_step(part, x, cot, table, at, ident):
    return call(
        functools.partial(turn_kernel, at),
        [(SHARD, F32), ((8, WIDTH), F32), (ALL, BF16)],
        RING_SCRATCH,
        ident,
        (part, x, cot, table),
    )


def backward_kernel(
    at, part, value, dx, branch, table, dx_out, sums, d_out, fin, relay, stage, send, recv
):
    greet_ring()
    total, sent = ring_reduce(part, fin, relay, stage, send, recv)
    gain, scale = (table[r : r + 1, :] for r in at)
    dr, gain_sum, shift_sum = norm_back(total, value[...], gain)
    dx_new = dx[...] + dr
    dx_out[...] = dx_new
    df = (dx_new * scale).astype(BF16)
    d_out[lax.axis_index("z")] = df
    sums[...] = jnp.zeros_like(sums)
    sums[0:1, :] = gain_sum
    sums[1:2, :] = shift_sum
    sums[2:3, :] = jnp.sum(dx_new * branch[...], axis=0, keepdims=True)
    sums[3:4, :] = jnp.sum(df.astype(F32), axis=0, keepdims=True)
    for c in sent + ring_gather(d_out, send, recv, 6):
        c.wait_send()


def backward_step(part, value, dx, branch, table, at, ident):
    return call(
        functools.partial(backward_kernel, at),
        [(SHARD, F32), ((8, WIDTH), F32), (ALL, BF16)],
        RING_SCRATCH,
        ident,
        (part, value, dx, branch, table),
    )


def cols(q):
    return pl.ds(q * 128, 128)


def first_kernel(
    pieces, pack, x_out, cot_out, n_out, pack_out, landed, psend, precv, ksend, krecv, send, recv
):
    x_, yl, co, yh, z = (lax.axis_index(a) for a in AXES)
    me = yh * 4 + z
    home = yh == co
    for j in range(8):
        to = device(yh=j // 4, z=j % 4)

        @pl.when(me != j)
        def _():
            signal(to)

        mine = home & (me == j)

        @pl.when(jnp.logical_not(mine))
        def _():
            signal(device(yh=j // 4, z=j % 4, co=yh))

    barrier = pltpu.get_barrier_semaphore()

    @pl.when(home)
    def _():
        pl.semaphore_wait(barrier, 14)

    @pl.when(jnp.logical_not(home))
    def _():
        pl.semaphore_wait(barrier, 15)

    def piece(j):
        src = pieces.at[:, pl.ds(j * REAL, ROWS), :]
        dst = landed.at[:, :, pl.ds(pl.multiple_of(me * 128, 128), 128)]
        to = device(yh=co, co=j // 4, z=j % 4)
        there = remote(src, dst, psend.at[j], precv.at[me], to)
        here = pltpu.make_async_copy(src, dst, precv.at[me])
        return there, here, home & (co * 4 + z == j)

    def note(j):
        return remote(
            pack, pack_out.at[me], ksend.at[j], krecv.at[me], device(yh=j // 4, z=j % 4)
        )

    pack_out[me] = pack[...]
    for j in range(8):
        there, here, own = piece(j)

        @pl.when(own)
        def _():
            here.start()

        @pl.when(jnp.logical_not(own))
        def _():
            there.start()

    for j in range(8):

        @pl.when(me != j)
        def _():
            note(j).start()

    for q in range(8):
        dst = landed.at[:, :, cols(q)]
        got = remote(dst, dst, psend.at[q], precv.at[q], device(z=lax.rem(z + 1, 4)))
        own = home & (me == q)

        @pl.when(own)
        def _():
            pltpu.make_async_copy(dst, dst, precv.at[q]).wait()

        @pl.when(jnp.logical_not(own))
        def _():
            got.wait_recv()

        @pl.when(me != q)
        def _():
            remote(
                pack, pack_out.at[q], ksend.at[q], krecv.at[q], device(z=lax.rem(z + 1, 4))
            ).wait_recv()

    value = landed[0].astype(F32)
    x_out[...] = value
    row = lax.broadcasted_iota(jnp.int32, (ROWS, 1), 0)
    last = jnp.where((co == 1) & (z == 3), REAL + 1, REAL)
    cot_out[...] = jnp.where(row < last, landed[1].astype(F32), 0.0)
    gain = jnp.concatenate([pack_out[q, GAIN : GAIN + 1, :] for q in range(8)], axis=1)
    shift = jnp.concatenate([pack_out[q, SHIFT : SHIFT + 1, :] for q in range(8)], axis=1)
    hat, _ = norm_of(value)
    n_out[z] = (hat * gain + shift).astype(BF16)
    for c in ring_gather(n_out, send, recv, 0):
        c.wait_send()
    for j in range(8):
        there, here, own = piece(j)

        @pl.when(jnp.logical_not(own))
        def _():
            there.wait_send()

        @pl.when(me != j)
        def _():
            note(j).wait_send()


def first_step(pieces, pack, ident):
    return call(
        first_kernel,
        [(SHARD, F32), (SHARD, F32), (ALL, BF16), ((8, 32, 128), F32)],
        [
            pltpu.VMEM((2, ROWS, WIDTH), BF16),
            pltpu.SemaphoreType.DMA((8,)),
            pltpu.SemaphoreType.DMA((8,)),
            pltpu.SemaphoreType.DMA((8,)),
            pltpu.SemaphoreType.DMA((8,)),
            pltpu.SemaphoreType.DMA((6,)),
            pltpu.SemaphoreType.DMA((6,)),
        ],
        ident,
        (pieces, pack),
    )


def last_kernel(
    at,
    part,
    value,
    dx,
    x_end,
    table,
    landed,
    sums,
    both,
    fin,
    relay,
    stage,
    send,
    recv,
    psend,
    precv,
):
    x_, yl, co, yh, z = (lax.axis_index(a) for a in AXES)
    shard = co * 4 + z
    home = yh == co
    greeted = 0
    _, _, _, _, to_right, to_left = ring()
    signal(to_right)
    signal(to_left)
    for s in range(8):

        @pl.when(jnp.logical_not(home & (shard == s)))
        def _():
            signal(device(yh=co, co=s // 4, z=s % 4))

    barrier = pltpu.get_barrier_semaphore()

    @pl.when(home)
    def _():
        pl.semaphore_wait(barrier, 9)

    @pl.when(jnp.logical_not(home))
    def _():
        pl.semaphore_wait(barrier, 10)

    def piece(k, q):
        src = both.at[k, :, cols(q)]
        dst = landed.at[k, shard]
        to = device(co=yh, yh=q // 4, z=q % 4)
        there = remote(src, dst, psend.at[k, q], precv.at[k, shard], to)
        here = pltpu.make_async_copy(src, dst, precv.at[k, shard])
        return there, here, home & (yh * 4 + z == q)

    def send_all(k):
        for q in range(8):
            there, here, own = piece(k, q)

            @pl.when(own)
            def _():
                here.start()

            @pl.when(jnp.logical_not(own))
            def _():
                there.start()

    both[0] = x_end[...].astype(BF16)
    send_all(0)
    total, sent = ring_reduce(part, fin, relay, stage, send, recv)
    (gain,) = (table[r : r + 1, :] for r in at)
    dr, gain_sum, shift_sum = norm_back(total, value[...], gain)
    both[1] = (dx[...] + dr).astype(BF16)
    send_all(1)
    sums[...] = jnp.zeros_like(sums)
    sums[0:1, :] = gain_sum
    sums[1:2, :] = shift_sum
    for c in sent:
        c.wait_send()
    for k in range(2):
        for s in range(8):
            dst = landed.at[k, s]
            got = remote(dst, dst, psend.at[k, s], precv.at[k, s], to_right)
            own = home & (shard == s)

            @pl.when(own)
            def _():
                pltpu.make_async_copy(dst, dst, precv.at[k, s]).wait()

            @pl.when(jnp.logical_not(own))
            def _():
                got.wait_recv()

            there, here, mine = piece(k, s)

            @pl.when(jnp.logical_not(mine))
            def _():
                there.wait_send()


def last_step(part, value, dx, x_end, table, at, ident):
    return call(
        functools.partial(last_kernel, at),
        [((2, 8, ROWS, 128), BF16), ((8, WIDTH), F32)],
        [pltpu.VMEM((2,) + SHARD, BF16)]
        + RING_SCRATCH
        + [pltpu.SemaphoreType.DMA((2, 8)), pltpu.SemaphoreType.DMA((2, 8))],
        ident,
        (part, value, dx, x_end, table),
    )


def swap_kernel(own, other, send, recv):
    co = lax.axis_index("co")
    to = device(co=1 - co)
    signal(to)
    pl.semaphore_wait(pltpu.get_barrier_semaphore(), 1)
    c = remote(own, other, send, recv, to)
    c.start()
    c.wait()


def swap(own, ident):
    return call(
        swap_kernel,
        [(own.shape, own.dtype)],
        [pltpu.SemaphoreType.DMA, pltpu.SemaphoreType.DMA],
        ident,
        (own,),
    )[0]


def lane_heads(value):
    lane = lax.broadcasted_iota(jnp.int32, value.shape, 1)
    zero = jnp.zeros_like(value)
    return jnp.where(lane < 64, value, zero), jnp.where(lane < 64, zero, value)


def attend_kernel(q, k, v, ko, vo, mask, att, lse, kall, vt, qpad, ot):
    kall[0:OWN] = k[...]
    kall[OWN:KEYS] = ko[...]
    vt[:, 0:OWN] = v[...].T
    vt[:, OWN:KEYS] = vo[...].T
    for hh, qh in enumerate(lane_heads(q[...] * 0.125)):
        qpad[hh, 0:OWN] = qh
        qpad[hh, OWN:QROWS] = jnp.zeros((QROWS - OWN, 128), BF16)
    lse[...] = jnp.zeros_like(lse)
    for hh in range(2):
        for lo, n in CHUNKS:
            bias = mask[...] if n == 128 else jnp.concatenate([mask[...]] * 2, axis=1)
            s = dot_nt(kall[...], qpad[hh, lo : lo + n]) + bias
            top = jnp.max(s, axis=0, keepdims=True)
            e = jnp.exp(s - top)
            total = jnp.sum(e, axis=0, keepdims=True)
            p = (e * (1.0 / total)).astype(BF16)
            ot[hh * 64 : hh * 64 + 64, lo : lo + n] = dot_nn(vt[hh * 64 : hh * 64 + 64], p)
            lse[hh : hh + 1, lo : lo + n] = top + jnp.log(total)
    att[...] = ot[...].T[0:OWN].astype(BF16)


def attend(qkv, other, mask):
    def block(f):
        return pl.BlockSpec((OWN, 128), lambda h: (0, f(h)))

    return pl.pallas_call(
        attend_kernel,
        grid=(2,),
        out_shape=[
            jax.ShapeDtypeStruct((OWN, 256), BF16),
            jax.ShapeDtypeStruct((2, 8, QROWS), F32),
        ],
        in_specs=[
            block(lambda h: 3 * h),
            block(lambda h: 3 * h + 1),
            block(lambda h: 3 * h + 2),
            block(lambda h: 2 * h),
            block(lambda h: 2 * h + 1),
            pl.BlockSpec((KEYS, 128), lambda h: (0, 0)),
        ],
        out_specs=[
            block(lambda h: h),
            pl.BlockSpec((None, 8, QROWS), lambda h: (h, 0, 0)),
        ],
        scratch_shapes=[
            pltpu.VMEM((KEYS, 128), BF16),
            pltpu.VMEM((128, KEYS), BF16),
            pltpu.VMEM((2, QROWS, 128), BF16),
            pltpu.VMEM((128, QROWS), F32),
        ],
        compiler_params=pltpu.CompilerParams(vmem_limit_bytes=40 * 2**20),
    )(qkv, qkv, qkv, other, other, mask)


def attend_back_kernel(
    q, k, v, ko, vo, do, lse, mask, dq, own, oth, kall, vall, kt, qpad, dpad, dqt, dk, dv
):
    kall[0:OWN] = k[...]
    kall[OWN:KEYS] = ko[...]
    vall[0:OWN] = v[...]
    vall[OWN:KEYS] = vo[...]
    kt[:, 0:OWN] = k[...].T
    kt[:, OWN:KEYS] = ko[...].T
    for hh, (qh, dh) in enumerate(zip(lane_heads(q[...] * 0.125), lane_heads(do[...]))):
        qpad[hh, 0:OWN] = qh
        qpad[hh, OWN:QROWS] = jnp.zeros((QROWS - OWN, 128), BF16)
        dpad[hh, 0:OWN] = dh
        dpad[hh, OWN:QROWS] = jnp.zeros((QROWS - OWN, 128), BF16)
    dk[...] = jnp.zeros_like(dk)
    dv[...] = jnp.zeros_like(dv)
    for hh in range(2):
        for lo, n in CHUNKS:
            bias = mask[...] if n == 128 else jnp.concatenate([mask[...]] * 2, axis=1)
            qc = qpad[hh, lo : lo + n]
            dc = dpad[hh, lo : lo + n]
            s = dot_nt(kall[...], qc) + bias
            p = jnp.exp(s - lse[hh : hh + 1, lo : lo + n])
            dp = dot_nt(vall[...], dc)
            delta = jnp.sum(p * dp, axis=0, keepdims=True)
            ds = (p * (dp - delta)).astype(BF16)
            dv[...] += dot_nn(p.astype(BF16), dc)
            dk[...] += dot_nn(ds, qc)
            dqt[hh * 64 : hh * 64 + 64, lo : lo + n] = dot_nn(kt[hh * 64 : hh * 64 + 64], ds)
    dq[...] = (dqt[...].T[0:OWN] * 0.125).astype(BF16)
    own[:, 0:128] = dk[0:OWN]
    own[:, 128:256] = dv[0:OWN]
    oth[:, 0:128] = dk[OWN:KEYS].astype(BF16)
    oth[:, 128:256] = dv[OWN:KEYS].astype(BF16)


def attend_back(qkv, other, datt, lse, mask):
    def block(f):
        return pl.BlockSpec((OWN, 128), lambda h: (0, f(h)))

    wide = pl.BlockSpec((OWN, 256), lambda h: (0, h))
    return pl.pallas_call(
        attend_back_kernel,
        grid=(2,),
        out_shape=[
            jax.ShapeDtypeStruct((OWN, 256), BF16),
            jax.ShapeDtypeStruct((OWN, 512), F32),
            jax.ShapeDtypeStruct((OWN, 512), BF16),
        ],
        in_specs=[
            block(lambda h: 3 * h),
            block(lambda h: 3 * h + 1),
            block(lambda h: 3 * h + 2),
            block(lambda h: 2 * h),
            block(lambda h: 2 * h + 1),
            block(lambda h: h),
            pl.BlockSpec((None, 8, QROWS), lambda h: (h, 0, 0)),
            pl.BlockSpec((KEYS, 128), lambda h: (0, 0)),
        ],
        out_specs=[block(lambda h: h), wide, wide],
        scratch_shapes=[
            pltpu.VMEM((KEYS, 128), BF16),
            pltpu.VMEM((KEYS, 128), BF16),
            pltpu.VMEM((128, KEYS), BF16),
            pltpu.VMEM((2, QROWS, 128), BF16),
            pltpu.VMEM((2, QROWS, 128), BF16),
            pltpu.VMEM((128, QROWS), F32),
            pltpu.VMEM((KEYS, 128), F32),
            pltpu.VMEM((KEYS, 128), F32),
        ],
        compiler_params=pltpu.CompilerParams(vmem_limit_bytes=48 * 2**20),
    )(qkv, qkv, qkv, other, other, datt, lse, mask)


ROW8 = ("yl", "co", "yh")


def gather_weight(shard, side):
    stacked = lax.all_gather(shard, ROW8).reshape((4, 2) + shard.shape)
    if side == 0:
        moved = stacked.transpose(0, 2, 1, 3)
        return moved.reshape(4 * shard.shape[0], 2 * shard.shape[1])
    return stacked.transpose(1, 2, 0, 3).reshape(2 * shard.shape[0], 4 * shard.shape[1])


def reduce_weight(part, side):
    rows, columns = part.shape
    if side == 0:
        blocks = part.reshape(4, rows // 4, 2, columns // 2).transpose(0, 2, 1, 3)
    else:
        blocks = part.reshape(2, rows // 2, 4, columns // 4).transpose(2, 0, 1, 3)
    blocks = blocks.reshape((8,) + blocks.shape[2:]).astype(BF16)
    mine = lax.psum_scatter(blocks, ROW8, scatter_dimension=0, tiled=False)
    return lax.psum(mine, "x").astype(F32)


def on_device(
    tokens,
    cotangent,
    attend_weight,
    output_weight,
    up_weight,
    down_weight,
    norm_gain,
    norm_shift,
    attend_bias,
    branch_bias,
    layer_scale,
    hidden_bias,
):
    co, yh, z = (lax.axis_index(a) for a in ("co", "yh", "z"))
    weights = [
        (
            gather_weight(attend_weight[l].reshape(256, 384), 0),
            gather_weight(output_weight[l], 1),
            gather_weight(up_weight[l], 0),
            gather_weight(down_weight[l], 1),
        )
        for l in range(LAYERS)
    ]
    pieces = jnp.pad(jnp.stack([tokens, cotangent.astype(BF16)]), ((0, 0), (0, 15), (0, 0)))
    pack = jnp.concatenate(
        [
            norm_gain.reshape(4, 128),
            norm_shift.reshape(4, 128),
            branch_bias.reshape(4, 128),
            layer_scale.reshape(4, 128),
            attend_bias.reshape(4, 128),
            hidden_bias.reshape(8, 128),
            jnp.zeros((4, 128), F32),
        ]
    )
    ident = iter(range(40))
    x, cot, n_all, packs = first_step(pieces, pack, next(ident))
    table = packs[:, 0:16].transpose(1, 0, 2).reshape(16, WIDTH)
    here = jnp.stack(
        [
            lax.dynamic_index_in_dim(packs, z, keepdims=False),
            lax.dynamic_index_in_dim(packs, z + 4, keepdims=False),
        ]
    )
    row = jnp.arange(OWN)
    block, inside = row // ROWS, row % ROWS

    def hidden_keys(half):
        real = (inside < REAL) | ((inside == REAL) & (block == 3) & (half == 1))
        return jnp.where(real, 0.0, -1e30).astype(F32)

    mask = jnp.concatenate([hidden_keys(co), hidden_keys(1 - co)])
    mask = jnp.broadcast_to(mask[:, None], (KEYS, 128))

    saved = []
    for l in range(LAYERS):
        wqkv, wout, wup, wdown = weights[l]
        ab = here[:, 16 + 2 * l : 18 + 2 * l]
        qkv_bias = jnp.concatenate(
            [ab[0, 0], jnp.zeros(128), ab[0, 1], ab[1, 0], jnp.zeros(128), ab[1, 1]]
        )
        n1 = n_all.reshape(OWN, WIDTH)
        qkv = (dot_nn(n1, wqkv) + qkv_bias).astype(BF16)
        kv = jnp.concatenate([qkv[:, 128:384], qkv[:, 512:768]], axis=1)
        other = swap(kv, next(ident))
        att, lse = attend(qkv, other, mask)
        part = dot_nn(att, wout).astype(BF16).reshape(ALL)
        at = (BRANCH + 2 * l, SCALE + 2 * l, GAIN + 2 * l + 1, SHIFT + 2 * l + 1)
        a, m, n_all = forward_step(part, x, table, at, next(ident))
        n2 = n_all.reshape(OWN, WIDTH)
        hb = here[:, 20 + 4 * l : 24 + 4 * l].reshape(WIDTH)
        u = dot_nn(n2, wup) + hb
        g = gelu_value(u).astype(BF16)
        part = dot_nn(g, wdown).astype(BF16).reshape(ALL)
        saved.append([x, n1, qkv, other, att, lse, a, m, n2, u, g])
        if l + 1 < LAYERS:
            at = (BRANCH + 2 * l + 1, SCALE + 2 * l + 1, GAIN + 2 * l + 2, SHIFT + 2 * l + 2)
            f, x, n_all = forward_step(part, m, table, at, next(ident))
            saved[l].append(f)
        else:
            at = (BRANCH + 2 * l + 1, SCALE + 2 * l + 1)
            x_end, sums, d_all = turn_step(part, m, cot, table, at, next(ident))

    gain_sums, shift_sums, scale_sums, branch_sums = ([None] * 4 for _ in range(4))
    scale_sums[3], branch_sums[3] = sums[2], sums[3]
    hidden_sums, qkv_sums, grads = [None] * LAYERS, [None] * LAYERS, [None] * LAYERS
    dx = cot
    for l in reversed(range(LAYERS)):
        wqkv, wout, wup, wdown = weights[l]
        x, n1, qkv, other, att, lse, a, m, n2, u, g = saved[l][:11]
        df = d_all.reshape(OWN, WIDTH)
        du = (dot_nt(df, wdown) * gelu_slope(u)).astype(BF16)
        part = dot_nt(du, wup).astype(BF16).reshape(ALL)
        hidden_sums[l] = jnp.sum(du.astype(F32), axis=0)
        at = (GAIN + 2 * l + 1, SCALE + 2 * l)
        dm, sums, d_all = backward_step(part, m, dx, a, table, at, next(ident))
        gain_sums[2 * l + 1], shift_sums[2 * l + 1] = sums[0], sums[1]
        scale_sums[2 * l], branch_sums[2 * l] = sums[2], sums[3]
        down_grad = reduce_weight(dot_tn(g, df), 1)
        up_grad = reduce_weight(dot_tn(n2, du), 0)
        da = d_all.reshape(OWN, WIDTH)
        datt = dot_nt(da, wout).astype(BF16)
        output_grad = reduce_weight(dot_tn(att, da), 1)
        dq, own, oth = attend_back(qkv, other, datt, lse, mask)
        dkv = (own + swap(oth, next(ident)).astype(F32)).astype(BF16)
        dqkv = jnp.concatenate(
            [dq[:, 0:128], dkv[:, 0:256], dq[:, 128:256], dkv[:, 256:512]], axis=1
        )
        qkv_sums[l] = jnp.sum(dqkv.astype(F32), axis=0)
        part = dot_nt(dqkv, wqkv).astype(BF16).reshape(ALL)
        attend_grad = reduce_weight(dot_tn(n1, dqkv), 0)
        if l > 0:
            at = (GAIN + 2 * l, SCALE + 2 * l - 1)
            dx, sums, d_all = backward_step(
                part, x, dm, saved[l - 1][11], table, at, next(ident)
            )
            scale_sums[2 * l - 1], branch_sums[2 * l - 1] = sums[2], sums[3]
        else:
            landed, sums = last_step(part, x, dm, x_end, table, (GAIN + 2 * l,), next(ident))
        gain_sums[2 * l], shift_sums[2 * l] = sums[0], sums[1]
        grads[l] = (attend_grad.reshape(256, 3, 128), output_grad, up_grad, down_grad)

    everywhere = jnp.stack(gain_sums + shift_sums + branch_sums + scale_sums)
    everywhere = lax.psum(everywhere, "z")
    everywhere = everywhere.reshape(16, 2, 4, 128)
    everywhere = lax.dynamic_index_in_dim(everywhere, z, axis=2, keepdims=False)
    ringed = jnp.concatenate(
        [
            everywhere.transpose(1, 0, 2),
            jnp.stack(qkv_sums).reshape(2, 2, 3, 128).transpose(1, 0, 2, 3).reshape(2, 6, 128),
            jnp.stack(hidden_sums).reshape(2, 2, 4, 128).transpose(1, 0, 2, 3).reshape(2, 8, 128),
        ],
        axis=1,
    )
    small = lax.psum(ringed, ("x", "yl", "co", "yh"))
    small = lax.dynamic_index_in_dim(small, yh, keepdims=False)
    bias_grad = small[16:22].reshape(2, 3, 128)[:, 0::2]

    def rows(k):
        return jnp.concatenate(
            [landed[k, 0:7, 0:REAL].reshape(7 * REAL, 128), landed[k, 7, 0 : REAL + 1]]
        ).astype(F32)

    return (
        rows(0),
        rows(1),
        jnp.stack([grads[l][0] for l in range(LAYERS)]),
        jnp.stack([grads[l][1] for l in range(LAYERS)]),
        jnp.stack([grads[l][2] for l in range(LAYERS)]),
        jnp.stack([grads[l][3] for l in range(LAYERS)]),
        small[0:4].reshape(2, 2, 128),
        small[4:8].reshape(2, 2, 128),
        bias_grad,
        small[8:12].reshape(2, 2, 128),
        small[12:16].reshape(2, 2, 128),
        small[22:30].reshape(2, 512),
    )


def solution(mesh):
    split = Mesh(mesh.devices.reshape(4, 2, 2, 2, 4), AXES)
    images, row, col = ("x", "yl", "co"), ("yl", "co"), ("yh", "z")
    placed = (
        P(images, col),
        P(images, col),
        P(None, row, None, col),
        P(None, col, row),
        P(None, row, col),
        P(None, col, row),
        P(None, None, col),
        P(None, None, col),
        P(None, None, col),
        P(None, None, col),
        P(None, None, col),
        P(None, col),
    )
    return jax.shard_map(
        on_device, mesh=split, in_specs=placed, out_specs=placed, check_vma=False
    )
```

```python
import jax
import jax.numpy as jnp
from jax import lax
from jax.experimental import pallas as pl
from jax.experimental.pallas import tpu as pltpu
from jax.sharding import Mesh, PartitionSpec as P

WIDTH = 1024
HALF = WIDTH // 2
SEQ = 1025
LAYERS = 2
REAL = 128
ROWS = 144
OWN = 4 * ROWS
KEYS = 2 * OWN
QROWS = 640
CHUNKS = ((0, 256), (256, 256), (512, 128))
EPS = 1e-06
ROOT_HALF = 0.7071067811865476
INV_ROOT_TWO_PI = 0.3989422804014327
MESH = pl.DeviceIdType.MESH
AXES = ("x", "yl", "co", "yh", "z")
VM = pl.BlockSpec(memory_space=pltpu.VMEM)
ANY = pl.BlockSpec(memory_space=pl.ANY)
F32 = jnp.float32
BF16 = jnp.bfloat16


def gelu_value(value):
    return 0.5 * value * (1.0 + lax.erf(value * ROOT_HALF))


def gelu_slope(value):
    return 0.5 * (1.0 + lax.erf(value * ROOT_HALF)) + value * INV_ROOT_TWO_PI * jnp.exp(
        -0.5 * value * value
    )


def dot_nt(left, right):
    return lax.dot_general(left, right, (((1,), (1,)), ((), ())), preferred_element_type=F32)


def dot_tn(left, right):
    return lax.dot_general(left, right, (((0,), (0,)), ((), ())), preferred_element_type=F32)


def dot_nn(left, right):
    return jnp.dot(left, right, preferred_element_type=F32)


def device(**moved):
    return tuple(moved[a] if a in moved else lax.axis_index(a) for a in AXES)


def remote(src, dst, send, recv, to):
    return pltpu.make_async_remote_copy(
        src_ref=src, dst_ref=dst, send_sem=send, recv_sem=recv, device_id=to, device_id_type=MESH
    )


def signal(to):
    pl.semaphore_signal(
        pltpu.get_barrier_semaphore(), inc=1, device_id=to, device_id_type=MESH
    )


class Ring:
    def __init__(self, axis):
        self.axis = axis
        if axis == "y":
            self.me = lax.axis_index("yh") * 2 + lax.axis_index("yl")
        else:
            self.me = lax.axis_index(axis)
        self.right = lax.rem(self.me + 1, 4)
        self.left = lax.rem(self.me + 3, 4)
        self.across = lax.rem(self.me + 2, 4)
        self.to_right, self.to_left = self.at(self.right), self.at(self.left)

    def at(self, index):
        if self.axis == "y":
            return device(yh=index // 2, yl=lax.rem(index, 2))
        return device(**{self.axis: index})


def greet(links, more=0, home=None):
    count = more
    for link in links:
        if link == "core":
            signal(device(co=1 - lax.axis_index("co")))
            count += 1
        else:
            ring = Ring(link)
            signal(ring.to_right)
            signal(ring.to_left)
            count += 2
    barrier = pltpu.get_barrier_semaphore()
    if home is None:
        pl.semaphore_wait(barrier, count)
    else:

        @pl.when(home)
        def _():
            pl.semaphore_wait(barrier, count + 7)

        @pl.when(jnp.logical_not(home))
        def _():
            pl.semaphore_wait(barrier, count + 8)


def in_turns(jobs):
    jobs = list(jobs)
    while jobs:
        for job in list(jobs):
            try:
                next(job)
            except StopIteration:
                jobs.remove(job)


def by_columns(ref, lead, half):
    return ref.at[lead, :, pl.ds(half * HALF, HALF)]


def by_rows(ref, lead, half):
    rows = ref.shape[1] // 2
    return ref.at[lead, pl.ds(half * rows, rows), :]


def reduce_on(ring, half, part, fin, relay, stage, send, recv, sent):
    def copy(i, src, dst, to):
        c = remote(src, dst, send.at[i], recv.at[i], to)
        c.start()
        sent.append(c)
        return c

    far_r = copy(0, half(part, ring.across, 0), relay.at[0], ring.to_right)
    far_l = copy(1, half(part, ring.across, 1), relay.at[1], ring.to_left)
    near_r = copy(2, half(part, ring.right, 1), half(fin, 0, 1), ring.to_right)
    near_l = copy(3, half(part, ring.left, 0), half(fin, 1, 0), ring.to_left)
    yield
    far_r.wait_recv()
    stage[0] = (half(part, ring.right, 0)[...].astype(F32) + relay[0].astype(F32)).astype(BF16)
    sum_r = copy(4, stage.at[0], half(fin, 0, 0), ring.to_right)
    far_l.wait_recv()
    stage[1] = (half(part, ring.left, 1)[...].astype(F32) + relay[1].astype(F32)).astype(BF16)
    sum_l = copy(5, stage.at[1], half(fin, 1, 1), ring.to_left)
    yield
    for c in (near_r, near_l, sum_r, sum_l):
        c.wait_recv()
    return part[ring.me].astype(F32) + fin[0].astype(F32) + fin[1].astype(F32)


def gather_on(ring, slot, own, send, recv, sent, landed=None):
    def copy(i, src, owner, half, to):
        return remote(src, slot(owner, half), send.at[i], recv.at[i], to)

    def go(*what):
        c = copy(*what)
        c.start()
        sent.append(c)

    def lands(i, owner, half):
        copy(i, slot(owner, half), owner, half, ring.to_right).wait_recv()

    go(0, own(0), ring.me, 0, ring.to_right)
    go(1, own(1), ring.me, 1, ring.to_left)
    go(2, own(1), ring.me, 1, ring.to_right)
    go(3, own(0), ring.me, 0, ring.to_left)
    yield
    lands(0, ring.left, 0)
    go(4, slot(ring.left, 0), ring.left, 0, ring.to_right)
    lands(1, ring.right, 1)
    go(5, slot(ring.right, 1), ring.right, 1, ring.to_left)
    yield
    lands(2, ring.left, 1)
    if landed is not None:
        landed(ring.left)
    lands(3, ring.right, 0)
    if landed is not None:
        landed(ring.right)
    yield
    lands(4, ring.across, 0)
    lands(5, ring.across, 1)
    if landed is not None:
        landed(ring.across)


def gather_slots(ring, out, half, send, recv, sent):
    def slot(owner, h):
        return half(out, owner, h)

    yield from gather_on(ring, slot, lambda h: slot(ring.me, h), send, recv, sent)


def sems(*counts):
    return [pltpu.SemaphoreType.DMA((c,)) for c in counts]


class GatherWeight:
    links = ("y", "core")

    def __init__(self, shards, layer, side):
        rows, columns = shards.shape[1:]
        self.layer, self.side, self.rows, self.columns = layer, side, rows, columns
        full = (4 * rows, 2 * columns) if side == 0 else (2 * rows, 4 * columns)
        self.inputs = [(shards, ANY)]
        self.outs = [(full, BF16, ANY)]
        self.scratch = sems(6, 6, 4, 4, 1)

    def run(self, inputs, outs, scratch, sent):
        (shards,), (out,) = inputs, outs
        send, recv, csend, crecv, local = scratch
        own = shards.at[self.layer]
        ring, co = Ring("y"), lax.axis_index("co")
        rows, columns = self.rows, self.columns

        def block(y, core, half=None):
            yh, r = y // 2, lax.rem(y, 2) * 2 + core
            down, along = (r, yh) if self.side == 0 else (yh, r)
            first, count = down * rows, rows
            if half is not None:
                count = rows // 2
                first = first + half * count
            return out.at[
                pl.ds(pl.multiple_of(first, 16), count),
                pl.ds(pl.multiple_of(along * columns, 128), columns),
            ]

        def to_core(i, src, y):
            c = remote(src, block(y, co), csend.at[i], crecv.at[i], device(co=1 - co))
            c.start()
            sent.append(c)

        keep = pltpu.make_async_copy(own, block(ring.me, co), local.at[0])
        keep.start()
        to_core(0, own, ring.me)
        numbers = iter((1, 2, 3))
        yield from gather_on(
            ring,
            lambda y, half: block(y, co, half),
            lambda half: own.at[pl.ds(half * (rows // 2), rows // 2), :],
            send,
            recv,
            sent,
            lambda y: to_core(next(numbers), block(y, co), y),
        )
        keep.wait()
        yield
        for i, y in enumerate((ring.me, ring.left, ring.right, ring.across)):
            there = block(y, 1 - co)
            remote(there, there, csend.at[i], crecv.at[i], device(co=1 - co)).wait_recv()


class ReduceWeight:
    links = ("y", "core")

    def __init__(self, part, side):
        rows, columns = part.shape
        rows, columns = (rows // 4, columns // 2) if side == 0 else (rows // 2, columns // 4)
        self.side, self.rows, self.columns = side, rows, columns
        self.inputs = [(part, VM)]
        self.outs = [((rows, columns), BF16, VM)]
        self.scratch = [
            pltpu.VMEM((4, rows, columns), BF16),
            pltpu.VMEM((4, rows, columns), BF16),
            pltpu.VMEM((2, rows, columns), BF16),
            pltpu.VMEM((2, rows // 2, columns), BF16),
            pltpu.VMEM((2, rows // 2, columns), BF16),
        ] + sems(4, 4, 6, 6)

    def run(self, inputs, outs, scratch, sent):
        total = yield from self.total(inputs[0], scratch, sent)
        outs[0][...] = total.astype(BF16)

    def total(self, part, scratch, sent):
        got, pair, fin, relay, stage, csend, crecv, send, recv = scratch
        co = lax.axis_index("co")
        rows, columns = self.rows, self.columns

        def block(y, core):
            yh, r = y // 2, (y % 2) * 2 + core
            down, along = (r, yh) if self.side == 0 else (yh, r)
            return part.at[
                pl.ds(pl.multiple_of(down * rows, 16), rows),
                pl.ds(pl.multiple_of(along * columns, 128), columns),
            ]

        copies = []
        for y in range(4):
            c = remote(
                block(y, 1 - co), got.at[y], csend.at[y], crecv.at[y], device(co=1 - co)
            )
            c.start()
            copies.append(c)
        sent.extend(copies)
        yield
        for y in range(4):
            copies[y].wait_recv()
            pair[y] = (block(y, co)[...].astype(F32) + got[y].astype(F32)).astype(BF16)
        total = yield from reduce_on(
            Ring("y"), by_rows, pair, fin, relay, stage, send, recv, sent
        )
        return total


class SumBlock:
    links = ("x",)

    def __init__(self, shape, block=None):
        rows, columns = shape
        self.shape, self.rows = shape, rows // 4
        self.inputs = [] if block is None else [(block, VM)]
        self.outs = [(shape, F32, VM)]
        quarter = (rows // 4, columns)
        self.scratch = [
            pltpu.VMEM((4,) + quarter, BF16),
            pltpu.VMEM((4,) + quarter, BF16),
            pltpu.VMEM((2,) + quarter, BF16),
            pltpu.VMEM((2, rows // 8, columns), BF16),
            pltpu.VMEM((2, rows // 8, columns), BF16),
        ] + sems(6, 6, 6, 6)

    def run(self, inputs, outs, scratch, sent):
        yield from self.total(inputs[0][...], outs[0], scratch, sent)

    def total(self, value, out, scratch, sent):
        part, every, fin, relay, stage, send, recv, gsend, grecv = scratch
        ring = Ring("x")
        for i in range(4):
            part[i] = value[i * self.rows : (i + 1) * self.rows].astype(BF16)
        mine = yield from reduce_on(ring, by_rows, part, fin, relay, stage, send, recv, sent)
        every[ring.me] = mine.astype(BF16)
        yield from gather_slots(ring, every, by_rows, gsend, grecv, sent)
        for i in range(4):
            out[i * self.rows : (i + 1) * self.rows] = every[i].astype(F32)


class ReduceSum:
    links = ("y", "core", "x")

    def __init__(self, part, side):
        self.first = ReduceWeight(part, side)
        self.second = SumBlock((self.first.rows, self.first.columns))
        self.inputs, self.outs = self.first.inputs, self.second.outs
        self.scratch = self.first.scratch + self.second.scratch

    def run(self, inputs, outs, scratch, sent):
        n = len(self.first.scratch)
        total = yield from self.first.total(inputs[0], scratch[:n], sent)
        yield from self.second.total(total, outs[0], scratch[n:], sent)


class Pieces:
    links = ()

    def __init__(self, source):
        self.inputs = [(source, VM)]
        self.outs = [(SHARD, BF16, VM)]
        self.scratch = sems(8, 8)

    def run(self, inputs, outs, scratch, sent):
        (source,), (landed,), (send, recv) = inputs, outs, scratch
        co, yh, z = (lax.axis_index(a) for a in ("co", "yh", "z"))
        me, home = yh * 4 + z, yh == co

        def piece(j):
            src = source.at[pl.ds(j * REAL, ROWS), :]
            dst = landed.at[:, pl.ds(pl.multiple_of(me * 128, 128), 128)]
            to = device(yh=co, co=j // 4, z=j % 4)
            there = remote(src, dst, send.at[j], recv.at[me], to)
            return there, pltpu.make_async_copy(src, dst, recv.at[me]), home & (co * 4 + z == j)

        for j in range(8):
            there, here, own = piece(j)

            @pl.when(own)
            def _():
                here.start()

            @pl.when(jnp.logical_not(own))
            def _():
                there.start()

        yield
        for q in range(8):
            dst = landed.at[:, pl.ds(q * 128, 128)]
            own = home & (me == q)

            @pl.when(own)
            def _():
                pltpu.make_async_copy(dst, dst, recv.at[q]).wait()

            @pl.when(jnp.logical_not(own))
            def _():
                remote(dst, dst, send.at[q], recv.at[q], Ring("z").to_right).wait_recv()

        for j in range(8):
            there, here, own = piece(j)

            @pl.when(jnp.logical_not(own))
            def _():
                there.wait_send()


def greet_pieces():
    co, yh, z = (lax.axis_index(a) for a in ("co", "yh", "z"))
    home = yh == co
    for j in range(8):

        @pl.when(jnp.logical_not(home & (yh * 4 + z == j)))
        def _():
            signal(device(yh=j // 4, z=j % 4, co=yh))

    return home


def norm_of(value):
    mean = jnp.mean(value, axis=1, keepdims=True)
    meansq = jnp.mean(value * value, axis=1, keepdims=True)
    rstd = lax.rsqrt(meansq - mean * mean + EPS)
    return (value - mean) * rstd, rstd


def norm_back(grad, value, gain):
    hat, rstd = norm_of(value)
    e = grad * gain
    return (
        rstd
        * (
            e
            - jnp.mean(e, axis=1, keepdims=True)
            - hat * jnp.mean(e * hat, axis=1, keepdims=True)
        ),
        jnp.sum(grad * hat, axis=0, keepdims=True),
        jnp.sum(grad, axis=0, keepdims=True),
    )


RING_SCRATCH = [
    pltpu.VMEM((2, ROWS, WIDTH), BF16),
    pltpu.VMEM((2, ROWS, HALF), BF16),
    pltpu.VMEM((2, ROWS, HALF), BF16),
] + sems(6, 6, 6, 6)
GAIN, SHIFT, BRANCH, SCALE = 0, 4, 8, 12
SHARD = (ROWS, WIDTH)
ALL = (4, ROWS, WIDTH)
SUMS = (8, WIDTH)


def call(main, inputs, outs, scratch, ident, riders=(), entry=None):
    inputs = [(a, VM) for a in inputs]
    outs = [(s, d, VM) for s, d in outs]
    jobs = [(inputs, outs, list(scratch))] + [(r.inputs, r.outs, r.scratch) for r in riders]
    links = {"z": None}
    for r in riders:
        links.update({link: None for link in r.links})
    runs = [main] + [r.run for r in riders]

    def kernel(*refs):
        refs, split = list(refs), []
        for kind in range(3):
            for job in jobs:
                split.append([refs.pop(0) for _ in job[kind]])
        n = len(jobs)
        if entry is None:
            greet(links)
        else:
            entry(links)
        sent = []
        in_turns(
            run(split[i], split[n + i], split[2 * n + i], sent) for i, run in enumerate(runs)
        )
        for c in sent:
            c.wait_send()

    results = pl.pallas_call(
        kernel,
        out_shape=[jax.ShapeDtypeStruct(o[0], o[1]) for job in jobs for o in job[1]],
        in_specs=[i[1] for job in jobs for i in job[0]],
        out_specs=[o[2] for job in jobs for o in job[1]],
        scratch_shapes=[s for job in jobs for s in job[2]],
        compiler_params=pltpu.CompilerParams(
            collective_id=ident, has_side_effects=True, vmem_limit_bytes=32 * 2**20
        ),
    )(*[i[0] for job in jobs for i in job[0]])
    n = len(outs)
    return results[:n], results[n:]


def forward_step(part, x, table, at, ident, riders=(), pieces=False):
    def main(inputs, outs, scratch, sent):
        (part, x, table), (branch_out, x_out, n_out) = inputs, outs
        ring = Ring("z")
        total = yield from reduce_on(ring, by_columns, part, *scratch[:5], sent)
        bias, scale, gain, shift = (table[r : r + 1, :] for r in at)
        branch = total + bias
        x_new = x[...] + scale * branch
        branch_out[...] = branch
        x_out[...] = x_new
        hat, _ = norm_of(x_new)
        n_out[ring.me] = (hat * gain + shift).astype(BF16)
        yield from gather_slots(ring, n_out, by_columns, *scratch[5:], sent)

    def entry(links):
        greet(links, home=greet_pieces())

    return call(
        main,
        (part, x, table),
        [(SHARD, F32), (SHARD, F32), (ALL, BF16)],
        RING_SCRATCH,
        ident,
        riders,
        entry if pieces else None,
    )


def turn_step(part, x, cot, table, at, ident, riders=()):
    def main(inputs, outs, scratch, sent):
        (part, x, cot, table), (x_out, sums, d_out) = inputs, outs
        ring = Ring("z")
        bias, scale = (table[r : r + 1, :] for r in at)
        df = (cot[...] * scale).astype(BF16)
        d_out[ring.me] = df
        total = yield from reduce_on(ring, by_columns, part, *scratch[:5], sent)
        spread = gather_slots(ring, d_out, by_columns, *scratch[5:], sent)
        next(spread)
        branch = total + bias
        x_out[...] = x[...] + scale * branch
        sums[...] = jnp.zeros_like(sums)
        sums[2:3, :] = jnp.sum(cot[...] * branch, axis=0, keepdims=True)
        sums[3:4, :] = jnp.sum(df.astype(F32), axis=0, keepdims=True)
        yield from spread

    return call(
        main,
        (part, x, cot, table),
        [(SHARD, F32), (SUMS, F32), (ALL, BF16)],
        RING_SCRATCH,
        ident,
        riders,
    )


def backward_step(part, value, dx, branch, table, at, ident, riders=()):
    def main(inputs, outs, scratch, sent):
        (part, value, dx, branch, table), (dx_out, sums, d_out) = inputs, outs
        ring = Ring("z")
        total = yield from reduce_on(ring, by_columns, part, *scratch[:5], sent)
        gain, scale = (table[r : r + 1, :] for r in at)
        dr, gain_sum, shift_sum = norm_back(total, value[...], gain)
        dx_new = dx[...] + dr
        dx_out[...] = dx_new
        df = (dx_new * scale).astype(BF16)
        d_out[ring.me] = df
        spread = gather_slots(ring, d_out, by_columns, *scratch[5:], sent)
        next(spread)
        sums[...] = jnp.zeros_like(sums)
        sums[0:1, :] = gain_sum
        sums[1:2, :] = shift_sum
        sums[2:3, :] = jnp.sum(dx_new * branch[...], axis=0, keepdims=True)
        sums[3:4, :] = jnp.sum(df.astype(F32), axis=0, keepdims=True)
        yield from spread

    return call(
        main,
        (part, value, dx, branch, table),
        [(SHARD, F32), (SUMS, F32), (ALL, BF16)],
        RING_SCRATCH,
        ident,
        riders,
    )


def first_step(tokens, pack, ident, riders):
    pieces = Pieces(tokens)

    def main(inputs, outs, scratch, sent):
        tokens, pack = inputs
        x_out, n_out, pack_out = outs
        landed, psend, precv, ksend, krecv, send, recv = scratch
        ring = Ring("z")
        z = ring.me
        me = lax.axis_index("yh") * 4 + z
        arrive = pieces.run([tokens], [landed], [psend, precv], sent)
        next(arrive)
        pack_out[me] = pack[...]

        def note(j, slot):
            return remote(
                pack, pack_out.at[slot], ksend.at[j], krecv.at[slot], device(yh=j // 4, z=j % 4)
            )

        for j in range(8):

            @pl.when(me != j)
            def _():
                note(j, me).start()

        yield
        for _ in arrive:
            pass
        for q in range(8):

            @pl.when(me != q)
            def _():
                note(q, q).wait_recv()

        value = landed[...].astype(F32)
        x_out[...] = value
        gain = jnp.concatenate([pack_out[q, GAIN : GAIN + 1, :] for q in range(8)], axis=1)
        shift = jnp.concatenate([pack_out[q, SHIFT : SHIFT + 1, :] for q in range(8)], axis=1)
        hat, _ = norm_of(value)
        n_out[z] = (hat * gain + shift).astype(BF16)
        yield from gather_slots(ring, n_out, by_columns, send, recv, sent)
        for j in range(8):

            @pl.when(me != j)
            def _():
                note(j, me).wait_send()

    def entry(links):
        yh, z = lax.axis_index("yh"), lax.axis_index("z")
        for j in range(8):

            @pl.when(yh * 4 + z != j)
            def _():
                signal(device(yh=j // 4, z=j % 4))

        greet(links, 7, greet_pieces())

    return call(
        main,
        (tokens, pack),
        [(SHARD, F32), (ALL, BF16), ((8, 32, 128), F32)],
        [pltpu.VMEM(SHARD, BF16)] + sems(8, 8, 8, 8, 6, 6),
        ident,
        riders,
        entry,
    )


def last_step(part, value, dx, x_end, table, known, blocks, at, ident, riders):
    def main(inputs, outs, scratch, sent):
        part, value, dx, x_end, table, known, blocks = inputs
        landed, small = outs
        ring_scratch, scratch = scratch[:5], scratch[5:]
        both, psend, precv, vectors, zgot, zsend, zrecv = scratch[:7]
        owned, ygot, ysend, yrecv, sub, xgot, xsend, xrecv = scratch[7:]
        x_, yl, co, yh, z = (lax.axis_index(a) for a in AXES)
        shard, home = co * 4 + z, yh == co

        def piece(k, q):
            src = both.at[k, :, pl.ds(q * 128, 128)]
            dst = landed.at[k, shard]
            to = device(co=yh, yh=q // 4, z=q % 4)
            there = remote(src, dst, psend.at[k, q], precv.at[k, shard], to)
            here = pltpu.make_async_copy(src, dst, precv.at[k, shard])
            return there, here, home & (yh * 4 + z == q)

        def send_all(k):
            for q in range(8):
                there, here, own = piece(k, q)

                @pl.when(own)
                def _():
                    here.start()

                @pl.when(jnp.logical_not(own))
                def _():
                    there.start()

        reduction = reduce_on(Ring("z"), by_columns, part, *ring_scratch, sent)
        next(reduction)
        both[0] = x_end[...].astype(BF16)
        send_all(0)
        total = yield from reduction
        (gain,) = (table[r : r + 1, :] for r in at)
        dr, gain_sum, shift_sum = norm_back(total, value[...], gain)
        both[1] = (dx[...] + dr).astype(BF16)
        send_all(1)

        vectors[...] = known[...]
        vectors[at[0] : at[0] + 1, :] = gain_sum
        vectors[at[0] + SHIFT : at[0] + SHIFT + 1, :] = shift_sum

        def on_z(there, slot, h):
            cut = vectors.at[:, pl.ds((h * 4 + there) * 128, 128)]
            return remote(
                cut, zgot.at[slot, h], zsend.at[there, h], zrecv.at[slot, h], device(z=there)
            )

        def on_y(there, slot):
            to = device(yh=there // 4, yl=(there // 2) % 2, co=there % 2)
            return remote(
                owned.at[there // 4], ygot.at[slot], ysend.at[there], yrecv.at[slot], to
            )

        def on_x(there, slot):
            return remote(sub, xgot.at[slot], xsend.at[there], xrecv.at[slot], device(x=there))

        def others(me, count, do):
            for i in range(count):

                @pl.when(me != i)
                def _():
                    do(i)

        me = yh * 4 + yl * 2 + co

        def both_halves(do):
            def run(i):
                do(i, 0)
                do(i, 1)

            return run

        others(z, 4, both_halves(lambda i, h: on_z(i, z, h).start()))
        for h in range(2):
            zgot[z, h] = vectors[:, pl.ds(pl.multiple_of((h * 4 + z) * 128, 128), 128)]
        yield
        others(z, 4, both_halves(lambda i, h: on_z(i, i, h).wait_recv()))
        owned[:, 0:16] = zgot[0] + zgot[1] + zgot[2] + zgot[3]
        owned[:, 16:32] = blocks[...]
        others(me, 8, lambda i: on_y(i, me).start())
        ygot[me] = owned[yh]
        yield
        others(me, 8, lambda i: on_y(i, i).wait_recv())
        sub[...] = sum(ygot[i] for i in range(8))
        others(x_, 4, lambda i: on_x(i, x_).start())
        xgot[x_] = sub[...]
        yield
        others(x_, 4, lambda i: on_x(i, i).wait_recv())
        small[...] = sum(xgot[i] for i in range(4))
        others(z, 4, both_halves(lambda i, h: on_z(i, z, h).wait_send()))
        others(me, 8, lambda i: on_y(i, me).wait_send())
        others(x_, 4, lambda i: on_x(i, x_).wait_send())
        for k in range(2):
            for s in range(8):
                dst = landed.at[k, s]
                own = home & (shard == s)

                @pl.when(own)
                def _():
                    pltpu.make_async_copy(dst, dst, precv.at[k, s]).wait()

                @pl.when(jnp.logical_not(own))
                def _():
                    remote(
                        dst, dst, psend.at[k, s], precv.at[k, s], Ring("z").to_right
                    ).wait_recv()

                there, here, mine = piece(k, s)

                @pl.when(jnp.logical_not(mine))
                def _():
                    there.wait_send()

    def entry(links):
        x_, yl, co, yh, z = (lax.axis_index(a) for a in AXES)
        home, me = yh == co, yh * 4 + yl * 2 + co
        for i in range(8):

            @pl.when(jnp.logical_not(home & (co * 4 + z == i)))
            def _():
                signal(device(yh=co, co=i // 4, z=i % 4))

            @pl.when(me != i)
            def _():
                signal(device(yh=i // 4, yl=(i // 2) % 2, co=i % 2))

        for i in range(4):

            @pl.when(x_ != i)
            def _():
                signal(device(x=i))

            @pl.when(z != i)
            def _():
                signal(device(z=i))

        greet(links, 7 + 3 + 3, home)

    return call(
        main,
        (part, value, dx, x_end, table, known, blocks),
        [((2, 8, ROWS, 128), BF16), ((32, 128), F32)],
        RING_SCRATCH[:5]
        + [
            pltpu.VMEM((2,) + SHARD, BF16),
            pltpu.SemaphoreType.DMA((2, 8)),
            pltpu.SemaphoreType.DMA((2, 8)),
            pltpu.VMEM((16, WIDTH), F32),
            pltpu.VMEM((4, 2, 16, 128), F32),
            pltpu.SemaphoreType.DMA((4, 2)),
            pltpu.SemaphoreType.DMA((4, 2)),
            pltpu.VMEM((2, 32, 128), F32),
            pltpu.VMEM((8, 32, 128), F32),
            *sems(8, 8),
            pltpu.VMEM((32, 128), F32),
            pltpu.VMEM((4, 32, 128), F32),
            *sems(4, 4),
        ],
        ident,
        riders,
        entry,
    )


def swap_kernel(own, other, send, recv):
    co = lax.axis_index("co")
    to = device(co=1 - co)
    signal(to)
    pl.semaphore_wait(pltpu.get_barrier_semaphore(), 1)
    c = remote(own, other, send, recv, to)
    c.start()
    c.wait()


def swap(own, ident):
    return pl.pallas_call(
        swap_kernel,
        out_shape=jax.ShapeDtypeStruct(own.shape, own.dtype),
        in_specs=[VM],
        out_specs=VM,
        scratch_shapes=[pltpu.SemaphoreType.DMA, pltpu.SemaphoreType.DMA],
        compiler_params=pltpu.CompilerParams(collective_id=ident, has_side_effects=True),
    )(own)


def lane_heads(value):
    lane = lax.broadcasted_iota(jnp.int32, value.shape, 1)
    zero = jnp.zeros_like(value)
    return jnp.where(lane < 64, value, zero), jnp.where(lane < 64, zero, value)


def attend_kernel(q, k, v, ko, vo, mask, att, lse, kall, vt, qpad, ot):
    kall[0:OWN] = k[...]
    kall[OWN:KEYS] = ko[...]
    vt[:, 0:OWN] = v[...].T
    vt[:, OWN:KEYS] = vo[...].T
    for hh, qh in enumerate(lane_heads(q[...] * 0.125)):
        qpad[hh, 0:OWN] = qh
        qpad[hh, OWN:QROWS] = jnp.zeros((QROWS - OWN, 128), BF16)
    lse[...] = jnp.zeros_like(lse)
    for hh in range(2):
        for lo, n in CHUNKS:
            bias = mask[...] if n == 128 else jnp.concatenate([mask[...]] * 2, axis=1)
            s = dot_nt(kall[...], qpad[hh, lo : lo + n]) + bias
            top = jnp.max(s, axis=0, keepdims=True)
            e = jnp.exp(s - top)
            total = jnp.sum(e, axis=0, keepdims=True)
            p = (e * (1.0 / total)).astype(BF16)
            ot[hh * 64 : hh * 64 + 64, lo : lo + n] = dot_nn(vt[hh * 64 : hh * 64 + 64], p)
            lse[hh : hh + 1, lo : lo + n] = top + jnp.log(total)
    att[...] = ot[...].T[0:OWN].astype(BF16)


def attend(qkv, other, mask):
    def block(f):
        return pl.BlockSpec((OWN, 128), lambda h: (0, f(h)))

    return pl.pallas_call(
        attend_kernel,
        grid=(2,),
        out_shape=[
            jax.ShapeDtypeStruct((OWN, 256), BF16),
            jax.ShapeDtypeStruct((2, 8, QROWS), F32),
        ],
        in_specs=[
            block(lambda h: 3 * h),
            block(lambda h: 3 * h + 1),
            block(lambda h: 3 * h + 2),
            block(lambda h: 2 * h),
            block(lambda h: 2 * h + 1),
            pl.BlockSpec((KEYS, 128), lambda h: (0, 0)),
        ],
        out_specs=[
            block(lambda h: h),
            pl.BlockSpec((None, 8, QROWS), lambda h: (h, 0, 0)),
        ],
        scratch_shapes=[
            pltpu.VMEM((KEYS, 128), BF16),
            pltpu.VMEM((128, KEYS), BF16),
            pltpu.VMEM((2, QROWS, 128), BF16),
            pltpu.VMEM((128, QROWS), F32),
        ],
        compiler_params=pltpu.CompilerParams(vmem_limit_bytes=40 * 2**20),
    )(qkv, qkv, qkv, other, other, mask)


def attend_back_kernel(
    q, k, v, ko, vo, do, lse, mask, dq, own, oth, kall, vall, kt, qpad, dpad, dqt, dk, dv
):
    kall[0:OWN] = k[...]
    kall[OWN:KEYS] = ko[...]
    vall[0:OWN] = v[...]
    vall[OWN:KEYS] = vo[...]
    kt[:, 0:OWN] = k[...].T
    kt[:, OWN:KEYS] = ko[...].T
    for hh, (qh, dh) in enumerate(zip(lane_heads(q[...] * 0.125), lane_heads(do[...]))):
        qpad[hh, 0:OWN] = qh
        qpad[hh, OWN:QROWS] = jnp.zeros((QROWS - OWN, 128), BF16)
        dpad[hh, 0:OWN] = dh
        dpad[hh, OWN:QROWS] = jnp.zeros((QROWS - OWN, 128), BF16)
    dk[...] = jnp.zeros_like(dk)
    dv[...] = jnp.zeros_like(dv)
    for hh in range(2):
        for lo, n in CHUNKS:
            bias = mask[...] if n == 128 else jnp.concatenate([mask[...]] * 2, axis=1)
            qc = qpad[hh, lo : lo + n]
            dc = dpad[hh, lo : lo + n]
            s = dot_nt(kall[...], qc) + bias
            p = jnp.exp(s - lse[hh : hh + 1, lo : lo + n])
            dp = dot_nt(vall[...], dc)
            delta = jnp.sum(p * dp, axis=0, keepdims=True)
            ds = (p * (dp - delta)).astype(BF16)
            dv[...] += dot_nn(p.astype(BF16), dc)
            dk[...] += dot_nn(ds, qc)
            dqt[hh * 64 : hh * 64 + 64, lo : lo + n] = dot_nn(kt[hh * 64 : hh * 64 + 64], ds)
    dq[...] = (dqt[...].T[0:OWN] * 0.125).astype(BF16)
    own[:, 0:128] = dk[0:OWN]
    own[:, 128:256] = dv[0:OWN]
    oth[:, 0:128] = dk[OWN:KEYS].astype(BF16)
    oth[:, 128:256] = dv[OWN:KEYS].astype(BF16)


def attend_back(qkv, other, datt, lse, mask):
    def block(f):
        return pl.BlockSpec((OWN, 128), lambda h: (0, f(h)))

    wide = pl.BlockSpec((OWN, 256), lambda h: (0, h))
    return pl.pallas_call(
        attend_back_kernel,
        grid=(2,),
        out_shape=[
            jax.ShapeDtypeStruct((OWN, 256), BF16),
            jax.ShapeDtypeStruct((OWN, 512), F32),
            jax.ShapeDtypeStruct((OWN, 512), BF16),
        ],
        in_specs=[
            block(lambda h: 3 * h),
            block(lambda h: 3 * h + 1),
            block(lambda h: 3 * h + 2),
            block(lambda h: 2 * h),
            block(lambda h: 2 * h + 1),
            block(lambda h: h),
            pl.BlockSpec((None, 8, QROWS), lambda h: (h, 0, 0)),
            pl.BlockSpec((KEYS, 128), lambda h: (0, 0)),
        ],
        out_specs=[block(lambda h: h), wide, wide],
        scratch_shapes=[
            pltpu.VMEM((KEYS, 128), BF16),
            pltpu.VMEM((KEYS, 128), BF16),
            pltpu.VMEM((128, KEYS), BF16),
            pltpu.VMEM((2, QROWS, 128), BF16),
            pltpu.VMEM((2, QROWS, 128), BF16),
            pltpu.VMEM((128, QROWS), F32),
            pltpu.VMEM((KEYS, 128), F32),
            pltpu.VMEM((KEYS, 128), F32),
        ],
        compiler_params=pltpu.CompilerParams(vmem_limit_bytes=48 * 2**20),
    )(qkv, qkv, qkv, other, other, datt, lse, mask)


def on_device(
    tokens,
    cotangent,
    attend_weight,
    output_weight,
    up_weight,
    down_weight,
    norm_gain,
    norm_shift,
    attend_bias,
    branch_bias,
    layer_scale,
    hidden_bias,
):
    co, yh, z = (lax.axis_index(a) for a in ("co", "yh", "z"))
    attend_weight = attend_weight.reshape(LAYERS, 256, 384)
    first = jnp.pad(tokens, ((0, 15), (0, 0)))
    cot_pieces = jnp.pad(cotangent.astype(BF16), ((0, 15), (0, 0)))
    pack = jnp.concatenate(
        [
            norm_gain.reshape(4, 128),
            norm_shift.reshape(4, 128),
            branch_bias.reshape(4, 128),
            layer_scale.reshape(4, 128),
            attend_bias.reshape(4, 128),
            hidden_bias.reshape(8, 128),
            jnp.zeros((4, 128), F32),
        ]
    )

    def attend_of(l):
        return GatherWeight(attend_weight, l, 0)

    def output_of(l):
        return GatherWeight(output_weight, l, 1)

    def up_of(l):
        return GatherWeight(up_weight, l, 0)

    def down_of(l):
        return GatherWeight(down_weight, l, 1)

    weights = [[None] * 4 for _ in range(LAYERS)]
    ident = iter(range(40))
    (x, n_all, packs), (weights[0][0], weights[0][1]) = first_step(
        first, pack, next(ident), [attend_of(0), output_of(0)]
    )
    table = packs[:, 0:16].transpose(1, 0, 2).reshape(16, WIDTH)
    here = jnp.stack(
        [
            lax.dynamic_index_in_dim(packs, z, keepdims=False),
            lax.dynamic_index_in_dim(packs, z + 4, keepdims=False),
        ]
    )
    row = jnp.arange(OWN)
    block, inside = row // ROWS, row % ROWS

    def hidden_keys(half):
        real = (inside < REAL) | ((inside == REAL) & (block == 3) & (half == 1))
        return jnp.where(real, 0.0, -1e30).astype(F32)

    mask = jnp.concatenate([hidden_keys(co), hidden_keys(1 - co)])
    mask = jnp.broadcast_to(mask[:, None], (KEYS, 128))

    saved = []
    for l in range(LAYERS):
        wqkv, wout = weights[l][:2]
        ab = here[:, 16 + 2 * l : 18 + 2 * l]
        qkv_bias = jnp.concatenate(
            [ab[0, 0], jnp.zeros(128), ab[0, 1], ab[1, 0], jnp.zeros(128), ab[1, 1]]
        )
        n1 = n_all.reshape(OWN, WIDTH)
        qkv = (dot_nn(n1, wqkv) + qkv_bias).astype(BF16)
        kv = jnp.concatenate([qkv[:, 128:384], qkv[:, 512:768]], axis=1)
        other = swap(kv, next(ident))
        att, lse = attend(qkv, other, mask)
        part = dot_nn(att, wout).astype(BF16).reshape(ALL)
        at = (BRANCH + 2 * l, SCALE + 2 * l, GAIN + 2 * l + 1, SHIFT + 2 * l + 1)
        riders = [up_of(0), down_of(0)] if l == 0 else [down_of(1)]
        (a, m, n_all), got = forward_step(part, x, table, at, next(ident), riders)
        if l == 0:
            weights[0][2:] = got
        else:
            weights[1][3] = got[0]
        wup, wdown = weights[l][2:]
        n2 = n_all.reshape(OWN, WIDTH)
        hb = here[:, 20 + 4 * l : 24 + 4 * l].reshape(WIDTH)
        u = dot_nn(n2, wup) + hb
        g = gelu_value(u).astype(BF16)
        part = dot_nn(g, wdown).astype(BF16).reshape(ALL)
        saved.append([x, n1, qkv, other, att, lse, a, m, n2, u, g])
        if l + 1 < LAYERS:
            at = (BRANCH + 2 * l + 1, SCALE + 2 * l + 1, GAIN + 2 * l + 2, SHIFT + 2 * l + 2)
            (f, x, n_all), got = forward_step(
                part,
                m,
                table,
                at,
                next(ident),
                [Pieces(cot_pieces), attend_of(1), output_of(1), up_of(1)],
                True,
            )
            saved[l].append(f)
            weights[1][:3] = got[1:]
            last = jnp.where((co == 1) & (z == 3), REAL + 1, REAL)
            cot = jnp.where(jnp.arange(ROWS)[:, None] < last, got[0].astype(F32), 0.0)
        else:
            at = (BRANCH + 2 * l + 1, SCALE + 2 * l + 1)
            (x_end, sums, d_all), _ = turn_step(part, m, cot, table, at, next(ident))

    gain_sums, shift_sums, scale_sums, branch_sums = ([None] * 4 for _ in range(4))
    scale_sums[3], branch_sums[3] = sums[2], sums[3]
    hidden_sums, qkv_sums, grads = [None] * LAYERS, [None] * LAYERS, [[None] * 4, [None] * 4]
    dx, waiting = cot, []
    for l in reversed(range(LAYERS)):
        wqkv, wout, wup, wdown = weights[l]
        x, n1, qkv, other, att, lse, a, m, n2, u, g = saved[l][:11]
        df = d_all.reshape(OWN, WIDTH)
        du = (dot_nt(df, wdown) * gelu_slope(u)).astype(BF16)
        part = dot_nt(du, wup).astype(BF16).reshape(ALL)
        hidden_sums[l] = jnp.sum(du.astype(F32), axis=0)
        at = (GAIN + 2 * l + 1, SCALE + 2 * l)
        riders = [SumBlock(b.shape, b) for b in waiting] + [
            ReduceWeight(dot_tn(g, df).astype(BF16), 1),
            ReduceWeight(dot_tn(n2, du).astype(BF16), 0),
        ]
        (dm, sums, d_all), got = backward_step(part, m, dx, a, table, at, next(ident), riders)
        if waiting:
            grads[l + 1][:2] = got[:2]
        waiting = got[-2:]
        gain_sums[2 * l + 1], shift_sums[2 * l + 1] = sums[0], sums[1]
        scale_sums[2 * l], branch_sums[2 * l] = sums[2], sums[3]
        da = d_all.reshape(OWN, WIDTH)
        datt = dot_nt(da, wout).astype(BF16)
        dq, own, oth = attend_back(qkv, other, datt, lse, mask)
        dkv = (own + swap(oth, next(ident)).astype(F32)).astype(BF16)
        dqkv = jnp.concatenate(
            [dq[:, 0:128], dkv[:, 0:256], dq[:, 128:256], dkv[:, 256:512]], axis=1
        )
        qkv_sums[l] = jnp.sum(dqkv.astype(F32), axis=0)
        part = dot_nt(dqkv, wqkv).astype(BF16).reshape(ALL)
        attend_part = dot_tn(n1, dqkv).astype(BF16)
        output_part = dot_tn(att, da).astype(BF16)
        riders = [SumBlock(b.shape, b) for b in waiting]
        if l > 0:
            at = (GAIN + 2 * l, SCALE + 2 * l - 1)
            riders += [ReduceWeight(attend_part, 0), ReduceWeight(output_part, 1)]
            (dx, sums, d_all), got = backward_step(
                part, x, dm, saved[l - 1][11], table, at, next(ident), riders
            )
            waiting = got[-2:]
            scale_sums[2 * l - 1], branch_sums[2 * l - 1] = sums[2], sums[3]
            gain_sums[2 * l], shift_sums[2 * l] = sums[0], sums[1]
        else:
            riders += [ReduceSum(attend_part, 0), ReduceSum(output_part, 1)]
            zero = jnp.zeros(WIDTH)
            known = jnp.stack(
                [zero] + gain_sums[1:] + [zero] + shift_sums[1:] + branch_sums + scale_sums
            )
            blocks = jnp.concatenate(
                [
                    jnp.stack(qkv_sums).reshape(2, 2, 3, 128).transpose(1, 0, 2, 3).reshape(2, 6, 128),
                    jnp.stack(hidden_sums).reshape(2, 2, 4, 128).transpose(1, 0, 2, 3).reshape(2, 8, 128),
                    jnp.zeros((2, 2, 128), F32),
                ],
                axis=1,
            )
            (landed, small), got = last_step(
                part, x, dm, x_end, table, known, blocks, (GAIN,), next(ident), riders
            )
            grads[0][:2] = got[-2:]
        grads[l][2:] = [got[1], got[0]]

    bias_grad = small[16:22].reshape(2, 3, 128)[:, 0::2]

    def rows(k):
        return jnp.concatenate(
            [landed[k, 0:7, 0:REAL].reshape(7 * REAL, 128), landed[k, 7, 0 : REAL + 1]]
        ).astype(F32)

    return (
        rows(0),
        rows(1),
        jnp.stack([grads[l][0] for l in range(LAYERS)]).reshape(LAYERS, 256, 3, 128),
        jnp.stack([grads[l][1] for l in range(LAYERS)]),
        jnp.stack([grads[l][2] for l in range(LAYERS)]),
        jnp.stack([grads[l][3] for l in range(LAYERS)]),
        small[0:4].reshape(2, 2, 128),
        small[4:8].reshape(2, 2, 128),
        bias_grad,
        small[8:12].reshape(2, 2, 128),
        small[12:16].reshape(2, 2, 128),
        small[22:30].reshape(2, 512),
    )


def solution(mesh):
    split = Mesh(mesh.devices.reshape(4, 2, 2, 2, 4), AXES)
    images, row, col = ("x", "yl", "co"), ("yl", "co"), ("yh", "z")
    placed = (
        P(images, col),
        P(images, col),
        P(None, row, None, col),
        P(None, col, row),
        P(None, row, col),
        P(None, col, row),
        P(None, None, col),
        P(None, None, col),
        P(None, None, col),
        P(None, None, col),
        P(None, None, col),
        P(None, col),
    )
    return jax.shard_map(
        on_device, mesh=split, in_specs=placed, out_specs=placed, check_vma=False
    )
```

```python
import jax
import jax.numpy as jnp
from jax import lax
from jax.experimental import pallas as pl
from jax.experimental.pallas import tpu as pltpu
from jax.sharding import Mesh, PartitionSpec as P

WIDTH = 1024
HALF = WIDTH // 2
SEQ = 1025
LAYERS = 2
REAL = 128
ROWS = 144
OWN = 4 * ROWS
KEYS = 2 * OWN
QROWS = 640
CHUNKS = ((0, 256), (256, 256), (512, 128))
EPS = 1e-06
ROOT_HALF = 0.7071067811865476
INV_ROOT_TWO_PI = 0.3989422804014327
MESH = pl.DeviceIdType.MESH
AXES = ("x", "yl", "co", "yh", "z")
VM = pl.BlockSpec(memory_space=pltpu.VMEM)
ANY = pl.BlockSpec(memory_space=pl.ANY)
F32 = jnp.float32
BF16 = jnp.bfloat16


def gelu_value(value):
    return 0.5 * value * (1.0 + lax.erf(value * ROOT_HALF))


def gelu_slope(value):
    return 0.5 * (1.0 + lax.erf(value * ROOT_HALF)) + value * INV_ROOT_TWO_PI * jnp.exp(
        -0.5 * value * value
    )


def dot_nt(left, right):
    return lax.dot_general(left, right, (((1,), (1,)), ((), ())), preferred_element_type=F32)


def dot_tn(left, right):
    return lax.dot_general(left, right, (((0,), (0,)), ((), ())), preferred_element_type=F32)


def dot_nn(left, right):
    return jnp.dot(left, right, preferred_element_type=F32)


def device(**moved):
    return tuple(moved[a] if a in moved else lax.axis_index(a) for a in AXES)


def remote(src, dst, send, recv, to):
    return pltpu.make_async_remote_copy(
        src_ref=src, dst_ref=dst, send_sem=send, recv_sem=recv, device_id=to, device_id_type=MESH
    )


def signal(to):
    pl.semaphore_signal(
        pltpu.get_barrier_semaphore(), inc=1, device_id=to, device_id_type=MESH
    )


class Ring:
    def __init__(self, axis):
        self.axis = axis
        if axis == "y":
            self.me = lax.axis_index("yh") * 2 + lax.axis_index("yl")
        else:
            self.me = lax.axis_index(axis)
        self.right = lax.rem(self.me + 1, 4)
        self.left = lax.rem(self.me + 3, 4)
        self.across = lax.rem(self.me + 2, 4)
        self.to_right, self.to_left = self.at(self.right), self.at(self.left)

    def at(self, index):
        if self.axis == "y":
            return device(yh=index // 2, yl=lax.rem(index, 2))
        return device(**{self.axis: index})


def greet(links, more=0, home=None):
    count = more
    for link in links:
        if link == "core":
            signal(device(co=1 - lax.axis_index("co")))
            count += 1
        else:
            ring = Ring(link)
            signal(ring.to_right)
            signal(ring.to_left)
            count += 2
    barrier = pltpu.get_barrier_semaphore()
    if home is None:
        pl.semaphore_wait(barrier, count)
    else:

        @pl.when(home)
        def _():
            pl.semaphore_wait(barrier, count + 7)

        @pl.when(jnp.logical_not(home))
        def _():
            pl.semaphore_wait(barrier, count + 8)


def in_turns(jobs):
    jobs = list(jobs)
    while jobs:
        for job in list(jobs):
            try:
                next(job)
            except StopIteration:
                jobs.remove(job)


def by_columns(ref, lead, half):
    return ref.at[lead, :, pl.ds(half * HALF, HALF)]


def by_rows(ref, lead, half):
    rows = ref.shape[1] // 2
    return ref.at[lead, pl.ds(half * rows, rows), :]


def reduce_on(ring, half, part, fin, relay, stage, send, recv, sent):
    def copy(i, src, dst, to):
        c = remote(src, dst, send.at[i], recv.at[i], to)
        c.start()
        sent.append(c)
        return c

    far_r = copy(0, half(part, ring.across, 0), relay.at[0], ring.to_right)
    far_l = copy(1, half(part, ring.across, 1), relay.at[1], ring.to_left)
    near_r = copy(2, half(part, ring.right, 1), half(fin, 0, 1), ring.to_right)
    near_l = copy(3, half(part, ring.left, 0), half(fin, 1, 0), ring.to_left)
    yield
    far_r.wait_recv()
    stage[0] = (half(part, ring.right, 0)[...].astype(F32) + relay[0].astype(F32)).astype(BF16)
    sum_r = copy(4, stage.at[0], half(fin, 0, 0), ring.to_right)
    far_l.wait_recv()
    stage[1] = (half(part, ring.left, 1)[...].astype(F32) + relay[1].astype(F32)).astype(BF16)
    sum_l = copy(5, stage.at[1], half(fin, 1, 1), ring.to_left)
    yield
    for c in (near_r, near_l, sum_r, sum_l):
        c.wait_recv()
    return part[ring.me].astype(F32) + fin[0].astype(F32) + fin[1].astype(F32)


def gather_on(ring, slot, own, send, recv, sent, landed=None):
    def copy(i, src, owner, half, to):
        return remote(src, slot(owner, half), send.at[i], recv.at[i], to)

    def go(*what):
        c = copy(*what)
        c.start()
        sent.append(c)

    def lands(i, owner, half):
        copy(i, slot(owner, half), owner, half, ring.to_right).wait_recv()

    go(0, own(0), ring.me, 0, ring.to_right)
    go(1, own(1), ring.me, 1, ring.to_left)
    go(2, own(1), ring.me, 1, ring.to_right)
    go(3, own(0), ring.me, 0, ring.to_left)
    yield
    lands(0, ring.left, 0)
    go(4, slot(ring.left, 0), ring.left, 0, ring.to_right)
    lands(1, ring.right, 1)
    go(5, slot(ring.right, 1), ring.right, 1, ring.to_left)
    yield
    lands(2, ring.left, 1)
    if landed is not None:
        landed(ring.left)
    lands(3, ring.right, 0)
    if landed is not None:
        landed(ring.right)
    yield
    lands(4, ring.across, 0)
    lands(5, ring.across, 1)
    if landed is not None:
        landed(ring.across)


def gather_slots(ring, out, half, send, recv, sent):
    def slot(owner, h):
        return half(out, owner, h)

    yield from gather_on(ring, slot, lambda h: slot(ring.me, h), send, recv, sent)


def sems(*counts):
    return [pltpu.SemaphoreType.DMA((c,)) for c in counts]


class GatherWeight:
    links = ("y", "core")

    def __init__(self, shards, layer, side):
        rows, columns = shards.shape[1:]
        self.layer, self.side, self.rows, self.columns = layer, side, rows, columns
        full = (4 * rows, 2 * columns) if side == 0 else (2 * rows, 4 * columns)
        self.inputs = [(shards, ANY)]
        self.outs = [(full, BF16, ANY)]
        self.scratch = sems(6, 6, 4, 4, 1)

    def run(self, inputs, outs, scratch, sent):
        (shards,), (out,) = inputs, outs
        send, recv, csend, crecv, local = scratch
        own = shards.at[self.layer]
        ring, co = Ring("y"), lax.axis_index("co")
        rows, columns = self.rows, self.columns

        def block(y, core, half=None):
            yh, r = y // 2, lax.rem(y, 2) * 2 + core
            down, along = (r, yh) if self.side == 0 else (yh, r)
            first, count = down * rows, rows
            if half is not None:
                count = rows // 2
                first = first + half * count
            return out.at[
                pl.ds(pl.multiple_of(first, 16), count),
                pl.ds(pl.multiple_of(along * columns, 128), columns),
            ]

        def to_core(i, src, y):
            c = remote(src, block(y, co), csend.at[i], crecv.at[i], device(co=1 - co))
            c.start()
            sent.append(c)

        keep = pltpu.make_async_copy(own, block(ring.me, co), local.at[0])
        keep.start()
        to_core(0, own, ring.me)
        numbers = iter((1, 2, 3))
        yield from gather_on(
            ring,
            lambda y, half: block(y, co, half),
            lambda half: own.at[pl.ds(half * (rows // 2), rows // 2), :],
            send,
            recv,
            sent,
            lambda y: to_core(next(numbers), block(y, co), y),
        )
        keep.wait()
        yield
        for i, y in enumerate((ring.me, ring.left, ring.right, ring.across)):
            there = block(y, 1 - co)
            remote(there, there, csend.at[i], crecv.at[i], device(co=1 - co)).wait_recv()


class ReduceWeight:
    links = ("y", "core")

    def __init__(self, left, right, side):
        rows, columns = left.shape[1], right.shape[1]
        self.full = rows, columns
        rows, columns = (rows // 4, columns // 2) if side == 0 else (rows // 2, columns // 4)
        self.side, self.rows, self.columns = side, rows, columns
        self.inputs = [(left, VM), (right, VM)]
        self.outs = [((rows, columns), BF16, VM)]
        self.scratch = [
            pltpu.VMEM(self.full, BF16),
            pltpu.VMEM((4, rows, columns), BF16),
            pltpu.VMEM((4, rows, columns), BF16),
            pltpu.VMEM((2, rows, columns), BF16),
            pltpu.VMEM((2, rows // 2, columns), BF16),
            pltpu.VMEM((2, rows // 2, columns), BF16),
        ] + sems(4, 4, 6, 6)

    def run(self, inputs, outs, scratch, sent):
        total = yield from self.total(inputs, scratch, sent)
        outs[0][...] = total.astype(BF16)

    def total(self, inputs, scratch, sent):
        left, right = inputs
        part, got, pair, fin, relay, stage, csend, crecv, send, recv = scratch
        for first in range(0, self.full[0], 256):
            part[first : first + 256] = dot_tn(left[:, first : first + 256], right[...]).astype(
                BF16
            )
        co = lax.axis_index("co")
        rows, columns = self.rows, self.columns

        def block(y, core):
            yh, r = y // 2, (y % 2) * 2 + core
            down, along = (r, yh) if self.side == 0 else (yh, r)
            return part.at[
                pl.ds(pl.multiple_of(down * rows, 16), rows),
                pl.ds(pl.multiple_of(along * columns, 128), columns),
            ]

        copies = []
        for y in range(4):
            c = remote(
                block(y, 1 - co), got.at[y], csend.at[y], crecv.at[y], device(co=1 - co)
            )
            c.start()
            copies.append(c)
        sent.extend(copies)
        yield
        for y in range(4):
            copies[y].wait_recv()
            pair[y] = (block(y, co)[...].astype(F32) + got[y].astype(F32)).astype(BF16)
        total = yield from reduce_on(
            Ring("y"), by_rows, pair, fin, relay, stage, send, recv, sent
        )
        return total


class SumBlock:
    links = ("x",)

    def __init__(self, shape, block=None):
        rows, columns = shape
        self.shape, self.rows = shape, rows // 4
        self.inputs = [] if block is None else [(block, VM)]
        self.outs = [(shape, F32, VM)]
        quarter = (rows // 4, columns)
        self.scratch = [
            pltpu.VMEM((4,) + quarter, BF16),
            pltpu.VMEM((4,) + quarter, BF16),
            pltpu.VMEM((2,) + quarter, BF16),
            pltpu.VMEM((2, rows // 8, columns), BF16),
            pltpu.VMEM((2, rows // 8, columns), BF16),
        ] + sems(6, 6, 6, 6)

    def run(self, inputs, outs, scratch, sent):
        yield from self.total(inputs[0][...], outs[0], scratch, sent)

    def total(self, value, out, scratch, sent):
        part, every, fin, relay, stage, send, recv, gsend, grecv = scratch
        ring = Ring("x")
        for i in range(4):
            part[i] = value[i * self.rows : (i + 1) * self.rows].astype(BF16)
        mine = yield from reduce_on(ring, by_rows, part, fin, relay, stage, send, recv, sent)
        every[ring.me] = mine.astype(BF16)
        yield from gather_slots(ring, every, by_rows, gsend, grecv, sent)
        for i in range(4):
            out[i * self.rows : (i + 1) * self.rows] = every[i].astype(F32)


class ReduceSum:
    links = ("y", "core", "x")

    def __init__(self, left, right, side):
        self.first = ReduceWeight(left, right, side)
        self.second = SumBlock((self.first.rows, self.first.columns))
        self.inputs, self.outs = self.first.inputs, self.second.outs
        self.scratch = self.first.scratch + self.second.scratch

    def run(self, inputs, outs, scratch, sent):
        n = len(self.first.scratch)
        total = yield from self.first.total(inputs, scratch[:n], sent)
        yield from self.second.total(total, outs[0], scratch[n:], sent)


class Pieces:
    links = ()
    pieces = "in"

    def __init__(self, source):
        self.inputs = [(source, VM)]
        self.outs = [(SHARD, BF16, VM)]
        self.scratch = sems(8, 8)

    def run(self, inputs, outs, scratch, sent):
        (source,), (landed,), (send, recv) = inputs, outs, scratch
        co, yh, z = (lax.axis_index(a) for a in ("co", "yh", "z"))
        me, home = yh * 4 + z, yh == co

        def piece(j):
            src = source.at[pl.ds(j * REAL, ROWS), :]
            dst = landed.at[:, pl.ds(pl.multiple_of(me * 128, 128), 128)]
            to = device(yh=co, co=j // 4, z=j % 4)
            there = remote(src, dst, send.at[j], recv.at[me], to)
            return there, pltpu.make_async_copy(src, dst, recv.at[me]), home & (co * 4 + z == j)

        for j in range(8):
            there, here, own = piece(j)

            @pl.when(own)
            def _():
                here.start()

            @pl.when(jnp.logical_not(own))
            def _():
                there.start()

        yield
        for q in range(8):
            dst = landed.at[:, pl.ds(q * 128, 128)]
            own = home & (me == q)

            @pl.when(own)
            def _():
                pltpu.make_async_copy(dst, dst, recv.at[q]).wait()

            @pl.when(jnp.logical_not(own))
            def _():
                remote(dst, dst, send.at[q], recv.at[q], Ring("z").to_right).wait_recv()

        for j in range(8):
            there, here, own = piece(j)

            @pl.when(jnp.logical_not(own))
            def _():
                there.wait_send()


class PiecesOut:
    links = ()
    pieces = "out"

    def __init__(self, source):
        self.inputs = [(source, VM)]
        self.outs = [((8, ROWS, 128), BF16, VM)]
        self.scratch = [pltpu.VMEM(SHARD, BF16)] + sems(8, 8)

    def run(self, inputs, outs, scratch, sent):
        scratch[0][...] = inputs[0][...].astype(BF16)
        yield from self.give(scratch[0], outs[0], *scratch[1:])

    @staticmethod
    def give(source, landed, send, recv):
        co, yh, z = (lax.axis_index(a) for a in ("co", "yh", "z"))
        shard, home = co * 4 + z, yh == co

        def piece(q):
            src = source.at[:, pl.ds(q * 128, 128)]
            dst = landed.at[shard]
            to = device(co=yh, yh=q // 4, z=q % 4)
            there = remote(src, dst, send.at[q], recv.at[shard], to)
            return there, pltpu.make_async_copy(src, dst, recv.at[shard]), home & (
                yh * 4 + z == q
            )

        for q in range(8):
            there, here, own = piece(q)

            @pl.when(own)
            def _():
                here.start()

            @pl.when(jnp.logical_not(own))
            def _():
                there.start()

        yield
        yield
        yield
        for s in range(8):
            dst = landed.at[s]
            own = home & (shard == s)

            @pl.when(own)
            def _():
                pltpu.make_async_copy(dst, dst, recv.at[s]).wait()

            @pl.when(jnp.logical_not(own))
            def _():
                remote(dst, dst, send.at[s], recv.at[s], Ring("z").to_right).wait_recv()

            there, here, mine = piece(s)

            @pl.when(jnp.logical_not(mine))
            def _():
                there.wait_send()


def greet_pieces(way):
    co, yh, z = (lax.axis_index(a) for a in ("co", "yh", "z"))
    home = yh == co
    for j in range(8):
        if way == "in":
            own, source = home & (yh * 4 + z == j), dict(yh=j // 4, z=j % 4, co=yh)
        else:
            own, source = home & (co * 4 + z == j), dict(yh=co, co=j // 4, z=j % 4)

        @pl.when(jnp.logical_not(own))
        def _():
            signal(device(**source))

    return home


class Spread:
    links = ("z",)

    def __init__(self, shard):
        self.inputs = [(shard, VM)]
        self.outs = [(ALL, BF16, VM)]
        self.scratch = sems(6, 6)

    def run(self, inputs, outs, scratch, sent):
        ring = Ring("z")
        outs[0][ring.me] = inputs[0][...]
        yield from gather_slots(ring, outs[0], by_columns, *scratch, sent)


class End:
    links = ("z",)

    def __init__(self, part, x, cot, table, at):
        self.at = at
        self.inputs = [(a, VM) for a in (part, x, cot, table)]
        self.outs = [(SHARD, F32, VM), (SUMS, F32, VM)]
        self.scratch = RING_SCRATCH[:5]

    def run(self, inputs, outs, scratch, sent):
        (part, x, cot, table), (x_out, sums) = inputs, outs
        total = yield from reduce_on(Ring("z"), by_columns, part, *scratch, sent)
        bias, scale = (table[r : r + 1, :] for r in self.at)
        branch = total + bias
        x_out[...] = x[...] + scale * branch
        df = (cot[...] * scale).astype(BF16)
        sums[...] = jnp.zeros_like(sums)
        sums[2:3, :] = jnp.sum(cot[...] * branch, axis=0, keepdims=True)
        sums[3:4, :] = jnp.sum(df.astype(F32), axis=0, keepdims=True)


def norm_of(value):
    mean = jnp.mean(value, axis=1, keepdims=True)
    meansq = jnp.mean(value * value, axis=1, keepdims=True)
    rstd = lax.rsqrt(meansq - mean * mean + EPS)
    return (value - mean) * rstd, rstd


def norm_back(grad, value, gain):
    hat, rstd = norm_of(value)
    e = grad * gain
    return (
        rstd
        * (
            e
            - jnp.mean(e, axis=1, keepdims=True)
            - hat * jnp.mean(e * hat, axis=1, keepdims=True)
        ),
        jnp.sum(grad * hat, axis=0, keepdims=True),
        jnp.sum(grad, axis=0, keepdims=True),
    )


RING_SCRATCH = [
    pltpu.VMEM((2, ROWS, WIDTH), BF16),
    pltpu.VMEM((2, ROWS, HALF), BF16),
    pltpu.VMEM((2, ROWS, HALF), BF16),
] + sems(6, 6, 6, 6)
GAIN, SHIFT, BRANCH, SCALE = 0, 4, 8, 12
SHARD = (ROWS, WIDTH)
ALL = (4, ROWS, WIDTH)
SUMS = (8, WIDTH)


def call(main, inputs, outs, scratch, ident, riders=(), links=("z",), pieces=None, entry=None):
    inputs = [(a, VM) for a in inputs]
    outs = [(s, d, VM) for s, d in outs]
    jobs = [(inputs, outs, list(scratch))] + [(r.inputs, r.outs, r.scratch) for r in riders]
    links = {link: None for link in links}
    for r in riders:
        links.update({link: None for link in r.links})
        pieces = pieces or getattr(r, "pieces", None)
    runs = [main] + [r.run for r in riders]

    def kernel(*refs):
        refs, split = list(refs), []
        for kind in range(3):
            for job in jobs:
                split.append([refs.pop(0) for _ in job[kind]])
        n = len(jobs)
        more = 0 if entry is None else entry()
        greet(links, more, None if pieces is None else greet_pieces(pieces))
        sent = []
        in_turns(
            run(split[i], split[n + i], split[2 * n + i], sent) for i, run in enumerate(runs)
        )
        for c in sent:
            c.wait_send()

    results = pl.pallas_call(
        kernel,
        out_shape=[jax.ShapeDtypeStruct(o[0], o[1]) for job in jobs for o in job[1]],
        in_specs=[i[1] for job in jobs for i in job[0]],
        out_specs=[o[2] for job in jobs for o in job[1]],
        scratch_shapes=[s for job in jobs for s in job[2]],
        compiler_params=pltpu.CompilerParams(
            collective_id=ident, has_side_effects=True, vmem_limit_bytes=40 * 2**20
        ),
    )(*[i[0] for job in jobs for i in job[0]])
    n = len(outs)
    return results[:n], results[n:]


def forward_step(part, x, table, at, ident, riders=()):
    def main(inputs, outs, scratch, sent):
        (part, x, table), (branch_out, x_out, n_out) = inputs, outs
        ring = Ring("z")
        total = yield from reduce_on(ring, by_columns, part, *scratch[:5], sent)
        bias, scale, gain, shift = (table[r : r + 1, :] for r in at)
        branch = total + bias
        x_new = x[...] + scale * branch
        branch_out[...] = branch
        x_out[...] = x_new
        hat, _ = norm_of(x_new)
        n_out[ring.me] = (hat * gain + shift).astype(BF16)
        yield from gather_slots(ring, n_out, by_columns, *scratch[5:], sent)

    return call(
        main,
        (part, x, table),
        [(SHARD, F32), (SHARD, F32), (ALL, BF16)],
        RING_SCRATCH,
        ident,
        riders,
    )


def backward_step(part, value, dx, branch, table, at, ident, riders=()):
    def main(inputs, outs, scratch, sent):
        (part, value, dx, branch, table), (dx_out, sums, d_out) = inputs, outs
        ring = Ring("z")
        total = yield from reduce_on(ring, by_columns, part, *scratch[:5], sent)
        gain, scale = (table[r : r + 1, :] for r in at)
        dr, gain_sum, shift_sum = norm_back(total, value[...], gain)
        dx_new = dx[...] + dr
        dx_out[...] = dx_new
        df = (dx_new * scale).astype(BF16)
        d_out[ring.me] = df
        spread = gather_slots(ring, d_out, by_columns, *scratch[5:], sent)
        next(spread)
        sums[...] = jnp.zeros_like(sums)
        sums[0:1, :] = gain_sum
        sums[1:2, :] = shift_sum
        sums[2:3, :] = jnp.sum(dx_new * branch[...], axis=0, keepdims=True)
        sums[3:4, :] = jnp.sum(df.astype(F32), axis=0, keepdims=True)
        yield from spread

    return call(
        main,
        (part, value, dx, branch, table),
        [(SHARD, F32), (SUMS, F32), (ALL, BF16)],
        RING_SCRATCH,
        ident,
        riders,
    )


def first_step(tokens, pack, ident, riders):
    pieces = Pieces(tokens)

    def main(inputs, outs, scratch, sent):
        tokens, pack = inputs
        x_out, n_out, pack_out = outs
        landed, psend, precv, ksend, krecv, send, recv = scratch
        ring = Ring("z")
        z = ring.me
        me = lax.axis_index("yh") * 4 + z
        arrive = pieces.run([tokens], [landed], [psend, precv], sent)
        next(arrive)
        pack_out[me] = pack[...]

        def note(j, slot):
            return remote(
                pack, pack_out.at[slot], ksend.at[j], krecv.at[slot], device(yh=j // 4, z=j % 4)
            )

        for j in range(8):

            @pl.when(me != j)
            def _():
                note(j, me).start()

        yield
        for _ in arrive:
            pass
        for q in range(8):

            @pl.when(me != q)
            def _():
                note(q, q).wait_recv()

        value = landed[...].astype(F32)
        x_out[...] = value
        gain = jnp.concatenate([pack_out[q, GAIN : GAIN + 1, :] for q in range(8)], axis=1)
        shift = jnp.concatenate([pack_out[q, SHIFT : SHIFT + 1, :] for q in range(8)], axis=1)
        hat, _ = norm_of(value)
        n_out[z] = (hat * gain + shift).astype(BF16)
        yield from gather_slots(ring, n_out, by_columns, send, recv, sent)
        for j in range(8):

            @pl.when(me != j)
            def _():
                note(j, me).wait_send()

    def entry():
        yh, z = lax.axis_index("yh"), lax.axis_index("z")
        for j in range(8):

            @pl.when(yh * 4 + z != j)
            def _():
                signal(device(yh=j // 4, z=j % 4))

        return 7

    return call(
        main,
        (tokens, pack),
        [(SHARD, F32), (ALL, BF16), ((8, 32, 128), F32)],
        [pltpu.VMEM(SHARD, BF16)] + sems(8, 8, 8, 8, 6, 6),
        ident,
        riders,
        pieces="in",
        entry=entry,
    )


def last_step(part, value, dx, table, known, blocks, at, ident, riders):
    def main(inputs, outs, scratch, sent):
        part, value, dx, table, known, blocks = inputs
        landed, small = outs
        ring_scratch, scratch = scratch[:5], scratch[5:]
        both, psend, precv, vectors, zgot, zsend, zrecv = scratch[:7]
        owned, ygot, ysend, yrecv, sub, xgot, xsend, xrecv = scratch[7:]
        x_, yl, co, yh, z = (lax.axis_index(a) for a in AXES)
        total = yield from reduce_on(Ring("z"), by_columns, part, *ring_scratch, sent)
        (gain,) = (table[r : r + 1, :] for r in at)
        dr, gain_sum, shift_sum = norm_back(total, value[...], gain)
        both[...] = (dx[...] + dr).astype(BF16)
        give = PiecesOut.give(both, landed, psend, precv)
        next(give)
        vectors[...] = known[...]
        vectors[at[0] : at[0] + 1, :] = gain_sum
        vectors[at[0] + SHIFT : at[0] + SHIFT + 1, :] = shift_sum

        def on_z(there, slot, h):
            cut = vectors.at[:, pl.ds((h * 4 + there) * 128, 128)]
            return remote(
                cut, zgot.at[slot, h], zsend.at[there, h], zrecv.at[slot, h], device(z=there)
            )

        def on_y(there, slot):
            to = device(yh=there // 4, yl=(there // 2) % 2, co=there % 2)
            return remote(
                owned.at[there // 4], ygot.at[slot], ysend.at[there], yrecv.at[slot], to
            )

        def on_x(there, slot):
            return remote(sub, xgot.at[slot], xsend.at[there], xrecv.at[slot], device(x=there))

        def others(me, count, do):
            for i in range(count):

                @pl.when(me != i)
                def _():
                    do(i)

        me = yh * 4 + yl * 2 + co

        def both_halves(do):
            def run(i):
                do(i, 0)
                do(i, 1)

            return run

        others(z, 4, both_halves(lambda i, h: on_z(i, z, h).start()))
        for h in range(2):
            zgot[z, h] = vectors[:, pl.ds(pl.multiple_of((h * 4 + z) * 128, 128), 128)]
        yield
        others(z, 4, both_halves(lambda i, h: on_z(i, i, h).wait_recv()))
        owned[:, 0:16] = zgot[0] + zgot[1] + zgot[2] + zgot[3]
        owned[:, 16:32] = blocks[...]
        others(me, 8, lambda i: on_y(i, me).start())
        ygot[me] = owned[yh]
        yield
        others(me, 8, lambda i: on_y(i, i).wait_recv())
        sub[...] = sum(ygot[i] for i in range(8))
        others(x_, 4, lambda i: on_x(i, x_).start())
        xgot[x_] = sub[...]
        yield
        others(x_, 4, lambda i: on_x(i, i).wait_recv())
        small[...] = sum(xgot[i] for i in range(4))
        others(z, 4, both_halves(lambda i, h: on_z(i, z, h).wait_send()))
        others(me, 8, lambda i: on_y(i, me).wait_send())
        others(x_, 4, lambda i: on_x(i, x_).wait_send())
        for _ in give:
            pass

    def entry():
        x_, yl, co, yh, z = (lax.axis_index(a) for a in AXES)
        me = yh * 4 + yl * 2 + co
        for i in range(8):

            @pl.when(me != i)
            def _():
                signal(device(yh=i // 4, yl=(i // 2) % 2, co=i % 2))

        for i in range(4):

            @pl.when(x_ != i)
            def _():
                signal(device(x=i))

            @pl.when(z != i)
            def _():
                signal(device(z=i))

        return 7 + 3 + 3

    return call(
        main,
        (part, value, dx, table, known, blocks),
        [((8, ROWS, 128), BF16), ((32, 128), F32)],
        RING_SCRATCH[:5]
        + [
            pltpu.VMEM(SHARD, BF16),
            *sems(8, 8),
            pltpu.VMEM((16, WIDTH), F32),
            pltpu.VMEM((4, 2, 16, 128), F32),
            pltpu.SemaphoreType.DMA((4, 2)),
            pltpu.SemaphoreType.DMA((4, 2)),
            pltpu.VMEM((2, 32, 128), F32),
            pltpu.VMEM((8, 32, 128), F32),
            *sems(8, 8),
            pltpu.VMEM((32, 128), F32),
            pltpu.VMEM((4, 32, 128), F32),
            *sems(4, 4),
        ],
        ident,
        riders,
        pieces="out",
        entry=entry,
    )


def lane_heads(value):
    lane = lax.broadcasted_iota(jnp.int32, value.shape, 1)
    zero = jnp.zeros_like(value)
    return jnp.where(lane < 64, value, zero), jnp.where(lane < 64, zero, value)


def put_heads(ref, h, value):
    for hh, one in enumerate(lane_heads(value)):
        ref[2 * h + hh, 0:OWN] = one
        ref[2 * h + hh, OWN:QROWS] = jnp.zeros((QROWS - OWN, 128), BF16)


def wide_mask(mask, n):
    return mask[...] if n == 128 else jnp.concatenate([mask[...]] * (n // 128), axis=1)


def attend_step(n_all, wqkv, wout, bias, mask, ident, riders=()):
    def main(inputs, outs, scratch, sent):
        n_all, wqkv, wout, bias, mask = inputs
        part, qkv, other, att, lse = outs
        kall, vt, qpad, ot, send, recv = scratch
        to = device(co=1 - lax.axis_index("co"))
        yield
        normed = n_all[...].reshape(OWN, WIDTH)
        lse[...] = jnp.zeros_like(lse)
        copies = []
        for h in range(2):
            cols = slice(h * 384, h * 384 + 384)
            block = (dot_nn(normed, wqkv[:, cols]) + bias[:, cols]).astype(BF16)
            qkv[:, cols] = block
            c = remote(
                qkv.at[:, pl.ds(h * 384 + 128, 256)],
                other.at[:, pl.ds(h * 256, 256)],
                send.at[h],
                recv.at[h],
                to,
            )
            c.start()
            copies.append(c)
            put_heads(qpad, h, block[:, 0:128] * 0.125)
            kall[h, 0:OWN] = block[:, 128:256]
            vt[h * 128 : h * 128 + 128, 0:OWN] = block[:, 256:384].T
        sent.extend(copies)
        yield
        for h in range(2):
            copies[h].wait_recv()
            kall[h, OWN:KEYS] = other[:, h * 256 : h * 256 + 128]
            vt[h * 128 : h * 128 + 128, OWN:KEYS] = other[:, h * 256 + 128 : h * 256 + 256].T

            def head(hh, _):
                i = 2 * h + hh
                rows = pl.ds(pl.multiple_of(i * 64, 64), 64)
                for lo, n in CHUNKS:
                    s = dot_nt(kall[h], qpad[i, lo : lo + n]) + wide_mask(mask, n)
                    top = jnp.max(s, axis=0, keepdims=True)
                    e = jnp.exp(s - top)
                    total = jnp.sum(e, axis=0, keepdims=True)
                    p = (e * (1.0 / total)).astype(BF16)
                    ot[rows, lo : lo + n] = dot_nn(vt[rows], p)
                    lse[i, 0:1, lo : lo + n] = top + jnp.log(total)
                return 0

            lax.fori_loop(0, 2, head, 0)
            yield
        att[...] = ot[...].T[0:OWN].astype(BF16)
        part[...] = dot_nn(att[...], wout[...]).astype(BF16).reshape(ALL)

    return call(
        main,
        (n_all, wqkv, wout, bias, mask),
        [
            (ALL, BF16),
            ((OWN, 768), BF16),
            ((OWN, 512), BF16),
            ((OWN, 256), BF16),
            ((4, 8, QROWS), F32),
        ],
        [
            pltpu.VMEM((2, KEYS, 128), BF16),
            pltpu.VMEM((256, KEYS), BF16),
            pltpu.VMEM((4, QROWS, 128), BF16),
            pltpu.VMEM((256, QROWS), F32),
        ]
        + sems(2, 2),
        ident,
        riders,
        links=("core",),
    )


def attend_back_step(d_all, wqkv, wout, qkv, other, lse, mask, ident, riders=()):
    def main(inputs, outs, scratch, sent):
        d_all, wqkv, wout, qkv, other, lse, mask = inputs
        part, dqkv, sums = outs
        kall, vall, kt, qpad, dpad, dqt, dk, dv, away, got, send, recv = scratch
        to = device(co=1 - lax.axis_index("co"))
        yield
        datt = dot_nt(d_all[...].reshape(OWN, WIDTH), wout[...]).astype(BF16)
        copies = []
        for h in range(2):
            base, half = h * 384, h * 256
            put_heads(qpad, h, qkv[:, base : base + 128] * 0.125)
            put_heads(dpad, h, datt[:, h * 128 : h * 128 + 128])
            kall[h, 0:OWN] = qkv[:, base + 128 : base + 256]
            kall[h, OWN:KEYS] = other[:, half : half + 128]
            vall[h, 0:OWN] = qkv[:, base + 256 : base + 384]
            vall[h, OWN:KEYS] = other[:, half + 128 : half + 256]
            kt[h * 128 : h * 128 + 128] = kall[h].T
            dk[h] = jnp.zeros((KEYS, 128), F32)
            dv[h] = jnp.zeros((KEYS, 128), F32)

            def head(hh, _):
                i = 2 * h + hh
                rows = pl.ds(pl.multiple_of(i * 64, 64), 64)
                for lo, n in CHUNKS:
                    qc, dc = qpad[i, lo : lo + n], dpad[i, lo : lo + n]
                    s = dot_nt(kall[h], qc) + wide_mask(mask, n)
                    p = jnp.exp(s - lse[i, 0:1, lo : lo + n])
                    dp = dot_nt(vall[h], dc)
                    delta = jnp.sum(p * dp, axis=0, keepdims=True)
                    ds = (p * (dp - delta)).astype(BF16)
                    dv[h] += dot_nn(p.astype(BF16), dc)
                    dk[h] += dot_nn(ds, qc)
                    dqt[rows, lo : lo + n] = dot_nn(kt[rows], ds)
                return 0

            lax.fori_loop(0, 2, head, 0)
            away[h, :, 0:128] = dk[h, OWN:KEYS].astype(BF16)
            away[h, :, 128:256] = dv[h, OWN:KEYS].astype(BF16)
            c = remote(away.at[h], got.at[h], send.at[h], recv.at[h], to)
            c.start()
            copies.append(c)
            yield
        sent.extend(copies)
        dq = dqt[...].T[0:OWN] * 0.125
        for h in range(2):
            base = h * 384
            dqkv[:, base : base + 128] = dq[:, h * 128 : h * 128 + 128].astype(BF16)
            copies[h].wait_recv()
            dqkv[:, base + 128 : base + 256] = (
                dk[h, 0:OWN] + got[h, :, 0:128].astype(F32)
            ).astype(BF16)
            dqkv[:, base + 256 : base + 384] = (
                dv[h, 0:OWN] + got[h, :, 128:256].astype(F32)
            ).astype(BF16)
        part[...] = dot_nt(dqkv[...], wqkv[...]).astype(BF16).reshape(ALL)
        sums[...] = jnp.zeros_like(sums)
        sums[0:1, :] = jnp.sum(dqkv[...].astype(F32), axis=0, keepdims=True)

    return call(
        main,
        (d_all, wqkv, wout, qkv, other, lse, mask),
        [(ALL, BF16), ((OWN, 768), BF16), ((8, 768), F32)],
        [
            pltpu.VMEM((2, KEYS, 128), BF16),
            pltpu.VMEM((2, KEYS, 128), BF16),
            pltpu.VMEM((256, KEYS), BF16),
            pltpu.VMEM((4, QROWS, 128), BF16),
            pltpu.VMEM((4, QROWS, 128), BF16),
            pltpu.VMEM((256, QROWS), F32),
            pltpu.VMEM((2, KEYS, 128), F32),
            pltpu.VMEM((2, KEYS, 128), F32),
            pltpu.VMEM((2, OWN, 256), BF16),
            pltpu.VMEM((2, OWN, 256), BF16),
        ]
        + sems(2, 2),
        ident,
        riders,
        links=("core",),
    )


def on_device(
    tokens,
    cotangent,
    attend_weight,
    output_weight,
    up_weight,
    down_weight,
    norm_gain,
    norm_shift,
    attend_bias,
    branch_bias,
    layer_scale,
    hidden_bias,
):
    co, yh, z = (lax.axis_index(a) for a in ("co", "yh", "z"))
    attend_weight = attend_weight.reshape(LAYERS, 256, 384)
    first = jnp.pad(tokens, ((0, 15), (0, 0)))
    cot_pieces = jnp.pad(cotangent.astype(BF16), ((0, 15), (0, 0)))
    pack = jnp.concatenate(
        [
            norm_gain.reshape(4, 128),
            norm_shift.reshape(4, 128),
            branch_bias.reshape(4, 128),
            layer_scale.reshape(4, 128),
            attend_bias.reshape(4, 128),
            hidden_bias.reshape(8, 128),
            jnp.zeros((4, 128), F32),
        ]
    )

    def attend_of(l):
        return GatherWeight(attend_weight, l, 0)

    def output_of(l):
        return GatherWeight(output_weight, l, 1)

    def up_of(l):
        return GatherWeight(up_weight, l, 0)

    def down_of(l):
        return GatherWeight(down_weight, l, 1)

    weights = [[None] * 4 for _ in range(LAYERS)]
    ident = iter(range(40))
    (x, n_all, packs), (weights[0][0], weights[0][1]) = first_step(
        first, pack, next(ident), [attend_of(0), output_of(0)]
    )
    table = packs[:, 0:16].transpose(1, 0, 2).reshape(16, WIDTH)
    here = jnp.stack(
        [
            lax.dynamic_index_in_dim(packs, z, keepdims=False),
            lax.dynamic_index_in_dim(packs, z + 4, keepdims=False),
        ]
    )
    row = jnp.arange(OWN)
    block, inside = row // ROWS, row % ROWS

    def hidden_keys(half):
        real = (inside < REAL) | ((inside == REAL) & (block == 3) & (half == 1))
        return jnp.where(real, 0.0, -1e30).astype(F32)

    mask = jnp.concatenate([hidden_keys(co), hidden_keys(1 - co)])
    mask = jnp.broadcast_to(mask[:, None], (KEYS, 128))

    last = jnp.where((co == 1) & (z == 3), REAL + 1, REAL)
    real_row = jnp.arange(ROWS)[:, None] < last

    saved = []
    for l in range(LAYERS):
        wqkv, wout = weights[l][:2]
        ab = here[:, 16 + 2 * l : 18 + 2 * l]
        qkv_bias = jnp.concatenate(
            [ab[0, 0], jnp.zeros(128), ab[0, 1], ab[1, 0], jnp.zeros(128), ab[1, 1]]
        )[None]
        riders = [up_of(l)]
        if l == 1:
            riders.append(Spread((cot * table[SCALE + 3]).astype(BF16)))
        n1 = n_all
        (part, qkv, other, att, lse), got = attend_step(
            n1, wqkv, wout, qkv_bias, mask, next(ident), riders
        )
        weights[l][2] = got[0]
        if l == 1:
            d_all = got[1]
        at = (BRANCH + 2 * l, SCALE + 2 * l, GAIN + 2 * l + 1, SHIFT + 2 * l + 1)
        riders = [down_of(l)] + ([Pieces(cot_pieces)] if l == 0 else [])
        (a, m, n_all), got = forward_step(part, x, table, at, next(ident), riders)
        weights[l][3] = got[0]
        if l == 0:
            cot = jnp.where(real_row, got[1].astype(F32), 0.0)
        wup, wdown = weights[l][2:]
        n2 = n_all.reshape(OWN, WIDTH)
        hb = here[:, 20 + 4 * l : 24 + 4 * l].reshape(WIDTH)
        u = dot_nn(n2, wup) + hb
        g = gelu_value(u).astype(BF16)
        part = dot_nn(g, wdown).astype(BF16).reshape(ALL)
        saved.append([x, n1.reshape(OWN, WIDTH), qkv, other, att, lse, a, m, n2, u, g])
        if l + 1 < LAYERS:
            at = (BRANCH + 2 * l + 1, SCALE + 2 * l + 1, GAIN + 2 * l + 2, SHIFT + 2 * l + 2)
            (f, x, n_all), weights[1][:2] = forward_step(
                part, m, table, at, next(ident), [attend_of(1), output_of(1)]
            )
            saved[l].append(f)
        else:
            end = End(part, m, cot, table, (BRANCH + 3, SCALE + 3))

    gain_sums, shift_sums, scale_sums, branch_sums = ([None] * 4 for _ in range(4))
    hidden_sums, qkv_sums, grads = [None] * LAYERS, [None] * LAYERS, [[None] * 4, [None] * 4]
    dx = cot

    def summing(block):
        return SumBlock(block.shape, block)

    for l in reversed(range(LAYERS)):
        wqkv, wout, wup, wdown = weights[l]
        x, n1, qkv, other, att, lse, a, m, n2, u, g = saved[l][:11]
        df = d_all.reshape(OWN, WIDTH)
        du = (dot_nt(df, wdown) * gelu_slope(u)).astype(BF16)
        part = dot_nt(du, wup).astype(BF16).reshape(ALL)
        hidden_sums[l] = jnp.sum(du.astype(F32), axis=0)
        at = (GAIN + 2 * l + 1, SCALE + 2 * l)
        riders = [ReduceWeight(g, df, 1)]
        if l == 0:
            riders += [summing(attend_block), summing(output_block)]
        (dm, sums, d_all), got = backward_step(part, m, dx, a, table, at, next(ident), riders)
        down_block = got[0]
        if l == 0:
            grads[1][:2] = got[1:]
        gain_sums[2 * l + 1], shift_sums[2 * l + 1] = sums[0], sums[1]
        scale_sums[2 * l], branch_sums[2 * l] = sums[2], sums[3]
        da = d_all.reshape(OWN, WIDTH)
        riders = [ReduceWeight(n2, du, 0), summing(down_block)]
        riders.append(end if l == 1 else PiecesOut(x_end))
        (part, dqkv, qkv_sum), got = attend_back_step(
            d_all, wqkv, wout, qkv, other, lse, mask, next(ident), riders
        )
        up_block, grads[l][3] = got[:2]
        qkv_sums[l] = qkv_sum[0]
        if l == 1:
            x_end, sums = got[2:]
            scale_sums[3], branch_sums[3] = sums[2], sums[3]
            at = (GAIN + 2 * l, SCALE + 2 * l - 1)
            riders = [ReduceWeight(n1, dqkv, 0), ReduceWeight(att, da, 1), summing(up_block)]
            (dx, sums, d_all), got = backward_step(
                part, x, dm, saved[l - 1][11], table, at, next(ident), riders
            )
            attend_block, output_block, grads[l][2] = got
            scale_sums[2 * l - 1], branch_sums[2 * l - 1] = sums[2], sums[3]
            gain_sums[2 * l], shift_sums[2 * l] = sums[0], sums[1]
        else:
            out_pieces = got[2]
            riders = [ReduceSum(n1, dqkv, 0), ReduceSum(att, da, 1), summing(up_block)]
            zero = jnp.zeros(WIDTH)
            known = jnp.stack(
                [zero] + gain_sums[1:] + [zero] + shift_sums[1:] + branch_sums + scale_sums
            )
            blocks = jnp.concatenate(
                [
                    jnp.stack(qkv_sums).reshape(2, 2, 3, 128).transpose(1, 0, 2, 3).reshape(2, 6, 128),
                    jnp.stack(hidden_sums).reshape(2, 2, 4, 128).transpose(1, 0, 2, 3).reshape(2, 8, 128),
                    jnp.zeros((2, 2, 128), F32),
                ],
                axis=1,
            )
            (grad_pieces, small), got = last_step(
                part, x, dm, table, known, blocks, (GAIN,), next(ident), riders
            )
            grads[0][:3] = got

    bias_grad = small[16:22].reshape(2, 3, 128)[:, 0::2]

    def rows(landed):
        return jnp.concatenate(
            [landed[0:7, 0:REAL].reshape(7 * REAL, 128), landed[7, 0 : REAL + 1]]
        ).astype(F32)

    return (
        rows(out_pieces),
        rows(grad_pieces),
        jnp.stack([grads[l][0] for l in range(LAYERS)]).reshape(LAYERS, 256, 3, 128),
        jnp.stack([grads[l][1] for l in range(LAYERS)]),
        jnp.stack([grads[l][2] for l in range(LAYERS)]),
        jnp.stack([grads[l][3] for l in range(LAYERS)]),
        small[0:4].reshape(2, 2, 128),
        small[4:8].reshape(2, 2, 128),
        bias_grad,
        small[8:12].reshape(2, 2, 128),
        small[12:16].reshape(2, 2, 128),
        small[22:30].reshape(2, 512),
    )


def solution(mesh):
    split = Mesh(mesh.devices.reshape(4, 2, 2, 2, 4), AXES)
    images, row, col = ("x", "yl", "co"), ("yl", "co"), ("yh", "z")
    placed = (
        P(images, col),
        P(images, col),
        P(None, row, None, col),
        P(None, col, row),
        P(None, row, col),
        P(None, col, row),
        P(None, None, col),
        P(None, None, col),
        P(None, None, col),
        P(None, None, col),
        P(None, None, col),
        P(None, col),
    )
    return jax.shard_map(
        on_device, mesh=split, in_specs=placed, out_specs=placed, check_vma=False
    )
```

```python
import jax
import jax.numpy as jnp
from jax import lax
from jax.experimental import pallas as pl
from jax.experimental.pallas import tpu as pltpu
from jax.sharding import Mesh, PartitionSpec as P

WIDTH = 1024
HALF = WIDTH // 2
SEQ = 1025
LAYERS = 2
REAL = 128
ROWS = 144
TAIL = ROWS - REAL
OWN = 4 * ROWS
KEYS = 2 * OWN
QROWS = 640
CHUNKS = ((0, 256), (256, 256), (512, 128))
EPS = 1e-06
ROOT_HALF = 0.7071067811865476
INV_ROOT_TWO_PI = 0.3989422804014327
MESH = pl.DeviceIdType.MESH
AXES = ("x", "yl", "co", "yh", "z")
VM = pl.BlockSpec(memory_space=pltpu.VMEM)
ANY = pl.BlockSpec(memory_space=pl.ANY)
F32 = jnp.float32
BF16 = jnp.bfloat16


def gelu_value(value):
    return 0.5 * value * (1.0 + lax.erf(value * ROOT_HALF))


def gelu_slope(value):
    return 0.5 * (1.0 + lax.erf(value * ROOT_HALF)) + value * INV_ROOT_TWO_PI * jnp.exp(
        -0.5 * value * value
    )


def dot_nt(left, right):
    return lax.dot_general(left, right, (((1,), (1,)), ((), ())), preferred_element_type=F32)


def dot_tn(left, right):
    return lax.dot_general(left, right, (((0,), (0,)), ((), ())), preferred_element_type=F32)


def dot_nn(left, right):
    return jnp.dot(left, right, preferred_element_type=F32)


def device(**moved):
    return tuple(moved[a] if a in moved else lax.axis_index(a) for a in AXES)


def remote(src, dst, send, recv, to):
    return pltpu.make_async_remote_copy(
        src_ref=src, dst_ref=dst, send_sem=send, recv_sem=recv, device_id=to, device_id_type=MESH
    )


def signal(to):
    pl.semaphore_signal(
        pltpu.get_barrier_semaphore(), inc=1, device_id=to, device_id_type=MESH
    )


class Ring:
    def __init__(self, axis):
        self.axis = axis
        if axis == "y":
            self.me = lax.axis_index("yh") * 2 + lax.axis_index("yl")
        else:
            self.me = lax.axis_index(axis)
        self.right = lax.rem(self.me + 1, 4)
        self.left = lax.rem(self.me + 3, 4)
        self.across = lax.rem(self.me + 2, 4)
        self.to_right, self.to_left = self.at(self.right), self.at(self.left)

    def at(self, index):
        if self.axis == "y":
            return device(yh=index // 2, yl=lax.rem(index, 2))
        return device(**{self.axis: index})


def greet(links, more=0, home=None):
    count = more
    for link in links:
        if link == "core":
            signal(device(co=1 - lax.axis_index("co")))
            count += 1
        else:
            ring = Ring(link)
            signal(ring.to_right)
            signal(ring.to_left)
            count += 2
            if link != "y":
                signal(ring.at(ring.across))
                count += 1
    barrier = pltpu.get_barrier_semaphore()
    if home is None:
        pl.semaphore_wait(barrier, count)
    else:

        @pl.when(home)
        def _():
            pl.semaphore_wait(barrier, count + 7)

        @pl.when(jnp.logical_not(home))
        def _():
            pl.semaphore_wait(barrier, count + 8)


def in_turns(jobs):
    waiting = [[0.0, i, job] for i, job in enumerate(jobs)]
    while waiting:
        first = min(waiting, key=lambda w: w[:2])
        try:
            first[0] = next(first[2])
        except StopIteration:
            waiting.remove(first)


def delayed(job, time):
    while True:
        try:
            yield time + next(job)
        except StopIteration as end:
            return end.value


def by_columns(ref, lead, half):
    return ref.at[lead, pl.ds(0, REAL), pl.ds(half * HALF, HALF)]


def by_rows(ref, lead, half):
    rows = ref.shape[1] // 2
    return ref.at[lead, pl.ds(half * rows, rows), :]


def reduce_on(ring, half, part, fin, relay, stage, send, recv, sent, unit=1.0):
    def copy(i, src, dst, to):
        c = remote(src, dst, send.at[i], recv.at[i], to)
        c.start()
        sent.append(c)
        return c

    far_r = copy(0, half(part, ring.across, 0), relay.at[0], ring.to_right)
    far_l = copy(1, half(part, ring.across, 1), relay.at[1], ring.to_left)
    near_r = copy(2, half(part, ring.right, 1), half(fin, 0, 1), ring.to_right)
    near_l = copy(3, half(part, ring.left, 0), half(fin, 1, 0), ring.to_left)
    yield 3.0 * unit
    far_r.wait_recv()
    stage[0] = (half(part, ring.right, 0)[...].astype(F32) + relay[0].astype(F32)).astype(BF16)
    sum_r = copy(4, stage.at[0], half(fin, 0, 0), ring.to_right)
    far_l.wait_recv()
    stage[1] = (half(part, ring.left, 1)[...].astype(F32) + relay[1].astype(F32)).astype(BF16)
    sum_l = copy(5, stage.at[1], half(fin, 1, 1), ring.to_left)
    yield 9.0 * unit
    for c in (near_r, near_l, sum_r, sum_l):
        c.wait_recv()
    own = part.at[ring.me, pl.ds(0, fin.shape[1])][...]
    return own.astype(F32) + fin[0].astype(F32) + fin[1].astype(F32)


def gather_on(ring, slot, own, send, recv, sent, landed=None, unit=1.0):
    def copy(i, src, owner, half, to):
        return remote(src, slot(owner, half), send.at[i], recv.at[i], to)

    def go(*what):
        c = copy(*what)
        c.start()
        sent.append(c)

    def lands(i, owner, half):
        copy(i, slot(owner, half), owner, half, ring.to_right).wait_recv()

    go(0, own(0), ring.me, 0, ring.to_right)
    go(1, own(1), ring.me, 1, ring.to_left)
    go(2, own(1), ring.me, 1, ring.to_right)
    go(3, own(0), ring.me, 0, ring.to_left)
    yield 3.5 * unit
    lands(0, ring.left, 0)
    go(4, slot(ring.left, 0), ring.left, 0, ring.to_right)
    lands(1, ring.right, 1)
    go(5, slot(ring.right, 1), ring.right, 1, ring.to_left)
    yield 6.5 * unit
    lands(2, ring.left, 1)
    if landed is not None:
        landed(ring.left)
    lands(3, ring.right, 0)
    if landed is not None:
        landed(ring.right)
    yield 9.0 * unit
    lands(4, ring.across, 0)
    lands(5, ring.across, 1)
    if landed is not None:
        landed(ring.across)


def gather_slots(ring, out, half, send, recv, sent):
    def slot(owner, h):
        return half(out, owner, h)

    yield from gather_on(ring, slot, lambda h: slot(ring.me, h), send, recv, sent)


def sems(*counts):
    return [pltpu.SemaphoreType.DMA((c,)) for c in counts]


def tail_roles():
    z, second = lax.axis_index("z"), lax.axis_index("co") == 1
    return z, second & (z == 3), second & (z != 3)


def shard_sum(part, fin, relay, stage, tails, tail, send, recv, tsend, trecv, sent):
    z, holds, gives = tail_roles()

    def tail_to(slot):
        src = part.at[3, pl.ds(REAL, TAIL), :]
        return remote(src, tails.at[slot], tsend.at[0], trecv.at[slot], device(z=3))

    @pl.when(gives)
    def _():
        tail_to(z).start()

    total = yield from reduce_on(
        Ring("z"), by_columns, part, fin, relay, stage, send, recv, sent
    )
    tail[...] = jnp.zeros_like(tail)

    @pl.when(holds)
    def _():
        for i in range(3):
            tail_to(i).wait_recv()
        tail[...] = part[3, REAL:ROWS].astype(F32) + sum(tails[i].astype(F32) for i in range(3))

    @pl.when(gives)
    def _():
        tail_to(z).wait_send()

    return jnp.concatenate([total, tail[...]], axis=0)


def shard_spread(out, send, recv, tsend, trecv, sent):
    z, holds, gives = tail_roles()

    def tail_to(i):
        ref = out.at[3, pl.ds(REAL, TAIL), :]
        return remote(ref, ref, tsend.at[i], trecv.at[0], device(z=i))

    @pl.when(holds)
    def _():
        for i in range(3):
            tail_to(i).start()

    yield from gather_slots(Ring("z"), out, by_columns, send, recv, sent)

    @pl.when(gives)
    def _():
        tail_to(0).wait_recv()

    @pl.when(holds)
    def _():
        for i in range(3):
            tail_to(i).wait_send()


SUM_SCRATCH = [
    pltpu.VMEM((2, REAL, WIDTH), BF16),
    pltpu.VMEM((2, REAL, HALF), BF16),
    pltpu.VMEM((2, REAL, HALF), BF16),
    pltpu.VMEM((3, TAIL, WIDTH), BF16),
    pltpu.VMEM((TAIL, WIDTH), F32),
] + sems(6, 6, 1, 3)
SPREAD_SCRATCH = sems(6, 6, 3, 1)
SUMMING = len(SUM_SCRATCH)
RING_SCRATCH = SUM_SCRATCH + SPREAD_SCRATCH


class GatherWeight:
    links = ("y", "core")

    def __init__(self, shards, layer, side):
        rows, columns = shards.shape[1:]
        self.layer, self.side, self.rows, self.columns = layer, side, rows, columns
        full = (4 * rows, 2 * columns) if side == 0 else (2 * rows, 4 * columns)
        self.inputs = [(shards, ANY)]
        self.outs = [(full, BF16, ANY)]
        self.scratch = sems(6, 6, 4, 4, 1)

    def run(self, inputs, outs, scratch, sent):
        (shards,), (out,) = inputs, outs
        send, recv, csend, crecv, local = scratch
        own = shards.at[self.layer]
        ring, co = Ring("y"), lax.axis_index("co")
        rows, columns = self.rows, self.columns

        def block(y, core, half=None):
            yh, r = y // 2, lax.rem(y, 2) * 2 + core
            down, along = (r, yh) if self.side == 0 else (yh, r)
            first, count = down * rows, rows
            if half is not None:
                count = rows // 2
                first = first + half * count
            return out.at[
                pl.ds(pl.multiple_of(first, 16), count),
                pl.ds(pl.multiple_of(along * columns, 128), columns),
            ]

        def to_core(i, src, y):
            c = remote(src, block(y, co), csend.at[i], crecv.at[i], device(co=1 - co))
            c.start()
            sent.append(c)

        keep = pltpu.make_async_copy(own, block(ring.me, co), local.at[0])
        keep.start()
        to_core(0, own, ring.me)
        numbers = iter((1, 2, 3))
        yield from gather_on(
            ring,
            lambda y, half: block(y, co, half),
            lambda half: own.at[pl.ds(half * (rows // 2), rows // 2), :],
            send,
            recv,
            sent,
            lambda y: to_core(next(numbers), block(y, co), y),
        )
        keep.wait()
        yield 12.0
        for i, y in enumerate((ring.me, ring.left, ring.right, ring.across)):
            there = block(y, 1 - co)
            remote(there, there, csend.at[i], crecv.at[i], device(co=1 - co)).wait_recv()


class ReduceWeight:
    links = ("y", "core")

    def __init__(self, left, right, side):
        rows, columns = left.shape[1], right.shape[1]
        self.full = rows, columns
        rows, columns = (rows // 4, columns // 2) if side == 0 else (rows // 2, columns // 4)
        self.side, self.rows, self.columns = side, rows, columns
        self.inputs = [(left, VM), (right, VM)]
        self.outs = [((rows, columns), BF16, VM)]
        self.scratch = [
            pltpu.VMEM(self.full, BF16),
            pltpu.VMEM((4, rows, columns), BF16),
            pltpu.VMEM((4, rows, columns), BF16),
            pltpu.VMEM((2, rows, columns), BF16),
            pltpu.VMEM((2, rows // 2, columns), BF16),
            pltpu.VMEM((2, rows // 2, columns), BF16),
        ] + sems(4, 4, 6, 6)

    def run(self, inputs, outs, scratch, sent):
        total = yield from self.total(inputs, scratch, sent)
        outs[0][...] = total.astype(BF16)

    def total(self, inputs, scratch, sent):
        left, right = inputs
        part, got, pair, fin, relay, stage, csend, crecv, send, recv = scratch
        for first in range(0, self.full[0], 256):
            part[first : first + 256] = dot_tn(left[:, first : first + 256], right[...]).astype(
                BF16
            )
        co = lax.axis_index("co")
        rows, columns = self.rows, self.columns

        def block(y, core):
            yh, r = y // 2, (y % 2) * 2 + core
            down, along = (r, yh) if self.side == 0 else (yh, r)
            return part.at[
                pl.ds(pl.multiple_of(down * rows, 16), rows),
                pl.ds(pl.multiple_of(along * columns, 128), columns),
            ]

        copies = []
        for y in range(4):
            c = remote(
                block(y, 1 - co), got.at[y], csend.at[y], crecv.at[y], device(co=1 - co)
            )
            c.start()
            copies.append(c)
        sent.extend(copies)
        yield 5.0
        for y in range(4):
            copies[y].wait_recv()
            pair[y] = (block(y, co)[...].astype(F32) + got[y].astype(F32)).astype(BF16)
        job = reduce_on(Ring("y"), by_rows, pair, fin, relay, stage, send, recv, sent)
        return (yield from delayed(job, 6.0))


class SumBlock:
    links = ("x",)

    def __init__(self, shape, block=None):
        rows, columns = shape
        self.shape, self.rows = shape, rows // 4
        self.inputs = [] if block is None else [(block, VM)]
        self.outs = [(shape, F32, VM)]
        quarters = (4, rows // 4, columns)
        self.scratch = [pltpu.VMEM(quarters, BF16) for _ in range(3)] + sems(4, 4, 4, 4)

    def run(self, inputs, outs, scratch, sent):
        yield from self.total(inputs[0][...], outs[0], scratch, sent)

    def total(self, value, out, scratch, sent):
        part, got, every, send, recv, gsend, grecv = scratch
        ring = Ring("x")
        others = (ring.across, ring.right, ring.left)
        for i in range(4):
            part[i] = value[i * self.rows : (i + 1) * self.rows].astype(BF16)

        def give(slot, to):
            return remote(part.at[to], got.at[slot], send.at[to], recv.at[slot], ring.at(to))

        def share(slot, to):
            return remote(
                every.at[slot], every.at[slot], gsend.at[to], grecv.at[slot], ring.at(to)
            )

        for i in others:
            c = give(ring.me, i)
            c.start()
            sent.append(c)
        got[ring.me] = part[ring.me]
        yield 4.0
        for i in others:
            give(i, i).wait_recv()
        every[ring.me] = sum(got[i].astype(F32) for i in range(4)).astype(BF16)
        for i in others:
            c = share(ring.me, i)
            c.start()
            sent.append(c)
        yield 8.0
        for i in others:
            share(i, i).wait_recv()
        for i in range(4):
            out[i * self.rows : (i + 1) * self.rows] = every[i].astype(F32)


class ReduceSum:
    links = ("y", "core", "x")

    def __init__(self, left, right, side):
        self.first = ReduceWeight(left, right, side)
        self.second = SumBlock((self.first.rows, self.first.columns))
        self.inputs, self.outs = self.first.inputs, self.second.outs
        self.scratch = self.first.scratch + self.second.scratch

    def run(self, inputs, outs, scratch, sent):
        n = len(self.first.scratch)
        total = yield from self.first.total(inputs, scratch[:n], sent)
        yield from delayed(self.second.total(total, outs[0], scratch[n:], sent), 15.0)


class Pieces:
    links = ()
    pieces = "in"

    def __init__(self, source):
        self.inputs = [(source, VM)]
        self.outs = [(SHARD, BF16, VM)]
        self.scratch = sems(8, 8)

    def run(self, inputs, outs, scratch, sent):
        (source,), (landed,), (send, recv) = inputs, outs, scratch
        co, yh, z = (lax.axis_index(a) for a in ("co", "yh", "z"))
        me, home = yh * 4 + z, yh == co

        def piece(j):
            src = source.at[pl.ds(j * REAL, ROWS), :]
            dst = landed.at[:, pl.ds(pl.multiple_of(me * 128, 128), 128)]
            to = device(yh=co, co=j // 4, z=j % 4)
            there = remote(src, dst, send.at[j], recv.at[me], to)
            return there, pltpu.make_async_copy(src, dst, recv.at[me]), home & (co * 4 + z == j)

        for j in range(8):
            there, here, own = piece(j)

            @pl.when(own)
            def _():
                here.start()

            @pl.when(jnp.logical_not(own))
            def _():
                there.start()

        yield 9.0
        for q in range(8):
            dst = landed.at[:, pl.ds(q * 128, 128)]
            own = home & (me == q)

            @pl.when(own)
            def _():
                pltpu.make_async_copy(dst, dst, recv.at[q]).wait()

            @pl.when(jnp.logical_not(own))
            def _():
                remote(dst, dst, send.at[q], recv.at[q], Ring("z").to_right).wait_recv()

        for j in range(8):
            there, here, own = piece(j)

            @pl.when(jnp.logical_not(own))
            def _():
                there.wait_send()


class PiecesOut:
    links = ()
    pieces = "out"

    def __init__(self, source):
        self.inputs = [(source, VM)]
        self.outs = [((8, ROWS, 128), BF16, VM)]
        self.scratch = [pltpu.VMEM(SHARD, BF16)] + sems(8, 8)

    def run(self, inputs, outs, scratch, sent):
        scratch[0][...] = inputs[0][...].astype(BF16)
        yield from self.give(scratch[0], outs[0], *scratch[1:])

    @staticmethod
    def give(source, landed, send, recv):
        co, yh, z = (lax.axis_index(a) for a in ("co", "yh", "z"))
        shard, home = co * 4 + z, yh == co

        def piece(q):
            src = source.at[:, pl.ds(q * 128, 128)]
            dst = landed.at[shard]
            to = device(co=yh, yh=q // 4, z=q % 4)
            there = remote(src, dst, send.at[q], recv.at[shard], to)
            return there, pltpu.make_async_copy(src, dst, recv.at[shard]), home & (
                yh * 4 + z == q
            )

        for q in range(8):
            there, here, own = piece(q)

            @pl.when(own)
            def _():
                here.start()

            @pl.when(jnp.logical_not(own))
            def _():
                there.start()

        yield 11.0
        for s in range(8):
            dst = landed.at[s]
            own = home & (shard == s)

            @pl.when(own)
            def _():
                pltpu.make_async_copy(dst, dst, recv.at[s]).wait()

            @pl.when(jnp.logical_not(own))
            def _():
                remote(dst, dst, send.at[s], recv.at[s], Ring("z").to_right).wait_recv()

            there, here, mine = piece(s)

            @pl.when(jnp.logical_not(mine))
            def _():
                there.wait_send()


def greet_pieces(way):
    co, yh, z = (lax.axis_index(a) for a in ("co", "yh", "z"))
    home = yh == co
    for j in range(8):
        if way == "in":
            own, source = home & (yh * 4 + z == j), dict(yh=j // 4, z=j % 4, co=yh)
        else:
            own, source = home & (co * 4 + z == j), dict(yh=co, co=j // 4, z=j % 4)

        @pl.when(jnp.logical_not(own))
        def _():
            signal(device(**source))

    return home


class Spread:
    links = ("z",)

    def __init__(self, shard):
        self.inputs = [(shard, VM)]
        self.outs = [(ALL, BF16, VM)]
        self.scratch = SPREAD_SCRATCH

    def run(self, inputs, outs, scratch, sent):
        outs[0][lax.axis_index("z")] = inputs[0][...]
        yield from shard_spread(outs[0], *scratch, sent)


class End:
    links = ("z",)

    def __init__(self, part, x, cot, table, at):
        self.at = at
        self.inputs = [(a, VM) for a in (part, x, cot, table)]
        self.outs = [(SHARD, F32, VM), (SUMS, F32, VM)]
        self.scratch = SUM_SCRATCH

    def run(self, inputs, outs, scratch, sent):
        (part, x, cot, table), (x_out, sums) = inputs, outs
        total = yield from shard_sum(part, *scratch, sent)
        bias, scale = (table[r : r + 1, :] for r in self.at)
        branch = total + bias
        x_out[...] = x[...] + scale * branch
        df = (cot[...] * scale).astype(BF16)
        sums[...] = jnp.zeros_like(sums)
        sums[2:3, :] = jnp.sum(cot[...] * branch, axis=0, keepdims=True)
        sums[3:4, :] = jnp.sum(df.astype(F32), axis=0, keepdims=True)


def norm_of(value):
    mean = jnp.mean(value, axis=1, keepdims=True)
    meansq = jnp.mean(value * value, axis=1, keepdims=True)
    rstd = lax.rsqrt(meansq - mean * mean + EPS)
    return (value - mean) * rstd, rstd


def norm_back(grad, value, gain):
    hat, rstd = norm_of(value)
    e = grad * gain
    return (
        rstd
        * (
            e
            - jnp.mean(e, axis=1, keepdims=True)
            - hat * jnp.mean(e * hat, axis=1, keepdims=True)
        ),
        jnp.sum(grad * hat, axis=0, keepdims=True),
        jnp.sum(grad, axis=0, keepdims=True),
    )


GAIN, SHIFT, BRANCH, SCALE = 0, 4, 8, 12
SHARD = (ROWS, WIDTH)
ALL = (4, ROWS, WIDTH)
SUMS = (8, WIDTH)


def call(main, inputs, outs, scratch, ident, riders=(), links=("z",), pieces=None, entry=None):
    inputs = [(a, VM) for a in inputs]
    outs = [(s, d, VM) for s, d in outs]
    jobs = [(inputs, outs, list(scratch))] + [(r.inputs, r.outs, r.scratch) for r in riders]
    links = {link: None for link in links}
    for r in riders:
        links.update({link: None for link in r.links})
        pieces = pieces or getattr(r, "pieces", None)
    runs = [main] + [r.run for r in riders]

    def kernel(*refs):
        refs, split = list(refs), []
        for kind in range(3):
            for job in jobs:
                split.append([refs.pop(0) for _ in job[kind]])
        n = len(jobs)
        for job, outs_here in zip(jobs, split[n : 2 * n]):
            for out, ref in zip(job[1], outs_here):
                if out[0] == ALL:
                    ref[:, REAL:ROWS] = jnp.zeros((4, TAIL, WIDTH), BF16)
        more = 0 if entry is None else entry()
        greet(links, more, None if pieces is None else greet_pieces(pieces))
        sent = []
        in_turns(
            run(split[i], split[n + i], split[2 * n + i], sent) for i, run in enumerate(runs)
        )
        for c in sent:
            c.wait_send()

    results = pl.pallas_call(
        kernel,
        out_shape=[jax.ShapeDtypeStruct(o[0], o[1]) for job in jobs for o in job[1]],
        in_specs=[i[1] for job in jobs for i in job[0]],
        out_specs=[o[2] for job in jobs for o in job[1]],
        scratch_shapes=[s for job in jobs for s in job[2]],
        compiler_params=pltpu.CompilerParams(
            collective_id=ident, has_side_effects=True, vmem_limit_bytes=28 * 2**20
        ),
    )(*[i[0] for job in jobs for i in job[0]])
    n = len(outs)
    return results[:n], results[n:]


def forward_step(part, x, table, at, ident, riders=()):
    def main(inputs, outs, scratch, sent):
        (part, x, table), (branch_out, x_out, n_out) = inputs, outs
        total = yield from shard_sum(part, *scratch[:SUMMING], sent)
        bias, scale, gain, shift = (table[r : r + 1, :] for r in at)
        branch = total + bias
        x_new = x[...] + scale * branch
        branch_out[...] = branch
        x_out[...] = x_new
        hat, _ = norm_of(x_new)
        n_out[lax.axis_index("z")] = (hat * gain + shift).astype(BF16)
        yield from delayed(shard_spread(n_out, *scratch[SUMMING:], sent), 10.0)

    return call(
        main,
        (part, x, table),
        [(SHARD, F32), (SHARD, F32), (ALL, BF16)],
        RING_SCRATCH,
        ident,
        riders,
    )


def backward_step(part, value, dx, branch, table, at, ident, riders=()):
    def main(inputs, outs, scratch, sent):
        (part, value, dx, branch, table), (dx_out, sums, d_out) = inputs, outs
        total = yield from shard_sum(part, *scratch[:SUMMING], sent)
        gain, scale = (table[r : r + 1, :] for r in at)
        dr, gain_sum, shift_sum = norm_back(total, value[...], gain)
        dx_new = dx[...] + dr
        dx_out[...] = dx_new
        df = (dx_new * scale).astype(BF16)
        d_out[lax.axis_index("z")] = df
        spread = delayed(shard_spread(d_out, *scratch[SUMMING:], sent), 10.0)
        time = next(spread)
        sums[...] = jnp.zeros_like(sums)
        sums[0:1, :] = gain_sum
        sums[1:2, :] = shift_sum
        sums[2:3, :] = jnp.sum(dx_new * branch[...], axis=0, keepdims=True)
        sums[3:4, :] = jnp.sum(df.astype(F32), axis=0, keepdims=True)
        yield time
        yield from spread

    return call(
        main,
        (part, value, dx, branch, table),
        [(SHARD, F32), (SUMS, F32), (ALL, BF16)],
        RING_SCRATCH,
        ident,
        riders,
    )


def first_step(tokens, pack, ident, riders):
    pieces = Pieces(tokens)

    def main(inputs, outs, scratch, sent):
        tokens, pack = inputs
        x_out, n_out, pack_out = outs
        landed, psend, precv, ksend, krecv = scratch[:5]
        z = lax.axis_index("z")
        me = lax.axis_index("yh") * 4 + z
        arrive = pieces.run([tokens], [landed], [psend, precv], sent)
        next(arrive)
        pack_out[me] = pack[...]

        def note(j, slot):
            return remote(
                pack, pack_out.at[slot], ksend.at[j], krecv.at[slot], device(yh=j // 4, z=j % 4)
            )

        for j in range(8):

            @pl.when(me != j)
            def _():
                note(j, me).start()

        yield 8.0
        for _ in arrive:
            pass
        for q in range(8):

            @pl.when(me != q)
            def _():
                note(q, q).wait_recv()

        value = landed[...].astype(F32)
        x_out[...] = value
        gain = jnp.concatenate([pack_out[q, GAIN : GAIN + 1, :] for q in range(8)], axis=1)
        shift = jnp.concatenate([pack_out[q, SHIFT : SHIFT + 1, :] for q in range(8)], axis=1)
        hat, _ = norm_of(value)
        n_out[z] = (hat * gain + shift).astype(BF16)
        yield from delayed(shard_spread(n_out, *scratch[5:], sent), 10.0)
        for j in range(8):

            @pl.when(me != j)
            def _():
                note(j, me).wait_send()

    def entry():
        yh, z = lax.axis_index("yh"), lax.axis_index("z")
        for j in range(8):

            @pl.when(yh * 4 + z != j)
            def _():
                signal(device(yh=j // 4, z=j % 4))

        return 7

    return call(
        main,
        (tokens, pack),
        [(SHARD, F32), (ALL, BF16), ((8, 32, 128), F32)],
        [pltpu.VMEM(SHARD, BF16)] + sems(8, 8, 8, 8) + SPREAD_SCRATCH,
        ident,
        riders,
        pieces="in",
        entry=entry,
    )


def last_step(part, value, dx, table, known, blocks, at, ident, riders):
    def main(inputs, outs, scratch, sent):
        part, value, dx, table, known, blocks = inputs
        landed, small = outs
        ring_scratch, scratch = scratch[:SUMMING], scratch[SUMMING:]
        both, psend, precv, vectors, zgot, zsend, zrecv = scratch[:7]
        owned, ygot, ysend, yrecv, sub, xgot, xsend, xrecv = scratch[7:]
        x_, yl, co, yh, z = (lax.axis_index(a) for a in AXES)
        total = yield from shard_sum(part, *ring_scratch, sent)
        (gain,) = (table[r : r + 1, :] for r in at)
        dr, gain_sum, shift_sum = norm_back(total, value[...], gain)
        both[...] = (dx[...] + dr).astype(BF16)
        give = PiecesOut.give(both, landed, psend, precv)
        next(give)
        vectors[...] = known[...]
        vectors[at[0] : at[0] + 1, :] = gain_sum
        vectors[at[0] + SHIFT : at[0] + SHIFT + 1, :] = shift_sum

        def on_z(there, slot, h):
            cut = vectors.at[:, pl.ds((h * 4 + there) * 128, 128)]
            return remote(
                cut, zgot.at[slot, h], zsend.at[there, h], zrecv.at[slot, h], device(z=there)
            )

        def on_y(there, slot):
            to = device(yh=there // 4, yl=(there // 2) % 2, co=there % 2)
            return remote(
                owned.at[there // 4], ygot.at[slot], ysend.at[there], yrecv.at[slot], to
            )

        def on_x(there, slot):
            return remote(sub, xgot.at[slot], xsend.at[there], xrecv.at[slot], device(x=there))

        def others(me, count, do):
            for i in range(count):

                @pl.when(me != i)
                def _():
                    do(i)

        me = yh * 4 + yl * 2 + co

        def both_halves(do):
            def run(i):
                do(i, 0)
                do(i, 1)

            return run

        others(z, 4, both_halves(lambda i, h: on_z(i, z, h).start()))
        for h in range(2):
            zgot[z, h] = vectors[:, pl.ds(pl.multiple_of((h * 4 + z) * 128, 128), 128)]
        yield 13.0
        others(z, 4, both_halves(lambda i, h: on_z(i, i, h).wait_recv()))
        owned[:, 0:16] = zgot[0] + zgot[1] + zgot[2] + zgot[3]
        owned[:, 16:32] = blocks[...]
        others(me, 8, lambda i: on_y(i, me).start())
        ygot[me] = owned[yh]
        yield 16.0
        others(me, 8, lambda i: on_y(i, i).wait_recv())
        sub[...] = sum(ygot[i] for i in range(8))
        others(x_, 4, lambda i: on_x(i, x_).start())
        xgot[x_] = sub[...]
        yield 19.0
        others(x_, 4, lambda i: on_x(i, i).wait_recv())
        small[...] = sum(xgot[i] for i in range(4))
        others(z, 4, both_halves(lambda i, h: on_z(i, z, h).wait_send()))
        others(me, 8, lambda i: on_y(i, me).wait_send())
        others(x_, 4, lambda i: on_x(i, x_).wait_send())
        for _ in give:
            pass

    def entry():
        x_, yl, co, yh, z = (lax.axis_index(a) for a in AXES)
        me = yh * 4 + yl * 2 + co
        for i in range(8):

            @pl.when(me != i)
            def _():
                signal(device(yh=i // 4, yl=(i // 2) % 2, co=i % 2))

        for i in range(4):

            @pl.when(x_ != i)
            def _():
                signal(device(x=i))

            @pl.when(z != i)
            def _():
                signal(device(z=i))

        return 7 + 3 + 3

    return call(
        main,
        (part, value, dx, table, known, blocks),
        [((8, ROWS, 128), BF16), ((32, 128), F32)],
        SUM_SCRATCH
        + [
            pltpu.VMEM(SHARD, BF16),
            *sems(8, 8),
            pltpu.VMEM((16, WIDTH), F32),
            pltpu.VMEM((4, 2, 16, 128), F32),
            pltpu.SemaphoreType.DMA((4, 2)),
            pltpu.SemaphoreType.DMA((4, 2)),
            pltpu.VMEM((2, 32, 128), F32),
            pltpu.VMEM((8, 32, 128), F32),
            *sems(8, 8),
            pltpu.VMEM((32, 128), F32),
            pltpu.VMEM((4, 32, 128), F32),
            *sems(4, 4),
        ],
        ident,
        riders,
        pieces="out",
        entry=entry,
    )


def lanes_of(head, shape):
    lane = lax.broadcasted_iota(jnp.int32, shape, 1)
    return (lane < 64, lane == 64) if head % 2 == 0 else (lane >= 64, lane == 0)


def put_head(ref, i, value, one=False):
    inside, extra = lanes_of(i, value.shape)
    ref[i, 0:OWN] = jnp.where(inside, value, jnp.where(extra & one, 1, 0).astype(BF16))
    ref[i, OWN:QROWS] = jnp.zeros((QROWS - OWN, 128), BF16)


def put_keys(ref, i, rows, value, mask):
    inside, extra = lanes_of(i, value.shape)
    ref[i, rows] = jnp.where(inside, value, jnp.where(extra, mask[rows], jnp.zeros_like(value)))


def attend_step(n_all, wqkv, wout, bias, mask, ident, riders=()):
    def main(inputs, outs, scratch, sent):
        n_all, wqkv, wout, bias, mask = inputs
        part, qkv, other, att, lse = outs
        kall, vt, qpad, ot, send, recv = scratch
        to = device(co=1 - lax.axis_index("co"))
        mine, theirs = slice(0, OWN), slice(OWN, KEYS)
        yield 0.1
        normed = n_all[...].reshape(OWN, WIDTH)
        lse[...] = jnp.zeros_like(lse)
        copies = []
        for h in range(2):
            cols = slice(h * 384, h * 384 + 384)
            block = (dot_nn(normed, wqkv[:, cols]) + bias[:, cols]).astype(BF16)
            qkv[:, cols] = block
            c = remote(
                qkv.at[:, pl.ds(h * 384 + 128, 256)],
                other.at[:, pl.ds(h * 256, 256)],
                send.at[h],
                recv.at[h],
                to,
            )
            c.start()
            copies.append(c)
            for i in (2 * h, 2 * h + 1):
                put_head(qpad, i, block[:, 0:128] * 0.125, True)
                put_keys(kall, i, mine, block[:, 128:256], mask)
            vt[h * 128 : h * 128 + 128, 0:OWN] = block[:, 256:384].T
        sent.extend(copies)
        yield 3.0
        for h in range(2):
            copies[h].wait_recv()
            for i in (2 * h, 2 * h + 1):
                put_keys(kall, i, theirs, other[:, h * 256 : h * 256 + 128], mask)
            vt[h * 128 : h * 128 + 128, OWN:KEYS] = other[:, h * 256 + 128 : h * 256 + 256].T

            def head(hh, _):
                i = 2 * h + hh
                rows = pl.ds(pl.multiple_of(i * 64, 64), 64)
                for lo, n in CHUNKS:
                    s = dot_nt(kall[i], qpad[i, lo : lo + n])
                    top = jnp.max(s, axis=0, keepdims=True)
                    e = jnp.exp(s - top)
                    total = jnp.sum(e, axis=0, keepdims=True)
                    ot[rows, lo : lo + n] = dot_nn(vt[rows], e.astype(BF16)) * (1.0 / total)
                    lse[i, 0:1, lo : lo + n] = top + jnp.log(total)
                return 0

            lax.fori_loop(0, 2, head, 0)
            yield 8.0 + 4.0 * h
        att[...] = ot[...].T[0:OWN].astype(BF16)
        part[...] = dot_nn(att[...], wout[...]).astype(BF16).reshape(ALL)

    return call(
        main,
        (n_all, wqkv, wout, bias, mask),
        [
            (ALL, BF16),
            ((OWN, 768), BF16),
            ((OWN, 512), BF16),
            ((OWN, 256), BF16),
            ((4, 8, QROWS), F32),
        ],
        [
            pltpu.VMEM((4, KEYS, 128), BF16),
            pltpu.VMEM((256, KEYS), BF16),
            pltpu.VMEM((4, QROWS, 128), BF16),
            pltpu.VMEM((256, QROWS), F32),
        ]
        + sems(2, 2),
        ident,
        riders,
        links=("core",),
    )


def attend_back_step(d_all, wqkv, wout, qkv, other, att, lse, mask, ident, riders=()):
    def main(inputs, outs, scratch, sent):
        d_all, wqkv, wout, qkv, other, att, lse, mask = inputs
        part, dqkv, sums = outs
        kall, vall, kt, qone, qpad, dpad, delta, dqt, dk, dv, away, got, send, recv = scratch
        to = device(co=1 - lax.axis_index("co"))
        mine, theirs = slice(0, OWN), slice(OWN, KEYS)
        yield 0.1
        datt = dot_nt(d_all[...].reshape(OWN, WIDTH), wout[...]).astype(BF16)
        copies = []
        along = (datt.astype(F32) * att[...].astype(F32)).T
        delta[...] = jnp.zeros_like(delta)
        for i in range(4):
            delta[i, 0:1, 0:OWN] = jnp.sum(along[i * 64 : i * 64 + 64], axis=0, keepdims=True)
        for h in range(2):
            base, half = h * 384, h * 256
            own_keys, other_keys = qkv[:, base + 128 : base + 256], other[:, half : half + 128]
            for i in (2 * h, 2 * h + 1):
                query = qkv[:, base : base + 128] * 0.125
                put_head(qone, i, query, True)
                put_head(qpad, i, query)
                put_head(dpad, i, datt[:, h * 128 : h * 128 + 128])
                put_keys(kall, i, mine, own_keys, mask)
                put_keys(kall, i, theirs, other_keys, mask)
            vall[h, 0:OWN] = qkv[:, base + 256 : base + 384]
            vall[h, OWN:KEYS] = other[:, half + 128 : half + 256]
            kt[h * 128 : h * 128 + 128, 0:OWN] = own_keys.T
            kt[h * 128 : h * 128 + 128, OWN:KEYS] = other_keys.T
            dk[h] = jnp.zeros((KEYS, 128), F32)
            dv[h] = jnp.zeros((KEYS, 128), F32)

            def head(hh, _):
                i = 2 * h + hh
                rows = pl.ds(pl.multiple_of(i * 64, 64), 64)
                for lo, n in CHUNKS:
                    qc, dc = qpad[i, lo : lo + n], dpad[i, lo : lo + n]
                    s = dot_nt(kall[i], qone[i, lo : lo + n])
                    p = jnp.exp(s - lse[i, 0:1, lo : lo + n])
                    dp = dot_nt(vall[h], dc)
                    ds = (p * (dp - delta[i, 0:1, lo : lo + n])).astype(BF16)
                    dv[h] += dot_nn(p.astype(BF16), dc)
                    dk[h] += dot_nn(ds, qc)
                    dqt[rows, lo : lo + n] = dot_nn(kt[rows], ds)
                return 0

            lax.fori_loop(0, 2, head, 0)
            away[h, :, 0:128] = dk[h, OWN:KEYS].astype(BF16)
            away[h, :, 128:256] = dv[h, OWN:KEYS].astype(BF16)
            c = remote(away.at[h], got.at[h], send.at[h], recv.at[h], to)
            c.start()
            copies.append(c)
            yield 7.0 + 5.0 * h
        sent.extend(copies)
        dq = dqt[...].T[0:OWN] * 0.125
        for h in range(2):
            base = h * 384
            dqkv[:, base : base + 128] = dq[:, h * 128 : h * 128 + 128].astype(BF16)
            copies[h].wait_recv()
            dqkv[:, base + 128 : base + 256] = (
                dk[h, 0:OWN] + got[h, :, 0:128].astype(F32)
            ).astype(BF16)
            dqkv[:, base + 256 : base + 384] = (
                dv[h, 0:OWN] + got[h, :, 128:256].astype(F32)
            ).astype(BF16)
        part[...] = dot_nt(dqkv[...], wqkv[...]).astype(BF16).reshape(ALL)
        sums[...] = jnp.zeros_like(sums)
        sums[0:1, :] = jnp.sum(dqkv[...].astype(F32), axis=0, keepdims=True)

    return call(
        main,
        (d_all, wqkv, wout, qkv, other, att, lse, mask),
        [(ALL, BF16), ((OWN, 768), BF16), ((8, 768), F32)],
        [
            pltpu.VMEM((4, KEYS, 128), BF16),
            pltpu.VMEM((2, KEYS, 128), BF16),
            pltpu.VMEM((256, KEYS), BF16),
            pltpu.VMEM((4, QROWS, 128), BF16),
            pltpu.VMEM((4, QROWS, 128), BF16),
            pltpu.VMEM((4, QROWS, 128), BF16),
            pltpu.VMEM((4, 8, QROWS), F32),
            pltpu.VMEM((256, QROWS), F32),
            pltpu.VMEM((2, KEYS, 128), F32),
            pltpu.VMEM((2, KEYS, 128), F32),
            pltpu.VMEM((2, OWN, 256), BF16),
            pltpu.VMEM((2, OWN, 256), BF16),
        ]
        + sems(2, 2),
        ident,
        riders,
        links=("core",),
    )


def on_device(
    tokens,
    cotangent,
    attend_weight,
    output_weight,
    up_weight,
    down_weight,
    norm_gain,
    norm_shift,
    attend_bias,
    branch_bias,
    layer_scale,
    hidden_bias,
):
    co, yh, z = (lax.axis_index(a) for a in ("co", "yh", "z"))
    attend_weight = attend_weight.reshape(LAYERS, 256, 384)
    first = jnp.pad(tokens, ((0, 15), (0, 0)))
    cot_pieces = jnp.pad(cotangent.astype(BF16), ((0, 15), (0, 0)))
    pack = jnp.concatenate(
        [
            norm_gain.reshape(4, 128),
            norm_shift.reshape(4, 128),
            branch_bias.reshape(4, 128),
            layer_scale.reshape(4, 128),
            attend_bias.reshape(4, 128),
            hidden_bias.reshape(8, 128),
            jnp.zeros((4, 128), F32),
        ]
    )

    def attend_of(l):
        return GatherWeight(attend_weight, l, 0)

    def output_of(l):
        return GatherWeight(output_weight, l, 1)

    def up_of(l):
        return GatherWeight(up_weight, l, 0)

    def down_of(l):
        return GatherWeight(down_weight, l, 1)

    weights = [[None] * 4 for _ in range(LAYERS)]
    ident = iter(range(40))
    (x, n_all, packs), (weights[0][0], weights[0][1]) = first_step(
        first, pack, next(ident), [attend_of(0), output_of(0)]
    )
    table = packs[:, 0:16].transpose(1, 0, 2).reshape(16, WIDTH)
    here = jnp.stack(
        [
            lax.dynamic_index_in_dim(packs, z, keepdims=False),
            lax.dynamic_index_in_dim(packs, z + 4, keepdims=False),
        ]
    )
    row = jnp.arange(OWN)
    block, inside = row // ROWS, row % ROWS

    def hidden_keys(half):
        real = (inside < REAL) | ((inside == REAL) & (block == 3) & (half == 1))
        return jnp.where(real, 0.0, -1e30).astype(BF16)

    mask = jnp.concatenate([hidden_keys(co), hidden_keys(1 - co)])
    mask = jnp.broadcast_to(mask[:, None], (KEYS, 128))

    last = jnp.where((co == 1) & (z == 3), REAL + 1, REAL)
    real_row = jnp.arange(ROWS)[:, None] < last

    saved = []
    for l in range(LAYERS):
        wqkv, wout = weights[l][:2]
        ab = here[:, 16 + 2 * l : 18 + 2 * l]
        qkv_bias = jnp.concatenate(
            [ab[0, 0], jnp.zeros(128), ab[0, 1], ab[1, 0], jnp.zeros(128), ab[1, 1]]
        )[None]
        riders = [up_of(l)]
        if l == 1:
            riders.append(Spread((cot * table[SCALE + 3]).astype(BF16)))
        n1 = n_all
        (part, qkv, other, att, lse), got = attend_step(
            n1, wqkv, wout, qkv_bias, mask, next(ident), riders
        )
        weights[l][2] = got[0]
        if l == 1:
            d_all = got[1]
        at = (BRANCH + 2 * l, SCALE + 2 * l, GAIN + 2 * l + 1, SHIFT + 2 * l + 1)
        riders = [down_of(l)] + ([Pieces(cot_pieces)] if l == 0 else [])
        (a, m, n_all), got = forward_step(part, x, table, at, next(ident), riders)
        weights[l][3] = got[0]
        if l == 0:
            cot = jnp.where(real_row, got[1].astype(F32), 0.0)
        wup, wdown = weights[l][2:]
        n2 = n_all.reshape(OWN, WIDTH)
        hb = here[:, 20 + 4 * l : 24 + 4 * l].reshape(WIDTH)
        u = dot_nn(n2, wup) + hb
        g = gelu_value(u).astype(BF16)
        part = dot_nn(g, wdown).astype(BF16).reshape(ALL)
        saved.append([x, n1.reshape(OWN, WIDTH), qkv, other, att, lse, a, m, n2, u, g])
        if l + 1 < LAYERS:
            at = (BRANCH + 2 * l + 1, SCALE + 2 * l + 1, GAIN + 2 * l + 2, SHIFT + 2 * l + 2)
            (f, x, n_all), weights[1][:2] = forward_step(
                part, m, table, at, next(ident), [attend_of(1), output_of(1)]
            )
            saved[l].append(f)
        else:
            end = End(part, m, cot, table, (BRANCH + 3, SCALE + 3))

    gain_sums, shift_sums, scale_sums, branch_sums = ([None] * 4 for _ in range(4))
    hidden_sums, qkv_sums, grads = [None] * LAYERS, [None] * LAYERS, [[None] * 4, [None] * 4]
    dx = cot

    def summing(block):
        return SumBlock(block.shape, block)

    for l in reversed(range(LAYERS)):
        wqkv, wout, wup, wdown = weights[l]
        x, n1, qkv, other, att, lse, a, m, n2, u, g = saved[l][:11]
        df = d_all.reshape(OWN, WIDTH)
        du = (dot_nt(df, wdown) * gelu_slope(u)).astype(BF16)
        part = dot_nt(du, wup).astype(BF16).reshape(ALL)
        hidden_sums[l] = jnp.sum(du.astype(F32), axis=0)
        at = (GAIN + 2 * l + 1, SCALE + 2 * l)
        riders = [ReduceWeight(g, df, 1)]
        if l == 0:
            riders += [summing(attend_block), summing(output_block)]
        (dm, sums, d_all), got = backward_step(part, m, dx, a, table, at, next(ident), riders)
        down_block = got[0]
        if l == 0:
            grads[1][:2] = got[1:]
        gain_sums[2 * l + 1], shift_sums[2 * l + 1] = sums[0], sums[1]
        scale_sums[2 * l], branch_sums[2 * l] = sums[2], sums[3]
        da = d_all.reshape(OWN, WIDTH)
        riders = [ReduceWeight(n2, du, 0), summing(down_block)]
        riders.append(end if l == 1 else PiecesOut(x_end))
        (part, dqkv, qkv_sum), got = attend_back_step(
            d_all, wqkv, wout, qkv, other, att, lse, mask, next(ident), riders
        )
        up_block, grads[l][3] = got[:2]
        qkv_sums[l] = qkv_sum[0]
        if l == 1:
            x_end, sums = got[2:]
            scale_sums[3], branch_sums[3] = sums[2], sums[3]
            at = (GAIN + 2 * l, SCALE + 2 * l - 1)
            riders = [ReduceWeight(n1, dqkv, 0), ReduceWeight(att, da, 1), summing(up_block)]
            (dx, sums, d_all), got = backward_step(
                part, x, dm, saved[l - 1][11], table, at, next(ident), riders
            )
            attend_block, output_block, grads[l][2] = got
            scale_sums[2 * l - 1], branch_sums[2 * l - 1] = sums[2], sums[3]
            gain_sums[2 * l], shift_sums[2 * l] = sums[0], sums[1]
        else:
            out_pieces = got[2]
            riders = [ReduceSum(n1, dqkv, 0), ReduceSum(att, da, 1), summing(up_block)]
            zero = jnp.zeros(WIDTH)
            known = jnp.stack(
                [zero] + gain_sums[1:] + [zero] + shift_sums[1:] + branch_sums + scale_sums
            )
            blocks = jnp.concatenate(
                [
                    jnp.stack(qkv_sums).reshape(2, 2, 3, 128).transpose(1, 0, 2, 3).reshape(2, 6, 128),
                    jnp.stack(hidden_sums).reshape(2, 2, 4, 128).transpose(1, 0, 2, 3).reshape(2, 8, 128),
                    jnp.zeros((2, 2, 128), F32),
                ],
                axis=1,
            )
            (grad_pieces, small), got = last_step(
                part, x, dm, table, known, blocks, (GAIN,), next(ident), riders
            )
            grads[0][:3] = got

    bias_grad = small[16:22].reshape(2, 3, 128)[:, 0::2]

    def rows(landed):
        return jnp.concatenate(
            [landed[0:7, 0:REAL].reshape(7 * REAL, 128), landed[7, 0 : REAL + 1]]
        ).astype(F32)

    return (
        rows(out_pieces),
        rows(grad_pieces),
        jnp.stack([grads[l][0] for l in range(LAYERS)]).reshape(LAYERS, 256, 3, 128),
        jnp.stack([grads[l][1] for l in range(LAYERS)]),
        jnp.stack([grads[l][2] for l in range(LAYERS)]),
        jnp.stack([grads[l][3] for l in range(LAYERS)]),
        small[0:4].reshape(2, 2, 128),
        small[4:8].reshape(2, 2, 128),
        bias_grad,
        small[8:12].reshape(2, 2, 128),
        small[12:16].reshape(2, 2, 128),
        small[22:30].reshape(2, 512),
    )


def solution(mesh):
    split = Mesh(mesh.devices.reshape(4, 2, 2, 2, 4), AXES)
    images, row, col = ("x", "yl", "co"), ("yl", "co"), ("yh", "z")
    placed = (
        P(images, col),
        P(images, col),
        P(None, row, None, col),
        P(None, col, row),
        P(None, row, col),
        P(None, col, row),
        P(None, None, col),
        P(None, None, col),
        P(None, None, col),
        P(None, None, col),
        P(None, None, col),
        P(None, col),
    )
    return jax.shard_map(
        on_device, mesh=split, in_specs=placed, out_specs=placed, check_vma=False
    )
```

```python
import jax
import jax.numpy as jnp
from jax import lax
from jax.experimental import pallas as pl
from jax.experimental.pallas import tpu as pltpu
from jax.sharding import Mesh, PartitionSpec as P

WIDTH = 1024
HALF = WIDTH // 2
SEQ = 1025
LAYERS = 2
REAL = 128
ROWS = 144
TAIL = ROWS - REAL
OWN = 4 * ROWS
KEYS = 2 * OWN
QROWS = 640
CHUNKS = ((0, 256), (256, 256), (512, 128))
EPS = 1e-06
ROOT_HALF = 0.7071067811865476
INV_ROOT_TWO_PI = 0.3989422804014327
MESH = pl.DeviceIdType.MESH
AXES = ("x", "yl", "co", "yh", "z")
VM = pl.BlockSpec(memory_space=pltpu.VMEM)
ANY = pl.BlockSpec(memory_space=pl.ANY)
F32 = jnp.float32
BF16 = jnp.bfloat16


def gelu_value(value):
    return 0.5 * value * (1.0 + lax.erf(value * ROOT_HALF))


def gelu_slope(value):
    return 0.5 * (1.0 + lax.erf(value * ROOT_HALF)) + value * INV_ROOT_TWO_PI * jnp.exp(
        -0.5 * value * value
    )


def dot_nt(left, right):
    return lax.dot_general(left, right, (((1,), (1,)), ((), ())), preferred_element_type=F32)


def dot_tn(left, right):
    return lax.dot_general(left, right, (((0,), (0,)), ((), ())), preferred_element_type=F32)


def dot_nn(left, right):
    return jnp.dot(left, right, preferred_element_type=F32)


def device(**moved):
    return tuple(moved[a] if a in moved else lax.axis_index(a) for a in AXES)


def remote(src, dst, send, recv, to):
    return pltpu.make_async_remote_copy(
        src_ref=src, dst_ref=dst, send_sem=send, recv_sem=recv, device_id=to, device_id_type=MESH
    )


def signal(to):
    pl.semaphore_signal(
        pltpu.get_barrier_semaphore(), inc=1, device_id=to, device_id_type=MESH
    )


class Ring:
    def __init__(self, axis):
        self.axis = axis
        if axis == "y":
            self.me = lax.axis_index("yh") * 2 + lax.axis_index("yl")
        else:
            self.me = lax.axis_index(axis)
        self.right = lax.rem(self.me + 1, 4)
        self.left = lax.rem(self.me + 3, 4)
        self.across = lax.rem(self.me + 2, 4)
        self.to_right, self.to_left = self.at(self.right), self.at(self.left)

    def at(self, index):
        if self.axis == "y":
            return device(yh=index // 2, yl=lax.rem(index, 2))
        return device(**{self.axis: index})


def greet(links, more=0, home=None):
    count = more
    for link in links:
        if link == "core":
            signal(device(co=1 - lax.axis_index("co")))
            count += 1
        else:
            ring = Ring(link)
            signal(ring.to_right)
            signal(ring.to_left)
            count += 2
            if link != "y":
                signal(ring.at(ring.across))
                count += 1
    barrier = pltpu.get_barrier_semaphore()
    if home is None:
        pl.semaphore_wait(barrier, count)
    else:

        @pl.when(home)
        def _():
            pl.semaphore_wait(barrier, count + 7)

        @pl.when(jnp.logical_not(home))
        def _():
            pl.semaphore_wait(barrier, count + 8)


def in_turns(jobs):
    waiting = [[0.0, i, job] for i, job in enumerate(jobs)]
    while waiting:
        first = min(waiting, key=lambda w: w[:2])
        try:
            first[0] = next(first[2])
        except StopIteration:
            waiting.remove(first)


def delayed(job, time):
    while True:
        try:
            yield time + next(job)
        except StopIteration as end:
            return end.value


def by_rows(ref, lead, half):
    rows = ref.shape[1] // 2
    return ref.at[lead, pl.ds(half * rows, rows), :]


def reduce_on(ring, half, part, fin, relay, stage, send, recv, sent, first=0):
    def copy(i, src, dst, to):
        c = remote(src, dst, send.at[i], recv.at[i], to)
        c.start()
        sent.append(c)
        return c

    far_r = copy(0, half(part, ring.across, 0), relay.at[0], ring.to_right)
    far_l = copy(1, half(part, ring.across, 1), relay.at[1], ring.to_left)
    near_r = copy(2, half(part, ring.right, 1), half(fin, 0, 1), ring.to_right)
    near_l = copy(3, half(part, ring.left, 0), half(fin, 1, 0), ring.to_left)
    yield 3.0
    far_r.wait_recv()
    stage[0] = (half(part, ring.right, 0)[...].astype(F32) + relay[0].astype(F32)).astype(BF16)
    sum_r = copy(4, stage.at[0], half(fin, 0, 0), ring.to_right)
    far_l.wait_recv()
    stage[1] = (half(part, ring.left, 1)[...].astype(F32) + relay[1].astype(F32)).astype(BF16)
    sum_l = copy(5, stage.at[1], half(fin, 1, 1), ring.to_left)
    yield 7.0
    for c in (near_r, near_l, sum_r, sum_l):
        c.wait_recv()
    own = part.at[ring.me, pl.ds(first, fin.shape[1])][...]
    return own.astype(F32) + fin[0].astype(F32) + fin[1].astype(F32)


def gather_on(ring, slot, own, send, recv, sent, landed=None):
    def copy(i, src, owner, half, to):
        return remote(src, slot(owner, half), send.at[i], recv.at[i], to)

    def go(*what):
        c = copy(*what)
        c.start()
        sent.append(c)

    def lands(i, owner, half):
        copy(i, slot(owner, half), owner, half, ring.to_right).wait_recv()

    go(0, own(0), ring.me, 0, ring.to_right)
    go(1, own(1), ring.me, 1, ring.to_left)
    go(2, own(1), ring.me, 1, ring.to_right)
    go(3, own(0), ring.me, 0, ring.to_left)
    yield 2.5
    lands(0, ring.left, 0)
    go(4, slot(ring.left, 0), ring.left, 0, ring.to_right)
    lands(1, ring.right, 1)
    go(5, slot(ring.right, 1), ring.right, 1, ring.to_left)
    yield 5.0
    lands(2, ring.left, 1)
    if landed is not None:
        landed(ring.left)
    lands(3, ring.right, 0)
    if landed is not None:
        landed(ring.right)
    yield 7.0
    lands(4, ring.across, 0)
    lands(5, ring.across, 1)
    if landed is not None:
        landed(ring.across)


def gather_slots(ring, out, half, send, recv, sent):
    def slot(owner, h):
        return half(out, owner, h)

    yield from gather_on(ring, slot, lambda h: slot(ring.me, h), send, recv, sent)


def sems(*counts):
    return [pltpu.SemaphoreType.DMA((c,)) for c in counts]


def tail_roles():
    z, second = lax.axis_index("z"), lax.axis_index("co") == 1
    return z, second & (z == 3), second & (z != 3)


WHOLE, BATCHES = (0, REAL, ROWS), ((0, REAL // 2, REAL // 2), (REAL // 2, REAL // 2, ROWS - REAL // 2))


def shard_sum(batch, part, scratch, sent):
    first, count, rows = batch
    fin, relay, stage, tails, tail, send, recv, tsend, trecv = scratch
    z, holds, gives = tail_roles()
    ends = first + rows == ROWS

    def half(ref, lead, h):
        lo = first if ref.shape[1] == ROWS else 0
        return ref.at[lead, pl.ds(lo, count), pl.ds(h * HALF, HALF)]

    def tail_to(slot):
        src = part.at[3, pl.ds(REAL, TAIL), :]
        return remote(src, tails.at[slot], tsend.at[0], trecv.at[slot], device(z=3))

    if ends:

        @pl.when(gives)
        def _():
            tail_to(z).start()

    total = yield from reduce_on(
        Ring("z"), half, part, fin, relay, stage, send, recv, sent, first
    )
    if not ends:
        return total
    tail[...] = jnp.zeros_like(tail)

    @pl.when(holds)
    def _():
        for i in range(3):
            tail_to(i).wait_recv()
        tail[...] = part[3, REAL:ROWS].astype(F32) + sum(tails[i].astype(F32) for i in range(3))

    @pl.when(gives)
    def _():
        tail_to(z).wait_send()

    return jnp.concatenate([total, tail[...]], axis=0)


def shard_spread(batch, out, scratch, sent):
    first, count, rows = batch
    send, recv, tsend, trecv = scratch
    z, holds, gives = tail_roles()
    ends = first + rows == ROWS

    def half(ref, lead, h):
        return ref.at[lead, pl.ds(first, count), pl.ds(h * HALF, HALF)]

    def tail_to(i):
        ref = out.at[3, pl.ds(REAL, TAIL), :]
        return remote(ref, ref, tsend.at[i], trecv.at[0], device(z=i))

    if ends:

        @pl.when(holds)
        def _():
            for i in range(3):
                tail_to(i).start()

    yield from gather_slots(Ring("z"), out, half, send, recv, sent)
    if ends:

        @pl.when(gives)
        def _():
            tail_to(0).wait_recv()

        @pl.when(holds)
        def _():
            for i in range(3):
                tail_to(i).wait_send()


def sum_scratch(batch):
    count = batch[1]
    return [
        pltpu.VMEM((2, count, WIDTH), BF16),
        pltpu.VMEM((2, count, HALF), BF16),
        pltpu.VMEM((2, count, HALF), BF16),
        pltpu.VMEM((3, TAIL, WIDTH), BF16),
        pltpu.VMEM((TAIL, WIDTH), F32),
    ] + sems(6, 6, 1, 3)


SPREAD_SCRATCH = sems(6, 6, 3, 1)
SUMMING = len(sum_scratch(WHOLE))


class GatherWeight:
    links = ("y", "core")

    def __init__(self, shards, layer, side, spec=ANY, board=None):
        rows, columns = shards.shape[1:]
        self.board = board
        self.layer, self.side, self.rows, self.columns = layer, side, rows, columns
        full = (4 * rows, 2 * columns) if side == 0 else (2 * rows, 4 * columns)
        self.inputs = [(shards, ANY)]
        self.outs = [(full, BF16, spec)]
        self.scratch = sems(6, 6, 4, 4, 1)

    def run(self, inputs, outs, scratch, sent):
        (shards,), (out,) = inputs, outs
        send, recv, csend, crecv, local = scratch
        own = shards.at[self.layer]
        ring, co = Ring("y"), lax.axis_index("co")
        rows, columns = self.rows, self.columns

        def block(y, core, half=None):
            yh, r = y // 2, lax.rem(y, 2) * 2 + core
            down, along = (r, yh) if self.side == 0 else (yh, r)
            first, count = down * rows, rows
            if half is not None:
                count = rows // 2
                first = first + half * count
            return out.at[
                pl.ds(pl.multiple_of(first, 16), count),
                pl.ds(pl.multiple_of(along * columns, 128), columns),
            ]

        def to_core(i, src, y):
            c = remote(src, block(y, co), csend.at[i], crecv.at[i], device(co=1 - co))
            c.start()
            sent.append(c)

        keep = pltpu.make_async_copy(own, block(ring.me, co), local.at[0])
        keep.start()
        to_core(0, own, ring.me)
        numbers = iter((1, 2, 3))
        yield from gather_on(
            ring,
            lambda y, half: block(y, co, half),
            lambda half: own.at[pl.ds(half * (rows // 2), rows // 2), :],
            send,
            recv,
            sent,
            lambda y: to_core(next(numbers), block(y, co), y),
        )
        keep.wait()
        yield 12.0
        for i, y in enumerate((ring.me, ring.left, ring.right, ring.across)):
            there = block(y, 1 - co)
            remote(there, there, csend.at[i], crecv.at[i], device(co=1 - co)).wait_recv()
        if self.board is not None:
            self.board.append(out)


class ReduceWeight:
    links = ("y", "core")

    def __init__(self, left, right, side, board=None):
        self.board = board
        rows, columns = left.shape[-1], right.shape[-1]
        self.full = rows, columns
        rows, columns = (rows // 4, columns // 2) if side == 0 else (rows // 2, columns // 4)
        self.side, self.rows, self.columns = side, rows, columns
        self.inputs = [] if board is not None else [(left, VM), (right, VM)]
        self.outs = [((rows, columns), BF16, VM)]
        self.scratch = [
            pltpu.VMEM(self.full, BF16),
            pltpu.VMEM((4, rows, columns), BF16),
            pltpu.VMEM((4, rows, columns), BF16),
            pltpu.VMEM((2, rows, columns), BF16),
            pltpu.VMEM((2, rows // 2, columns), BF16),
            pltpu.VMEM((2, rows // 2, columns), BF16),
        ] + sems(4, 4, 6, 6)

    def run(self, inputs, outs, scratch, sent):
        total = yield from self.total(inputs, scratch, sent)
        outs[0][...] = total.astype(BF16)

    def total(self, inputs, scratch, sent):
        if self.board is not None:
            time = 16.0
            while len(self.board) < 2:
                yield time
                time += 2.0
            inputs = self.board
        left, right = inputs
        part, got, pair, fin, relay, stage, csend, crecv, send, recv = scratch

        def columns_of(ref, first):
            if len(ref.shape) == 2:
                return ref[:, first : first + 256]
            return ref[:, :, first : first + 256].reshape(OWN, 256)

        whole = right[...] if len(right.shape) == 2 else right[...].reshape(OWN, self.full[1])
        for first in range(0, self.full[0], 256):
            part[first : first + 256] = dot_tn(columns_of(left, first), whole).astype(BF16)
        co = lax.axis_index("co")
        rows, columns = self.rows, self.columns

        def block(y, core):
            yh, r = y // 2, (y % 2) * 2 + core
            down, along = (r, yh) if self.side == 0 else (yh, r)
            return part.at[
                pl.ds(pl.multiple_of(down * rows, 16), rows),
                pl.ds(pl.multiple_of(along * columns, 128), columns),
            ]

        copies = []
        for y in range(4):
            c = remote(
                block(y, 1 - co), got.at[y], csend.at[y], crecv.at[y], device(co=1 - co)
            )
            c.start()
            copies.append(c)
        sent.extend(copies)
        yield 5.0 if self.board is None else 22.0
        for y in range(4):
            copies[y].wait_recv()
            pair[y] = (block(y, co)[...].astype(F32) + got[y].astype(F32)).astype(BF16)
        job = reduce_on(Ring("y"), by_rows, pair, fin, relay, stage, send, recv, sent)
        return (yield from delayed(job, 6.0 if self.board is None else 24.0))


class SumBlock:
    links = ("x",)

    def __init__(self, shape, block=None):
        rows, columns = shape
        self.shape, self.rows = shape, rows // 4
        self.inputs = [] if block is None else [(block, VM)]
        self.outs = [(shape, F32, VM)]
        quarters = (4, rows // 4, columns)
        self.scratch = [pltpu.VMEM(quarters, BF16) for _ in range(3)] + sems(4, 4, 4, 4)

    def run(self, inputs, outs, scratch, sent):
        yield from self.total(inputs[0][...], outs[0], scratch, sent)

    def total(self, value, out, scratch, sent):
        part, got, every, send, recv, gsend, grecv = scratch
        ring = Ring("x")
        others = (ring.across, ring.right, ring.left)
        for i in range(4):
            part[i] = value[i * self.rows : (i + 1) * self.rows].astype(BF16)

        def give(slot, to):
            return remote(part.at[to], got.at[slot], send.at[to], recv.at[slot], ring.at(to))

        def share(slot, to):
            return remote(
                every.at[slot], every.at[slot], gsend.at[to], grecv.at[slot], ring.at(to)
            )

        for i in others:
            c = give(ring.me, i)
            c.start()
            sent.append(c)
        got[ring.me] = part[ring.me]
        yield 4.0
        for i in others:
            give(i, i).wait_recv()
        every[ring.me] = sum(got[i].astype(F32) for i in range(4)).astype(BF16)
        for i in others:
            c = share(ring.me, i)
            c.start()
            sent.append(c)
        yield 8.0
        for i in others:
            share(i, i).wait_recv()
        for i in range(4):
            out[i * self.rows : (i + 1) * self.rows] = every[i].astype(F32)


class ReduceSum:
    links = ("y", "core", "x")

    def __init__(self, left, right, side):
        self.first = ReduceWeight(left, right, side)
        self.second = SumBlock((self.first.rows, self.first.columns))
        self.inputs, self.outs = self.first.inputs, self.second.outs
        self.scratch = self.first.scratch + self.second.scratch

    def run(self, inputs, outs, scratch, sent):
        n = len(self.first.scratch)
        total = yield from self.first.total(inputs, scratch[:n], sent)
        yield from delayed(self.second.total(total, outs[0], scratch[n:], sent), 15.0)


class Pieces:
    links = ()
    pieces = "in"

    def __init__(self, source):
        self.inputs = [(source, VM)]
        self.outs = [(SHARD, BF16, VM)]
        self.scratch = sems(8, 8)

    def run(self, inputs, outs, scratch, sent):
        (source,), (landed,), (send, recv) = inputs, outs, scratch
        co, yh, z = (lax.axis_index(a) for a in ("co", "yh", "z"))
        me, home = yh * 4 + z, yh == co

        def piece(j):
            src = source.at[pl.ds(j * REAL, ROWS), :]
            dst = landed.at[:, pl.ds(pl.multiple_of(me * 128, 128), 128)]
            to = device(yh=co, co=j // 4, z=j % 4)
            there = remote(src, dst, send.at[j], recv.at[me], to)
            return there, pltpu.make_async_copy(src, dst, recv.at[me]), home & (co * 4 + z == j)

        for j in range(8):
            there, here, own = piece(j)

            @pl.when(own)
            def _():
                here.start()

            @pl.when(jnp.logical_not(own))
            def _():
                there.start()

        yield 9.0
        for q in range(8):
            dst = landed.at[:, pl.ds(q * 128, 128)]
            own = home & (me == q)

            @pl.when(own)
            def _():
                pltpu.make_async_copy(dst, dst, recv.at[q]).wait()

            @pl.when(jnp.logical_not(own))
            def _():
                remote(dst, dst, send.at[q], recv.at[q], Ring("z").to_right).wait_recv()

        for j in range(8):
            there, here, own = piece(j)

            @pl.when(jnp.logical_not(own))
            def _():
                there.wait_send()


class PiecesOut:
    links = ()
    pieces = "out"

    def __init__(self, source):
        self.inputs = [(source, VM)]
        self.outs = [((8, ROWS, 128), BF16, VM)]
        self.scratch = [pltpu.VMEM(SHARD, BF16)] + sems(8, 8)

    def run(self, inputs, outs, scratch, sent):
        scratch[0][...] = inputs[0][...].astype(BF16)
        yield from self.give(scratch[0], outs[0], *scratch[1:])

    @staticmethod
    def give(source, landed, send, recv):
        co, yh, z = (lax.axis_index(a) for a in ("co", "yh", "z"))
        shard, home = co * 4 + z, yh == co

        def piece(q):
            src = source.at[:, pl.ds(q * 128, 128)]
            dst = landed.at[shard]
            to = device(co=yh, yh=q // 4, z=q % 4)
            there = remote(src, dst, send.at[q], recv.at[shard], to)
            return there, pltpu.make_async_copy(src, dst, recv.at[shard]), home & (
                yh * 4 + z == q
            )

        for q in range(8):
            there, here, own = piece(q)

            @pl.when(own)
            def _():
                here.start()

            @pl.when(jnp.logical_not(own))
            def _():
                there.start()

        yield 11.0
        for s in range(8):
            dst = landed.at[s]
            own = home & (shard == s)

            @pl.when(own)
            def _():
                pltpu.make_async_copy(dst, dst, recv.at[s]).wait()

            @pl.when(jnp.logical_not(own))
            def _():
                remote(dst, dst, send.at[s], recv.at[s], Ring("z").to_right).wait_recv()

            there, here, mine = piece(s)

            @pl.when(jnp.logical_not(mine))
            def _():
                there.wait_send()


def greet_pieces(way):
    co, yh, z = (lax.axis_index(a) for a in ("co", "yh", "z"))
    home = yh == co
    for j in range(8):
        if way == "in":
            own, source = home & (yh * 4 + z == j), dict(yh=j // 4, z=j % 4, co=yh)
        else:
            own, source = home & (co * 4 + z == j), dict(yh=co, co=j // 4, z=j % 4)

        @pl.when(jnp.logical_not(own))
        def _():
            signal(device(**source))

    return home


class Spread:
    links = ("z",)

    def __init__(self, shard):
        self.inputs = [(shard, VM)]
        self.outs = [(ALL, BF16, VM)]
        self.scratch = SPREAD_SCRATCH

    def run(self, inputs, outs, scratch, sent):
        outs[0][lax.axis_index("z")] = inputs[0][...]
        yield from shard_spread(WHOLE, outs[0], scratch, sent)


class End:
    links = ("z",)

    def __init__(self, part, x, cot, table, at):
        self.at = at
        self.inputs = [(a, VM) for a in (part, x, cot, table)]
        self.outs = [(SHARD, F32, VM), (SUMS, F32, VM)]
        self.scratch = sum_scratch(WHOLE)

    def run(self, inputs, outs, scratch, sent):
        (part, x, cot, table), (x_out, sums) = inputs, outs
        total = yield from shard_sum(WHOLE, part, scratch, sent)
        bias, scale = (table[r : r + 1, :] for r in self.at)
        branch = total + bias
        x_out[...] = x[...] + scale * branch
        df = (cot[...] * scale).astype(BF16)
        sums[...] = jnp.zeros_like(sums)
        sums[2:3, :] = jnp.sum(cot[...] * branch, axis=0, keepdims=True)
        sums[3:4, :] = jnp.sum(df.astype(F32), axis=0, keepdims=True)


def norm_of(value):
    mean = jnp.mean(value, axis=1, keepdims=True)
    meansq = jnp.mean(value * value, axis=1, keepdims=True)
    rstd = lax.rsqrt(meansq - mean * mean + EPS)
    return (value - mean) * rstd, rstd


def norm_back(grad, value, gain):
    hat, rstd = norm_of(value)
    e = grad * gain
    return (
        rstd
        * (
            e
            - jnp.mean(e, axis=1, keepdims=True)
            - hat * jnp.mean(e * hat, axis=1, keepdims=True)
        ),
        jnp.sum(grad * hat, axis=0, keepdims=True),
        jnp.sum(grad, axis=0, keepdims=True),
    )


GAIN, SHIFT, BRANCH, SCALE = 0, 4, 8, 12
SHARD = (ROWS, WIDTH)
ALL = (4, ROWS, WIDTH)
SUMS = (8, WIDTH)


def call(mains, inputs, outs, scratch, ident, riders=(), links=("z",), pieces=None, entry=None):
    mains = mains if isinstance(mains, list) else [mains]
    inputs = [(a, VM) for a in inputs]
    outs = [(s, d, VM) for s, d in outs]
    jobs = [(inputs, outs, list(scratch))] + [(r.inputs, r.outs, r.scratch) for r in riders]
    links = {link: None for link in links}
    for r in riders:
        links.update({link: None for link in r.links})
        pieces = pieces or getattr(r, "pieces", None)
    runs = [(0, main) for main in mains] + [(i + 1, r.run) for i, r in enumerate(riders)]

    def kernel(*refs):
        refs, split = list(refs), []
        for kind in range(3):
            for job in jobs:
                split.append([refs.pop(0) for _ in job[kind]])
        n = len(jobs)
        for job, outs_here in zip(jobs, split[n : 2 * n]):
            for out, ref in zip(job[1], outs_here):
                if out[0] == ALL and out[1] == BF16:
                    ref[:, REAL:ROWS] = jnp.zeros((4, TAIL, WIDTH), BF16)
        more = 0 if entry is None else entry()
        greet(links, more, None if pieces is None else greet_pieces(pieces))
        sent = []
        in_turns(
            run(split[i], split[n + i], split[2 * n + i], sent) for i, run in runs
        )
        for c in sent:
            c.wait_send()

    results = pl.pallas_call(
        kernel,
        out_shape=[jax.ShapeDtypeStruct(o[0], o[1]) for job in jobs for o in job[1]],
        in_specs=[i[1] for job in jobs for i in job[0]],
        out_specs=[o[2] for job in jobs for o in job[1]],
        scratch_shapes=[s for job in jobs for s in job[2]],
        compiler_params=pltpu.CompilerParams(
            collective_id=ident, has_side_effects=True, vmem_limit_bytes=28 * 2**20
        ),
        cost_estimate=pl.CostEstimate(
            flops=2 * 10**10, bytes_accessed=6 * 10**7, transcendentals=0
        ),
    )(*[i[0] for job in jobs for i in job[0]])
    n = len(outs)
    return results[:n], results[n:]


def spread_norm(value, table, at, out, rows):
    hat, _ = norm_of(value)
    gain, shift = (table[r : r + 1, :] for r in at)
    out[lax.axis_index("z"), rows] = (hat * gain + shift).astype(BF16)


def back_through_norm(total, value, dx, branch, table, at, dx_out, sums, d_out, rows):
    gain, scale = (table[r : r + 1, :] for r in at)
    dr, gain_sum, shift_sum = norm_back(total, value[rows], gain)
    dx_new = dx[rows] + dr
    dx_out[rows] = dx_new
    df = (dx_new * scale).astype(BF16)
    d_out[lax.axis_index("z"), rows] = df
    sums[0:1, :] += gain_sum
    sums[1:2, :] += shift_sum
    sums[2:3, :] += jnp.sum(dx_new * branch[rows], axis=0, keepdims=True)
    sums[3:4, :] += jnp.sum(df.astype(F32), axis=0, keepdims=True)


def batch_rows(ref, rows):
    value = ref[:, rows]
    return value.reshape(4 * value.shape[1], WIDTH)


def put_rows(ref, rows, value):
    ref[:, rows] = value.reshape(4, rows.stop - rows.start, WIDTH).astype(ref.dtype)


def back_through_hidden(d_all, u, wup, wdown, du_out, hidden, part, rows):
    du = (dot_nt(batch_rows(d_all, rows), wdown[...]) * gelu_slope(batch_rows(u, rows))).astype(
        BF16
    )
    put_rows(du_out, rows, du)
    hidden[0:1, :] += jnp.sum(du.astype(F32), axis=0, keepdims=True)
    put_rows(part, rows, dot_nt(du, wup[...]))


LAG = 4.0
STARTS = (0.0, 7.5, 17.0, 25.0)


def until(board, count, time):
    while len(board) < count:
        yield time
        time += 1.0


def chain(work, inputs, outs, extra, ident, riders):
    each = 2 * (SUMMING + len(SPREAD_SCRATCH))
    scratch = list(extra)
    for batch in BATCHES:
        scratch += 2 * sum_scratch(batch) + 2 * SPREAD_SCRATCH

    def main_of(number, batch):
        rows = slice(batch[0], batch[0] + batch[2])
        lag = number * LAG

        def main(inputs_, outs_, scratch_, sent):
            more, own = scratch_[: len(extra)], scratch_[len(extra) + number * each :][:each]
            parts = [own[:SUMMING], own[SUMMING : 2 * SUMMING]]
            rest = own[2 * SUMMING :]
            parts += [rest[: len(SPREAD_SCRATCH)], rest[len(SPREAD_SCRATCH) :]]

            def add(i, ref):
                job = shard_sum(batch, ref, parts[i], sent)
                return (yield from delayed(job, lag + STARTS[2 * i]))

            def share(i, ref):
                job = shard_spread(batch, ref, parts[2 + i], sent)
                yield from delayed(job, lag + STARTS[2 * i + 1])

            if number == 0:
                for ref, out in zip(outs_, outs):
                    if out[0] == SUMS:
                        ref[...] = jnp.zeros_like(ref)
            else:
                yield lag
            yield from work(add, share, inputs_, outs_, more, rows, lag)

        return main

    return call(
        [main_of(i, b) for i, b in enumerate(BATCHES)], inputs, outs, scratch, ident, riders
    )


def hidden_forward(n_out, wup, wdown, hb, u, g, part, rows):
    value = dot_nn(batch_rows(n_out, rows), wup[...]) + hb[...]
    put_rows(u, rows, value)
    active = gelu_value(value).astype(BF16)
    put_rows(g, rows, active)
    put_rows(part, rows, dot_nn(active, wdown[...]))
    return value


def branch_forward(total, x, table, at, branch_out, x_out, rows):
    bias, scale = (table[r : r + 1, :] for r in at)
    branch = total + bias
    branch_out[rows] = branch
    value = x[rows] + scale * branch
    x_out[rows] = value
    return value


def forward_chain(part, x, table, wup, hb, board, ident, riders):
    def work(add, share, inputs, outs, more, rows, lag):
        part, x, table, wup, hb = inputs
        a, m, n2, u, g, f, x_new, n1 = outs
        (part2,) = more
        total = yield from add(0, part)
        value = branch_forward(total, x, table, (BRANCH, SCALE), a, m, rows)
        spread_norm(value, table, (GAIN + 1, SHIFT + 1), n2, rows)
        yield from share(0, n2)
        yield from until(board, 1, lag + STARTS[2])
        hidden_forward(n2, wup, board[0], hb, u, g, part2, rows)
        total = yield from add(1, part2)
        value = branch_forward(total, m, table, (BRANCH + 1, SCALE + 1), f, x_new, rows)
        spread_norm(value, table, (GAIN + 2, SHIFT + 2), n1, rows)
        yield from share(1, n1)

    shard, whole = (SHARD, F32), (ALL, BF16)
    return chain(
        work,
        (part, x, table, wup, hb),
        [shard, shard, whole, (ALL, F32), whole, shard, shard, whole],
        [pltpu.VMEM(ALL, BF16)],
        ident,
        riders,
    )


def turn_chain(part, x, cot, d_all, table, wup, hb, board, ident, riders):
    def work(add, share, inputs, outs, more, rows, lag):
        part, x, cot, d_all, table, wup, hb = inputs
        a, m, n2, g, end_part, du, hidden, dm, sums, d_out = outs
        u, part2 = more
        total = yield from add(0, part)
        value = branch_forward(total, x, table, (BRANCH + 2, SCALE + 2), a, m, rows)
        spread_norm(value, table, (GAIN + 3, SHIFT + 3), n2, rows)
        yield from share(0, n2)
        yield from until(board, 1, lag + STARTS[2])
        wdown = board[0]
        hidden_forward(n2, wup, wdown, hb, u, g, end_part, rows)
        back_through_hidden(d_all, u, wup, wdown, du, hidden, part2, rows)
        total = yield from add(1, part2)
        back_through_norm(
            total, m, cot, a, table, (GAIN + 3, SCALE + 2), dm, sums, d_out, rows
        )
        yield from share(1, d_out)

    shard, whole, sums = (SHARD, F32), (ALL, BF16), (SUMS, F32)
    return chain(
        work,
        (part, x, cot, d_all, table, wup, hb),
        [shard, shard, whole, whole, whole, whole, sums, shard, sums, whole],
        [pltpu.VMEM(ALL, F32), pltpu.VMEM(ALL, BF16)],
        ident,
        riders,
    )


def backward_chain(part, x, dm, f, m, a, u, g, table, wup, wdown, board, ident, riders):
    def work(add, share, inputs, outs, more, rows, lag):
        part, x, dm, f, m, a, u, g, table, wup, wdown = inputs
        sums1, df, du, hidden, dm_out, sums, d_out = outs
        part2, dx = more
        total = yield from add(0, part)
        back_through_norm(total, x, dm, f, table, (GAIN + 2, SCALE + 1), dx, sums1, df, rows)
        yield from share(0, df)
        if lag > 0:
            board.extend([g, df])
        back_through_hidden(df, u, wup, wdown, du, hidden, part2, rows)
        total = yield from add(1, part2)
        back_through_norm(
            total, m, dx, a, table, (GAIN + 1, SCALE), dm_out, sums, d_out, rows
        )
        yield from share(1, d_out)

    shard, whole, sums = (SHARD, F32), (ALL, BF16), (SUMS, F32)
    return chain(
        work,
        (part, x, dm, f, m, a, u, g, table, wup, wdown),
        [sums, whole, whole, sums, shard, sums, whole],
        [pltpu.VMEM(ALL, BF16), pltpu.VMEM(SHARD, F32)],
        ident,
        riders,
    )


def first_step(tokens, pack, ident, riders):
    pieces = Pieces(tokens)

    def main(inputs, outs, scratch, sent):
        tokens, pack = inputs
        x_out, n_out, pack_out = outs
        landed, psend, precv, ksend, krecv = scratch[:5]
        z = lax.axis_index("z")
        me = lax.axis_index("yh") * 4 + z
        arrive = pieces.run([tokens], [landed], [psend, precv], sent)
        next(arrive)
        pack_out[me] = pack[...]

        def note(j, slot):
            return remote(
                pack, pack_out.at[slot], ksend.at[j], krecv.at[slot], device(yh=j // 4, z=j % 4)
            )

        for j in range(8):

            @pl.when(me != j)
            def _():
                note(j, me).start()

        yield 8.0
        for _ in arrive:
            pass
        for q in range(8):

            @pl.when(me != q)
            def _():
                note(q, q).wait_recv()

        value = landed[...].astype(F32)
        x_out[...] = value
        gain = jnp.concatenate([pack_out[q, GAIN : GAIN + 1, :] for q in range(8)], axis=1)
        shift = jnp.concatenate([pack_out[q, SHIFT : SHIFT + 1, :] for q in range(8)], axis=1)
        hat, _ = norm_of(value)
        n_out[z] = (hat * gain + shift).astype(BF16)
        yield from delayed(shard_spread(WHOLE, n_out, scratch[5:], sent), 10.0)
        for j in range(8):

            @pl.when(me != j)
            def _():
                note(j, me).wait_send()

    def entry():
        yh, z = lax.axis_index("yh"), lax.axis_index("z")
        for j in range(8):

            @pl.when(yh * 4 + z != j)
            def _():
                signal(device(yh=j // 4, z=j % 4))

        return 7

    return call(
        main,
        (tokens, pack),
        [(SHARD, F32), (ALL, BF16), ((8, 32, 128), F32)],
        [pltpu.VMEM(SHARD, BF16)] + sems(8, 8, 8, 8) + SPREAD_SCRATCH,
        ident,
        riders,
        pieces="in",
        entry=entry,
    )


def last_step(part, value, dx, table, known, blocks, at, ident, riders):
    def main(inputs, outs, scratch, sent):
        part, value, dx, table, known, blocks = inputs
        landed, small = outs
        ring_scratch, scratch = scratch[:SUMMING], scratch[SUMMING:]
        both, psend, precv, vectors, zgot, zsend, zrecv = scratch[:7]
        owned, ygot, ysend, yrecv, sub, xgot, xsend, xrecv = scratch[7:]
        x_, yl, co, yh, z = (lax.axis_index(a) for a in AXES)
        total = yield from shard_sum(WHOLE, part, ring_scratch, sent)
        (gain,) = (table[r : r + 1, :] for r in at)
        dr, gain_sum, shift_sum = norm_back(total, value[...], gain)
        both[...] = (dx[...] + dr).astype(BF16)
        give = PiecesOut.give(both, landed, psend, precv)
        next(give)
        vectors[...] = known[...]
        vectors[at[0] : at[0] + 1, :] = gain_sum
        vectors[at[0] + SHIFT : at[0] + SHIFT + 1, :] = shift_sum

        def on_z(there, slot, h):
            cut = vectors.at[:, pl.ds((h * 4 + there) * 128, 128)]
            return remote(
                cut, zgot.at[slot, h], zsend.at[there, h], zrecv.at[slot, h], device(z=there)
            )

        def on_y(there, slot):
            to = device(yh=there // 4, yl=(there // 2) % 2, co=there % 2)
            return remote(
                owned.at[there // 4], ygot.at[slot], ysend.at[there], yrecv.at[slot], to
            )

        def on_x(there, slot):
            return remote(sub, xgot.at[slot], xsend.at[there], xrecv.at[slot], device(x=there))

        def others(me, count, do):
            for i in range(count):

                @pl.when(me != i)
                def _():
                    do(i)

        me = yh * 4 + yl * 2 + co

        def both_halves(do):
            def run(i):
                do(i, 0)
                do(i, 1)

            return run

        others(z, 4, both_halves(lambda i, h: on_z(i, z, h).start()))
        for h in range(2):
            zgot[z, h] = vectors[:, pl.ds(pl.multiple_of((h * 4 + z) * 128, 128), 128)]
        yield 13.0
        others(z, 4, both_halves(lambda i, h: on_z(i, i, h).wait_recv()))
        owned[:, 0:16] = zgot[0] + zgot[1] + zgot[2] + zgot[3]
        owned[:, 16:32] = blocks[...]
        others(me, 8, lambda i: on_y(i, me).start())
        ygot[me] = owned[yh]
        yield 16.0
        others(me, 8, lambda i: on_y(i, i).wait_recv())
        sub[...] = sum(ygot[i] for i in range(8))
        others(x_, 4, lambda i: on_x(i, x_).start())
        xgot[x_] = sub[...]
        yield 19.0
        others(x_, 4, lambda i: on_x(i, i).wait_recv())
        small[...] = sum(xgot[i] for i in range(4))
        others(z, 4, both_halves(lambda i, h: on_z(i, z, h).wait_send()))
        others(me, 8, lambda i: on_y(i, me).wait_send())
        others(x_, 4, lambda i: on_x(i, x_).wait_send())
        for _ in give:
            pass

    def entry():
        x_, yl, co, yh, z = (lax.axis_index(a) for a in AXES)
        me = yh * 4 + yl * 2 + co
        for i in range(8):

            @pl.when(me != i)
            def _():
                signal(device(yh=i // 4, yl=(i // 2) % 2, co=i % 2))

        for i in range(4):

            @pl.when(x_ != i)
            def _():
                signal(device(x=i))

            @pl.when(z != i)
            def _():
                signal(device(z=i))

        return 7 + 3 + 3

    return call(
        main,
        (part, value, dx, table, known, blocks),
        [((8, ROWS, 128), BF16), ((32, 128), F32)],
        sum_scratch(WHOLE)
        + [
            pltpu.VMEM(SHARD, BF16),
            *sems(8, 8),
            pltpu.VMEM((16, WIDTH), F32),
            pltpu.VMEM((4, 2, 16, 128), F32),
            pltpu.SemaphoreType.DMA((4, 2)),
            pltpu.SemaphoreType.DMA((4, 2)),
            pltpu.VMEM((2, 32, 128), F32),
            pltpu.VMEM((8, 32, 128), F32),
            *sems(8, 8),
            pltpu.VMEM((32, 128), F32),
            pltpu.VMEM((4, 32, 128), F32),
            *sems(4, 4),
        ],
        ident,
        riders,
        pieces="out",
        entry=entry,
    )


def lanes_of(head, shape):
    lane = lax.broadcasted_iota(jnp.int32, shape, 1)
    return (lane < 64, lane == 64) if head % 2 == 0 else (lane >= 64, lane == 0)


def put_head(ref, i, value, one=False):
    inside, extra = lanes_of(i, value.shape)
    ref[i, 0:OWN] = jnp.where(inside, value, jnp.where(extra & one, 1, 0).astype(BF16))
    ref[i, OWN:QROWS] = jnp.zeros((QROWS - OWN, 128), BF16)


def put_keys(ref, i, rows, value, mask):
    inside, extra = lanes_of(i, value.shape)
    ref[i, rows] = jnp.where(inside, value, jnp.where(extra, mask[rows], jnp.zeros_like(value)))


def attend_step(n_all, wqkv, wout, bias, mask, ident, riders=()):
    def main(inputs, outs, scratch, sent):
        n_all, wqkv, wout, bias, mask = inputs
        part, qkv, other, att, lse = outs
        kall, vt, qpad, ot, send, recv = scratch
        to = device(co=1 - lax.axis_index("co"))
        mine, theirs = slice(0, OWN), slice(OWN, KEYS)
        yield 0.1
        normed = n_all[...].reshape(OWN, WIDTH)
        lse[...] = jnp.zeros_like(lse)
        copies = []
        for h in range(2):
            cols = slice(h * 384, h * 384 + 384)
            block = (dot_nn(normed, wqkv[:, cols]) + bias[:, cols]).astype(BF16)
            qkv[:, cols] = block
            c = remote(
                qkv.at[:, pl.ds(h * 384 + 128, 256)],
                other.at[:, pl.ds(h * 256, 256)],
                send.at[h],
                recv.at[h],
                to,
            )
            c.start()
            copies.append(c)
            for i in (2 * h, 2 * h + 1):
                put_head(qpad, i, block[:, 0:128] * 0.125, True)
                put_keys(kall, i, mine, block[:, 128:256], mask)
            vt[h * 128 : h * 128 + 128, 0:OWN] = block[:, 256:384].T
        sent.extend(copies)
        yield 3.0
        for h in range(2):
            copies[h].wait_recv()
            for i in (2 * h, 2 * h + 1):
                put_keys(kall, i, theirs, other[:, h * 256 : h * 256 + 128], mask)
            vt[h * 128 : h * 128 + 128, OWN:KEYS] = other[:, h * 256 + 128 : h * 256 + 256].T

            def head(hh, _):
                i = 2 * h + hh
                rows = pl.ds(pl.multiple_of(i * 64, 64), 64)
                for lo, n in CHUNKS:
                    s = dot_nt(kall[i], qpad[i, lo : lo + n])
                    top = jnp.max(s, axis=0, keepdims=True)
                    e = jnp.exp(s - top)
                    total = jnp.sum(e, axis=0, keepdims=True)
                    ot[rows, lo : lo + n] = dot_nn(vt[rows], e.astype(BF16)) * (1.0 / total)
                    lse[i, 0:1, lo : lo + n] = top + jnp.log(total)
                return 0

            lax.fori_loop(0, 2, head, 0)
            yield 8.0 + 4.0 * h
        att[...] = ot[...].T[0:OWN].astype(BF16)
        part[...] = dot_nn(att[...], wout[...]).astype(BF16).reshape(ALL)

    return call(
        main,
        (n_all, wqkv, wout, bias, mask),
        [
            (ALL, BF16),
            ((OWN, 768), BF16),
            ((OWN, 512), BF16),
            ((OWN, 256), BF16),
            ((4, 8, QROWS), F32),
        ],
        [
            pltpu.VMEM((4, KEYS, 128), BF16),
            pltpu.VMEM((256, KEYS), BF16),
            pltpu.VMEM((4, QROWS, 128), BF16),
            pltpu.VMEM((256, QROWS), F32),
        ]
        + sems(2, 2),
        ident,
        riders,
        links=("core",),
    )


def attend_back_step(d_all, wqkv, wout, qkv, other, att, lse, mask, ident, riders=()):
    def main(inputs, outs, scratch, sent):
        d_all, wqkv, wout, qkv, other, att, lse, mask = inputs
        part, dqkv, sums = outs
        kall, vall, kt, qone, qpad, dpad, delta, dqt, dk, dv, away, got, send, recv = scratch
        to = device(co=1 - lax.axis_index("co"))
        mine, theirs = slice(0, OWN), slice(OWN, KEYS)
        yield 0.1
        datt = dot_nt(d_all[...].reshape(OWN, WIDTH), wout[...]).astype(BF16)
        copies = []
        along = (datt.astype(F32) * att[...].astype(F32)).T
        delta[...] = jnp.zeros_like(delta)
        for i in range(4):
            delta[i, 0:1, 0:OWN] = jnp.sum(along[i * 64 : i * 64 + 64], axis=0, keepdims=True)
        for h in range(2):
            base, half = h * 384, h * 256
            own_keys, other_keys = qkv[:, base + 128 : base + 256], other[:, half : half + 128]
            for i in (2 * h, 2 * h + 1):
                query = qkv[:, base : base + 128] * 0.125
                put_head(qone, i, query, True)
                put_head(qpad, i, query)
                put_head(dpad, i, datt[:, h * 128 : h * 128 + 128])
                put_keys(kall, i, mine, own_keys, mask)
                put_keys(kall, i, theirs, other_keys, mask)
            vall[h, 0:OWN] = qkv[:, base + 256 : base + 384]
            vall[h, OWN:KEYS] = other[:, half + 128 : half + 256]
            kt[h * 128 : h * 128 + 128, 0:OWN] = own_keys.T
            kt[h * 128 : h * 128 + 128, OWN:KEYS] = other_keys.T
            dk[h] = jnp.zeros((KEYS, 128), F32)
            dv[h] = jnp.zeros((KEYS, 128), F32)

            def head(hh, _):
                i = 2 * h + hh
                rows = pl.ds(pl.multiple_of(i * 64, 64), 64)
                for lo, n in CHUNKS:
                    qc, dc = qpad[i, lo : lo + n], dpad[i, lo : lo + n]
                    s = dot_nt(kall[i], qone[i, lo : lo + n])
                    p = jnp.exp(s - lse[i, 0:1, lo : lo + n])
                    dp = dot_nt(vall[h], dc)
                    ds = (p * (dp - delta[i, 0:1, lo : lo + n])).astype(BF16)
                    dv[h] += dot_nn(p.astype(BF16), dc)
                    dk[h] += dot_nn(ds, qc)
                    dqt[rows, lo : lo + n] = dot_nn(kt[rows], ds)
                return 0

            lax.fori_loop(0, 2, head, 0)
            away[h, :, 0:128] = dk[h, OWN:KEYS].astype(BF16)
            away[h, :, 128:256] = dv[h, OWN:KEYS].astype(BF16)
            c = remote(away.at[h], got.at[h], send.at[h], recv.at[h], to)
            c.start()
            copies.append(c)
            yield 7.0 + 5.0 * h
        sent.extend(copies)
        dq = dqt[...].T[0:OWN] * 0.125
        for h in range(2):
            base = h * 384
            dqkv[:, base : base + 128] = dq[:, h * 128 : h * 128 + 128].astype(BF16)
            copies[h].wait_recv()
            dqkv[:, base + 128 : base + 256] = (
                dk[h, 0:OWN] + got[h, :, 0:128].astype(F32)
            ).astype(BF16)
            dqkv[:, base + 256 : base + 384] = (
                dv[h, 0:OWN] + got[h, :, 128:256].astype(F32)
            ).astype(BF16)
        part[...] = dot_nt(dqkv[...], wqkv[...]).astype(BF16).reshape(ALL)
        sums[...] = jnp.zeros_like(sums)
        sums[0:1, :] = jnp.sum(dqkv[...].astype(F32), axis=0, keepdims=True)

    return call(
        main,
        (d_all, wqkv, wout, qkv, other, att, lse, mask),
        [(ALL, BF16), ((OWN, 768), BF16), ((8, 768), F32)],
        [
            pltpu.VMEM((4, KEYS, 128), BF16),
            pltpu.VMEM((2, KEYS, 128), BF16),
            pltpu.VMEM((256, KEYS), BF16),
            pltpu.VMEM((4, QROWS, 128), BF16),
            pltpu.VMEM((4, QROWS, 128), BF16),
            pltpu.VMEM((4, QROWS, 128), BF16),
            pltpu.VMEM((4, 8, QROWS), F32),
            pltpu.VMEM((256, QROWS), F32),
            pltpu.VMEM((2, KEYS, 128), F32),
            pltpu.VMEM((2, KEYS, 128), F32),
            pltpu.VMEM((2, OWN, 256), BF16),
            pltpu.VMEM((2, OWN, 256), BF16),
        ]
        + sems(2, 2),
        ident,
        riders,
        links=("core",),
    )


def on_device(
    tokens,
    cotangent,
    attend_weight,
    output_weight,
    up_weight,
    down_weight,
    norm_gain,
    norm_shift,
    attend_bias,
    branch_bias,
    layer_scale,
    hidden_bias,
):
    co, yh, z = (lax.axis_index(a) for a in ("co", "yh", "z"))
    attend_weight = attend_weight.reshape(LAYERS, 256, 384)
    first = jnp.pad(tokens, ((0, 15), (0, 0)))
    cot_pieces = jnp.pad(cotangent.astype(BF16), ((0, 15), (0, 0)))
    pack = jnp.concatenate(
        [
            norm_gain.reshape(4, 128),
            norm_shift.reshape(4, 128),
            branch_bias.reshape(4, 128),
            layer_scale.reshape(4, 128),
            attend_bias.reshape(4, 128),
            hidden_bias.reshape(8, 128),
            jnp.zeros((4, 128), F32),
        ]
    )

    def attend_of(l):
        return GatherWeight(attend_weight, l, 0)

    def output_of(l):
        return GatherWeight(output_weight, l, 1)

    def up_of(l):
        return GatherWeight(up_weight, l, 0)

    def hidden_of(l):
        return here[:, 20 + 4 * l : 24 + 4 * l].reshape(1, WIDTH)

    def down_of(l, board):
        return GatherWeight(down_weight, l, 1, VM, board)

    weights = [[None] * 4 for _ in range(LAYERS)]
    ident = iter(range(40))
    (x, n_all, packs), (weights[0][0], weights[0][1]) = first_step(
        first, pack, next(ident), [attend_of(0), output_of(0)]
    )
    table = packs[:, 0:16].transpose(1, 0, 2).reshape(16, WIDTH)
    here = jnp.stack(
        [
            lax.dynamic_index_in_dim(packs, z, keepdims=False),
            lax.dynamic_index_in_dim(packs, z + 4, keepdims=False),
        ]
    )
    row = jnp.arange(OWN)
    block, inside = row // ROWS, row % ROWS

    def hidden_keys(half):
        real = (inside < REAL) | ((inside == REAL) & (block == 3) & (half == 1))
        return jnp.where(real, 0.0, -1e30).astype(BF16)

    mask = jnp.concatenate([hidden_keys(co), hidden_keys(1 - co)])
    mask = jnp.broadcast_to(mask[:, None], (KEYS, 128))

    last = jnp.where((co == 1) & (z == 3), REAL + 1, REAL)
    real_row = jnp.arange(ROWS)[:, None] < last

    saved = []
    for l in range(LAYERS):
        wqkv, wout = weights[l][:2]
        ab = here[:, 16 + 2 * l : 18 + 2 * l]
        qkv_bias = jnp.concatenate(
            [ab[0, 0], jnp.zeros(128), ab[0, 1], ab[1, 0], jnp.zeros(128), ab[1, 1]]
        )[None]
        riders = [up_of(l)]
        if l == 1:
            riders.append(Spread((cot * table[SCALE + 3]).astype(BF16)))
        n1 = n_all
        (part, qkv, other, att, lse), got = attend_step(
            n1, wqkv, wout, qkv_bias, mask, next(ident), riders
        )
        weights[l][2] = got[0]
        if l == 1:
            d_all = d_last = got[1]
        saved.append([x, n1, qkv, other, att, lse])
        board = []
        if l == 0:
            riders = [
                down_of(0, board), Pieces(cot_pieces), attend_of(1), output_of(1)
            ]
            (a, m, n2, u, g, f, x, n_all), got = forward_chain(
                part, x, table, weights[0][2], hidden_of(0), board, next(ident), riders
            )
            weights[0][3], weights[1][:2] = got[0], got[2:]
            cot = jnp.where(real_row, got[1].astype(F32), 0.0)
            saved[0] += [a, m, n2, u, g, f]
        else:
            riders = [down_of(1, board)]
            (a, m, n2, g, end_part, du, hidden, dm, sums, d_all), got = turn_chain(
                part, x, cot, d_all, table, weights[1][2], hidden_of(1), board, next(ident), riders
            )
            weights[1][3] = got[0]

    gain_sums, shift_sums, scale_sums, branch_sums = ([None] * 4 for _ in range(4))
    hidden_sums, qkv_sums, grads = [None, hidden[0]], [None] * LAYERS, [[None] * 4, [None] * 4]

    def keep(sums, norm, branch):
        gain_sums[norm], shift_sums[norm] = sums[0], sums[1]
        scale_sums[branch], branch_sums[branch] = sums[2], sums[3]

    def summing(block):
        return SumBlock(block.shape, block)

    keep(sums, 3, 2)
    x1, n1, qkv, other, att, lse = saved[1]
    da = d_all
    riders = [
        ReduceWeight(n2, du, 0),
        End(end_part, m, cot, table, (BRANCH + 3, SCALE + 3)),
    ]
    (part, dqkv, qkv_sum), got = attend_back_step(
        d_all, *weights[1][:2], qkv, other, att, lse, mask, next(ident), riders
    )
    up_block, x_end, sums = got
    scale_sums[3], branch_sums[3] = sums[2], sums[3]
    qkv_sums[1] = qkv_sum[0]
    x, n1_0, qkv, other, att_0, lse, a, m, n2, u, g0, f = saved[0]
    board = []
    late = ReduceWeight(g0, g0, 1, board)
    riders = [
        ReduceWeight(n1, dqkv, 0),
        ReduceWeight(att, da, 1),
        ReduceWeight(g, d_last, 1),
        summing(up_block),
        late,
    ]
    (sums1, df, du, hidden, dm, sums, d_all), got = backward_chain(
        part, x1, dm, f, m, a, u, g0, table, *weights[0][2:], board, next(ident), riders
    )
    attend_block, output_block, down_block, grads[1][2], down_block_0 = got
    keep(sums1, 2, 1)
    keep(sums, 1, 0)
    hidden_sums[0] = hidden[0]
    riders = [
        ReduceWeight(n2, du, 0),
        summing(attend_block),
        summing(output_block),
        summing(down_block),
        PiecesOut(x_end),
    ]
    (part, dqkv, qkv_sum), got = attend_back_step(
        d_all, *weights[0][:2], qkv, other, att_0, lse, mask, next(ident), riders
    )
    up_block, grads[1][0], grads[1][1], grads[1][3], out_pieces = got
    qkv_sums[0] = qkv_sum[0]
    riders = [
        ReduceSum(n1_0, dqkv, 0),
        ReduceSum(att_0, d_all, 1),
        summing(up_block),
        summing(down_block_0),
    ]
    zero = jnp.zeros(WIDTH)
    known = jnp.stack(
        [zero] + gain_sums[1:] + [zero] + shift_sums[1:] + branch_sums + scale_sums
    )
    blocks = jnp.concatenate(
        [
            jnp.stack(qkv_sums).reshape(2, 2, 3, 128).transpose(1, 0, 2, 3).reshape(2, 6, 128),
            jnp.stack(hidden_sums).reshape(2, 2, 4, 128).transpose(1, 0, 2, 3).reshape(2, 8, 128),
            jnp.zeros((2, 2, 128), F32),
        ],
        axis=1,
    )
    (grad_pieces, small), grads[0] = last_step(
        part, x, dm, table, known, blocks, (GAIN,), next(ident), riders
    )

    bias_grad = small[16:22].reshape(2, 3, 128)[:, 0::2]

    def rows(landed):
        return jnp.concatenate(
            [landed[0:7, 0:REAL].reshape(7 * REAL, 128), landed[7, 0 : REAL + 1]]
        ).astype(F32)

    return (
        rows(out_pieces),
        rows(grad_pieces),
        jnp.stack([grads[l][0] for l in range(LAYERS)]).reshape(LAYERS, 256, 3, 128),
        jnp.stack([grads[l][1] for l in range(LAYERS)]),
        jnp.stack([grads[l][2] for l in range(LAYERS)]),
        jnp.stack([grads[l][3] for l in range(LAYERS)]),
        small[0:4].reshape(2, 2, 128),
        small[4:8].reshape(2, 2, 128),
        bias_grad,
        small[8:12].reshape(2, 2, 128),
        small[12:16].reshape(2, 2, 128),
        small[22:30].reshape(2, 512),
    )


def solution(mesh):
    split = Mesh(mesh.devices.reshape(4, 2, 2, 2, 4), AXES)
    images, row, col = ("x", "yl", "co"), ("yl", "co"), ("yh", "z")
    placed = (
        P(images, col),
        P(images, col),
        P(None, row, None, col),
        P(None, col, row),
        P(None, row, col),
        P(None, col, row),
        P(None, None, col),
        P(None, None, col),
        P(None, None, col),
        P(None, None, col),
        P(None, None, col),
        P(None, col),
    )
    return jax.shard_map(
        on_device, mesh=split, in_specs=placed, out_specs=placed, check_vma=False
    )
```

```python
import jax
import jax.numpy as jnp
from jax import lax
from jax.experimental import pallas as pl
from jax.experimental.pallas import tpu as pltpu
from jax.sharding import Mesh, PartitionSpec as P

WIDTH = 1024
HALF = WIDTH // 2
SEQ = 1025
LAYERS = 2
REAL = 128
ROWS = 144
TAIL = ROWS - REAL
OWN = 4 * ROWS
KEYS = 2 * OWN
QROWS = 640
CHUNKS = ((0, 256), (256, 256), (512, 128))
EPS = 1e-06
ROOT_HALF = 0.7071067811865476
INV_ROOT_TWO_PI = 0.3989422804014327
MESH = pl.DeviceIdType.MESH
AXES = ("x", "yl", "co", "yh", "z")
VM = pl.BlockSpec(memory_space=pltpu.VMEM)
ANY = pl.BlockSpec(memory_space=pl.ANY)
F32 = jnp.float32
BF16 = jnp.bfloat16


def gelu_value(value):
    return 0.5 * value * (1.0 + lax.erf(value * ROOT_HALF))


def gelu_slope(value):
    return 0.5 * (1.0 + lax.erf(value * ROOT_HALF)) + value * INV_ROOT_TWO_PI * jnp.exp(
        -0.5 * value * value
    )


def dot_nt(left, right):
    return lax.dot_general(left, right, (((1,), (1,)), ((), ())), preferred_element_type=F32)


def dot_tn(left, right):
    return lax.dot_general(left, right, (((0,), (0,)), ((), ())), preferred_element_type=F32)


def dot_nn(left, right):
    return jnp.dot(left, right, preferred_element_type=F32)


def device(**moved):
    return tuple(moved[a] if a in moved else lax.axis_index(a) for a in AXES)


def remote(src, dst, send, recv, to):
    return pltpu.make_async_remote_copy(
        src_ref=src, dst_ref=dst, send_sem=send, recv_sem=recv, device_id=to, device_id_type=MESH
    )


def signal(to):
    pl.semaphore_signal(
        pltpu.get_barrier_semaphore(), inc=1, device_id=to, device_id_type=MESH
    )


class Ring:
    def __init__(self, axis):
        self.axis = axis
        if axis == "y":
            self.me = lax.axis_index("yh") * 2 + lax.axis_index("yl")
        else:
            self.me = lax.axis_index(axis)
        self.right = lax.rem(self.me + 1, 4)
        self.left = lax.rem(self.me + 3, 4)
        self.across = lax.rem(self.me + 2, 4)
        self.to_right, self.to_left = self.at(self.right), self.at(self.left)

    def at(self, index):
        if self.axis == "y":
            return device(yh=index // 2, yl=lax.rem(index, 2))
        return device(**{self.axis: index})


def greet(links, more=0, home=None):
    count = more
    for link in links:
        if link == "core":
            signal(device(co=1 - lax.axis_index("co")))
            count += 1
        else:
            ring = Ring(link)
            signal(ring.to_right)
            signal(ring.to_left)
            count += 2
            if link != "y":
                signal(ring.at(ring.across))
                count += 1
    barrier = pltpu.get_barrier_semaphore()
    if home is None:
        pl.semaphore_wait(barrier, count)
    else:

        @pl.when(home)
        def _():
            pl.semaphore_wait(barrier, count + 7)

        @pl.when(jnp.logical_not(home))
        def _():
            pl.semaphore_wait(barrier, count + 8)


def in_turns(jobs, done):
    waiting = [[0.0, i, job, number] for i, (number, job) in enumerate(jobs)]
    while waiting:
        first = min(waiting, key=lambda w: w[:2])
        try:
            first[0] = next(first[2])
        except StopIteration:
            waiting.remove(first)
            if all(w[3] != first[3] for w in waiting):
                done(first[3])


class Sent(list):
    def __init__(self):
        self.results = []

    def flush(self, *refs):
        for ref in refs:
            for result in self.results:
                if result[0] is ref and not result[2]:
                    result[1].start()
                    result[2] = True

    def finish(self):
        for c in self:
            c.wait_send()
        for _, copy, _ in self.results:
            copy.wait()


def until(board, count, time):
    while len(board) < count:
        yield time
        time += 1.0


def delayed(job, time):
    while True:
        try:
            yield time + next(job)
        except StopIteration as end:
            return end.value


def by_rows(ref, lead, half):
    rows = ref.shape[1] // 2
    return ref.at[lead, pl.ds(half * rows, rows), :]


def reduce_on(ring, half, part, fin, relay, stage, send, recv, sent, first=0):
    def copy(i, src, dst, to):
        c = remote(src, dst, send.at[i], recv.at[i], to)
        c.start()
        sent.append(c)
        return c

    far_r = copy(0, half(part, ring.across, 0), relay.at[0], ring.to_right)
    far_l = copy(1, half(part, ring.across, 1), relay.at[1], ring.to_left)
    near_r = copy(2, half(part, ring.right, 1), half(fin, 0, 1), ring.to_right)
    near_l = copy(3, half(part, ring.left, 0), half(fin, 1, 0), ring.to_left)
    yield 3.0
    far_r.wait_recv()
    stage[0] = (half(part, ring.right, 0)[...].astype(F32) + relay[0].astype(F32)).astype(BF16)
    sum_r = copy(4, stage.at[0], half(fin, 0, 0), ring.to_right)
    far_l.wait_recv()
    stage[1] = (half(part, ring.left, 1)[...].astype(F32) + relay[1].astype(F32)).astype(BF16)
    sum_l = copy(5, stage.at[1], half(fin, 1, 1), ring.to_left)
    yield 7.0
    for c in (near_r, near_l, sum_r, sum_l):
        c.wait_recv()
    own = part.at[ring.me, pl.ds(first, fin.shape[1])][...]
    return own.astype(F32) + fin[0].astype(F32) + fin[1].astype(F32)


def gather_on(ring, slot, own, send, recv, sent, landed=None):
    def copy(i, src, owner, half, to):
        return remote(src, slot(owner, half), send.at[i], recv.at[i], to)

    def go(*what):
        c = copy(*what)
        c.start()
        sent.append(c)

    def lands(i, owner, half):
        copy(i, slot(owner, half), owner, half, ring.to_right).wait_recv()

    go(0, own(0), ring.me, 0, ring.to_right)
    go(1, own(1), ring.me, 1, ring.to_left)
    go(2, own(1), ring.me, 1, ring.to_right)
    go(3, own(0), ring.me, 0, ring.to_left)
    yield 2.5
    lands(0, ring.left, 0)
    go(4, slot(ring.left, 0), ring.left, 0, ring.to_right)
    lands(1, ring.right, 1)
    go(5, slot(ring.right, 1), ring.right, 1, ring.to_left)
    yield 5.0
    lands(2, ring.left, 1)
    if landed is not None:
        landed(ring.left)
    lands(3, ring.right, 0)
    if landed is not None:
        landed(ring.right)
    yield 7.0
    lands(4, ring.across, 0)
    lands(5, ring.across, 1)
    if landed is not None:
        landed(ring.across)


def gather_slots(ring, out, half, send, recv, sent):
    def slot(owner, h):
        return half(out, owner, h)

    yield from gather_on(ring, slot, lambda h: slot(ring.me, h), send, recv, sent)


def sems(*counts):
    return [pltpu.SemaphoreType.DMA((c,)) for c in counts]


def tail_roles():
    z, second = lax.axis_index("z"), lax.axis_index("co") == 1
    return z, second & (z == 3), second & (z != 3)


WHOLE, BATCHES = (0, REAL, ROWS), ((0, REAL // 2, REAL // 2), (REAL // 2, REAL // 2, ROWS - REAL // 2))


def shard_sum(batch, part, scratch, sent):
    first, count, rows = batch
    fin, relay, stage, tails, tail, send, recv, tsend, trecv = scratch
    z, holds, gives = tail_roles()
    ends = first + rows == ROWS

    def half(ref, lead, h):
        lo = first if ref.shape[1] == ROWS else 0
        return ref.at[lead, pl.ds(lo, count), pl.ds(h * HALF, HALF)]

    def tail_to(slot):
        src = part.at[3, pl.ds(REAL, TAIL), :]
        return remote(src, tails.at[slot], tsend.at[0], trecv.at[slot], device(z=3))

    if ends:

        @pl.when(gives)
        def _():
            tail_to(z).start()

    total = yield from reduce_on(
        Ring("z"), half, part, fin, relay, stage, send, recv, sent, first
    )
    if not ends:
        return total
    tail[...] = jnp.zeros_like(tail)

    @pl.when(holds)
    def _():
        for i in range(3):
            tail_to(i).wait_recv()
        tail[...] = part[3, REAL:ROWS].astype(F32) + sum(tails[i].astype(F32) for i in range(3))

    @pl.when(gives)
    def _():
        tail_to(z).wait_send()

    return jnp.concatenate([total, tail[...]], axis=0)


def shard_spread(batch, out, scratch, sent):
    first, count, rows = batch
    send, recv, tsend, trecv = scratch
    z, holds, gives = tail_roles()
    ends = first + rows == ROWS

    def half(ref, lead, h):
        return ref.at[lead, pl.ds(first, count), pl.ds(h * HALF, HALF)]

    def tail_to(i):
        ref = out.at[3, pl.ds(REAL, TAIL), :]
        return remote(ref, ref, tsend.at[i], trecv.at[0], device(z=i))

    if ends:

        @pl.when(holds)
        def _():
            for i in range(3):
                tail_to(i).start()

    yield from gather_slots(Ring("z"), out, half, send, recv, sent)
    if ends:

        @pl.when(gives)
        def _():
            tail_to(0).wait_recv()

        @pl.when(holds)
        def _():
            for i in range(3):
                tail_to(i).wait_send()


def sum_scratch(batch):
    count = batch[1]
    return [
        pltpu.VMEM((2, count, WIDTH), BF16),
        pltpu.VMEM((2, count, HALF), BF16),
        pltpu.VMEM((2, count, HALF), BF16),
        pltpu.VMEM((3, TAIL, WIDTH), BF16),
        pltpu.VMEM((TAIL, WIDTH), F32),
    ] + sems(6, 6, 1, 3)


SPREAD_SCRATCH = sems(6, 6, 3, 1)
SUMMING = len(sum_scratch(WHOLE))


class GatherWeight:
    links = ("y", "core")

    def __init__(self, shards, layer, side, spec=ANY, board=None, start=0.0):
        rows, columns = shards.shape[1:]
        self.board, self.start = board, start
        self.layer, self.side, self.rows, self.columns = layer, side, rows, columns
        full = (4 * rows, 2 * columns) if side == 0 else (2 * rows, 4 * columns)
        self.inputs = [(shards, ANY)]
        self.outs = [(full, BF16, spec)]
        self.scratch = sems(6, 6, 4, 4, 1)

    def run(self, inputs, outs, scratch, sent):
        if self.start > 0.0:
            yield self.start
        yield from delayed(self.go(inputs, outs, scratch, sent), self.start)

    def go(self, inputs, outs, scratch, sent):
        (shards,), (out,) = inputs, outs
        send, recv, csend, crecv, local = scratch
        own = shards.at[self.layer]
        ring, co = Ring("y"), lax.axis_index("co")
        rows, columns = self.rows, self.columns

        def block(y, core, half=None):
            yh, r = y // 2, lax.rem(y, 2) * 2 + core
            down, along = (r, yh) if self.side == 0 else (yh, r)
            first, count = down * rows, rows
            if half is not None:
                count = rows // 2
                first = first + half * count
            return out.at[
                pl.ds(pl.multiple_of(first, 16), count),
                pl.ds(pl.multiple_of(along * columns, 128), columns),
            ]

        def to_core(i, src, y):
            c = remote(src, block(y, co), csend.at[i], crecv.at[i], device(co=1 - co))
            c.start()
            sent.append(c)

        keep = pltpu.make_async_copy(own, block(ring.me, co), local.at[0])
        keep.start()
        to_core(0, own, ring.me)
        numbers = iter((1, 2, 3))
        yield from gather_on(
            ring,
            lambda y, half: block(y, co, half),
            lambda half: own.at[pl.ds(half * (rows // 2), rows // 2), :],
            send,
            recv,
            sent,
            lambda y: to_core(next(numbers), block(y, co), y),
        )
        keep.wait()
        yield 12.0
        for i, y in enumerate((ring.me, ring.left, ring.right, ring.across)):
            there = block(y, 1 - co)
            remote(there, there, csend.at[i], crecv.at[i], device(co=1 - co)).wait_recv()
        if self.board is not None:
            self.board.append(out)


class ReduceWeight:
    links = ("y", "core")

    def __init__(self, left, right, side, board=None, start=0.0):
        self.board, self.start = board, start
        rows, columns = left.shape[-1], right.shape[-1]
        self.full = rows, columns
        rows, columns = (rows // 4, columns // 2) if side == 0 else (rows // 2, columns // 4)
        self.side, self.rows, self.columns = side, rows, columns
        self.inputs = [] if board is not None else [(left, VM), (right, VM)]
        self.outs = [((rows, columns), BF16, VM)]
        self.scratch = [
            pltpu.VMEM(self.full, BF16),
            pltpu.VMEM((4, rows, columns), BF16),
            pltpu.VMEM((4, rows, columns), BF16),
            pltpu.VMEM((2, rows, columns), BF16),
            pltpu.VMEM((2, rows // 2, columns), BF16),
            pltpu.VMEM((2, rows // 2, columns), BF16),
        ] + sems(4, 4, 6, 6)

    def run(self, inputs, outs, scratch, sent):
        total = yield from self.total(inputs, scratch, sent)
        outs[0][...] = total.astype(BF16)

    def total(self, inputs, scratch, sent):
        if self.board is not None:
            yield from until(self.board, 2, self.start)
            inputs = self.board
        elif self.start > 0.0:
            yield self.start
        left, right = inputs
        part, got, pair, fin, relay, stage, csend, crecv, send, recv = scratch

        def columns_of(ref, first):
            if len(ref.shape) == 2:
                return ref[:, first : first + 256]
            return ref[:, :, first : first + 256].reshape(OWN, 256)

        whole = right[...] if len(right.shape) == 2 else right[...].reshape(OWN, self.full[1])
        for first in range(0, self.full[0], 256):
            part[first : first + 256] = dot_tn(columns_of(left, first), whole).astype(BF16)
            if self.start > 0.0:
                yield self.start + first / 512
        co = lax.axis_index("co")
        rows, columns = self.rows, self.columns

        def block(y, core):
            yh, r = y // 2, (y % 2) * 2 + core
            down, along = (r, yh) if self.side == 0 else (yh, r)
            return part.at[
                pl.ds(pl.multiple_of(down * rows, 16), rows),
                pl.ds(pl.multiple_of(along * columns, 128), columns),
            ]

        copies = []
        for y in range(4):
            c = remote(
                block(y, 1 - co), got.at[y], csend.at[y], crecv.at[y], device(co=1 - co)
            )
            c.start()
            copies.append(c)
        sent.extend(copies)
        yield self.start + 5.0
        for y in range(4):
            copies[y].wait_recv()
            pair[y] = (block(y, co)[...].astype(F32) + got[y].astype(F32)).astype(BF16)
        job = reduce_on(Ring("y"), by_rows, pair, fin, relay, stage, send, recv, sent)
        return (yield from delayed(job, self.start + 6.0))


class SumBlock:
    links = ("x",)

    def __init__(self, shape, block=None):
        rows, columns = shape
        self.shape, self.rows = shape, rows // 4
        self.inputs = [] if block is None else [(block, VM)]
        self.outs = [(shape, F32, VM)]
        quarters = (4, rows // 4, columns)
        self.scratch = [pltpu.VMEM(quarters, BF16) for _ in range(3)] + sems(4, 4, 4, 4)

    def run(self, inputs, outs, scratch, sent):
        yield from self.total(inputs[0][...], outs[0], scratch, sent)

    def total(self, value, out, scratch, sent):
        part, got, every, send, recv, gsend, grecv = scratch
        ring = Ring("x")
        others = (ring.across, ring.right, ring.left)
        for i in range(4):
            part[i] = value[i * self.rows : (i + 1) * self.rows].astype(BF16)

        def give(slot, to):
            return remote(part.at[to], got.at[slot], send.at[to], recv.at[slot], ring.at(to))

        def share(slot, to):
            return remote(
                every.at[slot], every.at[slot], gsend.at[to], grecv.at[slot], ring.at(to)
            )

        for i in others:
            c = give(ring.me, i)
            c.start()
            sent.append(c)
        got[ring.me] = part[ring.me]
        yield 4.0
        for i in others:
            give(i, i).wait_recv()
        every[ring.me] = sum(got[i].astype(F32) for i in range(4)).astype(BF16)
        for i in others:
            c = share(ring.me, i)
            c.start()
            sent.append(c)
        yield 8.0
        for i in others:
            share(i, i).wait_recv()
        for i in range(4):
            out[i * self.rows : (i + 1) * self.rows] = every[i].astype(F32)


class ReduceSum:
    links = ("y", "core", "x")

    def __init__(self, left, right, side):
        self.first = ReduceWeight(left, right, side)
        self.second = SumBlock((self.first.rows, self.first.columns))
        self.inputs, self.outs = self.first.inputs, self.second.outs
        self.scratch = self.first.scratch + self.second.scratch

    def run(self, inputs, outs, scratch, sent):
        n = len(self.first.scratch)
        total = yield from self.first.total(inputs, scratch[:n], sent)
        yield from delayed(self.second.total(total, outs[0], scratch[n:], sent), 15.0)


class Pieces:
    links = ()
    pieces = "in"

    def __init__(self, source, start=0.0):
        self.start = start
        self.inputs = [(source, VM)]
        self.outs = [(SHARD, BF16, VM)]
        self.scratch = sems(8, 8)

    def run(self, inputs, outs, scratch, sent):
        if self.start > 0.0:
            yield self.start
        (source,), (landed,), (send, recv) = inputs, outs, scratch
        co, yh, z = (lax.axis_index(a) for a in ("co", "yh", "z"))
        me, home = yh * 4 + z, yh == co

        def piece(j):
            src = source.at[pl.ds(j * REAL, ROWS), :]
            dst = landed.at[:, pl.ds(pl.multiple_of(me * 128, 128), 128)]
            to = device(yh=co, co=j // 4, z=j % 4)
            there = remote(src, dst, send.at[j], recv.at[me], to)
            return there, pltpu.make_async_copy(src, dst, recv.at[me]), home & (co * 4 + z == j)

        for j in range(8):
            there, here, own = piece(j)

            @pl.when(own)
            def _():
                here.start()

            @pl.when(jnp.logical_not(own))
            def _():
                there.start()

        yield self.start + 9.0
        for q in range(8):
            dst = landed.at[:, pl.ds(q * 128, 128)]
            own = home & (me == q)

            @pl.when(own)
            def _():
                pltpu.make_async_copy(dst, dst, recv.at[q]).wait()

            @pl.when(jnp.logical_not(own))
            def _():
                remote(dst, dst, send.at[q], recv.at[q], Ring("z").to_right).wait_recv()

        for j in range(8):
            there, here, own = piece(j)

            @pl.when(jnp.logical_not(own))
            def _():
                there.wait_send()


class PiecesOut:
    links = ()
    pieces = "out"

    def __init__(self, source):
        self.inputs = [(source, VM)]
        self.outs = [((8, ROWS, 128), BF16, VM)]
        self.scratch = [pltpu.VMEM(SHARD, BF16)] + sems(8, 8)

    def run(self, inputs, outs, scratch, sent):
        scratch[0][...] = inputs[0][...].astype(BF16)
        yield from self.give(scratch[0], outs[0], *scratch[1:])

    @staticmethod
    def give(source, landed, send, recv):
        co, yh, z = (lax.axis_index(a) for a in ("co", "yh", "z"))
        shard, home = co * 4 + z, yh == co

        def piece(q):
            src = source.at[:, pl.ds(q * 128, 128)]
            dst = landed.at[shard]
            to = device(co=yh, yh=q // 4, z=q % 4)
            there = remote(src, dst, send.at[q], recv.at[shard], to)
            return there, pltpu.make_async_copy(src, dst, recv.at[shard]), home & (
                yh * 4 + z == q
            )

        for q in range(8):
            there, here, own = piece(q)

            @pl.when(own)
            def _():
                here.start()

            @pl.when(jnp.logical_not(own))
            def _():
                there.start()

        yield 11.0
        for s in range(8):
            dst = landed.at[s]
            own = home & (shard == s)

            @pl.when(own)
            def _():
                pltpu.make_async_copy(dst, dst, recv.at[s]).wait()

            @pl.when(jnp.logical_not(own))
            def _():
                remote(dst, dst, send.at[s], recv.at[s], Ring("z").to_right).wait_recv()

            there, here, mine = piece(s)

            @pl.when(jnp.logical_not(mine))
            def _():
                there.wait_send()


def greet_pieces(way):
    co, yh, z = (lax.axis_index(a) for a in ("co", "yh", "z"))
    home = yh == co
    for j in range(8):
        if way == "in":
            own, source = home & (yh * 4 + z == j), dict(yh=j // 4, z=j % 4, co=yh)
        else:
            own, source = home & (co * 4 + z == j), dict(yh=co, co=j // 4, z=j % 4)

        @pl.when(jnp.logical_not(own))
        def _():
            signal(device(**source))

    return home


class Spread:
    links = ("z",)

    def __init__(self, shard):
        self.inputs = [(shard, VM)]
        self.outs = [(ALL, BF16, VM)]
        self.scratch = SPREAD_SCRATCH

    def run(self, inputs, outs, scratch, sent):
        outs[0][lax.axis_index("z")] = inputs[0][...]
        yield from shard_spread(WHOLE, outs[0], scratch, sent)


class End:
    links = ("z",)

    def __init__(self, part, x, cot, table, at):
        self.at = at
        self.inputs = [(a, VM) for a in (part, x, cot, table)]
        self.outs = [(SHARD, F32, VM), (SUMS, F32, VM)]
        self.scratch = sum_scratch(WHOLE)

    def run(self, inputs, outs, scratch, sent):
        (part, x, cot, table), (x_out, sums) = inputs, outs
        total = yield from shard_sum(WHOLE, part, scratch, sent)
        bias, scale = (table[r : r + 1, :] for r in self.at)
        branch = total + bias
        x_out[...] = x[...] + scale * branch
        df = (cot[...] * scale).astype(BF16)
        sums[...] = jnp.zeros_like(sums)
        sums[2:3, :] = jnp.sum(cot[...] * branch, axis=0, keepdims=True)
        sums[3:4, :] = jnp.sum(df.astype(F32), axis=0, keepdims=True)


def norm_of(value):
    mean = jnp.mean(value, axis=1, keepdims=True)
    meansq = jnp.mean(value * value, axis=1, keepdims=True)
    rstd = lax.rsqrt(meansq - mean * mean + EPS)
    return (value - mean) * rstd, rstd


def norm_back(grad, value, gain):
    hat, rstd = norm_of(value)
    e = grad * gain
    return (
        rstd
        * (
            e
            - jnp.mean(e, axis=1, keepdims=True)
            - hat * jnp.mean(e * hat, axis=1, keepdims=True)
        ),
        jnp.sum(grad * hat, axis=0, keepdims=True),
        jnp.sum(grad, axis=0, keepdims=True),
    )


GAIN, SHIFT, BRANCH, SCALE = 0, 4, 8, 12
SHARD = (ROWS, WIDTH)
ALL = (4, ROWS, WIDTH)
SUMS = (8, WIDTH)


def call(mains, inputs, outs, scratch, ident, riders=(), links=("z",), pieces=None, entry=None):
    mains = mains if isinstance(mains, list) else [mains]
    inputs = [(a, VM) for a in inputs]
    outs = [(s, d, VM) for s, d in outs]
    jobs = [(inputs, outs, list(scratch))] + [(r.inputs, r.outs, r.scratch) for r in riders]
    links = {link: None for link in links}
    for r in riders:
        links.update({link: None for link in r.links})
        pieces = pieces or getattr(r, "pieces", None)
    runs = [(0, main) for main in mains] + [(i + 1, r.run) for i, r in enumerate(riders)]
    n = len(jobs)
    flat_in = [(i, a, spec is VM) for i, job in enumerate(jobs) for a, spec in job[0]]
    flat_out = [(i, s, d, spec is VM) for i, job in enumerate(jobs) for s, d, spec in job[1]]
    held = [pltpu.VMEM(a.shape, a.dtype) for _, a, inside in flat_in if inside]
    made = [pltpu.VMEM(s, d) for _, s, d, inside in flat_out if inside]

    def kernel(*refs):
        refs = list(refs)
        take = lambda count: [refs.pop(0) for _ in range(count)]
        in_refs, out_refs = take(len(flat_in)), take(len(flat_out))
        own = [take(len(job[2])) for job in jobs]
        held_refs, made_refs = take(len(held)), take(len(made))
        in_sem, out_sem = take(2)
        sent, loads = Sent(), []
        job_in, job_out = [[] for _ in jobs], [[] for _ in jobs]
        for (i, _, inside), ref in zip(flat_in, in_refs):
            if inside:
                there = held_refs[len(loads)]
                loads.append(pltpu.make_async_copy(ref, there, in_sem.at[len(loads)]))
                loads[-1].start()
                ref = there
            job_in[i].append(ref)
        for (i, shape, kind, inside), ref in zip(flat_out, out_refs):
            if inside:
                number = len(sent.results)
                here = made_refs[number]
                copy = pltpu.make_async_copy(here, ref, out_sem.at[number])
                sent.results.append([here, copy, False])
                if shape == ALL and kind == BF16:
                    here[:, REAL:ROWS] = jnp.zeros((4, TAIL, WIDTH), BF16)
                ref = here
            job_out[i].append(ref)
        more = 0 if entry is None else entry()
        greet(links, more, None if pieces is None else greet_pieces(pieces))
        for c in loads:
            c.wait()
        in_turns(
            [(i, run(job_in[i], job_out[i], own[i], sent)) for i, run in runs],
            lambda i: sent.flush(*job_out[i]),
        )
        sent.finish()

    results = pl.pallas_call(
        kernel,
        out_shape=[jax.ShapeDtypeStruct(s, d) for _, s, d, _ in flat_out],
        in_specs=[ANY] * len(flat_in),
        out_specs=[ANY] * len(flat_out),
        scratch_shapes=[s for job in jobs for s in job[2]]
        + held
        + made
        + sems(max(len(held), 1), max(len(made), 1)),
        compiler_params=pltpu.CompilerParams(
            collective_id=ident, has_side_effects=True, vmem_limit_bytes=60 * 2**20
        ),
    )(*[a for _, a, _ in flat_in])
    return results[: len(outs)], results[len(outs) :]


def spread_norm(value, table, at, out, rows):
    hat, _ = norm_of(value)
    gain, shift = (table[r : r + 1, :] for r in at)
    out[lax.axis_index("z"), rows] = (hat * gain + shift).astype(BF16)


def back_through_norm(total, value, dx, branch, table, at, dx_out, sums, d_out, rows):
    gain, scale = (table[r : r + 1, :] for r in at)
    dr, gain_sum, shift_sum = norm_back(total, value[rows], gain)
    dx_new = dx[rows] + dr
    dx_out[rows] = dx_new
    df = (dx_new * scale).astype(BF16)
    d_out[lax.axis_index("z"), rows] = df
    sums[0:1, :] += gain_sum
    sums[1:2, :] += shift_sum
    sums[2:3, :] += jnp.sum(dx_new * branch[rows], axis=0, keepdims=True)
    sums[3:4, :] += jnp.sum(df.astype(F32), axis=0, keepdims=True)


def batch_rows(ref, rows):
    value = ref[:, rows]
    return value.reshape(4 * value.shape[1], WIDTH)


def put_rows(ref, rows, value):
    ref[:, rows] = value.reshape(4, rows.stop - rows.start, WIDTH).astype(ref.dtype)


def back_through_hidden(d_all, u, wup, wdown, du_out, hidden, part, rows, time):
    slope = gelu_slope(batch_rows(u, rows))
    du = (dot_nt(batch_rows(d_all, rows), wdown[...]) * slope).astype(BF16)
    put_rows(du_out, rows, du)
    hidden[0:1, :] += jnp.sum(du.astype(F32), axis=0, keepdims=True)
    yield time
    put_rows(part, rows, dot_nt(batch_rows(du_out, rows), wup[...]))


LAG = 2.0
STARTS = (0.0, 7.5, 17.0, 25.0)


def chain(work, inputs, outs, extra, ident, riders):
    each = 2 * (SUMMING + len(SPREAD_SCRATCH))
    scratch = list(extra)
    for batch in BATCHES:
        scratch += 2 * sum_scratch(batch) + 2 * SPREAD_SCRATCH

    def main_of(number, batch):
        rows = slice(batch[0], batch[0] + batch[2])
        lag = number * LAG

        def main(inputs_, outs_, scratch_, sent):
            more, own = scratch_[: len(extra)], scratch_[len(extra) + number * each :][:each]
            parts = [own[:SUMMING], own[SUMMING : 2 * SUMMING]]
            rest = own[2 * SUMMING :]
            parts += [rest[: len(SPREAD_SCRATCH)], rest[len(SPREAD_SCRATCH) :]]

            def add(i, ref):
                job = shard_sum(batch, ref, parts[i], sent)
                return (yield from delayed(job, lag + STARTS[2 * i]))

            def share(i, ref):
                job = shard_spread(batch, ref, parts[2 + i], sent)
                yield from delayed(job, lag + STARTS[2 * i + 1])

            if number == 0:
                for ref, out in zip(outs_, outs):
                    if out[0] == SUMS:
                        ref[...] = jnp.zeros_like(ref)
            else:
                yield lag
            yield from work(add, share, inputs_, outs_, more, rows, lag, sent)

        return main

    return call(
        [main_of(i, b) for i, b in enumerate(BATCHES)], inputs, outs, scratch, ident, riders
    )


def hidden_forward(n_out, wup, wdown, layer, hb, u, g, part, rows, time):
    value = dot_nn(batch_rows(n_out, rows), wup[...]) + hb[layer : layer + 1, :]
    put_rows(u, rows, value)
    yield time
    put_rows(g, rows, gelu_value(batch_rows(u, rows)).astype(BF16))
    yield time + 0.5
    put_rows(part, rows, dot_nn(batch_rows(g, rows), wdown[...]))
    yield time + 1.0


def branch_forward(total, x, table, at, branch_out, x_out, rows):
    bias, scale = (table[r : r + 1, :] for r in at)
    branch = total + bias
    branch_out[rows] = branch
    value = x[rows] + scale * branch
    x_out[rows] = value
    return value


def forward_chain(part, x, table, wup, hb, board, ident, riders):
    def work(add, share, inputs, outs, more, rows, lag, sent):
        part, x, table, wup, hb = inputs
        a, m, n2, u, g, f, x_new, n1 = outs
        (part2,) = more
        total = yield from add(0, part)
        value = branch_forward(total, x, table, (BRANCH, SCALE), a, m, rows)
        spread_norm(value, table, (GAIN + 1, SHIFT + 1), n2, rows)
        yield from share(0, n2)
        yield from until(board, 1, lag + STARTS[2] - 3.0)
        yield from hidden_forward(
            n2, wup, board[0], 0, hb, u, g, part2, rows, lag + STARTS[2] - 2.0
        )
        if lag > 0:
            sent.flush(a, m, n2, u, g)
        total = yield from add(1, part2)
        value = branch_forward(total, m, table, (BRANCH + 1, SCALE + 1), f, x_new, rows)
        spread_norm(value, table, (GAIN + 2, SHIFT + 2), n1, rows)
        yield from share(1, n1)

    shard, whole = (SHARD, F32), (ALL, BF16)
    return chain(
        work,
        (part, x, table, wup, hb),
        [shard, shard, whole, (ALL, F32), whole, shard, shard, whole],
        [pltpu.VMEM(ALL, BF16)],
        ident,
        riders,
    )


def turn_chain(part, x, cot, d_all, table, wup, hb, board, ident, riders):
    def work(add, share, inputs, outs, more, rows, lag, sent):
        part, x, cot, d_all, table, wup, hb = inputs
        a, m, n2, g, end_part, du, hidden, dm, sums, d_out = outs
        u, part2 = more
        total = yield from add(0, part)
        value = branch_forward(total, x, table, (BRANCH + 2, SCALE + 2), a, m, rows)
        spread_norm(value, table, (GAIN + 3, SHIFT + 3), n2, rows)
        yield from share(0, n2)
        yield from until(board, 1, lag + STARTS[2] - 3.0)
        wdown = board[0]
        yield from hidden_forward(
            n2, wup, wdown, 1, hb, u, g, end_part, rows, lag + STARTS[2] - 2.0
        )
        yield from back_through_hidden(
            d_all, u, wup, wdown, du, hidden, part2, rows, lag + STARTS[2]
        )
        if lag > 0:
            sent.flush(a, m, n2, g, end_part, du, hidden)
        total = yield from add(1, part2)
        back_through_norm(
            total, m, cot, a, table, (GAIN + 3, SCALE + 2), dm, sums, d_out, rows
        )
        yield from share(1, d_out)

    shard, whole, sums = (SHARD, F32), (ALL, BF16), (SUMS, F32)
    return chain(
        work,
        (part, x, cot, d_all, table, wup, hb),
        [shard, shard, whole, whole, whole, whole, sums, shard, sums, whole],
        [pltpu.VMEM(ALL, F32), pltpu.VMEM(ALL, BF16)],
        ident,
        riders,
    )


def backward_chain(part, x, dm, f, m, a, u, g, table, wup, wdown, board, ident, riders):
    def work(add, share, inputs, outs, more, rows, lag, sent):
        part, x, dm, f, m, a, u, g, table, wup, wdown = inputs
        sums1, df, du, hidden, dm_out, sums, d_out = outs
        part2, dx = more
        total = yield from add(0, part)
        back_through_norm(total, x, dm, f, table, (GAIN + 2, SCALE + 1), dx, sums1, df, rows)
        yield from share(0, df)
        if lag > 0:
            board.extend([g, df])
        yield from back_through_hidden(
            df, u, wup, wdown, du, hidden, part2, rows, lag + STARTS[2] - 1.0
        )
        if lag > 0:
            sent.flush(sums1, df, du, hidden)
        total = yield from add(1, part2)
        back_through_norm(
            total, m, dx, a, table, (GAIN + 1, SCALE), dm_out, sums, d_out, rows
        )
        yield from share(1, d_out)

    shard, whole, sums = (SHARD, F32), (ALL, BF16), (SUMS, F32)
    return chain(
        work,
        (part, x, dm, f, m, a, u, g, table, wup, wdown),
        [sums, whole, whole, sums, shard, sums, whole],
        [pltpu.VMEM(ALL, BF16), pltpu.VMEM(SHARD, F32)],
        ident,
        riders,
    )


def first_step(tokens, small, ident, riders):
    pieces = Pieces(tokens)

    def main(inputs, outs, scratch, sent):
        tokens, params, hidden_bias = inputs[0], inputs[1:6], inputs[6]
        x_out, n_out, table, query_bias, up_bias = outs
        landed, pack, pack_out, psend, precv, ksend, krecv = scratch[:7]
        pack[...] = jnp.zeros_like(pack)
        for i, param in enumerate(params):
            for j in range(4):
                pack[4 * i + j : 4 * i + j + 1, :] = param[j // 2, j % 2 : j % 2 + 1, :]
        for j in range(8):
            lanes = slice(j % 4 * 128, j % 4 * 128 + 128)
            pack[20 + j : 21 + j, :] = hidden_bias[j // 4 : j // 4 + 1, lanes]
        z = lax.axis_index("z")
        me = lax.axis_index("yh") * 4 + z
        arrive = pieces.run([tokens], [landed], [psend, precv], sent)
        next(arrive)
        pack_out[me] = pack[...]

        def note(j, slot):
            return remote(
                pack, pack_out.at[slot], ksend.at[j], krecv.at[slot], device(yh=j // 4, z=j % 4)
            )

        for j in range(8):

            @pl.when(me != j)
            def _():
                note(j, me).start()

        yield 8.0
        for _ in arrive:
            pass
        for q in range(8):

            @pl.when(me != q)
            def _():
                note(q, q).wait_recv()

        value = landed[...].astype(F32)
        x_out[...] = value
        for q in range(8):
            table[:, q * 128 : q * 128 + 128] = pack_out[q, 0:16, :]
        spread_norm(value, table, (GAIN, SHIFT), n_out, slice(0, ROWS))
        spread = delayed(shard_spread(WHOLE, n_out, scratch[7:], sent), 10.0)
        time = next(spread)
        query_bias[...] = jnp.zeros_like(query_bias)
        up_bias[...] = jnp.zeros_like(up_bias)
        for half in range(2):
            block = pack_out[z + 4 * half]
            for l in range(LAYERS):
                for k in range(2):
                    lo = half * 384 + k * 256
                    r = 16 + 2 * l + k
                    query_bias[l : l + 1, lo : lo + 128] = block[r : r + 1]
                for k in range(4):
                    lo = half * 512 + k * 128
                    r = 20 + 4 * l + k
                    up_bias[l : l + 1, lo : lo + 128] = block[r : r + 1]
        yield time
        yield from spread
        for j in range(8):

            @pl.when(me != j)
            def _():
                note(j, me).wait_send()

    def entry():
        yh, z = lax.axis_index("yh"), lax.axis_index("z")
        for j in range(8):

            @pl.when(yh * 4 + z != j)
            def _():
                signal(device(yh=j // 4, z=j % 4))

        return 7

    return call(
        main,
        (tokens,) + small,
        [(SHARD, F32), (ALL, BF16), ((16, WIDTH), F32), ((8, 768), F32), ((8, WIDTH), F32)],
        [
            pltpu.VMEM(SHARD, BF16),
            pltpu.VMEM((32, 128), F32),
            pltpu.VMEM((8, 32, 128), F32),
        ]
        + sems(8, 8, 8, 8)
        + SPREAD_SCRATCH,
        ident,
        riders,
        pieces="in",
        entry=entry,
    )


def last_step(part, value, dx, table, vector_sums, qkv_sums, hidden_sums, at, ident, riders):
    def main(inputs, outs, scratch, sent):
        part, value, dx, table = inputs[:4]
        sum_refs = inputs[4 : 4 + len(vector_sums)]
        qkv_refs, hidden_refs = inputs[-4:-2], inputs[-2:]
        landed, small = outs
        ring_scratch, scratch = scratch[:SUMMING], scratch[SUMMING:]
        both, psend, precv, vectors, zgot, zsend, zrecv = scratch[:7]
        owned, ygot, ysend, yrecv, sub, xgot, xsend, xrecv = scratch[7:]
        x_, yl, co, yh, z = (lax.axis_index(a) for a in AXES)
        total = yield from shard_sum(WHOLE, part, ring_scratch, sent)
        (gain,) = (table[r : r + 1, :] for r in at)
        dr, gain_sum, shift_sum = norm_back(total, value[...], gain)
        for ref, (_, norm, branch) in zip(sum_refs, vector_sums):
            for row, kind, i in ((0, GAIN, norm), (1, SHIFT, norm), (2, 12, branch), (3, 8, branch)):
                if i is not None:
                    vectors[kind + i : kind + i + 1, :] = ref[row : row + 1, :]
        vectors[at[0] : at[0] + 1, :] = gain_sum
        vectors[at[0] + SHIFT : at[0] + SHIFT + 1, :] = shift_sum

        def on_z(there, slot, h):
            cut = vectors.at[:, pl.ds((h * 4 + there) * 128, 128)]
            return remote(
                cut, zgot.at[slot, h], zsend.at[there, h], zrecv.at[slot, h], device(z=there)
            )

        def on_y(there, slot):
            to = device(yh=there // 4, yl=(there // 2) % 2, co=there % 2)
            return remote(
                sub.at[there // 4], ygot.at[slot], ysend.at[there], yrecv.at[slot], to
            )

        def on_x(there, slot):
            return remote(owned, xgot.at[slot], xsend.at[there], xrecv.at[slot], device(x=there))

        def others(me, count, do):
            for i in range(count):

                @pl.when(me != i)
                def _():
                    do(i)

        me = yh * 4 + yl * 2 + co

        def both_halves(do):
            def run(i):
                do(i, 0)
                do(i, 1)

            return run

        others(z, 4, both_halves(lambda i, h: on_z(i, z, h).start()))
        both[...] = (dx[...] + dr).astype(BF16)
        give = PiecesOut.give(both, landed, psend, precv)
        next(give)
        for h in range(2):
            zgot[z, h] = vectors[:, pl.ds(pl.multiple_of((h * 4 + z) * 128, 128), 128)]
        yield 13.0
        others(z, 4, both_halves(lambda i, h: on_z(i, i, h).wait_recv()))
        owned[:, 0:16] = zgot[0] + zgot[1] + zgot[2] + zgot[3]
        owned[:, 16:32] = jnp.zeros((2, 16, 128), F32)
        for h in range(2):
            for l in range(LAYERS):
                for k in range(3):
                    lo, r = h * 384 + k * 128, 16 + 3 * l + k
                    owned[h, r : r + 1, :] = qkv_refs[l][0:1, lo : lo + 128]
                for k in range(4):
                    lo, r = h * 512 + k * 128, 22 + 4 * l + k
                    owned[h, r : r + 1, :] = hidden_refs[l][0:1, lo : lo + 128]
        others(x_, 4, lambda i: on_x(i, x_).start())
        xgot[x_] = owned[...]
        yield 16.0
        others(x_, 4, lambda i: on_x(i, i).wait_recv())
        sub[...] = sum(xgot[i] for i in range(4))
        others(me, 8, lambda i: on_y(i, me).start())
        ygot[me] = sub[yh]
        yield 19.0
        others(me, 8, lambda i: on_y(i, i).wait_recv())
        small[...] = sum(ygot[i] for i in range(8))
        others(z, 4, both_halves(lambda i, h: on_z(i, z, h).wait_send()))
        others(me, 8, lambda i: on_y(i, me).wait_send())
        others(x_, 4, lambda i: on_x(i, x_).wait_send())
        for _ in give:
            pass

    def entry():
        x_, yl, co, yh, z = (lax.axis_index(a) for a in AXES)
        me = yh * 4 + yl * 2 + co
        for i in range(8):

            @pl.when(me != i)
            def _():
                signal(device(yh=i // 4, yl=(i // 2) % 2, co=i % 2))

        for i in range(4):

            @pl.when(x_ != i)
            def _():
                signal(device(x=i))

            @pl.when(z != i)
            def _():
                signal(device(z=i))

        return 7 + 3 + 3

    return call(
        main,
        (part, value, dx, table, *[v[0] for v in vector_sums], *qkv_sums, *hidden_sums),
        [((8, ROWS, 128), BF16), ((32, 128), F32)],
        sum_scratch(WHOLE)
        + [
            pltpu.VMEM(SHARD, BF16),
            *sems(8, 8),
            pltpu.VMEM((16, WIDTH), F32),
            pltpu.VMEM((4, 2, 16, 128), F32),
            pltpu.SemaphoreType.DMA((4, 2)),
            pltpu.SemaphoreType.DMA((4, 2)),
            pltpu.VMEM((2, 32, 128), F32),
            pltpu.VMEM((8, 32, 128), F32),
            *sems(8, 8),
            pltpu.VMEM((2, 32, 128), F32),
            pltpu.VMEM((4, 2, 32, 128), F32),
            *sems(4, 4),
        ],
        ident,
        riders,
        pieces="out",
        entry=entry,
    )


def lanes_of(head, shape):
    lane = lax.broadcasted_iota(jnp.int32, shape, 1)
    return (lane < 64, lane == 64) if head % 2 == 0 else (lane >= 64, lane == 0)


def put_head(ref, i, value, one=False):
    inside, extra = lanes_of(i, value.shape)
    ref[i, 0:OWN] = jnp.where(inside, value, jnp.where(extra & one, 1, 0).astype(BF16))
    ref[i, OWN:QROWS] = jnp.zeros((QROWS - OWN, 128), BF16)


def put_keys(ref, i, rows, value, mask):
    inside, extra = lanes_of(i, value.shape)
    ref[i, rows] = jnp.where(inside, value, jnp.where(extra, mask[rows], jnp.zeros_like(value)))


def attend_step(n_all, wqkv, wout, bias, layer, mask, ident, riders=()):
    def main(inputs, outs, scratch, sent):
        n_all, wqkv, wout, bias, mask = inputs
        part, qkv, other, att, lse = outs
        kall, vt, qpad, ot, send, recv = scratch
        to = device(co=1 - lax.axis_index("co"))
        mine, theirs = slice(0, OWN), slice(OWN, KEYS)
        yield 0.1
        normed = n_all[...].reshape(OWN, WIDTH)
        lse[...] = jnp.zeros_like(lse)
        copies = []
        for h in range(2):
            cols = slice(h * 384, h * 384 + 384)
            block = (dot_nn(normed, wqkv[:, cols]) + bias[layer : layer + 1, cols]).astype(BF16)
            qkv[:, cols] = block
            c = remote(
                qkv.at[:, pl.ds(h * 384 + 128, 256)],
                other.at[:, pl.ds(h * 256, 256)],
                send.at[h],
                recv.at[h],
                to,
            )
            c.start()
            copies.append(c)
            for i in (2 * h, 2 * h + 1):
                put_head(qpad, i, block[:, 0:128] * 0.125, True)
                put_keys(kall, i, mine, block[:, 128:256], mask)
            vt[h * 128 : h * 128 + 128, 0:OWN] = block[:, 256:384].T
        sent.extend(copies)
        yield 3.0
        for h in range(2):
            copies[h].wait_recv()
            for i in (2 * h, 2 * h + 1):
                put_keys(kall, i, theirs, other[:, h * 256 : h * 256 + 128], mask)
            vt[h * 128 : h * 128 + 128, OWN:KEYS] = other[:, h * 256 + 128 : h * 256 + 256].T

            for i in (2 * h, 2 * h + 1):
                rows = slice(i * 64, i * 64 + 64)
                for lo, n in CHUNKS:
                    s = dot_nt(kall[i], qpad[i, lo : lo + n])
                    top = jnp.max(s, axis=0, keepdims=True)
                    e = jnp.exp(s - top)
                    total = jnp.sum(e, axis=0, keepdims=True)
                    ot[rows, lo : lo + n] = dot_nn(vt[rows], e.astype(BF16)) * (1.0 / total)
                    lse[i, 0:1, lo : lo + n] = top + jnp.log(total)
                yield 6.0 + 2.0 * i
        sent.flush(qkv, other, lse)
        att[...] = ot[...].T[0:OWN].astype(BF16)
        part[...] = dot_nn(att[...], wout[...]).astype(BF16).reshape(ALL)

    return call(
        main,
        (n_all, wqkv, wout, bias, mask),
        [
            (ALL, BF16),
            ((OWN, 768), BF16),
            ((OWN, 512), BF16),
            ((OWN, 256), BF16),
            ((4, 8, QROWS), F32),
        ],
        [
            pltpu.VMEM((4, KEYS, 128), BF16),
            pltpu.VMEM((256, KEYS), BF16),
            pltpu.VMEM((4, QROWS, 128), BF16),
            pltpu.VMEM((256, QROWS), F32),
        ]
        + sems(2, 2),
        ident,
        riders,
        links=("core",),
    )


def attend_back_step(d_all, wqkv, wout, qkv, other, att, lse, mask, ident, riders=()):
    def main(inputs, outs, scratch, sent):
        d_all, wqkv, wout, qkv, other, att, lse, mask = inputs
        part, dqkv, sums = outs
        kall, vall, kt, qone, qpad, dpad, delta, dqt, dk, dv, away, got, send, recv = scratch
        to = device(co=1 - lax.axis_index("co"))
        mine, theirs = slice(0, OWN), slice(OWN, KEYS)
        yield 0.1
        datt = dot_nt(d_all[...].reshape(OWN, WIDTH), wout[...]).astype(BF16)
        copies = []
        along = (datt.astype(F32) * att[...].astype(F32)).T
        delta[...] = jnp.zeros_like(delta)
        for i in range(4):
            delta[i, 0:1, 0:OWN] = jnp.sum(along[i * 64 : i * 64 + 64], axis=0, keepdims=True)
        for h in range(2):
            base, half = h * 384, h * 256
            own_keys, other_keys = qkv[:, base + 128 : base + 256], other[:, half : half + 128]
            for i in (2 * h, 2 * h + 1):
                query = qkv[:, base : base + 128] * 0.125
                put_head(qone, i, query, True)
                put_head(qpad, i, query)
                put_head(dpad, i, datt[:, h * 128 : h * 128 + 128])
                put_keys(kall, i, mine, own_keys, mask)
                put_keys(kall, i, theirs, other_keys, mask)
            vall[h, 0:OWN] = qkv[:, base + 256 : base + 384]
            vall[h, OWN:KEYS] = other[:, half + 128 : half + 256]
            kt[h * 128 : h * 128 + 128, 0:OWN] = own_keys.T
            kt[h * 128 : h * 128 + 128, OWN:KEYS] = other_keys.T
            dk[h] = jnp.zeros((KEYS, 128), F32)
            dv[h] = jnp.zeros((KEYS, 128), F32)

            for i in (2 * h, 2 * h + 1):
                rows = slice(i * 64, i * 64 + 64)
                for lo, n in CHUNKS:
                    qc, dc = qpad[i, lo : lo + n], dpad[i, lo : lo + n]
                    s = dot_nt(kall[i], qone[i, lo : lo + n])
                    p = jnp.exp(s - lse[i, 0:1, lo : lo + n])
                    dp = dot_nt(vall[h], dc)
                    ds = (p * (dp - delta[i, 0:1, lo : lo + n])).astype(BF16)
                    dv[h] += dot_nn(p.astype(BF16), dc)
                    dk[h] += dot_nn(ds, qc)
                    dqt[rows, lo : lo + n] = dot_nn(kt[rows], ds)
                yield 5.0 + 2.5 * i
            away[h, :, 0:128] = dk[h, OWN:KEYS].astype(BF16)
            away[h, :, 128:256] = dv[h, OWN:KEYS].astype(BF16)
            c = remote(away.at[h], got.at[h], send.at[h], recv.at[h], to)
            c.start()
            copies.append(c)
        sent.extend(copies)
        dq = dqt[...].T[0:OWN] * 0.125
        for h in range(2):
            base = h * 384
            dqkv[:, base : base + 128] = dq[:, h * 128 : h * 128 + 128].astype(BF16)
            copies[h].wait_recv()
            dqkv[:, base + 128 : base + 256] = (
                dk[h, 0:OWN] + got[h, :, 0:128].astype(F32)
            ).astype(BF16)
            dqkv[:, base + 256 : base + 384] = (
                dv[h, 0:OWN] + got[h, :, 128:256].astype(F32)
            ).astype(BF16)
        part[...] = dot_nt(dqkv[...], wqkv[...]).astype(BF16).reshape(ALL)
        sums[...] = jnp.zeros_like(sums)
        sums[0:1, :] = jnp.sum(dqkv[...].astype(F32), axis=0, keepdims=True)

    return call(
        main,
        (d_all, wqkv, wout, qkv, other, att, lse, mask),
        [(ALL, BF16), ((OWN, 768), BF16), ((8, 768), F32)],
        [
            pltpu.VMEM((4, KEYS, 128), BF16),
            pltpu.VMEM((2, KEYS, 128), BF16),
            pltpu.VMEM((256, KEYS), BF16),
            pltpu.VMEM((4, QROWS, 128), BF16),
            pltpu.VMEM((4, QROWS, 128), BF16),
            pltpu.VMEM((4, QROWS, 128), BF16),
            pltpu.VMEM((4, 8, QROWS), F32),
            pltpu.VMEM((256, QROWS), F32),
            pltpu.VMEM((2, KEYS, 128), F32),
            pltpu.VMEM((2, KEYS, 128), F32),
            pltpu.VMEM((2, OWN, 256), BF16),
            pltpu.VMEM((2, OWN, 256), BF16),
        ]
        + sems(2, 2),
        ident,
        riders,
        links=("core",),
    )


def on_device(
    tokens,
    cotangent,
    attend_weight,
    output_weight,
    up_weight,
    down_weight,
    norm_gain,
    norm_shift,
    attend_bias,
    branch_bias,
    layer_scale,
    hidden_bias,
):
    co, yh, z = (lax.axis_index(a) for a in ("co", "yh", "z"))
    attend_weight = attend_weight.reshape(LAYERS, 256, 384)
    first = jnp.pad(tokens, ((0, 15), (0, 0)))
    cot_pieces = jnp.pad(cotangent.astype(BF16), ((0, 15), (0, 0)))
    def attend_of(l, start=0.0):
        return GatherWeight(attend_weight, l, 0, start=start)

    def output_of(l, start=0.0):
        return GatherWeight(output_weight, l, 1, start=start)

    def up_of(l):
        return GatherWeight(up_weight, l, 0)

    def down_of(l, board):
        return GatherWeight(down_weight, l, 1, VM, board)

    weights = [[None] * 4 for _ in range(LAYERS)]
    ident = iter(range(40))
    small = (norm_gain, norm_shift, branch_bias, layer_scale, attend_bias, hidden_bias)
    (x, n_all, table, query_bias, up_bias), (weights[0][0], weights[0][1]) = first_step(
        first, small, next(ident), [attend_of(0), output_of(0)]
    )
    row = jnp.arange(OWN)
    block, inside = row // ROWS, row % ROWS

    def hidden_keys(half):
        real = (inside < REAL) | ((inside == REAL) & (block == 3) & (half == 1))
        return jnp.where(real, 0.0, -1e30).astype(BF16)

    mask = jnp.concatenate([hidden_keys(co), hidden_keys(1 - co)])
    mask = jnp.broadcast_to(mask[:, None], (KEYS, 128))

    last = jnp.where((co == 1) & (z == 3), REAL + 1, REAL)
    real_row = jnp.arange(ROWS)[:, None] < last

    saved = []
    for l in range(LAYERS):
        wqkv, wout = weights[l][:2]
        riders = [up_of(l)]
        if l == 1:
            riders.append(Spread((cot * table[SCALE + 3]).astype(BF16)))
        n1 = n_all
        (part, qkv, other, att, lse), got = attend_step(
            n1, wqkv, wout, query_bias, l, mask, next(ident), riders
        )
        weights[l][2] = got[0]
        if l == 1:
            d_all = d_last = got[1]
        saved.append([x, n1, qkv, other, att, lse])
        board = []
        if l == 0:
            riders = [
                down_of(0, board), Pieces(cot_pieces, 12.0), attend_of(1, 14.0), output_of(1, 14.5)
            ]
            (a, m, n2, u, g, f, x, n_all), got = forward_chain(
                part, x, table, weights[0][2], up_bias, board, next(ident), riders
            )
            weights[0][3], weights[1][:2] = got[0], got[2:]
            cot = jnp.where(real_row, got[1].astype(F32), 0.0)
            saved[0] += [a, m, n2, u, g, f]
        else:
            riders = [down_of(1, board)]
            (a, m, n2, g, end_part, du, hidden, dm, sums, d_all), got = turn_chain(
                part, x, cot, d_all, table, weights[1][2], up_bias, board, next(ident), riders
            )
            weights[1][3] = got[0]

    hidden_sums, qkv_sums, grads = [None, hidden], [None] * LAYERS, [[None] * 4, [None] * 4]

    def summing(block):
        return SumBlock(block.shape, block)

    vector_sums = [(sums, 3, 2)]
    x1, n1, qkv, other, att, lse = saved[1]
    da = d_all
    riders = [
        ReduceWeight(n2, du, 0),
        End(end_part, m, cot, table, (BRANCH + 3, SCALE + 3)),
    ]
    (part, dqkv, qkv_sum), got = attend_back_step(
        d_all, *weights[1][:2], qkv, other, att, lse, mask, next(ident), riders
    )
    up_block, x_end, sums = got
    vector_sums.append((sums, None, 3))
    qkv_sums[1] = qkv_sum
    x, n1_0, qkv, other, att_0, lse, a, m, n2, u, g0, f = saved[0]
    board = []
    late = ReduceWeight(g0, g0, 1, board, 19.0)
    riders = [
        ReduceWeight(n1, dqkv, 0, start=1.0),
        ReduceWeight(att, da, 1, start=4.0),
        ReduceWeight(g, d_last, 1, start=10.0),
        summing(up_block),
        late,
    ]
    (sums1, df, du, hidden, dm, sums, d_all), got = backward_chain(
        part, x1, dm, f, m, a, u, g0, table, *weights[0][2:], board, next(ident), riders
    )
    attend_block, output_block, down_block, grads[1][2], down_block_0 = got
    vector_sums += [(sums1, 2, 1), (sums, 1, 0)]
    hidden_sums[0] = hidden
    riders = [
        ReduceWeight(n2, du, 0),
        summing(attend_block),
        summing(output_block),
        summing(down_block),
        PiecesOut(x_end),
    ]
    (part, dqkv, qkv_sum), got = attend_back_step(
        d_all, *weights[0][:2], qkv, other, att_0, lse, mask, next(ident), riders
    )
    up_block, grads[1][0], grads[1][1], grads[1][3], out_pieces = got
    qkv_sums[0] = qkv_sum
    riders = [
        ReduceSum(n1_0, dqkv, 0),
        ReduceSum(att_0, d_all, 1),
        summing(up_block),
        summing(down_block_0),
    ]
    (grad_pieces, small), grads[0] = last_step(
        part, x, dm, table, vector_sums, qkv_sums, hidden_sums, (GAIN,), next(ident), riders
    )

    bias_grad = small[16:22].reshape(2, 3, 128)[:, 0::2]

    def rows(landed):
        return jnp.concatenate(
            [landed[0:7, 0:REAL].reshape(7 * REAL, 128), landed[7, 0 : REAL + 1]]
        ).astype(F32)

    return (
        rows(out_pieces),
        rows(grad_pieces),
        jnp.stack([grads[l][0] for l in range(LAYERS)]).reshape(LAYERS, 256, 3, 128),
        jnp.stack([grads[l][1] for l in range(LAYERS)]),
        jnp.stack([grads[l][2] for l in range(LAYERS)]),
        jnp.stack([grads[l][3] for l in range(LAYERS)]),
        small[0:4].reshape(2, 2, 128),
        small[4:8].reshape(2, 2, 128),
        bias_grad,
        small[8:12].reshape(2, 2, 128),
        small[12:16].reshape(2, 2, 128),
        small[22:30].reshape(2, 512),
    )


def solution(mesh):
    split = Mesh(mesh.devices.reshape(4, 2, 2, 2, 4), AXES)
    images, row, col = ("x", "yl", "co"), ("yl", "co"), ("yh", "z")
    placed = (
        P(images, col),
        P(images, col),
        P(None, row, None, col),
        P(None, col, row),
        P(None, row, col),
        P(None, col, row),
        P(None, None, col),
        P(None, None, col),
        P(None, None, col),
        P(None, None, col),
        P(None, None, col),
        P(None, col),
    )
    return jax.shard_map(
        on_device, mesh=split, in_specs=placed, out_specs=placed, check_vma=False
    )
```

```python
import jax
import jax.numpy as jnp
from jax import lax
from jax.experimental import pallas as pl
from jax.experimental.pallas import tpu as pltpu
from jax.sharding import Mesh, PartitionSpec as P

WIDTH = 1024
HALF = WIDTH // 2
SEQ = 1025
LAYERS = 2
REAL = 128
ROWS = 144
TAIL = ROWS - REAL
OWN = 4 * ROWS
KEYS = 2 * OWN
QROWS = 640
CHUNKS = ((0, 256), (256, 256), (512, 128))
EPS = 1e-06
ROOT_HALF = 0.7071067811865476
INV_ROOT_TWO_PI = 0.3989422804014327
MESH = pl.DeviceIdType.MESH
AXES = ("x", "yl", "co", "yh", "z")
VM = pl.BlockSpec(memory_space=pltpu.VMEM)
ANY = pl.BlockSpec(memory_space=pl.ANY)
F32 = jnp.float32
BF16 = jnp.bfloat16


def gelu_value(value):
    return 0.5 * value * (1.0 + lax.erf(value * ROOT_HALF))


def gelu_slope(value):
    return 0.5 * (1.0 + lax.erf(value * ROOT_HALF)) + value * INV_ROOT_TWO_PI * jnp.exp(
        -0.5 * value * value
    )


def dot_nt(left, right):
    return lax.dot_general(left, right, (((1,), (1,)), ((), ())), preferred_element_type=F32)


def dot_tn(left, right):
    return lax.dot_general(left, right, (((0,), (0,)), ((), ())), preferred_element_type=F32)


def dot_nn(left, right):
    return jnp.dot(left, right, preferred_element_type=F32)


def device(**moved):
    return tuple(moved[a] if a in moved else lax.axis_index(a) for a in AXES)


def remote(src, dst, send, recv, to):
    return pltpu.make_async_remote_copy(
        src_ref=src, dst_ref=dst, send_sem=send, recv_sem=recv, device_id=to, device_id_type=MESH
    )


def signal(to):
    pl.semaphore_signal(
        pltpu.get_barrier_semaphore(), inc=1, device_id=to, device_id_type=MESH
    )


class Ring:
    def __init__(self, axis):
        self.axis = axis
        if axis == "y":
            self.me = lax.axis_index("yh") * 2 + lax.axis_index("yl")
        else:
            self.me = lax.axis_index(axis)
        self.right = lax.rem(self.me + 1, 4)
        self.left = lax.rem(self.me + 3, 4)
        self.across = lax.rem(self.me + 2, 4)
        self.to_right, self.to_left = self.at(self.right), self.at(self.left)

    def at(self, index):
        if self.axis == "y":
            return device(yh=index // 2, yl=lax.rem(index, 2))
        return device(**{self.axis: index})


def greet(links, more=0, home=None):
    count = more
    for link in links:
        if link == "core":
            signal(device(co=1 - lax.axis_index("co")))
            count += 1
        else:
            ring = Ring(link)
            signal(ring.to_right)
            signal(ring.to_left)
            count += 2
            if link != "y":
                signal(ring.at(ring.across))
                count += 1
    barrier = pltpu.get_barrier_semaphore()
    if home is None:
        pl.semaphore_wait(barrier, count)
    else:

        @pl.when(home)
        def _():
            pl.semaphore_wait(barrier, count + 7)

        @pl.when(jnp.logical_not(home))
        def _():
            pl.semaphore_wait(barrier, count + 8)


def in_turns(jobs, done):
    waiting = [[0.0, i, job, number] for i, (number, job) in enumerate(jobs)]
    while waiting:
        first = min(waiting, key=lambda w: w[:2])
        try:
            first[0] = next(first[2])
        except StopIteration:
            waiting.remove(first)
            if all(w[3] != first[3] for w in waiting):
                done(first[3])


class Sent(list):
    def __init__(self):
        self.results = []

    def flush(self, *refs):
        for ref in refs:
            for result in self.results:
                if result[0] is ref and not result[2]:
                    result[1].start()
                    result[2] = True

    def finish(self):
        for c in self:
            c.wait_send()
        for _, copy, _ in self.results:
            copy.wait()


def until(board, count, time):
    while len(board) < count:
        yield time
        time += 1.0


def paced(job, pace):
    for time in job:
        yield pace * time


def delayed(job, time):
    while True:
        try:
            yield time + next(job)
        except StopIteration as end:
            return end.value


def by_rows(ref, lead, half):
    rows = ref.shape[1] // 2
    return ref.at[lead, pl.ds(half * rows, rows), :]


def reduce_on(ring, half, part, fin, relay, stage, send, recv, sent, first=0):
    def copy(i, src, dst, to):
        c = remote(src, dst, send.at[i], recv.at[i], to)
        c.start()
        sent.append(c)
        return c

    far_r = copy(0, half(part, ring.across, 0), relay.at[0], ring.to_right)
    far_l = copy(1, half(part, ring.across, 1), relay.at[1], ring.to_left)
    near_r = copy(2, half(part, ring.right, 1), half(fin, 0, 1), ring.to_right)
    near_l = copy(3, half(part, ring.left, 0), half(fin, 1, 0), ring.to_left)
    yield 3.0
    far_r.wait_recv()
    stage[0] = (half(part, ring.right, 0)[...].astype(F32) + relay[0].astype(F32)).astype(BF16)
    sum_r = copy(4, stage.at[0], half(fin, 0, 0), ring.to_right)
    far_l.wait_recv()
    stage[1] = (half(part, ring.left, 1)[...].astype(F32) + relay[1].astype(F32)).astype(BF16)
    sum_l = copy(5, stage.at[1], half(fin, 1, 1), ring.to_left)
    yield 7.0
    for c in (near_r, near_l, sum_r, sum_l):
        c.wait_recv()
    own = part.at[ring.me, pl.ds(first, fin.shape[1])][...]
    return own.astype(F32) + fin[0].astype(F32) + fin[1].astype(F32)


def gather_on(ring, slot, own, send, recv, sent, landed=None):
    def copy(i, src, owner, half, to):
        return remote(src, slot(owner, half), send.at[i], recv.at[i], to)

    def go(*what):
        c = copy(*what)
        c.start()
        sent.append(c)

    def lands(i, owner, half):
        copy(i, slot(owner, half), owner, half, ring.to_right).wait_recv()

    go(0, own(0), ring.me, 0, ring.to_right)
    go(1, own(1), ring.me, 1, ring.to_left)
    go(2, own(1), ring.me, 1, ring.to_right)
    go(3, own(0), ring.me, 0, ring.to_left)
    yield 2.5
    lands(0, ring.left, 0)
    go(4, slot(ring.left, 0), ring.left, 0, ring.to_right)
    lands(1, ring.right, 1)
    go(5, slot(ring.right, 1), ring.right, 1, ring.to_left)
    yield 5.0
    lands(2, ring.left, 1)
    if landed is not None:
        landed(ring.left)
    lands(3, ring.right, 0)
    if landed is not None:
        landed(ring.right)
    yield 7.0
    lands(4, ring.across, 0)
    lands(5, ring.across, 1)
    if landed is not None:
        landed(ring.across)


def gather_slots(ring, out, half, send, recv, sent):
    def slot(owner, h):
        return half(out, owner, h)

    yield from gather_on(ring, slot, lambda h: slot(ring.me, h), send, recv, sent)


def sems(*counts):
    return [pltpu.SemaphoreType.DMA((c,)) for c in counts]


def tail_roles():
    z, second = lax.axis_index("z"), lax.axis_index("co") == 1
    return z, second & (z == 3), second & (z != 3)


WHOLE, BATCHES = (0, REAL, ROWS), ((0, REAL // 2, REAL // 2), (REAL // 2, REAL // 2, ROWS - REAL // 2))


def shard_sum(batch, part, scratch, sent):
    first, count, rows = batch
    fin, relay, stage, tails, tail, send, recv, tsend, trecv = scratch
    z, holds, gives = tail_roles()
    ends = first + rows == ROWS

    def half(ref, lead, h):
        lo = first if ref.shape[1] == ROWS else 0
        return ref.at[lead, pl.ds(lo, count), pl.ds(h * HALF, HALF)]

    def tail_to(slot):
        src = part.at[3, pl.ds(REAL, TAIL), :]
        return remote(src, tails.at[slot], tsend.at[0], trecv.at[slot], device(z=3))

    if ends:

        @pl.when(gives)
        def _():
            tail_to(z).start()

    total = yield from reduce_on(
        Ring("z"), half, part, fin, relay, stage, send, recv, sent, first
    )
    if not ends:
        return total
    tail[...] = jnp.zeros_like(tail)

    @pl.when(holds)
    def _():
        for i in range(3):
            tail_to(i).wait_recv()
        tail[...] = part[3, REAL:ROWS].astype(F32) + sum(tails[i].astype(F32) for i in range(3))

    @pl.when(gives)
    def _():
        tail_to(z).wait_send()

    return jnp.concatenate([total, tail[...]], axis=0)


def shard_spread(batch, out, scratch, sent):
    first, count, rows = batch
    send, recv, tsend, trecv = scratch
    z, holds, gives = tail_roles()
    ends = first + rows == ROWS

    def half(ref, lead, h):
        return ref.at[lead, pl.ds(first, count), pl.ds(h * HALF, HALF)]

    def tail_to(i):
        ref = out.at[3, pl.ds(REAL, TAIL), :]
        return remote(ref, ref, tsend.at[i], trecv.at[0], device(z=i))

    if ends:

        @pl.when(holds)
        def _():
            for i in range(3):
                tail_to(i).start()

    yield from gather_slots(Ring("z"), out, half, send, recv, sent)
    if ends:

        @pl.when(gives)
        def _():
            tail_to(0).wait_recv()

        @pl.when(holds)
        def _():
            for i in range(3):
                tail_to(i).wait_send()


def sum_scratch(batch):
    count = batch[1]
    return [
        pltpu.VMEM((2, count, WIDTH), BF16),
        pltpu.VMEM((2, count, HALF), BF16),
        pltpu.VMEM((2, count, HALF), BF16),
        pltpu.VMEM((3, TAIL, WIDTH), BF16),
        pltpu.VMEM((TAIL, WIDTH), F32),
    ] + sems(6, 6, 1, 3)


SPREAD_SCRATCH = sems(6, 6, 3, 1)
SUMMING = len(sum_scratch(WHOLE))


class GatherWeight:
    links = ("y", "core")

    def __init__(self, shards, layer, side, spec=ANY, board=None, start=0.0):
        rows, columns = shards.shape[1:]
        self.board, self.start = board, start
        self.layer, self.side, self.rows, self.columns = layer, side, rows, columns
        full = (4 * rows, 2 * columns) if side == 0 else (2 * rows, 4 * columns)
        self.inputs = [(shards, ANY)]
        self.outs = [(full, BF16, spec)]
        self.scratch = sems(6, 6, 4, 4, 1)

    def run(self, inputs, outs, scratch, sent):
        if self.start > 0.0:
            yield self.start
        yield from delayed(self.go(inputs, outs, scratch, sent), self.start)

    def go(self, inputs, outs, scratch, sent):
        (shards,), (out,) = inputs, outs
        send, recv, csend, crecv, local = scratch
        own = shards.at[self.layer]
        ring, co = Ring("y"), lax.axis_index("co")
        rows, columns = self.rows, self.columns

        def block(y, core, half=None):
            yh, r = y // 2, lax.rem(y, 2) * 2 + core
            down, along = (r, yh) if self.side == 0 else (yh, r)
            first, count = down * rows, rows
            if half is not None:
                count = rows // 2
                first = first + half * count
            return out.at[
                pl.ds(pl.multiple_of(first, 16), count),
                pl.ds(pl.multiple_of(along * columns, 128), columns),
            ]

        def to_core(i, src, y):
            c = remote(src, block(y, co), csend.at[i], crecv.at[i], device(co=1 - co))
            c.start()
            sent.append(c)

        keep = pltpu.make_async_copy(own, block(ring.me, co), local.at[0])
        keep.start()
        to_core(0, own, ring.me)
        numbers = iter((1, 2, 3))
        yield from gather_on(
            ring,
            lambda y, half: block(y, co, half),
            lambda half: own.at[pl.ds(half * (rows // 2), rows // 2), :],
            send,
            recv,
            sent,
            lambda y: to_core(next(numbers), block(y, co), y),
        )
        keep.wait()
        yield 12.0
        for i, y in enumerate((ring.me, ring.left, ring.right, ring.across)):
            there = block(y, 1 - co)
            remote(there, there, csend.at[i], crecv.at[i], device(co=1 - co)).wait_recv()
        if self.board is not None:
            self.board.append(out)


class ReduceWeight:
    links = ("y", "core")

    def __init__(self, left, right, side, board=None, start=0.0):
        self.board, self.start = board, start
        rows, columns = left.shape[-1], right.shape[-1]
        self.full = rows, columns
        rows, columns = (rows // 4, columns // 2) if side == 0 else (rows // 2, columns // 4)
        self.side, self.rows, self.columns = side, rows, columns
        self.inputs = [] if board is not None else [(left, VM), (right, VM)]
        self.outs = [((rows, columns), BF16, VM)]
        self.scratch = [
            pltpu.VMEM(self.full, BF16),
            pltpu.VMEM((4, rows, columns), BF16),
            pltpu.VMEM((4, rows, columns), BF16),
            pltpu.VMEM((2, rows, columns), BF16),
            pltpu.VMEM((2, rows // 2, columns), BF16),
            pltpu.VMEM((2, rows // 2, columns), BF16),
        ] + sems(4, 4, 6, 6)

    def run(self, inputs, outs, scratch, sent):
        total = yield from self.total(inputs, scratch, sent)
        outs[0][...] = total.astype(BF16)

    def total(self, inputs, scratch, sent):
        if self.board is not None:
            yield from until(self.board, 2, self.start)
            inputs = self.board
        elif self.start > 0.0:
            yield self.start
        left, right = inputs
        part, got, pair, fin, relay, stage, csend, crecv, send, recv = scratch

        def columns_of(ref, first):
            if len(ref.shape) == 2:
                return ref[:, first : first + 256]
            return ref[:, :, first : first + 256].reshape(OWN, 256)

        whole = right[...] if len(right.shape) == 2 else right[...].reshape(OWN, self.full[1])
        for first in range(0, self.full[0], 256):
            part[first : first + 256] = dot_tn(columns_of(left, first), whole).astype(BF16)
            if self.start > 0.0:
                yield self.start + first / 512
        co = lax.axis_index("co")
        rows, columns = self.rows, self.columns

        def block(y, core):
            yh, r = y // 2, (y % 2) * 2 + core
            down, along = (r, yh) if self.side == 0 else (yh, r)
            return part.at[
                pl.ds(pl.multiple_of(down * rows, 16), rows),
                pl.ds(pl.multiple_of(along * columns, 128), columns),
            ]

        copies = []
        for y in range(4):
            c = remote(
                block(y, 1 - co), got.at[y], csend.at[y], crecv.at[y], device(co=1 - co)
            )
            c.start()
            copies.append(c)
        sent.extend(copies)
        yield self.start + 5.0
        for y in range(4):
            copies[y].wait_recv()
            pair[y] = (block(y, co)[...].astype(F32) + got[y].astype(F32)).astype(BF16)
        job = reduce_on(Ring("y"), by_rows, pair, fin, relay, stage, send, recv, sent)
        return (yield from delayed(job, self.start + 6.0))


class SumBlock:
    links = ("x",)

    def __init__(self, shape, block=None):
        rows, columns = shape
        self.shape, self.rows = shape, rows // 4
        self.inputs = [] if block is None else [(block, VM)]
        self.outs = [(shape, F32, VM)]
        quarters = (4, rows // 4, columns)
        self.scratch = [pltpu.VMEM(quarters, BF16) for _ in range(3)] + sems(4, 4, 4, 4)

    def run(self, inputs, outs, scratch, sent):
        yield from self.total(inputs[0][...], outs[0], scratch, sent)

    def total(self, value, out, scratch, sent):
        part, got, every, send, recv, gsend, grecv = scratch
        ring = Ring("x")
        others = (ring.across, ring.right, ring.left)
        for i in range(4):
            part[i] = value[i * self.rows : (i + 1) * self.rows].astype(BF16)

        def give(slot, to):
            return remote(part.at[to], got.at[slot], send.at[to], recv.at[slot], ring.at(to))

        def share(slot, to):
            return remote(
                every.at[slot], every.at[slot], gsend.at[to], grecv.at[slot], ring.at(to)
            )

        for i in others:
            c = give(ring.me, i)
            c.start()
            sent.append(c)
        got[ring.me] = part[ring.me]
        yield 4.0
        for i in others:
            give(i, i).wait_recv()
        every[ring.me] = sum(got[i].astype(F32) for i in range(4)).astype(BF16)
        for i in others:
            c = share(ring.me, i)
            c.start()
            sent.append(c)
        yield 8.0
        for i in others:
            share(i, i).wait_recv()
        for i in range(4):
            out[i * self.rows : (i + 1) * self.rows] = every[i].astype(F32)


class ReduceSum:
    links = ("y", "core", "x")

    def __init__(self, left, right, side):
        self.first = ReduceWeight(left, right, side)
        self.second = SumBlock((self.first.rows, self.first.columns))
        self.inputs, self.outs = self.first.inputs, self.second.outs
        self.scratch = self.first.scratch + self.second.scratch

    def run(self, inputs, outs, scratch, sent):
        n = len(self.first.scratch)
        total = yield from self.first.total(inputs, scratch[:n], sent)
        yield from delayed(self.second.total(total, outs[0], scratch[n:], sent), 15.0)


class Pieces:
    links = ()
    pieces = "in"

    def __init__(self, source, start=0.0):
        self.start = start
        self.inputs = [(source, VM)]
        self.outs = [(SHARD, BF16, VM)]
        self.scratch = sems(8, 8)

    def run(self, inputs, outs, scratch, sent):
        if self.start > 0.0:
            yield self.start
        (source,), (landed,), (send, recv) = inputs, outs, scratch
        co, yh, z = (lax.axis_index(a) for a in ("co", "yh", "z"))
        me, home = yh * 4 + z, yh == co

        def piece(j):
            src = source.at[pl.ds(j * REAL, ROWS), :]
            dst = landed.at[:, pl.ds(pl.multiple_of(me * 128, 128), 128)]
            to = device(yh=co, co=j // 4, z=j % 4)
            there = remote(src, dst, send.at[j], recv.at[me], to)
            return there, pltpu.make_async_copy(src, dst, recv.at[me]), home & (co * 4 + z == j)

        for j in range(8):
            there, here, own = piece(j)

            @pl.when(own)
            def _():
                here.start()

            @pl.when(jnp.logical_not(own))
            def _():
                there.start()

        yield self.start + 9.0
        for q in range(8):
            dst = landed.at[:, pl.ds(q * 128, 128)]
            own = home & (me == q)

            @pl.when(own)
            def _():
                pltpu.make_async_copy(dst, dst, recv.at[q]).wait()

            @pl.when(jnp.logical_not(own))
            def _():
                remote(dst, dst, send.at[q], recv.at[q], Ring("z").to_right).wait_recv()

        for j in range(8):
            there, here, own = piece(j)

            @pl.when(jnp.logical_not(own))
            def _():
                there.wait_send()


class PiecesOut:
    links = ()
    pieces = "out"

    def __init__(self, source):
        self.inputs = [(source, VM)]
        self.outs = [((8, ROWS, 128), BF16, VM)]
        self.scratch = [pltpu.VMEM(SHARD, BF16)] + sems(8, 8)

    def run(self, inputs, outs, scratch, sent):
        scratch[0][...] = inputs[0][...].astype(BF16)
        yield from self.give(scratch[0], outs[0], *scratch[1:])

    @staticmethod
    def give(source, landed, send, recv):
        co, yh, z = (lax.axis_index(a) for a in ("co", "yh", "z"))
        shard, home = co * 4 + z, yh == co

        def piece(q):
            src = source.at[:, pl.ds(q * 128, 128)]
            dst = landed.at[shard]
            to = device(co=yh, yh=q // 4, z=q % 4)
            there = remote(src, dst, send.at[q], recv.at[shard], to)
            return there, pltpu.make_async_copy(src, dst, recv.at[shard]), home & (
                yh * 4 + z == q
            )

        for q in range(8):
            there, here, own = piece(q)

            @pl.when(own)
            def _():
                here.start()

            @pl.when(jnp.logical_not(own))
            def _():
                there.start()

        yield 11.0
        for s in range(8):
            dst = landed.at[s]
            own = home & (shard == s)

            @pl.when(own)
            def _():
                pltpu.make_async_copy(dst, dst, recv.at[s]).wait()

            @pl.when(jnp.logical_not(own))
            def _():
                remote(dst, dst, send.at[s], recv.at[s], Ring("z").to_right).wait_recv()

            there, here, mine = piece(s)

            @pl.when(jnp.logical_not(mine))
            def _():
                there.wait_send()


def greet_pieces(way):
    co, yh, z = (lax.axis_index(a) for a in ("co", "yh", "z"))
    home = yh == co
    for j in range(8):
        if way == "in":
            own, source = home & (yh * 4 + z == j), dict(yh=j // 4, z=j % 4, co=yh)
        else:
            own, source = home & (co * 4 + z == j), dict(yh=co, co=j // 4, z=j % 4)

        @pl.when(jnp.logical_not(own))
        def _():
            signal(device(**source))

    return home


class Spread:
    links = ("z",)

    def __init__(self, shard):
        self.inputs = [(shard, VM)]
        self.outs = [(ALL, BF16, VM)]
        self.scratch = SPREAD_SCRATCH

    def run(self, inputs, outs, scratch, sent):
        outs[0][lax.axis_index("z")] = inputs[0][...]
        yield from shard_spread(WHOLE, outs[0], scratch, sent)


class End:
    links = ("z",)

    def __init__(self, part, x, cot, table, at):
        self.at = at
        self.inputs = [(a, VM) for a in (part, x, cot, table)]
        self.outs = [(SHARD, F32, VM), (SUMS, F32, VM)]
        self.scratch = sum_scratch(WHOLE)

    def run(self, inputs, outs, scratch, sent):
        (part, x, cot, table), (x_out, sums) = inputs, outs
        total = yield from shard_sum(WHOLE, part, scratch, sent)
        bias, scale = (table[r : r + 1, :] for r in self.at)
        branch = total + bias
        x_out[...] = x[...] + scale * branch
        df = (cot[...] * scale).astype(BF16)
        sums[...] = jnp.zeros_like(sums)
        sums[2:3, :] = jnp.sum(cot[...] * branch, axis=0, keepdims=True)
        sums[3:4, :] = jnp.sum(df.astype(F32), axis=0, keepdims=True)


def norm_of(value):
    mean = jnp.mean(value, axis=1, keepdims=True)
    meansq = jnp.mean(value * value, axis=1, keepdims=True)
    rstd = lax.rsqrt(meansq - mean * mean + EPS)
    return (value - mean) * rstd, rstd


def norm_back(grad, value, gain):
    hat, rstd = norm_of(value)
    e = grad * gain
    return (
        rstd
        * (
            e
            - jnp.mean(e, axis=1, keepdims=True)
            - hat * jnp.mean(e * hat, axis=1, keepdims=True)
        ),
        jnp.sum(grad * hat, axis=0, keepdims=True),
        jnp.sum(grad, axis=0, keepdims=True),
    )


GAIN, SHIFT, BRANCH, SCALE = 0, 4, 8, 12
SHARD = (ROWS, WIDTH)
ALL = (4, ROWS, WIDTH)
SUMS = (8, WIDTH)


def call(mains, inputs, outs, scratch, ident, riders=(), links=("z",), pieces=None, entry=None, pace=1.0):
    mains = mains if isinstance(mains, list) else [mains]
    inputs = [(a, VM) for a in inputs]
    outs = [(s, d, VM) for s, d in outs]
    jobs = [(inputs, outs, list(scratch))] + [(r.inputs, r.outs, r.scratch) for r in riders]
    links = {link: None for link in links}
    for r in riders:
        links.update({link: None for link in r.links})
        pieces = pieces or getattr(r, "pieces", None)
    runs = [(0, main) for main in mains] + [(i + 1, r.run) for i, r in enumerate(riders)]
    n = len(jobs)
    flat_in = [(i, a, spec is VM) for i, job in enumerate(jobs) for a, spec in job[0]]
    flat_out = [(i, s, d, spec is VM) for i, job in enumerate(jobs) for s, d, spec in job[1]]
    held = [pltpu.VMEM(a.shape, a.dtype) for _, a, inside in flat_in if inside]
    made = [pltpu.VMEM(s, d) for _, s, d, inside in flat_out if inside]

    def kernel(*refs):
        refs = list(refs)
        take = lambda count: [refs.pop(0) for _ in range(count)]
        in_refs, out_refs = take(len(flat_in)), take(len(flat_out))
        own = [take(len(job[2])) for job in jobs]
        held_refs, made_refs = take(len(held)), take(len(made))
        in_sem, out_sem = take(2)
        sent, loads = Sent(), []
        job_in, job_out = [[] for _ in jobs], [[] for _ in jobs]
        for (i, _, inside), ref in zip(flat_in, in_refs):
            if inside:
                there = held_refs[len(loads)]
                loads.append(pltpu.make_async_copy(ref, there, in_sem.at[len(loads)]))
                loads[-1].start()
                ref = there
            job_in[i].append(ref)
        for (i, shape, kind, inside), ref in zip(flat_out, out_refs):
            if inside:
                number = len(sent.results)
                here = made_refs[number]
                copy = pltpu.make_async_copy(here, ref, out_sem.at[number])
                sent.results.append([here, copy, False])
                if shape == ALL and kind == BF16:
                    here[:, REAL:ROWS] = jnp.zeros((4, TAIL, WIDTH), BF16)
                ref = here
            job_out[i].append(ref)
        more = 0 if entry is None else entry()
        greet(links, more, None if pieces is None else greet_pieces(pieces))
        for c in loads:
            c.wait()
        in_turns(
            [
                (i, paced(run(job_in[i], job_out[i], own[i], sent), pace if i > 0 else 1.0))
                for i, run in runs
            ],
            lambda i: sent.flush(*job_out[i]),
        )
        sent.finish()

    results = pl.pallas_call(
        kernel,
        out_shape=[jax.ShapeDtypeStruct(s, d) for _, s, d, _ in flat_out],
        in_specs=[ANY] * len(flat_in),
        out_specs=[ANY] * len(flat_out),
        scratch_shapes=[s for job in jobs for s in job[2]]
        + held
        + made
        + sems(max(len(held), 1), max(len(made), 1)),
        compiler_params=pltpu.CompilerParams(
            collective_id=ident, has_side_effects=True, vmem_limit_bytes=60 * 2**20
        ),
    )(*[a for _, a, _ in flat_in])
    return results[: len(outs)], results[len(outs) :]


def spread_norm(value, table, at, out, rows):
    hat, _ = norm_of(value)
    gain, shift = (table[r : r + 1, :] for r in at)
    out[lax.axis_index("z"), rows] = (hat * gain + shift).astype(BF16)


def back_through_norm(total, value, dx, branch, table, at, dx_out, sums, d_out, rows):
    gain, scale = (table[r : r + 1, :] for r in at)
    dr, gain_sum, shift_sum = norm_back(total, value[rows], gain)
    dx_new = dx[rows] + dr
    dx_out[rows] = dx_new
    df = (dx_new * scale).astype(BF16)
    d_out[lax.axis_index("z"), rows] = df
    sums[0:1, :] += gain_sum
    sums[1:2, :] += shift_sum
    sums[2:3, :] += jnp.sum(dx_new * branch[rows], axis=0, keepdims=True)
    sums[3:4, :] += jnp.sum(df.astype(F32), axis=0, keepdims=True)


def batch_rows(ref, rows):
    value = ref[:, rows]
    return value.reshape(4 * value.shape[1], WIDTH)


def put_rows(ref, rows, value):
    ref[:, rows] = value.reshape(4, rows.stop - rows.start, WIDTH).astype(ref.dtype)


def back_through_hidden(d_all, u, wup, wdown, du_out, hidden, part, rows, time):
    slope = gelu_slope(batch_rows(u, rows))
    du = (dot_nt(batch_rows(d_all, rows), wdown[...]) * slope).astype(BF16)
    put_rows(du_out, rows, du)
    hidden[0:1, :] += jnp.sum(du.astype(F32), axis=0, keepdims=True)
    yield time
    put_rows(part, rows, dot_nt(batch_rows(du_out, rows), wup[...]))


LAG = 2.0
STARTS = (0.0, 7.5, 17.0, 25.0)


def chain(work, inputs, outs, extra, ident, riders):
    each = 2 * (SUMMING + len(SPREAD_SCRATCH))
    scratch = list(extra)
    for batch in BATCHES:
        scratch += 2 * sum_scratch(batch) + 2 * SPREAD_SCRATCH

    def main_of(number, batch):
        rows = slice(batch[0], batch[0] + batch[2])
        lag = number * LAG

        def main(inputs_, outs_, scratch_, sent):
            more, own = scratch_[: len(extra)], scratch_[len(extra) + number * each :][:each]
            parts = [own[:SUMMING], own[SUMMING : 2 * SUMMING]]
            rest = own[2 * SUMMING :]
            parts += [rest[: len(SPREAD_SCRATCH)], rest[len(SPREAD_SCRATCH) :]]

            def add(i, ref):
                job = shard_sum(batch, ref, parts[i], sent)
                return (yield from delayed(job, lag + STARTS[2 * i]))

            def share(i, ref):
                job = shard_spread(batch, ref, parts[2 + i], sent)
                yield from delayed(job, lag + STARTS[2 * i + 1])

            if number == 0:
                for ref, out in zip(outs_, outs):
                    if out[0] == SUMS:
                        ref[...] = jnp.zeros_like(ref)
            else:
                yield lag
            yield from work(add, share, inputs_, outs_, more, rows, lag, sent)

        return main

    return call(
        [main_of(i, b) for i, b in enumerate(BATCHES)], inputs, outs, scratch, ident, riders
    )


def hidden_forward(n_out, wup, wdown, layer, hb, u, g, part, rows, time):
    value = dot_nn(batch_rows(n_out, rows), wup[...]) + hb[layer : layer + 1, :]
    put_rows(u, rows, value)
    yield time
    put_rows(g, rows, gelu_value(batch_rows(u, rows)).astype(BF16))
    yield time + 0.5
    put_rows(part, rows, dot_nn(batch_rows(g, rows), wdown[...]))
    yield time + 1.0


def branch_forward(total, x, table, at, branch_out, x_out, rows):
    bias, scale = (table[r : r + 1, :] for r in at)
    branch = total + bias
    branch_out[rows] = branch
    value = x[rows] + scale * branch
    x_out[rows] = value
    return value


def forward_chain(part, x, table, wup, hb, board, ident, riders):
    def work(add, share, inputs, outs, more, rows, lag, sent):
        part, x, table, wup, hb = inputs
        a, m, n2, u, g, f, x_new, n1 = outs
        (part2,) = more
        total = yield from add(0, part)
        value = branch_forward(total, x, table, (BRANCH, SCALE), a, m, rows)
        spread_norm(value, table, (GAIN + 1, SHIFT + 1), n2, rows)
        yield from share(0, n2)
        yield from until(board, 1, lag + STARTS[2] - 3.0)
        yield from hidden_forward(
            n2, wup, board[0], 0, hb, u, g, part2, rows, lag + STARTS[2] - 2.0
        )
        if lag > 0:
            sent.flush(a, m, n2, u, g)
        total = yield from add(1, part2)
        value = branch_forward(total, m, table, (BRANCH + 1, SCALE + 1), f, x_new, rows)
        spread_norm(value, table, (GAIN + 2, SHIFT + 2), n1, rows)
        yield from share(1, n1)

    shard, whole = (SHARD, F32), (ALL, BF16)
    return chain(
        work,
        (part, x, table, wup, hb),
        [shard, shard, whole, (ALL, F32), whole, shard, shard, whole],
        [pltpu.VMEM(ALL, BF16)],
        ident,
        riders,
    )


def turn_chain(part, x, cot, d_all, table, wup, hb, board, late_up, late_down, ident, riders):
    def work(add, share, inputs, outs, more, rows, lag, sent):
        part, x, cot, d_all, table, wup, hb = inputs
        a, m, n2, g, end_part, du, hidden, dm, sums, d_out = outs
        u, part2 = more
        total = yield from add(0, part)
        value = branch_forward(total, x, table, (BRANCH + 2, SCALE + 2), a, m, rows)
        spread_norm(value, table, (GAIN + 3, SHIFT + 3), n2, rows)
        yield from share(0, n2)
        yield from until(board, 1, lag + STARTS[2] - 3.0)
        wdown = board[0]
        yield from hidden_forward(
            n2, wup, wdown, 1, hb, u, g, end_part, rows, lag + STARTS[2] - 2.0
        )
        yield from back_through_hidden(
            d_all, u, wup, wdown, du, hidden, part2, rows, lag + STARTS[2]
        )
        if lag > 0:
            sent.flush(a, m, n2, g, end_part, du, hidden)
            late_up.extend([n2, du])
            late_down.extend([g, d_all])
        total = yield from add(1, part2)
        back_through_norm(
            total, m, cot, a, table, (GAIN + 3, SCALE + 2), dm, sums, d_out, rows
        )
        yield from share(1, d_out)

    shard, whole, sums = (SHARD, F32), (ALL, BF16), (SUMS, F32)
    return chain(
        work,
        (part, x, cot, d_all, table, wup, hb),
        [shard, shard, whole, whole, whole, whole, sums, shard, sums, whole],
        [pltpu.VMEM(ALL, F32), pltpu.VMEM(ALL, BF16)],
        ident,
        riders,
    )


def backward_chain(
    part, x, dm, f, m, a, n2, u, g, table, wup, wdown, late_down, late_up, ident, riders
):
    def work(add, share, inputs, outs, more, rows, lag, sent):
        part, x, dm, f, m, a, n2, u, g, table, wup, wdown = inputs
        sums1, df, du, hidden, dm_out, sums, d_out = outs
        part2, dx = more
        total = yield from add(0, part)
        back_through_norm(total, x, dm, f, table, (GAIN + 2, SCALE + 1), dx, sums1, df, rows)
        yield from share(0, df)
        if lag > 0:
            late_down.extend([g, df])
        yield from back_through_hidden(
            df, u, wup, wdown, du, hidden, part2, rows, lag + STARTS[2] - 1.0
        )
        if lag > 0:
            sent.flush(sums1, df, du, hidden)
            late_up.extend([n2, du])
        total = yield from add(1, part2)
        back_through_norm(
            total, m, dx, a, table, (GAIN + 1, SCALE), dm_out, sums, d_out, rows
        )
        yield from share(1, d_out)

    shard, whole, sums = (SHARD, F32), (ALL, BF16), (SUMS, F32)
    return chain(
        work,
        (part, x, dm, f, m, a, n2, u, g, table, wup, wdown),
        [sums, whole, whole, sums, shard, sums, whole],
        [pltpu.VMEM(ALL, BF16), pltpu.VMEM(SHARD, F32)],
        ident,
        riders,
    )


def first_step(tokens, small, ident, riders):
    pieces = Pieces(tokens)

    def main(inputs, outs, scratch, sent):
        tokens, params, hidden_bias = inputs[0], inputs[1:6], inputs[6]
        x_out, n_out, table, query_bias, up_bias = outs
        landed, pack, pack_out, psend, precv, ksend, krecv = scratch[:7]
        pack[...] = jnp.zeros_like(pack)
        for i, param in enumerate(params):
            for j in range(4):
                pack[4 * i + j : 4 * i + j + 1, :] = param[j // 2, j % 2 : j % 2 + 1, :]
        for j in range(8):
            lanes = slice(j % 4 * 128, j % 4 * 128 + 128)
            pack[20 + j : 21 + j, :] = hidden_bias[j // 4 : j // 4 + 1, lanes]
        z = lax.axis_index("z")
        me = lax.axis_index("yh") * 4 + z
        arrive = pieces.run([tokens], [landed], [psend, precv], sent)
        next(arrive)
        pack_out[me] = pack[...]

        def note(j, slot):
            return remote(
                pack, pack_out.at[slot], ksend.at[j], krecv.at[slot], device(yh=j // 4, z=j % 4)
            )

        for j in range(8):

            @pl.when(me != j)
            def _():
                note(j, me).start()

        yield 8.0
        for _ in arrive:
            pass
        for q in range(8):

            @pl.when(me != q)
            def _():
                note(q, q).wait_recv()

        value = landed[...].astype(F32)
        x_out[...] = value
        for q in range(8):
            table[:, q * 128 : q * 128 + 128] = pack_out[q, 0:16, :]
        spread_norm(value, table, (GAIN, SHIFT), n_out, slice(0, ROWS))
        spread = delayed(shard_spread(WHOLE, n_out, scratch[7:], sent), 10.0)
        time = next(spread)
        query_bias[...] = jnp.zeros_like(query_bias)
        up_bias[...] = jnp.zeros_like(up_bias)
        for half in range(2):
            block = pack_out[z + 4 * half]
            for l in range(LAYERS):
                for k in range(2):
                    lo = half * 384 + k * 256
                    r = 16 + 2 * l + k
                    query_bias[l : l + 1, lo : lo + 128] = block[r : r + 1]
                for k in range(4):
                    lo = half * 512 + k * 128
                    r = 20 + 4 * l + k
                    up_bias[l : l + 1, lo : lo + 128] = block[r : r + 1]
        yield time
        yield from spread
        for j in range(8):

            @pl.when(me != j)
            def _():
                note(j, me).wait_send()

    def entry():
        yh, z = lax.axis_index("yh"), lax.axis_index("z")
        for j in range(8):

            @pl.when(yh * 4 + z != j)
            def _():
                signal(device(yh=j // 4, z=j % 4))

        return 7

    return call(
        main,
        (tokens,) + small,
        [(SHARD, F32), (ALL, BF16), ((16, WIDTH), F32), ((8, 768), F32), ((8, WIDTH), F32)],
        [
            pltpu.VMEM(SHARD, BF16),
            pltpu.VMEM((32, 128), F32),
            pltpu.VMEM((8, 32, 128), F32),
        ]
        + sems(8, 8, 8, 8)
        + SPREAD_SCRATCH,
        ident,
        riders,
        pieces="in",
        entry=entry,
    )


def last_step(part, value, dx, table, vector_sums, qkv_sums, hidden_sums, at, ident, riders):
    def main(inputs, outs, scratch, sent):
        part, value, dx, table = inputs[:4]
        sum_refs = inputs[4 : 4 + len(vector_sums)]
        qkv_refs, hidden_refs = inputs[-4:-2], inputs[-2:]
        landed, small = outs
        ring_scratch, scratch = scratch[:SUMMING], scratch[SUMMING:]
        both, psend, precv, vectors, zgot, zsend, zrecv = scratch[:7]
        owned, ygot, ysend, yrecv, sub, xgot, xsend, xrecv = scratch[7:]
        x_, yl, co, yh, z = (lax.axis_index(a) for a in AXES)
        total = yield from shard_sum(WHOLE, part, ring_scratch, sent)
        (gain,) = (table[r : r + 1, :] for r in at)
        dr, gain_sum, shift_sum = norm_back(total, value[...], gain)
        for ref, (_, norm, branch) in zip(sum_refs, vector_sums):
            for row, kind, i in ((0, GAIN, norm), (1, SHIFT, norm), (2, 12, branch), (3, 8, branch)):
                if i is not None:
                    vectors[kind + i : kind + i + 1, :] = ref[row : row + 1, :]
        vectors[at[0] : at[0] + 1, :] = gain_sum
        vectors[at[0] + SHIFT : at[0] + SHIFT + 1, :] = shift_sum

        def on_z(there, slot, h):
            cut = vectors.at[:, pl.ds((h * 4 + there) * 128, 128)]
            return remote(
                cut, zgot.at[slot, h], zsend.at[there, h], zrecv.at[slot, h], device(z=there)
            )

        def on_y(there, slot):
            to = device(yh=there // 4, yl=(there // 2) % 2, co=there % 2)
            return remote(
                sub.at[there // 4], ygot.at[slot], ysend.at[there], yrecv.at[slot], to
            )

        def on_x(there, slot):
            return remote(owned, xgot.at[slot], xsend.at[there], xrecv.at[slot], device(x=there))

        def others(me, count, do):
            for i in range(count):

                @pl.when(me != i)
                def _():
                    do(i)

        me = yh * 4 + yl * 2 + co

        def both_halves(do):
            def run(i):
                do(i, 0)
                do(i, 1)

            return run

        others(z, 4, both_halves(lambda i, h: on_z(i, z, h).start()))
        both[...] = (dx[...] + dr).astype(BF16)
        give = PiecesOut.give(both, landed, psend, precv)
        next(give)
        for h in range(2):
            zgot[z, h] = vectors[:, pl.ds(pl.multiple_of((h * 4 + z) * 128, 128), 128)]
        yield 13.0
        others(z, 4, both_halves(lambda i, h: on_z(i, i, h).wait_recv()))
        owned[:, 0:16] = zgot[0] + zgot[1] + zgot[2] + zgot[3]
        owned[:, 16:32] = jnp.zeros((2, 16, 128), F32)
        for h in range(2):
            for l in range(LAYERS):
                for k in range(3):
                    lo, r = h * 384 + k * 128, 16 + 3 * l + k
                    owned[h, r : r + 1, :] = qkv_refs[l][0:1, lo : lo + 128]
                for k in range(4):
                    lo, r = h * 512 + k * 128, 22 + 4 * l + k
                    owned[h, r : r + 1, :] = hidden_refs[l][0:1, lo : lo + 128]
        others(x_, 4, lambda i: on_x(i, x_).start())
        xgot[x_] = owned[...]
        yield 16.0
        others(x_, 4, lambda i: on_x(i, i).wait_recv())
        sub[...] = sum(xgot[i] for i in range(4))
        others(me, 8, lambda i: on_y(i, me).start())
        ygot[me] = sub[yh]
        yield 19.0
        others(me, 8, lambda i: on_y(i, i).wait_recv())
        small[...] = sum(ygot[i] for i in range(8))
        others(z, 4, both_halves(lambda i, h: on_z(i, z, h).wait_send()))
        others(me, 8, lambda i: on_y(i, me).wait_send())
        others(x_, 4, lambda i: on_x(i, x_).wait_send())
        for _ in give:
            pass

    def entry():
        x_, yl, co, yh, z = (lax.axis_index(a) for a in AXES)
        me = yh * 4 + yl * 2 + co
        for i in range(8):

            @pl.when(me != i)
            def _():
                signal(device(yh=i // 4, yl=(i // 2) % 2, co=i % 2))

        for i in range(4):

            @pl.when(x_ != i)
            def _():
                signal(device(x=i))

            @pl.when(z != i)
            def _():
                signal(device(z=i))

        return 7 + 3 + 3

    return call(
        main,
        (part, value, dx, table, *[v[0] for v in vector_sums], *qkv_sums, *hidden_sums),
        [((8, ROWS, 128), BF16), ((32, 128), F32)],
        sum_scratch(WHOLE)
        + [
            pltpu.VMEM(SHARD, BF16),
            *sems(8, 8),
            pltpu.VMEM((16, WIDTH), F32),
            pltpu.VMEM((4, 2, 16, 128), F32),
            pltpu.SemaphoreType.DMA((4, 2)),
            pltpu.SemaphoreType.DMA((4, 2)),
            pltpu.VMEM((2, 32, 128), F32),
            pltpu.VMEM((8, 32, 128), F32),
            *sems(8, 8),
            pltpu.VMEM((2, 32, 128), F32),
            pltpu.VMEM((4, 2, 32, 128), F32),
            *sems(4, 4),
        ],
        ident,
        riders,
        pieces="out",
        entry=entry,
    )


def lanes_of(head, shape):
    lane = lax.broadcasted_iota(jnp.int32, shape, 1)
    return (lane < 64, lane == 64) if head % 2 == 0 else (lane >= 64, lane == 0)


def put_head(ref, i, value, one=False):
    inside, extra = lanes_of(i, value.shape)
    ref[i, 0:OWN] = jnp.where(inside, value, jnp.where(extra & one, 1, 0).astype(BF16))
    ref[i, OWN:QROWS] = jnp.zeros((QROWS - OWN, 128), BF16)


def put_keys(ref, i, rows, value, mask):
    inside, extra = lanes_of(i, value.shape)
    ref[i, rows] = jnp.where(inside, value, jnp.where(extra, mask[rows], jnp.zeros_like(value)))


def attend_step(n_all, wqkv, wout, bias, layer, mask, ident, riders=()):
    def main(inputs, outs, scratch, sent):
        n_all, wqkv, wout, bias, mask = inputs
        part, qkv, other, att, lse = outs
        kall, vt, qpad, ot, send, recv = scratch
        to = device(co=1 - lax.axis_index("co"))
        mine, theirs = slice(0, OWN), slice(OWN, KEYS)
        yield 0.1
        normed = n_all[...].reshape(OWN, WIDTH)
        lse[...] = jnp.zeros_like(lse)
        copies = []
        for h in range(2):
            cols = slice(h * 384, h * 384 + 384)
            block = (dot_nn(normed, wqkv[:, cols]) + bias[layer : layer + 1, cols]).astype(BF16)
            qkv[:, cols] = block
            c = remote(
                qkv.at[:, pl.ds(h * 384 + 128, 256)],
                other.at[:, pl.ds(h * 256, 256)],
                send.at[h],
                recv.at[h],
                to,
            )
            c.start()
            copies.append(c)
            for i in (2 * h, 2 * h + 1):
                put_head(qpad, i, block[:, 0:128] * 0.125, True)
                put_keys(kall, i, mine, block[:, 128:256], mask)
            vt[h * 128 : h * 128 + 128, 0:OWN] = block[:, 256:384].T
        sent.extend(copies)
        yield 3.0
        for h in range(2):
            copies[h].wait_recv()
            for i in (2 * h, 2 * h + 1):
                put_keys(kall, i, theirs, other[:, h * 256 : h * 256 + 128], mask)
            vt[h * 128 : h * 128 + 128, OWN:KEYS] = other[:, h * 256 + 128 : h * 256 + 256].T

            for i in (2 * h, 2 * h + 1):
                rows = slice(i * 64, i * 64 + 64)
                for lo, n in CHUNKS:
                    s = dot_nt(kall[i], qpad[i, lo : lo + n])
                    top = jnp.max(s, axis=0, keepdims=True)
                    e = jnp.exp(s - top)
                    total = jnp.sum(e, axis=0, keepdims=True)
                    ot[rows, lo : lo + n] = dot_nn(vt[rows], e.astype(BF16)) * (1.0 / total)
                    lse[i, 0:1, lo : lo + n] = top + jnp.log(total)
                yield 6.0 + 2.0 * i
        sent.flush(qkv, other, lse)
        att[...] = ot[...].T[0:OWN].astype(BF16)
        part[...] = dot_nn(att[...], wout[...]).astype(BF16).reshape(ALL)

    return call(
        main,
        (n_all, wqkv, wout, bias, mask),
        [
            (ALL, BF16),
            ((OWN, 768), BF16),
            ((OWN, 512), BF16),
            ((OWN, 256), BF16),
            ((4, 8, QROWS), F32),
        ],
        [
            pltpu.VMEM((4, KEYS, 128), BF16),
            pltpu.VMEM((256, KEYS), BF16),
            pltpu.VMEM((4, QROWS, 128), BF16),
            pltpu.VMEM((256, QROWS), F32),
        ]
        + sems(2, 2),
        ident,
        riders,
        links=("core",),
        pace=1.6,
    )


def attend_back_step(d_all, wqkv, wout, qkv, other, att, lse, mask, ident, riders=()):
    def main(inputs, outs, scratch, sent):
        d_all, wqkv, wout, qkv, other, att, lse, mask = inputs
        part, dqkv, sums = outs
        kall, vall, kt, qone, qpad, dpad, delta, dqt, dk, dv, away, got, send, recv = scratch
        to = device(co=1 - lax.axis_index("co"))
        mine, theirs = slice(0, OWN), slice(OWN, KEYS)
        yield 0.1
        datt = dot_nt(d_all[...].reshape(OWN, WIDTH), wout[...]).astype(BF16)
        copies = []
        along = (datt.astype(F32) * att[...].astype(F32)).T
        delta[...] = jnp.zeros_like(delta)
        for i in range(4):
            delta[i, 0:1, 0:OWN] = jnp.sum(along[i * 64 : i * 64 + 64], axis=0, keepdims=True)
        for h in range(2):
            base, half = h * 384, h * 256
            own_keys, other_keys = qkv[:, base + 128 : base + 256], other[:, half : half + 128]
            for i in (2 * h, 2 * h + 1):
                query = qkv[:, base : base + 128] * 0.125
                put_head(qone, i, query, True)
                put_head(qpad, i, query)
                put_head(dpad, i, datt[:, h * 128 : h * 128 + 128])
                put_keys(kall, i, mine, own_keys, mask)
                put_keys(kall, i, theirs, other_keys, mask)
            vall[h, 0:OWN] = qkv[:, base + 256 : base + 384]
            vall[h, OWN:KEYS] = other[:, half + 128 : half + 256]
            kt[h * 128 : h * 128 + 128, 0:OWN] = own_keys.T
            kt[h * 128 : h * 128 + 128, OWN:KEYS] = other_keys.T
            dk[h] = jnp.zeros((KEYS, 128), F32)
            dv[h] = jnp.zeros((KEYS, 128), F32)

            for i in (2 * h, 2 * h + 1):
                rows = slice(i * 64, i * 64 + 64)
                for lo, n in CHUNKS:
                    qc, dc = qpad[i, lo : lo + n], dpad[i, lo : lo + n]
                    s = dot_nt(kall[i], qone[i, lo : lo + n])
                    p = jnp.exp(s - lse[i, 0:1, lo : lo + n])
                    dp = dot_nt(vall[h], dc)
                    ds = (p * (dp - delta[i, 0:1, lo : lo + n])).astype(BF16)
                    dv[h] += dot_nn(p.astype(BF16), dc)
                    dk[h] += dot_nn(ds, qc)
                    dqt[rows, lo : lo + n] = dot_nn(kt[rows], ds)
                yield 5.0 + 2.5 * i
            away[h, :, 0:128] = dk[h, OWN:KEYS].astype(BF16)
            away[h, :, 128:256] = dv[h, OWN:KEYS].astype(BF16)
            c = remote(away.at[h], got.at[h], send.at[h], recv.at[h], to)
            c.start()
            copies.append(c)
        sent.extend(copies)
        dq = dqt[...].T[0:OWN] * 0.125
        for h in range(2):
            base = h * 384
            dqkv[:, base : base + 128] = dq[:, h * 128 : h * 128 + 128].astype(BF16)
            copies[h].wait_recv()
            dqkv[:, base + 128 : base + 256] = (
                dk[h, 0:OWN] + got[h, :, 0:128].astype(F32)
            ).astype(BF16)
            dqkv[:, base + 256 : base + 384] = (
                dv[h, 0:OWN] + got[h, :, 128:256].astype(F32)
            ).astype(BF16)
        part[...] = dot_nt(dqkv[...], wqkv[...]).astype(BF16).reshape(ALL)
        sums[...] = jnp.zeros_like(sums)
        sums[0:1, :] = jnp.sum(dqkv[...].astype(F32), axis=0, keepdims=True)

    return call(
        main,
        (d_all, wqkv, wout, qkv, other, att, lse, mask),
        [(ALL, BF16), ((OWN, 768), BF16), ((8, 768), F32)],
        [
            pltpu.VMEM((4, KEYS, 128), BF16),
            pltpu.VMEM((2, KEYS, 128), BF16),
            pltpu.VMEM((256, KEYS), BF16),
            pltpu.VMEM((4, QROWS, 128), BF16),
            pltpu.VMEM((4, QROWS, 128), BF16),
            pltpu.VMEM((4, QROWS, 128), BF16),
            pltpu.VMEM((4, 8, QROWS), F32),
            pltpu.VMEM((256, QROWS), F32),
            pltpu.VMEM((2, KEYS, 128), F32),
            pltpu.VMEM((2, KEYS, 128), F32),
            pltpu.VMEM((2, OWN, 256), BF16),
            pltpu.VMEM((2, OWN, 256), BF16),
        ]
        + sems(2, 2),
        ident,
        riders,
        links=("core",),
        pace=1.6,
    )


def on_device(
    tokens,
    cotangent,
    attend_weight,
    output_weight,
    up_weight,
    down_weight,
    norm_gain,
    norm_shift,
    attend_bias,
    branch_bias,
    layer_scale,
    hidden_bias,
):
    co, yh, z = (lax.axis_index(a) for a in ("co", "yh", "z"))
    attend_weight = attend_weight.reshape(LAYERS, 256, 384)
    first = jnp.pad(tokens, ((0, 15), (0, 0)))
    cot_pieces = jnp.pad(cotangent.astype(BF16), ((0, 15), (0, 0)))
    def attend_of(l, start=0.0):
        return GatherWeight(attend_weight, l, 0, start=start)

    def output_of(l, start=0.0):
        return GatherWeight(output_weight, l, 1, start=start)

    def up_of(l):
        return GatherWeight(up_weight, l, 0)

    def down_of(l, board):
        return GatherWeight(down_weight, l, 1, VM, board)

    weights = [[None] * 4 for _ in range(LAYERS)]
    ident = iter(range(40))
    small = (norm_gain, norm_shift, branch_bias, layer_scale, attend_bias, hidden_bias)
    (x, n_all, table, query_bias, up_bias), (weights[0][0], weights[0][1]) = first_step(
        first, small, next(ident), [attend_of(0), output_of(0)]
    )
    row = jnp.arange(OWN)
    block, inside = row // ROWS, row % ROWS

    def hidden_keys(half):
        real = (inside < REAL) | ((inside == REAL) & (block == 3) & (half == 1))
        return jnp.where(real, 0.0, -1e30).astype(BF16)

    mask = jnp.concatenate([hidden_keys(co), hidden_keys(1 - co)])
    mask = jnp.broadcast_to(mask[:, None], (KEYS, 128))

    last = jnp.where((co == 1) & (z == 3), REAL + 1, REAL)
    real_row = jnp.arange(ROWS)[:, None] < last

    saved = []
    for l in range(LAYERS):
        wqkv, wout = weights[l][:2]
        riders = [up_of(l)]
        if l == 1:
            riders.append(Spread((cot * table[SCALE + 3]).astype(BF16)))
        n1 = n_all
        (part, qkv, other, att, lse), got = attend_step(
            n1, wqkv, wout, query_bias, l, mask, next(ident), riders
        )
        weights[l][2] = got[0]
        if l == 1:
            d_all = d_last = got[1]
        saved.append([x, n1, qkv, other, att, lse])
        board = []
        if l == 0:
            riders = [
                down_of(0, board), Pieces(cot_pieces, 12.0), attend_of(1, 14.0), output_of(1, 14.5)
            ]
            (a, m, n2, u, g, f, x, n_all), got = forward_chain(
                part, x, table, weights[0][2], up_bias, board, next(ident), riders
            )
            weights[0][3], weights[1][:2] = got[0], got[2:]
            cot = jnp.where(real_row, got[1].astype(F32), 0.0)
            saved[0] += [a, m, n2, u, g, f]
        else:
            late_up, late_down = [], []
            like = n_all
            riders = [
                down_of(1, board),
                ReduceWeight(like, like, 0, late_up, 20.0),
                ReduceWeight(like, like, 1, late_down, 24.0),
            ]
            (a, m, n2, g, end_part, du, hidden, dm, sums, d_all), got = turn_chain(
                part,
                x,
                cot,
                d_all,
                table,
                weights[1][2],
                up_bias,
                board,
                late_up,
                late_down,
                next(ident),
                riders,
            )
            weights[1][3], up_block, down_block = got

    hidden_sums, qkv_sums, grads = [None, hidden], [None] * LAYERS, [[None] * 4, [None] * 4]

    def summing(block):
        return SumBlock(block.shape, block)

    vector_sums = [(sums, 3, 2)]
    x1, n1, qkv, other, att, lse = saved[1]
    da = d_all
    riders = [
        End(end_part, m, cot, table, (BRANCH + 3, SCALE + 3)),
        summing(up_block),
        summing(down_block),
    ]
    (part, dqkv, qkv_sum), got = attend_back_step(
        d_all, *weights[1][:2], qkv, other, att, lse, mask, next(ident), riders
    )
    x_end, sums, grads[1][2], grads[1][3] = got
    vector_sums.append((sums, None, 3))
    qkv_sums[1] = qkv_sum
    x, n1_0, qkv, other, att_0, lse, a, m, n2, u, g0, f = saved[0]
    late_down, late_up = [], []
    riders = [
        ReduceWeight(n1, dqkv, 0, start=1.0),
        ReduceWeight(att, da, 1, start=4.0),
        ReduceWeight(like, like, 1, late_down, 17.0),
        ReduceWeight(like, like, 0, late_up, 22.0),
    ]
    (sums1, df, du, hidden, dm, sums, d_all), got = backward_chain(
        part,
        x1,
        dm,
        f,
        m,
        a,
        n2,
        u,
        g0,
        table,
        *weights[0][2:],
        late_down,
        late_up,
        next(ident),
        riders,
    )
    attend_block, output_block, down_block, up_block = got
    vector_sums += [(sums1, 2, 1), (sums, 1, 0)]
    hidden_sums[0] = hidden
    riders = [
        PiecesOut(x_end),
        ReduceWeight(att_0, d_all, 1),
        summing(attend_block),
        summing(output_block),
        summing(down_block),
    ]
    (part, dqkv, qkv_sum), got = attend_back_step(
        d_all, *weights[0][:2], qkv, other, att_0, lse, mask, next(ident), riders
    )
    out_pieces, output_block, grads[1][0], grads[1][1], grads[0][3] = got
    qkv_sums[0] = qkv_sum
    riders = [
        ReduceSum(n1_0, dqkv, 0),
        summing(output_block),
        summing(up_block),
    ]
    (grad_pieces, small), grads[0][:3] = last_step(
        part, x, dm, table, vector_sums, qkv_sums, hidden_sums, (GAIN,), next(ident), riders
    )

    bias_grad = small[16:22].reshape(2, 3, 128)[:, 0::2]

    def rows(landed):
        return jnp.concatenate(
            [landed[0:7, 0:REAL].reshape(7 * REAL, 128), landed[7, 0 : REAL + 1]]
        ).astype(F32)

    return (
        rows(out_pieces),
        rows(grad_pieces),
        jnp.stack([grads[l][0] for l in range(LAYERS)]).reshape(LAYERS, 256, 3, 128),
        jnp.stack([grads[l][1] for l in range(LAYERS)]),
        jnp.stack([grads[l][2] for l in range(LAYERS)]),
        jnp.stack([grads[l][3] for l in range(LAYERS)]),
        small[0:4].reshape(2, 2, 128),
        small[4:8].reshape(2, 2, 128),
        bias_grad,
        small[8:12].reshape(2, 2, 128),
        small[12:16].reshape(2, 2, 128),
        small[22:30].reshape(2, 512),
    )


def solution(mesh):
    split = Mesh(mesh.devices.reshape(4, 2, 2, 2, 4), AXES)
    images, row, col = ("x", "yl", "co"), ("yl", "co"), ("yh", "z")
    placed = (
        P(images, col),
        P(images, col),
        P(None, row, None, col),
        P(None, col, row),
        P(None, row, col),
        P(None, col, row),
        P(None, None, col),
        P(None, None, col),
        P(None, None, col),
        P(None, None, col),
        P(None, None, col),
        P(None, col),
    )
    return jax.shard_map(
        on_device, mesh=split, in_specs=placed, out_specs=placed, check_vma=False
    )
```

```python
import jax
import jax.numpy as jnp
from jax import lax
from jax.experimental import pallas as pl
from jax.experimental.pallas import tpu as pltpu
from jax.sharding import Mesh, PartitionSpec as P

WIDTH = 1024
HALF = WIDTH // 2
SEQ = 1025
LAYERS = 2
REAL = 128
ROWS = 144
TAIL = ROWS - REAL
OWN = 4 * ROWS
KEYS = 2 * OWN
QROWS = 640
CHUNKS = ((0, 256), (256, 256), (512, 128))
EPS = 1e-06
ROOT_HALF = 0.7071067811865476
INV_ROOT_TWO_PI = 0.3989422804014327
MESH = pl.DeviceIdType.MESH
AXES = ("x", "yl", "co", "yh", "z")
VM = pl.BlockSpec(memory_space=pltpu.VMEM)
ANY = pl.BlockSpec(memory_space=pl.ANY)
F32 = jnp.float32
BF16 = jnp.bfloat16


def gelu_value(value):
    return 0.5 * value * (1.0 + lax.erf(value * ROOT_HALF))


def gelu_slope(value):
    return 0.5 * (1.0 + lax.erf(value * ROOT_HALF)) + value * INV_ROOT_TWO_PI * jnp.exp(
        -0.5 * value * value
    )


def dot_nt(left, right):
    return lax.dot_general(left, right, (((1,), (1,)), ((), ())), preferred_element_type=F32)


def dot_tn(left, right):
    return lax.dot_general(left, right, (((0,), (0,)), ((), ())), preferred_element_type=F32)


def dot_nn(left, right):
    return jnp.dot(left, right, preferred_element_type=F32)


def device(**moved):
    return tuple(moved[a] if a in moved else lax.axis_index(a) for a in AXES)


def remote(src, dst, send, recv, to):
    return pltpu.make_async_remote_copy(
        src_ref=src, dst_ref=dst, send_sem=send, recv_sem=recv, device_id=to, device_id_type=MESH
    )


def signal(to):
    pl.semaphore_signal(
        pltpu.get_barrier_semaphore(), inc=1, device_id=to, device_id_type=MESH
    )


class Ring:
    def __init__(self, axis):
        self.axis = axis
        if axis == "y":
            self.me = lax.axis_index("yh") * 2 + lax.axis_index("yl")
        else:
            self.me = lax.axis_index(axis)
        self.right = lax.rem(self.me + 1, 4)
        self.left = lax.rem(self.me + 3, 4)
        self.across = lax.rem(self.me + 2, 4)
        self.to_right, self.to_left = self.at(self.right), self.at(self.left)

    def at(self, index):
        if self.axis == "y":
            return device(yh=index // 2, yl=lax.rem(index, 2))
        return device(**{self.axis: index})


def greet(links, more=0, home=None):
    count = more
    for link in links:
        if link == "core":
            signal(device(co=1 - lax.axis_index("co")))
            count += 1
        else:
            ring = Ring(link)
            signal(ring.to_right)
            signal(ring.to_left)
            count += 2
            if link != "y":
                signal(ring.at(ring.across))
                count += 1
    barrier = pltpu.get_barrier_semaphore()
    if home is None:
        pl.semaphore_wait(barrier, count)
    else:

        @pl.when(home)
        def _():
            pl.semaphore_wait(barrier, count + 7)

        @pl.when(jnp.logical_not(home))
        def _():
            pl.semaphore_wait(barrier, count + 8)


def in_turns(jobs, done):
    waiting = [[0.0, i, job, number] for i, (number, job) in enumerate(jobs)]
    while waiting:
        first = min(waiting, key=lambda w: w[:2])
        try:
            first[0] = next(first[2])
        except StopIteration:
            waiting.remove(first)
            if all(w[3] != first[3] for w in waiting):
                done(first[3])


class Sent(list):
    def __init__(self):
        self.results = []

    def flush(self, *refs):
        for ref in refs:
            for result in self.results:
                if result[0] is ref and not result[2]:
                    result[1].start()
                    result[2] = True

    def finish(self):
        for c in self:
            c.wait_send()
        for _, copy, _ in self.results:
            copy.wait()


def until(board, count, time):
    while len(board) < count:
        yield time
        time += 1.0


def paced(job, pace):
    for time in job:
        yield pace * time


def delayed(job, time):
    while True:
        try:
            yield time + next(job)
        except StopIteration as end:
            return end.value


def by_rows(ref, lead, half):
    rows = ref.shape[1] // 2
    return ref.at[lead, pl.ds(half * rows, rows), :]


def reduce_on(ring, half, part, fin, relay, stage, send, recv, sent, first=0):
    def copy(i, src, dst, to):
        c = remote(src, dst, send.at[i], recv.at[i], to)
        c.start()
        sent.append(c)
        return c

    far_r = copy(0, half(part, ring.across, 0), relay.at[0], ring.to_right)
    far_l = copy(1, half(part, ring.across, 1), relay.at[1], ring.to_left)
    near_r = copy(2, half(part, ring.right, 1), half(fin, 0, 1), ring.to_right)
    near_l = copy(3, half(part, ring.left, 0), half(fin, 1, 0), ring.to_left)
    yield 3.0
    far_r.wait_recv()
    stage[0] = (half(part, ring.right, 0)[...].astype(F32) + relay[0].astype(F32)).astype(BF16)
    sum_r = copy(4, stage.at[0], half(fin, 0, 0), ring.to_right)
    far_l.wait_recv()
    stage[1] = (half(part, ring.left, 1)[...].astype(F32) + relay[1].astype(F32)).astype(BF16)
    sum_l = copy(5, stage.at[1], half(fin, 1, 1), ring.to_left)
    yield 7.0
    for c in (near_r, near_l, sum_r, sum_l):
        c.wait_recv()
    own = part.at[ring.me, pl.ds(first, fin.shape[1])][...]
    return own.astype(F32) + fin[0].astype(F32) + fin[1].astype(F32)


def gather_on(ring, slot, own, send, recv, sent, landed=None):
    def copy(i, src, owner, half, to):
        return remote(src, slot(owner, half), send.at[i], recv.at[i], to)

    def go(*what):
        c = copy(*what)
        c.start()
        sent.append(c)

    def lands(i, owner, half):
        copy(i, slot(owner, half), owner, half, ring.to_right).wait_recv()

    go(0, own(0), ring.me, 0, ring.to_right)
    go(1, own(1), ring.me, 1, ring.to_left)
    go(2, own(1), ring.me, 1, ring.to_right)
    go(3, own(0), ring.me, 0, ring.to_left)
    yield 2.5
    lands(0, ring.left, 0)
    go(4, slot(ring.left, 0), ring.left, 0, ring.to_right)
    lands(1, ring.right, 1)
    go(5, slot(ring.right, 1), ring.right, 1, ring.to_left)
    yield 5.0
    lands(2, ring.left, 1)
    if landed is not None:
        landed(ring.left)
    lands(3, ring.right, 0)
    if landed is not None:
        landed(ring.right)
    yield 7.0
    lands(4, ring.across, 0)
    lands(5, ring.across, 1)
    if landed is not None:
        landed(ring.across)


def gather_slots(ring, out, half, send, recv, sent):
    def slot(owner, h):
        return half(out, owner, h)

    yield from gather_on(ring, slot, lambda h: slot(ring.me, h), send, recv, sent)


def sems(*counts):
    return [pltpu.SemaphoreType.DMA((c,)) for c in counts]


def tail_roles():
    z, second = lax.axis_index("z"), lax.axis_index("co") == 1
    return z, second & (z == 3), second & (z != 3)


WHOLE, BATCHES = (0, REAL, ROWS), ((0, REAL // 2, REAL // 2), (REAL // 2, REAL // 2, ROWS - REAL // 2))


def shard_sum(batch, part, scratch, sent):
    first, count, rows = batch
    fin, relay, stage, tails, tail, send, recv, tsend, trecv = scratch
    z, holds, gives = tail_roles()
    ends = first + rows == ROWS

    def half(ref, lead, h):
        lo = first if ref.shape[1] == ROWS else 0
        return ref.at[lead, pl.ds(lo, count), pl.ds(h * HALF, HALF)]

    def tail_to(slot):
        src = part.at[3, pl.ds(REAL, TAIL), :]
        return remote(src, tails.at[slot], tsend.at[0], trecv.at[slot], device(z=3))

    if ends:

        @pl.when(gives)
        def _():
            tail_to(z).start()

    total = yield from reduce_on(
        Ring("z"), half, part, fin, relay, stage, send, recv, sent, first
    )
    if not ends:
        return total
    tail[...] = jnp.zeros_like(tail)

    @pl.when(holds)
    def _():
        for i in range(3):
            tail_to(i).wait_recv()
        tail[...] = part[3, REAL:ROWS].astype(F32) + sum(tails[i].astype(F32) for i in range(3))

    @pl.when(gives)
    def _():
        tail_to(z).wait_send()

    return jnp.concatenate([total, tail[...]], axis=0)


def shard_spread(batch, out, scratch, sent):
    first, count, rows = batch
    send, recv, tsend, trecv = scratch
    z, holds, gives = tail_roles()
    ends = first + rows == ROWS

    def half(ref, lead, h):
        return ref.at[lead, pl.ds(first, count), pl.ds(h * HALF, HALF)]

    def tail_to(i):
        ref = out.at[3, pl.ds(REAL, TAIL), :]
        return remote(ref, ref, tsend.at[i], trecv.at[0], device(z=i))

    if ends:

        @pl.when(holds)
        def _():
            for i in range(3):
                tail_to(i).start()

    yield from gather_slots(Ring("z"), out, half, send, recv, sent)
    if ends:

        @pl.when(gives)
        def _():
            tail_to(0).wait_recv()

        @pl.when(holds)
        def _():
            for i in range(3):
                tail_to(i).wait_send()


def sum_scratch(batch):
    count = batch[1]
    return [
        pltpu.VMEM((2, count, WIDTH), BF16),
        pltpu.VMEM((2, count, HALF), BF16),
        pltpu.VMEM((2, count, HALF), BF16),
        pltpu.VMEM((3, TAIL, WIDTH), BF16),
        pltpu.VMEM((TAIL, WIDTH), F32),
    ] + sems(6, 6, 1, 3)


SPREAD_SCRATCH = sems(6, 6, 3, 1)
SUMMING = len(sum_scratch(WHOLE))


class GatherWeight:
    links = ("y", "core")

    def __init__(self, shards, layer, side, spec=ANY, board=None, start=0.0):
        rows, columns = shards.shape[1:]
        self.board, self.start = board, start
        self.layer, self.side, self.rows, self.columns = layer, side, rows, columns
        full = (4 * rows, 2 * columns) if side == 0 else (2 * rows, 4 * columns)
        self.inputs = [(shards, ANY)]
        self.outs = [(full, BF16, spec)]
        self.scratch = sems(6, 6, 4, 4, 1)

    def run(self, inputs, outs, scratch, sent):
        if self.start > 0.0:
            yield self.start
        yield from delayed(self.go(inputs, outs, scratch, sent), self.start)

    def go(self, inputs, outs, scratch, sent):
        (shards,), (out,) = inputs, outs
        send, recv, csend, crecv, local = scratch
        own = shards.at[self.layer]
        ring, co = Ring("y"), lax.axis_index("co")
        rows, columns = self.rows, self.columns

        def block(y, core, half=None):
            yh, r = y // 2, lax.rem(y, 2) * 2 + core
            down, along = (r, yh) if self.side == 0 else (yh, r)
            first, count = down * rows, rows
            if half is not None:
                count = rows // 2
                first = first + half * count
            return out.at[
                pl.ds(pl.multiple_of(first, 16), count),
                pl.ds(pl.multiple_of(along * columns, 128), columns),
            ]

        def to_core(i, src, y):
            c = remote(src, block(y, co), csend.at[i], crecv.at[i], device(co=1 - co))
            c.start()
            sent.append(c)

        keep = pltpu.make_async_copy(own, block(ring.me, co), local.at[0])
        keep.start()
        to_core(0, own, ring.me)
        numbers = iter((1, 2, 3))
        yield from gather_on(
            ring,
            lambda y, half: block(y, co, half),
            lambda half: own.at[pl.ds(half * (rows // 2), rows // 2), :],
            send,
            recv,
            sent,
            lambda y: to_core(next(numbers), block(y, co), y),
        )
        keep.wait()
        yield 12.0
        for i, y in enumerate((ring.me, ring.left, ring.right, ring.across)):
            there = block(y, 1 - co)
            remote(there, there, csend.at[i], crecv.at[i], device(co=1 - co)).wait_recv()
        if self.board is not None:
            self.board.append(out)


class ReduceWeight:
    links = ("y", "core")

    def __init__(self, left, right, side, board=None, start=0.0):
        self.board, self.start = board, start
        rows, columns = left.shape[-1], right.shape[-1]
        self.full = rows, columns
        rows, columns = (rows // 4, columns // 2) if side == 0 else (rows // 2, columns // 4)
        self.side, self.rows, self.columns = side, rows, columns
        self.inputs = [] if board is not None else [(left, VM), (right, VM)]
        self.outs = [((rows, columns), BF16, VM)]
        self.scratch = [
            pltpu.VMEM(self.full, BF16),
            pltpu.VMEM((4, rows, columns), BF16),
            pltpu.VMEM((4, rows, columns), BF16),
            pltpu.VMEM((2, rows, columns), BF16),
            pltpu.VMEM((2, rows // 2, columns), BF16),
            pltpu.VMEM((2, rows // 2, columns), BF16),
        ] + sems(4, 4, 6, 6)

    def run(self, inputs, outs, scratch, sent):
        total = yield from self.total(inputs, scratch, sent)
        outs[0][...] = total.astype(BF16)

    def total(self, inputs, scratch, sent):
        if self.board is not None:
            yield from until(self.board, 2, self.start)
            inputs = self.board
        elif self.start > 0.0:
            yield self.start
        left, right = inputs
        part, got, pair, fin, relay, stage, csend, crecv, send, recv = scratch

        def columns_of(ref, first):
            if len(ref.shape) == 2:
                return ref[:, first : first + 256]
            return ref[:, :, first : first + 256].reshape(OWN, 256)

        whole = right[...] if len(right.shape) == 2 else right[...].reshape(OWN, self.full[1])
        for first in range(0, self.full[0], 256):
            part[first : first + 256] = dot_tn(columns_of(left, first), whole).astype(BF16)
            if self.start > 0.0:
                yield self.start + first / 512
        co = lax.axis_index("co")
        rows, columns = self.rows, self.columns

        def block(y, core):
            yh, r = y // 2, (y % 2) * 2 + core
            down, along = (r, yh) if self.side == 0 else (yh, r)
            return part.at[
                pl.ds(pl.multiple_of(down * rows, 16), rows),
                pl.ds(pl.multiple_of(along * columns, 128), columns),
            ]

        copies = []
        for y in range(4):
            c = remote(
                block(y, 1 - co), got.at[y], csend.at[y], crecv.at[y], device(co=1 - co)
            )
            c.start()
            copies.append(c)
        sent.extend(copies)
        yield self.start + 5.0
        for y in range(4):
            copies[y].wait_recv()
            pair[y] = (block(y, co)[...].astype(F32) + got[y].astype(F32)).astype(BF16)
        job = reduce_on(Ring("y"), by_rows, pair, fin, relay, stage, send, recv, sent)
        return (yield from delayed(job, self.start + 6.0))


class SumBlock:
    links = ("x",)

    def __init__(self, shape, block=None):
        rows, columns = shape
        self.shape, self.rows = shape, rows // 4
        self.inputs = [] if block is None else [(block, VM)]
        self.outs = [(shape, F32, VM)]
        quarters = (4, rows // 4, columns)
        self.scratch = [pltpu.VMEM(quarters, BF16) for _ in range(3)] + sems(4, 4, 4, 4)

    def run(self, inputs, outs, scratch, sent):
        yield from self.total(inputs[0][...], outs[0], scratch, sent)

    def total(self, value, out, scratch, sent):
        part, got, every, send, recv, gsend, grecv = scratch
        ring = Ring("x")
        others = (ring.across, ring.right, ring.left)
        for i in range(4):
            part[i] = value[i * self.rows : (i + 1) * self.rows].astype(BF16)

        def give(slot, to):
            return remote(part.at[to], got.at[slot], send.at[to], recv.at[slot], ring.at(to))

        def share(slot, to):
            return remote(
                every.at[slot], every.at[slot], gsend.at[to], grecv.at[slot], ring.at(to)
            )

        for i in others:
            c = give(ring.me, i)
            c.start()
            sent.append(c)
        got[ring.me] = part[ring.me]
        yield 4.0
        for i in others:
            give(i, i).wait_recv()
        every[ring.me] = sum(got[i].astype(F32) for i in range(4)).astype(BF16)
        for i in others:
            c = share(ring.me, i)
            c.start()
            sent.append(c)
        yield 8.0
        for i in others:
            share(i, i).wait_recv()
        for i in range(4):
            out[i * self.rows : (i + 1) * self.rows] = every[i].astype(F32)


class ReduceSum:
    links = ("y", "core", "x")

    def __init__(self, left, right, side):
        self.first = ReduceWeight(left, right, side)
        self.second = SumBlock((self.first.rows, self.first.columns))
        self.inputs, self.outs = self.first.inputs, self.second.outs
        self.scratch = self.first.scratch + self.second.scratch

    def run(self, inputs, outs, scratch, sent):
        n = len(self.first.scratch)
        total = yield from self.first.total(inputs, scratch[:n], sent)
        yield from delayed(self.second.total(total, outs[0], scratch[n:], sent), 15.0)


class Pieces:
    links = ()
    pieces = "in"

    def __init__(self, source, start=0.0):
        self.start = start
        self.inputs = [(source, VM)]
        self.outs = [(SHARD, BF16, VM)]
        self.scratch = sems(8, 8)

    def run(self, inputs, outs, scratch, sent):
        if self.start > 0.0:
            yield self.start
        (source,), (landed,), (send, recv) = inputs, outs, scratch
        co, yh, z = (lax.axis_index(a) for a in ("co", "yh", "z"))
        me, home = yh * 4 + z, yh == co

        def piece(j):
            src = source.at[pl.ds(j * REAL, ROWS), :]
            dst = landed.at[:, pl.ds(pl.multiple_of(me * 128, 128), 128)]
            to = device(yh=co, co=j // 4, z=j % 4)
            there = remote(src, dst, send.at[j], recv.at[me], to)
            return there, pltpu.make_async_copy(src, dst, recv.at[me]), home & (co * 4 + z == j)

        for j in range(8):
            there, here, own = piece(j)

            @pl.when(own)
            def _():
                here.start()

            @pl.when(jnp.logical_not(own))
            def _():
                there.start()

        yield self.start + 9.0
        for q in range(8):
            dst = landed.at[:, pl.ds(q * 128, 128)]
            own = home & (me == q)

            @pl.when(own)
            def _():
                pltpu.make_async_copy(dst, dst, recv.at[q]).wait()

            @pl.when(jnp.logical_not(own))
            def _():
                remote(dst, dst, send.at[q], recv.at[q], Ring("z").to_right).wait_recv()

        for j in range(8):
            there, here, own = piece(j)

            @pl.when(jnp.logical_not(own))
            def _():
                there.wait_send()


class PiecesOut:
    links = ()
    pieces = "out"

    def __init__(self, source):
        self.inputs = [(source, VM)]
        self.outs = [((8, ROWS, 128), BF16, VM)]
        self.scratch = [pltpu.VMEM(SHARD, BF16)] + sems(8, 8)

    def run(self, inputs, outs, scratch, sent):
        scratch[0][...] = inputs[0][...].astype(BF16)
        yield from self.give(scratch[0], outs[0], *scratch[1:])

    @staticmethod
    def give(source, landed, send, recv):
        co, yh, z = (lax.axis_index(a) for a in ("co", "yh", "z"))
        shard, home = co * 4 + z, yh == co

        def piece(q):
            src = source.at[:, pl.ds(q * 128, 128)]
            dst = landed.at[shard]
            to = device(co=yh, yh=q // 4, z=q % 4)
            there = remote(src, dst, send.at[q], recv.at[shard], to)
            return there, pltpu.make_async_copy(src, dst, recv.at[shard]), home & (
                yh * 4 + z == q
            )

        for q in range(8):
            there, here, own = piece(q)

            @pl.when(own)
            def _():
                here.start()

            @pl.when(jnp.logical_not(own))
            def _():
                there.start()

        yield 11.0
        for s in range(8):
            dst = landed.at[s]
            own = home & (shard == s)

            @pl.when(own)
            def _():
                pltpu.make_async_copy(dst, dst, recv.at[s]).wait()

            @pl.when(jnp.logical_not(own))
            def _():
                remote(dst, dst, send.at[s], recv.at[s], Ring("z").to_right).wait_recv()

            there, here, mine = piece(s)

            @pl.when(jnp.logical_not(mine))
            def _():
                there.wait_send()


def greet_pieces(way):
    co, yh, z = (lax.axis_index(a) for a in ("co", "yh", "z"))
    home = yh == co
    for j in range(8):
        if way == "in":
            own, source = home & (yh * 4 + z == j), dict(yh=j // 4, z=j % 4, co=yh)
        else:
            own, source = home & (co * 4 + z == j), dict(yh=co, co=j // 4, z=j % 4)

        @pl.when(jnp.logical_not(own))
        def _():
            signal(device(**source))

    return home


class Spread:
    links = ("z",)

    def __init__(self, shard):
        self.inputs = [(shard, VM)]
        self.outs = [(ALL, BF16, VM)]
        self.scratch = SPREAD_SCRATCH

    def run(self, inputs, outs, scratch, sent):
        outs[0][lax.axis_index("z")] = inputs[0][...]
        yield from shard_spread(WHOLE, outs[0], scratch, sent)


class End:
    links = ("z",)

    def __init__(self, part, x, cot, table, at):
        self.at = at
        self.inputs = [(a, VM) for a in (part, x, cot, table)]
        self.outs = [(SHARD, F32, VM), (SUMS, F32, VM)]
        self.scratch = sum_scratch(WHOLE)

    def run(self, inputs, outs, scratch, sent):
        (part, x, cot, table), (x_out, sums) = inputs, outs
        total = yield from shard_sum(WHOLE, part, scratch, sent)
        bias, scale = (table[r : r + 1, :] for r in self.at)
        branch = total + bias
        x_out[...] = x[...] + scale * branch
        df = (cot[...] * scale).astype(BF16)
        sums[...] = jnp.zeros_like(sums)
        sums[2:3, :] = jnp.sum(cot[...] * branch, axis=0, keepdims=True)
        sums[3:4, :] = jnp.sum(df.astype(F32), axis=0, keepdims=True)


def norm_of(value):
    mean = jnp.mean(value, axis=1, keepdims=True)
    meansq = jnp.mean(value * value, axis=1, keepdims=True)
    rstd = lax.rsqrt(meansq - mean * mean + EPS)
    return (value - mean) * rstd, rstd


def norm_back(grad, value, gain):
    hat, rstd = norm_of(value)
    e = grad * gain
    return (
        rstd
        * (
            e
            - jnp.mean(e, axis=1, keepdims=True)
            - hat * jnp.mean(e * hat, axis=1, keepdims=True)
        ),
        jnp.sum(grad * hat, axis=0, keepdims=True),
        jnp.sum(grad, axis=0, keepdims=True),
    )


GAIN, SHIFT, BRANCH, SCALE = 0, 4, 8, 12
SHARD = (ROWS, WIDTH)
ALL = (4, ROWS, WIDTH)
SUMS = (8, WIDTH)


def call(mains, inputs, outs, scratch, ident, riders=(), links=("z",), pieces=None, entry=None, pace=1.0):
    mains = mains if isinstance(mains, list) else [mains]
    inputs = [(a, VM) for a in inputs]
    outs = [(s, d, VM) for s, d in outs]
    jobs = [(inputs, outs, list(scratch))] + [(r.inputs, r.outs, r.scratch) for r in riders]
    links = {link: None for link in links}
    for r in riders:
        links.update({link: None for link in r.links})
        pieces = pieces or getattr(r, "pieces", None)
    runs = [(0, main) for main in mains] + [(i + 1, r.run) for i, r in enumerate(riders)]
    n = len(jobs)
    flat_in = [(i, a, spec is VM) for i, job in enumerate(jobs) for a, spec in job[0]]
    flat_out = [(i, s, d, spec is VM) for i, job in enumerate(jobs) for s, d, spec in job[1]]
    held = [pltpu.VMEM(a.shape, a.dtype) for _, a, inside in flat_in if inside]
    made = [pltpu.VMEM(s, d) for _, s, d, inside in flat_out if inside]

    def kernel(*refs):
        refs = list(refs)
        take = lambda count: [refs.pop(0) for _ in range(count)]
        in_refs, out_refs = take(len(flat_in)), take(len(flat_out))
        own = [take(len(job[2])) for job in jobs]
        held_refs, made_refs = take(len(held)), take(len(made))
        in_sem, out_sem = take(2)
        sent, loads = Sent(), []
        job_in, job_out = [[] for _ in jobs], [[] for _ in jobs]
        for (i, _, inside), ref in zip(flat_in, in_refs):
            if inside:
                there = held_refs[len(loads)]
                loads.append(pltpu.make_async_copy(ref, there, in_sem.at[len(loads)]))
                loads[-1].start()
                ref = there
            job_in[i].append(ref)
        for (i, shape, kind, inside), ref in zip(flat_out, out_refs):
            if inside:
                number = len(sent.results)
                here = made_refs[number]
                copy = pltpu.make_async_copy(here, ref, out_sem.at[number])
                sent.results.append([here, copy, False])
                if shape == ALL and kind == BF16:
                    here[:, REAL:ROWS] = jnp.zeros((4, TAIL, WIDTH), BF16)
                ref = here
            job_out[i].append(ref)
        more = 0 if entry is None else entry()
        greet(links, more, None if pieces is None else greet_pieces(pieces))
        for c in loads:
            c.wait()
        in_turns(
            [
                (i, paced(run(job_in[i], job_out[i], own[i], sent), pace if i > 0 else 1.0))
                for i, run in runs
            ],
            lambda i: sent.flush(*job_out[i]),
        )
        sent.finish()

    results = pl.pallas_call(
        kernel,
        out_shape=[jax.ShapeDtypeStruct(s, d) for _, s, d, _ in flat_out],
        in_specs=[ANY] * len(flat_in),
        out_specs=[ANY] * len(flat_out),
        scratch_shapes=[s for job in jobs for s in job[2]]
        + held
        + made
        + sems(max(len(held), 1), max(len(made), 1)),
        compiler_params=pltpu.CompilerParams(
            collective_id=ident, has_side_effects=True, vmem_limit_bytes=60 * 2**20
        ),
    )(*[a for _, a, _ in flat_in])
    return results[: len(outs)], results[len(outs) :]


def spread_norm(value, table, at, out, rows):
    hat, _ = norm_of(value)
    gain, shift = (table[r : r + 1, :] for r in at)
    out[lax.axis_index("z"), rows] = (hat * gain + shift).astype(BF16)


def back_through_norm(total, value, dx, branch, table, at, dx_out, sums, d_out, rows):
    gain, scale = (table[r : r + 1, :] for r in at)
    dr, gain_sum, shift_sum = norm_back(total, value[rows], gain)
    dx_new = dx[rows] + dr
    dx_out[rows] = dx_new
    df = (dx_new * scale).astype(BF16)
    d_out[lax.axis_index("z"), rows] = df
    sums[0:1, :] += gain_sum
    sums[1:2, :] += shift_sum
    sums[2:3, :] += jnp.sum(dx_new * branch[rows], axis=0, keepdims=True)
    sums[3:4, :] += jnp.sum(df.astype(F32), axis=0, keepdims=True)


def batch_rows(ref, rows):
    value = ref[:, rows]
    return value.reshape(4 * value.shape[1], WIDTH)


def put_rows(ref, rows, value):
    ref[:, rows] = value.reshape(4, rows.stop - rows.start, WIDTH).astype(ref.dtype)


def back_through_hidden(d_all, u, wup, wdown, du_out, hidden, part, rows, time):
    slope = gelu_slope(batch_rows(u, rows))
    du = (dot_nt(batch_rows(d_all, rows), wdown[...]) * slope).astype(BF16)
    put_rows(du_out, rows, du)
    hidden[0:1, :] += jnp.sum(du.astype(F32), axis=0, keepdims=True)
    yield time
    put_rows(part, rows, dot_nt(batch_rows(du_out, rows), wup[...]))


LAG = 2.0
STARTS = (0.0, 7.5, 17.0, 25.0)


def chain(work, inputs, outs, extra, ident, riders):
    each = 2 * (SUMMING + len(SPREAD_SCRATCH))
    scratch = list(extra)
    for batch in BATCHES:
        scratch += 2 * sum_scratch(batch) + 2 * SPREAD_SCRATCH

    def main_of(number, batch):
        rows = slice(batch[0], batch[0] + batch[2])
        lag = number * LAG

        def main(inputs_, outs_, scratch_, sent):
            more, own = scratch_[: len(extra)], scratch_[len(extra) + number * each :][:each]
            parts = [own[:SUMMING], own[SUMMING : 2 * SUMMING]]
            rest = own[2 * SUMMING :]
            parts += [rest[: len(SPREAD_SCRATCH)], rest[len(SPREAD_SCRATCH) :]]

            def add(i, ref):
                job = shard_sum(batch, ref, parts[i], sent)
                return (yield from delayed(job, lag + STARTS[2 * i]))

            def share(i, ref):
                job = shard_spread(batch, ref, parts[2 + i], sent)
                yield from delayed(job, lag + STARTS[2 * i + 1])

            if number == 0:
                for ref, out in zip(outs_, outs):
                    if out[0] == SUMS:
                        ref[...] = jnp.zeros_like(ref)
            else:
                yield lag
            yield from work(add, share, inputs_, outs_, more, rows, lag, sent)

        return main

    return call(
        [main_of(i, b) for i, b in enumerate(BATCHES)], inputs, outs, scratch, ident, riders
    )


def hidden_forward(n_out, wup, wdown, layer, hb, u, g, part, rows, time):
    value = dot_nn(batch_rows(n_out, rows), wup[...]) + hb[layer : layer + 1, :]
    put_rows(u, rows, value)
    yield time
    put_rows(g, rows, gelu_value(batch_rows(u, rows)).astype(BF16))
    yield time + 0.5
    put_rows(part, rows, dot_nn(batch_rows(g, rows), wdown[...]))
    yield time + 1.0


def branch_forward(total, x, table, at, branch_out, x_out, rows):
    bias, scale = (table[r : r + 1, :] for r in at)
    branch = total + bias
    branch_out[rows] = branch
    value = x[rows] + scale * branch
    x_out[rows] = value
    return value


def forward_chain(part, x, table, wup, hb, board, ident, riders):
    def work(add, share, inputs, outs, more, rows, lag, sent):
        part, x, table, wup, hb = inputs
        a, m, n2, u, g, f, x_new, n1 = outs
        (part2,) = more
        total = yield from add(0, part)
        value = branch_forward(total, x, table, (BRANCH, SCALE), a, m, rows)
        spread_norm(value, table, (GAIN + 1, SHIFT + 1), n2, rows)
        yield from share(0, n2)
        yield from until(board, 1, lag + STARTS[2] - 3.0)
        yield from hidden_forward(
            n2, wup, board[0], 0, hb, u, g, part2, rows, lag + STARTS[2] - 2.0
        )
        if lag > 0:
            sent.flush(a, m, n2, u, g)
        total = yield from add(1, part2)
        value = branch_forward(total, m, table, (BRANCH + 1, SCALE + 1), f, x_new, rows)
        spread_norm(value, table, (GAIN + 2, SHIFT + 2), n1, rows)
        yield from share(1, n1)

    shard, whole = (SHARD, F32), (ALL, BF16)
    return chain(
        work,
        (part, x, table, wup, hb),
        [shard, shard, whole, (ALL, F32), whole, shard, shard, whole],
        [pltpu.VMEM(ALL, BF16)],
        ident,
        riders,
    )


def turn_chain(part, x, cot, d_all, table, wup, hb, board, late_up, late_down, ident, riders):
    def work(add, share, inputs, outs, more, rows, lag, sent):
        part, x, cot, d_all, table, wup, hb = inputs
        a, m, n2, g, end_part, du, hidden, dm, sums, d_out = outs
        u, part2 = more
        total = yield from add(0, part)
        value = branch_forward(total, x, table, (BRANCH + 2, SCALE + 2), a, m, rows)
        spread_norm(value, table, (GAIN + 3, SHIFT + 3), n2, rows)
        yield from share(0, n2)
        yield from until(board, 1, lag + STARTS[2] - 3.0)
        wdown = board[0]
        yield from hidden_forward(
            n2, wup, wdown, 1, hb, u, g, end_part, rows, lag + STARTS[2] - 2.0
        )
        yield from back_through_hidden(
            d_all, u, wup, wdown, du, hidden, part2, rows, lag + STARTS[2]
        )
        if lag > 0:
            sent.flush(a, m, n2, g, end_part, du, hidden)
            late_up.extend([n2, du])
            late_down.extend([g, d_all])
        total = yield from add(1, part2)
        back_through_norm(
            total, m, cot, a, table, (GAIN + 3, SCALE + 2), dm, sums, d_out, rows
        )
        yield from share(1, d_out)

    shard, whole, sums = (SHARD, F32), (ALL, BF16), (SUMS, F32)
    return chain(
        work,
        (part, x, cot, d_all, table, wup, hb),
        [shard, shard, whole, whole, whole, whole, sums, shard, sums, whole],
        [pltpu.VMEM(ALL, F32), pltpu.VMEM(ALL, BF16)],
        ident,
        riders,
    )


def backward_chain(
    part, x, dm, f, m, a, n2, u, g, table, wup, wdown, late_down, late_up, ident, riders
):
    def work(add, share, inputs, outs, more, rows, lag, sent):
        part, x, dm, f, m, a, n2, u, g, table, wup, wdown = inputs
        sums1, df, du, hidden, dm_out, sums, d_out = outs
        part2, dx = more
        total = yield from add(0, part)
        back_through_norm(total, x, dm, f, table, (GAIN + 2, SCALE + 1), dx, sums1, df, rows)
        yield from share(0, df)
        if lag > 0:
            late_down.extend([g, df])
        yield from back_through_hidden(
            df, u, wup, wdown, du, hidden, part2, rows, lag + STARTS[2] - 1.0
        )
        if lag > 0:
            sent.flush(sums1, df, du, hidden)
            late_up.extend([n2, du])
        total = yield from add(1, part2)
        back_through_norm(
            total, m, dx, a, table, (GAIN + 1, SCALE), dm_out, sums, d_out, rows
        )
        yield from share(1, d_out)

    shard, whole, sums = (SHARD, F32), (ALL, BF16), (SUMS, F32)
    return chain(
        work,
        (part, x, dm, f, m, a, n2, u, g, table, wup, wdown),
        [sums, whole, whole, sums, shard, sums, whole],
        [pltpu.VMEM(ALL, BF16), pltpu.VMEM(SHARD, F32)],
        ident,
        riders,
    )


def first_step(tokens, small, ident, riders):
    pieces = Pieces(tokens)

    def main(inputs, outs, scratch, sent):
        tokens, params, hidden_bias = inputs[0], inputs[1:6], inputs[6]
        x_out, n_out, table, query_bias, up_bias = outs
        landed, pack, pack_out, psend, precv, ksend, krecv = scratch[:7]
        pack[...] = jnp.zeros_like(pack)
        for i, param in enumerate(params):
            for j in range(4):
                pack[4 * i + j : 4 * i + j + 1, :] = param[j // 2, j % 2 : j % 2 + 1, :]
        for j in range(8):
            lanes = slice(j % 4 * 128, j % 4 * 128 + 128)
            pack[20 + j : 21 + j, :] = hidden_bias[j // 4 : j // 4 + 1, lanes]
        z = lax.axis_index("z")
        me = lax.axis_index("yh") * 4 + z
        arrive = pieces.run([tokens], [landed], [psend, precv], sent)
        next(arrive)
        pack_out[me] = pack[...]

        def note(j, slot):
            return remote(
                pack, pack_out.at[slot], ksend.at[j], krecv.at[slot], device(yh=j // 4, z=j % 4)
            )

        for j in range(8):

            @pl.when(me != j)
            def _():
                note(j, me).start()

        yield 8.0
        for _ in arrive:
            pass
        for q in range(8):

            @pl.when(me != q)
            def _():
                note(q, q).wait_recv()

        value = landed[...].astype(F32)
        x_out[...] = value
        for q in range(8):
            table[:, q * 128 : q * 128 + 128] = pack_out[q, 0:16, :]
        spread_norm(value, table, (GAIN, SHIFT), n_out, slice(0, ROWS))
        spread = delayed(shard_spread(WHOLE, n_out, scratch[7:], sent), 10.0)
        time = next(spread)
        query_bias[...] = jnp.zeros_like(query_bias)
        up_bias[...] = jnp.zeros_like(up_bias)
        for half in range(2):
            block = pack_out[z + 4 * half]
            for l in range(LAYERS):
                for k in range(2):
                    lo = half * 384 + k * 256
                    r = 16 + 2 * l + k
                    query_bias[l : l + 1, lo : lo + 128] = block[r : r + 1]
                for k in range(4):
                    lo = half * 512 + k * 128
                    r = 20 + 4 * l + k
                    up_bias[l : l + 1, lo : lo + 128] = block[r : r + 1]
        yield time
        yield from spread
        for j in range(8):

            @pl.when(me != j)
            def _():
                note(j, me).wait_send()

    def entry():
        yh, z = lax.axis_index("yh"), lax.axis_index("z")
        for j in range(8):

            @pl.when(yh * 4 + z != j)
            def _():
                signal(device(yh=j // 4, z=j % 4))

        return 7

    return call(
        main,
        (tokens,) + small,
        [(SHARD, F32), (ALL, BF16), ((16, WIDTH), F32), ((8, 768), F32), ((8, WIDTH), F32)],
        [
            pltpu.VMEM(SHARD, BF16),
            pltpu.VMEM((32, 128), F32),
            pltpu.VMEM((8, 32, 128), F32),
        ]
        + sems(8, 8, 8, 8)
        + SPREAD_SCRATCH,
        ident,
        riders,
        pieces="in",
        entry=entry,
    )


def last_step(part, value, dx, table, vector_sums, qkv_sums, hidden_sums, at, ident, riders):
    def main(inputs, outs, scratch, sent):
        part, value, dx, table = inputs[:4]
        sum_refs = inputs[4 : 4 + len(vector_sums)]
        qkv_refs, hidden_refs = inputs[-4:-2], inputs[-2:]
        landed, small = outs
        ring_scratch, scratch = scratch[:SUMMING], scratch[SUMMING:]
        both, psend, precv, vectors, zgot, zsend, zrecv = scratch[:7]
        owned, ygot, ysend, yrecv, sub, xgot, xsend, xrecv = scratch[7:]
        x_, yl, co, yh, z = (lax.axis_index(a) for a in AXES)
        total = yield from shard_sum(WHOLE, part, ring_scratch, sent)
        (gain,) = (table[r : r + 1, :] for r in at)
        dr, gain_sum, shift_sum = norm_back(total, value[...], gain)
        for ref, (_, norm, branch) in zip(sum_refs, vector_sums):
            for row, kind, i in ((0, GAIN, norm), (1, SHIFT, norm), (2, 12, branch), (3, 8, branch)):
                if i is not None:
                    vectors[kind + i : kind + i + 1, :] = ref[row : row + 1, :]
        vectors[at[0] : at[0] + 1, :] = gain_sum
        vectors[at[0] + SHIFT : at[0] + SHIFT + 1, :] = shift_sum

        def on_z(there, slot, h):
            cut = vectors.at[:, pl.ds((h * 4 + there) * 128, 128)]
            return remote(
                cut, zgot.at[slot, h], zsend.at[there, h], zrecv.at[slot, h], device(z=there)
            )

        def on_y(there, slot):
            to = device(yh=there // 4, yl=(there // 2) % 2, co=there % 2)
            return remote(
                sub.at[there // 4], ygot.at[slot], ysend.at[there], yrecv.at[slot], to
            )

        def on_x(there, slot):
            return remote(owned, xgot.at[slot], xsend.at[there], xrecv.at[slot], device(x=there))

        def others(me, count, do):
            for i in range(count):

                @pl.when(me != i)
                def _():
                    do(i)

        me = yh * 4 + yl * 2 + co

        def both_halves(do):
            def run(i):
                do(i, 0)
                do(i, 1)

            return run

        others(z, 4, both_halves(lambda i, h: on_z(i, z, h).start()))
        both[...] = (dx[...] + dr).astype(BF16)
        give = PiecesOut.give(both, landed, psend, precv)
        next(give)
        for h in range(2):
            zgot[z, h] = vectors[:, pl.ds(pl.multiple_of((h * 4 + z) * 128, 128), 128)]
        yield 13.0
        others(z, 4, both_halves(lambda i, h: on_z(i, i, h).wait_recv()))
        owned[:, 0:16] = zgot[0] + zgot[1] + zgot[2] + zgot[3]
        owned[:, 16:32] = jnp.zeros((2, 16, 128), F32)
        for h in range(2):
            for l in range(LAYERS):
                for k in range(3):
                    lo, r = h * 384 + k * 128, 16 + 3 * l + k
                    owned[h, r : r + 1, :] = qkv_refs[l][0:1, lo : lo + 128]
                for k in range(4):
                    lo, r = h * 512 + k * 128, 22 + 4 * l + k
                    owned[h, r : r + 1, :] = hidden_refs[l][0:1, lo : lo + 128]
        others(x_, 4, lambda i: on_x(i, x_).start())
        xgot[x_] = owned[...]
        yield 16.0
        others(x_, 4, lambda i: on_x(i, i).wait_recv())
        sub[...] = sum(xgot[i] for i in range(4))
        others(me, 8, lambda i: on_y(i, me).start())
        ygot[me] = sub[yh]
        yield 19.0
        others(me, 8, lambda i: on_y(i, i).wait_recv())
        small[...] = sum(ygot[i] for i in range(8))
        others(z, 4, both_halves(lambda i, h: on_z(i, z, h).wait_send()))
        others(me, 8, lambda i: on_y(i, me).wait_send())
        others(x_, 4, lambda i: on_x(i, x_).wait_send())
        for _ in give:
            pass

    def entry():
        x_, yl, co, yh, z = (lax.axis_index(a) for a in AXES)
        me = yh * 4 + yl * 2 + co
        for i in range(8):

            @pl.when(me != i)
            def _():
                signal(device(yh=i // 4, yl=(i // 2) % 2, co=i % 2))

        for i in range(4):

            @pl.when(x_ != i)
            def _():
                signal(device(x=i))

            @pl.when(z != i)
            def _():
                signal(device(z=i))

        return 7 + 3 + 3

    return call(
        main,
        (part, value, dx, table, *[v[0] for v in vector_sums], *qkv_sums, *hidden_sums),
        [((8, ROWS, 128), BF16), ((32, 128), F32)],
        sum_scratch(WHOLE)
        + [
            pltpu.VMEM(SHARD, BF16),
            *sems(8, 8),
            pltpu.VMEM((16, WIDTH), F32),
            pltpu.VMEM((4, 2, 16, 128), F32),
            pltpu.SemaphoreType.DMA((4, 2)),
            pltpu.SemaphoreType.DMA((4, 2)),
            pltpu.VMEM((2, 32, 128), F32),
            pltpu.VMEM((8, 32, 128), F32),
            *sems(8, 8),
            pltpu.VMEM((2, 32, 128), F32),
            pltpu.VMEM((4, 2, 32, 128), F32),
            *sems(4, 4),
        ],
        ident,
        riders,
        pieces="out",
        entry=entry,
    )


def lanes_of(head, shape):
    lane = lax.broadcasted_iota(jnp.int32, shape, 1)
    return (lane < 64, lane == 64) if head % 2 == 0 else (lane >= 64, lane == 0)


def put_head(ref, i, value, one=False):
    inside, extra = lanes_of(i, value.shape)
    ref[i, 0:OWN] = jnp.where(inside, value, jnp.where(extra & one, 1, 0).astype(BF16))
    ref[i, OWN:QROWS] = jnp.zeros((QROWS - OWN, 128), BF16)


def put_keys(ref, i, rows, value, mask):
    inside, extra = lanes_of(i, value.shape)
    ref[i, rows] = jnp.where(inside, value, jnp.where(extra, mask[rows], jnp.zeros_like(value)))


def attend_step(n_all, wqkv, wout, bias, layer, mask, ident, riders=()):
    def main(inputs, outs, scratch, sent):
        n_all, wqkv, wout, bias, mask = inputs
        part, qkv, other, att, lse = outs
        kall, vt, qpad, ot, send, recv = scratch
        to = device(co=1 - lax.axis_index("co"))
        mine, theirs = slice(0, OWN), slice(OWN, KEYS)
        yield 0.1
        normed = n_all[...].reshape(OWN, WIDTH)
        lse[...] = jnp.zeros_like(lse)
        copies = []
        for h in range(2):
            cols = slice(h * 384, h * 384 + 384)
            block = (dot_nn(normed, wqkv[:, cols]) + bias[layer : layer + 1, cols]).astype(BF16)
            qkv[:, cols] = block
            c = remote(
                qkv.at[:, pl.ds(h * 384 + 128, 256)],
                other.at[:, pl.ds(h * 256, 256)],
                send.at[h],
                recv.at[h],
                to,
            )
            c.start()
            copies.append(c)
            for i in (2 * h, 2 * h + 1):
                put_head(qpad, i, block[:, 0:128] * 0.125, True)
                put_keys(kall, i, mine, block[:, 128:256], mask)
            vt[h * 128 : h * 128 + 128, 0:OWN] = block[:, 256:384].T
        sent.extend(copies)
        yield 3.0
        for h in range(2):
            copies[h].wait_recv()
            for i in (2 * h, 2 * h + 1):
                put_keys(kall, i, theirs, other[:, h * 256 : h * 256 + 128], mask)
            vt[h * 128 : h * 128 + 128, OWN:KEYS] = other[:, h * 256 + 128 : h * 256 + 256].T

            for i in (2 * h, 2 * h + 1):
                rows = slice(i * 64, i * 64 + 64)
                for lo, n in CHUNKS:
                    s = dot_nt(kall[i], qpad[i, lo : lo + n])
                    top = jnp.max(s, axis=0, keepdims=True)
                    e = jnp.exp(s - top)
                    total = jnp.sum(e, axis=0, keepdims=True)
                    ot[rows, lo : lo + n] = dot_nn(vt[rows], e.astype(BF16)) * (1.0 / total)
                    lse[i, 0:1, lo : lo + n] = top + jnp.log(total)
                yield 6.0 + 2.0 * i
        sent.flush(qkv, other, lse)
        att[...] = ot[...].T[0:OWN].astype(BF16)
        part[...] = dot_nn(att[...], wout[...]).astype(BF16).reshape(ALL)

    return call(
        main,
        (n_all, wqkv, wout, bias, mask),
        [
            (ALL, BF16),
            ((OWN, 768), BF16),
            ((OWN, 512), BF16),
            ((OWN, 256), BF16),
            ((4, 8, QROWS), F32),
        ],
        [
            pltpu.VMEM((4, KEYS, 128), BF16),
            pltpu.VMEM((256, KEYS), BF16),
            pltpu.VMEM((4, QROWS, 128), BF16),
            pltpu.VMEM((256, QROWS), F32),
        ]
        + sems(2, 2),
        ident,
        riders,
        links=("core",),
        pace=1.6,
    )


def attend_back_step(d_all, wqkv, wout, qkv, other, att, lse, mask, ident, riders=()):
    def main(inputs, outs, scratch, sent):
        d_all, wqkv, wout, qkv, other, att, lse, mask = inputs
        part, dqkv, sums = outs
        kall, vall, kt, qone, qpad, dpad, delta, dqt, dk, dv, away, got, send, recv = scratch
        to = device(co=1 - lax.axis_index("co"))
        mine, theirs = slice(0, OWN), slice(OWN, KEYS)
        yield 0.1
        datt = dot_nt(d_all[...].reshape(OWN, WIDTH), wout[...]).astype(BF16)
        copies = []
        along = (datt.astype(F32) * att[...].astype(F32)).T
        delta[...] = jnp.zeros_like(delta)
        for i in range(4):
            delta[i, 0:1, 0:OWN] = jnp.sum(along[i * 64 : i * 64 + 64], axis=0, keepdims=True)
        for h in range(2):
            base, half = h * 384, h * 256
            own_keys, other_keys = qkv[:, base + 128 : base + 256], other[:, half : half + 128]
            for i in (2 * h, 2 * h + 1):
                query = qkv[:, base : base + 128] * 0.125
                put_head(qone, i, query, True)
                put_head(qpad, i, query)
                put_head(dpad, i, datt[:, h * 128 : h * 128 + 128])
                put_keys(kall, i, mine, own_keys, mask)
                put_keys(kall, i, theirs, other_keys, mask)
            vall[h, 0:OWN] = qkv[:, base + 256 : base + 384]
            vall[h, OWN:KEYS] = other[:, half + 128 : half + 256]
            kt[h * 128 : h * 128 + 128, 0:OWN] = own_keys.T
            kt[h * 128 : h * 128 + 128, OWN:KEYS] = other_keys.T
            dk[h] = jnp.zeros((KEYS, 128), F32)
            dv[h] = jnp.zeros((KEYS, 128), F32)

            for i in (2 * h, 2 * h + 1):
                rows = slice(i * 64, i * 64 + 64)
                for lo, n in CHUNKS:
                    qc, dc = qpad[i, lo : lo + n], dpad[i, lo : lo + n]
                    s = dot_nt(kall[i], qone[i, lo : lo + n])
                    p = jnp.exp(s - lse[i, 0:1, lo : lo + n])
                    dp = dot_nt(vall[h], dc)
                    ds = (p * (dp - delta[i, 0:1, lo : lo + n])).astype(BF16)
                    dv[h] += dot_nn(p.astype(BF16), dc)
                    dk[h] += dot_nn(ds, qc)
                    dqt[rows, lo : lo + n] = dot_nn(kt[rows], ds)
                yield 5.0 + 2.5 * i
            away[h, :, 0:128] = dk[h, OWN:KEYS].astype(BF16)
            away[h, :, 128:256] = dv[h, OWN:KEYS].astype(BF16)
            c = remote(away.at[h], got.at[h], send.at[h], recv.at[h], to)
            c.start()
            copies.append(c)
        sent.extend(copies)
        dq = dqt[...].T[0:OWN] * 0.125
        for h in range(2):
            base = h * 384
            dqkv[:, base : base + 128] = dq[:, h * 128 : h * 128 + 128].astype(BF16)
            copies[h].wait_recv()
            dqkv[:, base + 128 : base + 256] = (
                dk[h, 0:OWN] + got[h, :, 0:128].astype(F32)
            ).astype(BF16)
            dqkv[:, base + 256 : base + 384] = (
                dv[h, 0:OWN] + got[h, :, 128:256].astype(F32)
            ).astype(BF16)
        part[...] = dot_nt(dqkv[...], wqkv[...]).astype(BF16).reshape(ALL)
        sums[...] = jnp.zeros_like(sums)
        sums[0:1, :] = jnp.sum(dqkv[...].astype(F32), axis=0, keepdims=True)

    return call(
        main,
        (d_all, wqkv, wout, qkv, other, att, lse, mask),
        [(ALL, BF16), ((OWN, 768), BF16), ((8, 768), F32)],
        [
            pltpu.VMEM((4, KEYS, 128), BF16),
            pltpu.VMEM((2, KEYS, 128), BF16),
            pltpu.VMEM((256, KEYS), BF16),
            pltpu.VMEM((4, QROWS, 128), BF16),
            pltpu.VMEM((4, QROWS, 128), BF16),
            pltpu.VMEM((4, QROWS, 128), BF16),
            pltpu.VMEM((4, 8, QROWS), F32),
            pltpu.VMEM((256, QROWS), F32),
            pltpu.VMEM((2, KEYS, 128), F32),
            pltpu.VMEM((2, KEYS, 128), F32),
            pltpu.VMEM((2, OWN, 256), BF16),
            pltpu.VMEM((2, OWN, 256), BF16),
        ]
        + sems(2, 2),
        ident,
        riders,
        links=("core",),
        pace=1.6,
    )


def on_device(
    tokens,
    cotangent,
    attend_weight,
    output_weight,
    up_weight,
    down_weight,
    norm_gain,
    norm_shift,
    attend_bias,
    branch_bias,
    layer_scale,
    hidden_bias,
):
    co, yh, z = (lax.axis_index(a) for a in ("co", "yh", "z"))
    attend_weight = attend_weight.reshape(LAYERS, 256, 384)
    first = jnp.pad(tokens, ((0, 15), (0, 0)))
    cot_pieces = jnp.pad(cotangent.astype(BF16), ((0, 15), (0, 0)))
    def attend_of(l, start=0.0):
        return GatherWeight(attend_weight, l, 0, start=start)

    def output_of(l, start=0.0):
        return GatherWeight(output_weight, l, 1, start=start)

    def up_of(l):
        return GatherWeight(up_weight, l, 0)

    def down_of(l, board):
        return GatherWeight(down_weight, l, 1, VM, board)

    weights = [[None] * 4 for _ in range(LAYERS)]
    ident = iter(range(40))
    small = (norm_gain, norm_shift, branch_bias, layer_scale, attend_bias, hidden_bias)
    (x, n_all, table, query_bias, up_bias), (weights[0][0], weights[0][1]) = first_step(
        first, small, next(ident), [attend_of(0), output_of(0)]
    )
    row = jnp.arange(OWN)
    block, inside = row // ROWS, row % ROWS

    def hidden_keys(half):
        real = (inside < REAL) | ((inside == REAL) & (block == 3) & (half == 1))
        return jnp.where(real, 0.0, -1e30).astype(BF16)

    mask = jnp.concatenate([hidden_keys(co), hidden_keys(1 - co)])
    mask = jnp.broadcast_to(mask[:, None], (KEYS, 128))

    last = jnp.where((co == 1) & (z == 3), REAL + 1, REAL)
    real_row = jnp.arange(ROWS)[:, None] < last

    saved = []
    for l in range(LAYERS):
        wqkv, wout = weights[l][:2]
        riders = [up_of(l)]
        if l == 1:
            riders.append(Spread((cot * table[SCALE + 3]).astype(BF16)))
        n1 = n_all
        (part, qkv, other, att, lse), got = attend_step(
            n1, wqkv, wout, query_bias, l, mask, next(ident), riders
        )
        weights[l][2] = got[0]
        if l == 1:
            d_all = d_last = got[1]
        saved.append([x, n1, qkv, other, att, lse])
        board = []
        if l == 0:
            riders = [
                down_of(0, board), Pieces(cot_pieces, 12.0), attend_of(1, 14.0), output_of(1, 14.5)
            ]
            (a, m, n2, u, g, f, x, n_all), got = forward_chain(
                part, x, table, weights[0][2], up_bias, board, next(ident), riders
            )
            weights[0][3], weights[1][:2] = got[0], got[2:]
            cot = jnp.where(real_row, got[1].astype(F32), 0.0)
            saved[0] += [a, m, n2, u, g, f]
        else:
            late_up, late_down = [], []
            like = n_all
            riders = [
                down_of(1, board),
                ReduceWeight(like, like, 0, late_up, 17.0),
                ReduceWeight(like, like, 1, late_down, 18.5),
            ]
            (a, m, n2, g, end_part, du, hidden, dm, sums, d_all), got = turn_chain(
                part,
                x,
                cot,
                d_all,
                table,
                weights[1][2],
                up_bias,
                board,
                late_up,
                late_down,
                next(ident),
                riders,
            )
            weights[1][3], up_block, down_block = got

    hidden_sums, qkv_sums, grads = [None, hidden], [None] * LAYERS, [[None] * 4, [None] * 4]

    def summing(block):
        return SumBlock(block.shape, block)

    vector_sums = [(sums, 3, 2)]
    x1, n1, qkv, other, att, lse = saved[1]
    da = d_all
    riders = [
        End(end_part, m, cot, table, (BRANCH + 3, SCALE + 3)),
        summing(up_block),
        summing(down_block),
    ]
    (part, dqkv, qkv_sum), got = attend_back_step(
        d_all, *weights[1][:2], qkv, other, att, lse, mask, next(ident), riders
    )
    x_end, sums, grads[1][2], grads[1][3] = got
    vector_sums.append((sums, None, 3))
    qkv_sums[1] = qkv_sum
    x, n1_0, qkv, other, att_0, lse, a, m, n2, u, g0, f = saved[0]
    late_down, late_up = [], []
    riders = [
        ReduceWeight(n1, dqkv, 0, start=1.0),
        ReduceWeight(att, da, 1, start=4.0),
        ReduceWeight(like, like, 1, late_down, 15.5),
        ReduceWeight(like, like, 0, late_up, 18.0),
    ]
    (sums1, df, du, hidden, dm, sums, d_all), got = backward_chain(
        part,
        x1,
        dm,
        f,
        m,
        a,
        n2,
        u,
        g0,
        table,
        *weights[0][2:],
        late_down,
        late_up,
        next(ident),
        riders,
    )
    attend_block, output_block, down_block, up_block = got
    vector_sums += [(sums1, 2, 1), (sums, 1, 0)]
    hidden_sums[0] = hidden
    riders = [
        PiecesOut(x_end),
        ReduceWeight(att_0, d_all, 1),
        summing(attend_block),
        summing(output_block),
        summing(down_block),
    ]
    (part, dqkv, qkv_sum), got = attend_back_step(
        d_all, *weights[0][:2], qkv, other, att_0, lse, mask, next(ident), riders
    )
    out_pieces, output_block, grads[1][0], grads[1][1], grads[0][3] = got
    qkv_sums[0] = qkv_sum
    riders = [
        ReduceSum(n1_0, dqkv, 0),
        summing(output_block),
        summing(up_block),
    ]
    (grad_pieces, small), grads[0][:3] = last_step(
        part, x, dm, table, vector_sums, qkv_sums, hidden_sums, (GAIN,), next(ident), riders
    )

    bias_grad = small[16:22].reshape(2, 3, 128)[:, 0::2]

    def rows(landed):
        return jnp.concatenate(
            [landed[0:7, 0:REAL].reshape(7 * REAL, 128), landed[7, 0 : REAL + 1]]
        ).astype(F32)

    return (
        rows(out_pieces),
        rows(grad_pieces),
        jnp.stack([grads[l][0] for l in range(LAYERS)]).reshape(LAYERS, 256, 3, 128),
        jnp.stack([grads[l][1] for l in range(LAYERS)]),
        jnp.stack([grads[l][2] for l in range(LAYERS)]),
        jnp.stack([grads[l][3] for l in range(LAYERS)]),
        small[0:4].reshape(2, 2, 128),
        small[4:8].reshape(2, 2, 128),
        bias_grad,
        small[8:12].reshape(2, 2, 128),
        small[12:16].reshape(2, 2, 128),
        small[22:30].reshape(2, 512),
    )


def solution(mesh):
    split = Mesh(mesh.devices.reshape(4, 2, 2, 2, 4), AXES)
    images, row, col = ("x", "yl", "co"), ("yl", "co"), ("yh", "z")
    placed = (
        P(images, col),
        P(images, col),
        P(None, row, None, col),
        P(None, col, row),
        P(None, row, col),
        P(None, col, row),
        P(None, None, col),
        P(None, None, col),
        P(None, None, col),
        P(None, None, col),
        P(None, None, col),
        P(None, col),
    )
    return jax.shard_map(
        on_device, mesh=split, in_specs=placed, out_specs=placed, check_vma=False
    )
```

```python
import jax
import jax.numpy as jnp
from jax import lax
from jax.experimental import pallas as pl
from jax.experimental.pallas import tpu as pltpu
from jax.sharding import Mesh, PartitionSpec as P

WIDTH = 1024
HALF = WIDTH // 2
SEQ = 1025
LAYERS = 2
REAL = 128
ROWS = 144
TAIL = ROWS - REAL
OWN = 4 * ROWS
KEYS = 2 * OWN
QROWS = 640
CHUNKS = ((0, 256), (256, 256), (512, 128))
EPS = 1e-06
ROOT_HALF = 0.7071067811865476
INV_ROOT_TWO_PI = 0.3989422804014327
MESH = pl.DeviceIdType.MESH
AXES = ("x", "yl", "co", "yh", "z")
VM = pl.BlockSpec(memory_space=pltpu.VMEM)
ANY = pl.BlockSpec(memory_space=pl.ANY)
F32 = jnp.float32
BF16 = jnp.bfloat16


def gelu_value(value):
    return 0.5 * value * (1.0 + lax.erf(value * ROOT_HALF))


def gelu_slope(value):
    return 0.5 * (1.0 + lax.erf(value * ROOT_HALF)) + value * INV_ROOT_TWO_PI * jnp.exp(
        -0.5 * value * value
    )


def dot_nt(left, right):
    return lax.dot_general(left, right, (((1,), (1,)), ((), ())), preferred_element_type=F32)


def dot_tn(left, right):
    return lax.dot_general(left, right, (((0,), (0,)), ((), ())), preferred_element_type=F32)


def dot_nn(left, right):
    return jnp.dot(left, right, preferred_element_type=F32)


def device(**moved):
    return tuple(moved[a] if a in moved else lax.axis_index(a) for a in AXES)


def remote(src, dst, send, recv, to):
    return pltpu.make_async_remote_copy(
        src_ref=src, dst_ref=dst, send_sem=send, recv_sem=recv, device_id=to, device_id_type=MESH
    )


def signal(to):
    pl.semaphore_signal(
        pltpu.get_barrier_semaphore(), inc=1, device_id=to, device_id_type=MESH
    )


class Ring:
    def __init__(self, axis):
        self.axis = axis
        if axis == "y":
            self.me = lax.axis_index("yh") * 2 + lax.axis_index("yl")
        else:
            self.me = lax.axis_index(axis)
        self.right = lax.rem(self.me + 1, 4)
        self.left = lax.rem(self.me + 3, 4)
        self.across = lax.rem(self.me + 2, 4)
        self.to_right, self.to_left = self.at(self.right), self.at(self.left)

    def at(self, index):
        if self.axis == "y":
            return device(yh=index // 2, yl=lax.rem(index, 2))
        return device(**{self.axis: index})


def greet(links, more=0, home=None):
    count = more
    for link in links:
        if link == "core":
            signal(device(co=1 - lax.axis_index("co")))
            count += 1
        else:
            ring = Ring(link)
            signal(ring.to_right)
            signal(ring.to_left)
            count += 2
            if link != "y":
                signal(ring.at(ring.across))
                count += 1
    barrier = pltpu.get_barrier_semaphore()
    if home is None:
        pl.semaphore_wait(barrier, count)
    else:

        @pl.when(home)
        def _():
            pl.semaphore_wait(barrier, count + 7)

        @pl.when(jnp.logical_not(home))
        def _():
            pl.semaphore_wait(barrier, count + 8)


def in_turns(jobs, done):
    waiting = [[0.0, i, job, number] for i, (number, job) in enumerate(jobs)]
    while waiting:
        first = min(waiting, key=lambda w: w[:2])
        try:
            first[0] = next(first[2])
        except StopIteration:
            waiting.remove(first)
            if all(w[3] != first[3] for w in waiting):
                done(first[3])


class Sent(list):
    def __init__(self):
        self.results = []

    def flush(self, *refs):
        for ref in refs:
            for result in self.results:
                if result[0] is ref and not result[2]:
                    result[1].start()
                    result[2] = True

    def finish(self):
        for c in self:
            c.wait_send()
        for _, copy, _ in self.results:
            copy.wait()


def until(board, count, time):
    while len(board) < count:
        yield time
        time += 1.0


def paced(job, pace):
    for time in job:
        yield pace * time


def delayed(job, time):
    while True:
        try:
            yield time + next(job)
        except StopIteration as end:
            return end.value


def by_rows(ref, lead, half):
    rows = ref.shape[1] // 2
    return ref.at[lead, pl.ds(half * rows, rows), :]


def reduce_on(ring, half, part, fin, relay, stage, send, recv, sent, first=0):
    def copy(i, src, dst, to):
        c = remote(src, dst, send.at[i], recv.at[i], to)
        c.start()
        sent.append(c)
        return c

    far_r = copy(0, half(part, ring.across, 0), relay.at[0], ring.to_right)
    far_l = copy(1, half(part, ring.across, 1), relay.at[1], ring.to_left)
    near_r = copy(2, half(part, ring.right, 1), half(fin, 0, 1), ring.to_right)
    near_l = copy(3, half(part, ring.left, 0), half(fin, 1, 0), ring.to_left)
    yield 3.0
    far_r.wait_recv()
    stage[0] = (half(part, ring.right, 0)[...].astype(F32) + relay[0].astype(F32)).astype(BF16)
    sum_r = copy(4, stage.at[0], half(fin, 0, 0), ring.to_right)
    far_l.wait_recv()
    stage[1] = (half(part, ring.left, 1)[...].astype(F32) + relay[1].astype(F32)).astype(BF16)
    sum_l = copy(5, stage.at[1], half(fin, 1, 1), ring.to_left)
    yield 7.0
    for c in (near_r, near_l, sum_r, sum_l):
        c.wait_recv()
    own = part.at[ring.me, pl.ds(first, fin.shape[1])][...]
    return own.astype(F32) + fin[0].astype(F32) + fin[1].astype(F32)


def gather_on(ring, slot, own, send, recv, sent, landed=None):
    def copy(i, src, owner, half, to):
        return remote(src, slot(owner, half), send.at[i], recv.at[i], to)

    def go(*what):
        c = copy(*what)
        c.start()
        sent.append(c)

    def lands(i, owner, half):
        copy(i, slot(owner, half), owner, half, ring.to_right).wait_recv()

    go(0, own(0), ring.me, 0, ring.to_right)
    go(1, own(1), ring.me, 1, ring.to_left)
    go(2, own(1), ring.me, 1, ring.to_right)
    go(3, own(0), ring.me, 0, ring.to_left)
    yield 2.5
    lands(0, ring.left, 0)
    go(4, slot(ring.left, 0), ring.left, 0, ring.to_right)
    lands(1, ring.right, 1)
    go(5, slot(ring.right, 1), ring.right, 1, ring.to_left)
    yield 5.0
    lands(2, ring.left, 1)
    if landed is not None:
        landed(ring.left)
    lands(3, ring.right, 0)
    if landed is not None:
        landed(ring.right)
    yield 7.0
    lands(4, ring.across, 0)
    lands(5, ring.across, 1)
    if landed is not None:
        landed(ring.across)


def gather_slots(ring, out, half, send, recv, sent):
    def slot(owner, h):
        return half(out, owner, h)

    yield from gather_on(ring, slot, lambda h: slot(ring.me, h), send, recv, sent)


def sems(*counts):
    return [pltpu.SemaphoreType.DMA((c,)) for c in counts]


def tail_roles():
    z, second = lax.axis_index("z"), lax.axis_index("co") == 1
    return z, second & (z == 3), second & (z != 3)


WHOLE, BATCHES = (0, REAL, ROWS), ((0, REAL // 2, REAL // 2), (REAL // 2, REAL // 2, ROWS - REAL // 2))


def shard_sum(batch, part, scratch, sent):
    first, count, rows = batch
    fin, relay, stage, tails, tail, send, recv, tsend, trecv = scratch
    z, holds, gives = tail_roles()
    ends = first + rows == ROWS

    def half(ref, lead, h):
        lo = first if ref.shape[1] == ROWS else 0
        return ref.at[lead, pl.ds(lo, count), pl.ds(h * HALF, HALF)]

    def tail_to(slot):
        src = part.at[3, pl.ds(REAL, TAIL), :]
        return remote(src, tails.at[slot], tsend.at[0], trecv.at[slot], device(z=3))

    if ends:

        @pl.when(gives)
        def _():
            tail_to(z).start()

    total = yield from reduce_on(
        Ring("z"), half, part, fin, relay, stage, send, recv, sent, first
    )
    if not ends:
        return total
    tail[...] = jnp.zeros_like(tail)

    @pl.when(holds)
    def _():
        for i in range(3):
            tail_to(i).wait_recv()
        tail[...] = part[3, REAL:ROWS].astype(F32) + sum(tails[i].astype(F32) for i in range(3))

    @pl.when(gives)
    def _():
        tail_to(z).wait_send()

    return jnp.concatenate([total, tail[...]], axis=0)


def shard_spread(batch, out, scratch, sent):
    first, count, rows = batch
    send, recv, tsend, trecv = scratch
    z, holds, gives = tail_roles()
    ends = first + rows == ROWS

    def half(ref, lead, h):
        return ref.at[lead, pl.ds(first, count), pl.ds(h * HALF, HALF)]

    def tail_to(i):
        ref = out.at[3, pl.ds(REAL, TAIL), :]
        return remote(ref, ref, tsend.at[i], trecv.at[0], device(z=i))

    if ends:

        @pl.when(holds)
        def _():
            for i in range(3):
                tail_to(i).start()

    yield from gather_slots(Ring("z"), out, half, send, recv, sent)
    if ends:

        @pl.when(gives)
        def _():
            tail_to(0).wait_recv()

        @pl.when(holds)
        def _():
            for i in range(3):
                tail_to(i).wait_send()


def sum_scratch(batch):
    count = batch[1]
    return [
        pltpu.VMEM((2, count, WIDTH), BF16),
        pltpu.VMEM((2, count, HALF), BF16),
        pltpu.VMEM((2, count, HALF), BF16),
        pltpu.VMEM((3, TAIL, WIDTH), BF16),
        pltpu.VMEM((TAIL, WIDTH), F32),
    ] + sems(6, 6, 1, 3)


SPREAD_SCRATCH = sems(6, 6, 3, 1)
SUMMING = len(sum_scratch(WHOLE))


class GatherWeight:
    links = ("y", "core")

    def __init__(self, shards, layer, side, spec=ANY, board=None, start=0.0):
        rows, columns = shards.shape[1:]
        self.board, self.start = board, start
        self.layer, self.side, self.rows, self.columns = layer, side, rows, columns
        full = (4 * rows, 2 * columns) if side == 0 else (2 * rows, 4 * columns)
        self.inputs = [(shards, ANY)]
        self.outs = [(full, BF16, spec)]
        self.scratch = sems(6, 6, 4, 4, 1)

    def run(self, inputs, outs, scratch, sent):
        if self.start > 0.0:
            yield self.start
        yield from delayed(self.go(inputs, outs, scratch, sent), self.start)

    def go(self, inputs, outs, scratch, sent):
        (shards,), (out,) = inputs, outs
        send, recv, csend, crecv, local = scratch
        own = shards.at[self.layer]
        ring, co = Ring("y"), lax.axis_index("co")
        rows, columns = self.rows, self.columns

        def block(y, core, half=None):
            yh, r = y // 2, lax.rem(y, 2) * 2 + core
            down, along = (r, yh) if self.side == 0 else (yh, r)
            first, count = down * rows, rows
            if half is not None:
                count = rows // 2
                first = first + half * count
            return out.at[
                pl.ds(pl.multiple_of(first, 16), count),
                pl.ds(pl.multiple_of(along * columns, 128), columns),
            ]

        def to_core(i, src, y):
            c = remote(src, block(y, co), csend.at[i], crecv.at[i], device(co=1 - co))
            c.start()
            sent.append(c)

        keep = pltpu.make_async_copy(own, block(ring.me, co), local.at[0])
        keep.start()
        to_core(0, own, ring.me)
        numbers = iter((1, 2, 3))
        yield from gather_on(
            ring,
            lambda y, half: block(y, co, half),
            lambda half: own.at[pl.ds(half * (rows // 2), rows // 2), :],
            send,
            recv,
            sent,
            lambda y: to_core(next(numbers), block(y, co), y),
        )
        keep.wait()
        yield 12.0
        for i, y in enumerate((ring.me, ring.left, ring.right, ring.across)):
            there = block(y, 1 - co)
            remote(there, there, csend.at[i], crecv.at[i], device(co=1 - co)).wait_recv()
        if self.board is not None:
            self.board.append(out)


class ReduceWeight:
    links = ("y", "core")

    def __init__(self, left, right, side, board=None, start=0.0):
        self.board, self.start = board, start
        rows, columns = left.shape[-1], right.shape[-1]
        self.full = rows, columns
        rows, columns = (rows // 4, columns // 2) if side == 0 else (rows // 2, columns // 4)
        self.side, self.rows, self.columns = side, rows, columns
        self.inputs = [] if board is not None else [(left, VM), (right, VM)]
        self.outs = [((rows, columns), BF16, VM)]
        self.scratch = [
            pltpu.VMEM(self.full, BF16),
            pltpu.VMEM((4, rows, columns), BF16),
            pltpu.VMEM((4, rows, columns), BF16),
            pltpu.VMEM((2, rows, columns), BF16),
            pltpu.VMEM((2, rows // 2, columns), BF16),
            pltpu.VMEM((2, rows // 2, columns), BF16),
        ] + sems(4, 4, 6, 6)

    def run(self, inputs, outs, scratch, sent):
        total = yield from self.total(inputs, scratch, sent)
        outs[0][...] = total.astype(BF16)

    def total(self, inputs, scratch, sent):
        if self.board is not None:
            yield from until(self.board, 2, self.start)
            inputs = self.board
        elif self.start > 0.0:
            yield self.start
        left, right = inputs
        part, got, pair, fin, relay, stage, csend, crecv, send, recv = scratch

        def columns_of(ref, first):
            if len(ref.shape) == 2:
                return ref[:, first : first + 256]
            return ref[:, :, first : first + 256].reshape(OWN, 256)

        co = lax.axis_index("co")
        rows, columns = self.rows, self.columns

        def block(y, core):
            yh, r = y // 2, (y % 2) * 2 + core
            down, along = (r, yh) if self.side == 0 else (yh, r)
            return part.at[
                pl.ds(pl.multiple_of(down * rows, 16), rows),
                pl.ds(pl.multiple_of(along * columns, 128), columns),
            ]

        copies = [
            remote(block(y, 1 - co), got.at[y], csend.at[y], crecv.at[y], device(co=1 - co))
            for y in range(4)
        ]
        whole = right[...] if len(right.shape) == 2 else right[...].reshape(OWN, self.full[1])
        for first in range(0, self.full[0], 256):
            part[first : first + 256] = dot_tn(columns_of(left, first), whole).astype(BF16)
            if self.side == 0:
                yl, core = first // rows // 2, first // rows % 2

                @pl.when(co != core)
                def _():
                    copies[yl].start()
                    copies[2 + yl].start()

            if self.start > 0.0:
                yield self.start + first / 512
        if self.side == 1:
            for c in copies:
                c.start()
        sent.extend(copies)
        yield self.start + 5.0
        for y in range(4):
            copies[y].wait_recv()
            pair[y] = (block(y, co)[...].astype(F32) + got[y].astype(F32)).astype(BF16)
        job = reduce_on(Ring("y"), by_rows, pair, fin, relay, stage, send, recv, sent)
        return (yield from delayed(job, self.start + 6.0))


class SumBlock:
    links = ("x",)

    def __init__(self, shape, block=None, cut=False):
        rows, columns = shape
        self.shape, self.rows, self.cut = shape, rows // 4, cut
        self.inputs = [] if block is None else [(block, VM)]
        self.outs = [((columns // 128, rows, 128) if cut else shape, F32, VM)]
        quarters = (4, rows // 4, columns)
        self.scratch = [pltpu.VMEM(quarters, BF16) for _ in range(3)] + sems(4, 4, 4, 4)

    def run(self, inputs, outs, scratch, sent):
        yield from self.total(inputs[0][...], outs[0], scratch, sent)

    def total(self, value, out, scratch, sent):
        part, got, every, send, recv, gsend, grecv = scratch
        ring = Ring("x")
        others = (ring.across, ring.right, ring.left)
        for i in range(4):
            part[i] = value[i * self.rows : (i + 1) * self.rows].astype(BF16)

        def give(slot, to):
            return remote(part.at[to], got.at[slot], send.at[to], recv.at[slot], ring.at(to))

        def share(slot, to):
            return remote(
                every.at[slot], every.at[slot], gsend.at[to], grecv.at[slot], ring.at(to)
            )

        for i in others:
            c = give(ring.me, i)
            c.start()
            sent.append(c)
        got[ring.me] = part[ring.me]
        yield 4.0
        for i in others:
            give(i, i).wait_recv()
        every[ring.me] = sum(got[i].astype(F32) for i in range(4)).astype(BF16)
        for i in others:
            c = share(ring.me, i)
            c.start()
            sent.append(c)
        yield 8.0
        for i in others:
            share(i, i).wait_recv()
        for i in range(4):
            rows, value = slice(i * self.rows, (i + 1) * self.rows), every[i].astype(F32)
            if self.cut:
                for k in range(self.shape[1] // 128):
                    out[k, rows] = value[:, k * 128 : k * 128 + 128]
            else:
                out[rows] = value


class ReduceSum:
    links = ("y", "core", "x")

    def __init__(self, left, right, side):
        self.first = ReduceWeight(left, right, side)
        self.second = SumBlock((self.first.rows, self.first.columns), cut=True)
        self.inputs, self.outs = self.first.inputs, self.second.outs
        self.scratch = self.first.scratch + self.second.scratch

    def run(self, inputs, outs, scratch, sent):
        n = len(self.first.scratch)
        total = yield from self.first.total(inputs, scratch[:n], sent)
        yield from delayed(self.second.total(total, outs[0], scratch[n:], sent), 15.0)


class Pieces:
    links = ()
    pieces = "in"

    def __init__(self, source, start=0.0):
        self.start = start
        self.inputs = [(source, VM)]
        self.outs = [(SHARD, BF16, VM)]
        self.scratch = sems(8, 8)

    def run(self, inputs, outs, scratch, sent):
        if self.start > 0.0:
            yield self.start
        (source,), (landed,), (send, recv) = inputs, outs, scratch
        co, yh, z = (lax.axis_index(a) for a in ("co", "yh", "z"))
        me, home = yh * 4 + z, yh == co

        def piece(j):
            src = source.at[pl.ds(j * REAL, ROWS), :]
            dst = landed.at[:, pl.ds(pl.multiple_of(me * 128, 128), 128)]
            to = device(yh=co, co=j // 4, z=j % 4)
            there = remote(src, dst, send.at[j], recv.at[me], to)
            return there, pltpu.make_async_copy(src, dst, recv.at[me]), home & (co * 4 + z == j)

        for j in range(8):
            there, here, own = piece(j)

            @pl.when(own)
            def _():
                here.start()

            @pl.when(jnp.logical_not(own))
            def _():
                there.start()

        yield self.start + 9.0
        for q in range(8):
            dst = landed.at[:, pl.ds(q * 128, 128)]
            own = home & (me == q)

            @pl.when(own)
            def _():
                pltpu.make_async_copy(dst, dst, recv.at[q]).wait()

            @pl.when(jnp.logical_not(own))
            def _():
                remote(dst, dst, send.at[q], recv.at[q], Ring("z").to_right).wait_recv()

        for j in range(8):
            there, here, own = piece(j)

            @pl.when(jnp.logical_not(own))
            def _():
                there.wait_send()


class PiecesOut:
    links = ()
    pieces = "out"

    def __init__(self, source):
        self.inputs = [(source, VM)]
        self.outs = [((8, ROWS, 128), BF16, VM)]
        self.scratch = [pltpu.VMEM(SHARD, BF16)] + sems(8, 8)

    def run(self, inputs, outs, scratch, sent):
        scratch[0][...] = inputs[0][...].astype(BF16)
        yield from self.give(scratch[0], outs[0], *scratch[1:])

    @staticmethod
    def give(source, landed, send, recv):
        co, yh, z = (lax.axis_index(a) for a in ("co", "yh", "z"))
        shard, home = co * 4 + z, yh == co

        def piece(q):
            src = source.at[:, pl.ds(q * 128, 128)]
            dst = landed.at[shard]
            to = device(co=yh, yh=q // 4, z=q % 4)
            there = remote(src, dst, send.at[q], recv.at[shard], to)
            return there, pltpu.make_async_copy(src, dst, recv.at[shard]), home & (
                yh * 4 + z == q
            )

        for q in range(8):
            there, here, own = piece(q)

            @pl.when(own)
            def _():
                here.start()

            @pl.when(jnp.logical_not(own))
            def _():
                there.start()

        yield 11.0
        for s in range(8):
            dst = landed.at[s]
            own = home & (shard == s)

            @pl.when(own)
            def _():
                pltpu.make_async_copy(dst, dst, recv.at[s]).wait()

            @pl.when(jnp.logical_not(own))
            def _():
                remote(dst, dst, send.at[s], recv.at[s], Ring("z").to_right).wait_recv()

            there, here, mine = piece(s)

            @pl.when(jnp.logical_not(mine))
            def _():
                there.wait_send()


def greet_pieces(way):
    co, yh, z = (lax.axis_index(a) for a in ("co", "yh", "z"))
    home = yh == co
    for j in range(8):
        if way == "in":
            own, source = home & (yh * 4 + z == j), dict(yh=j // 4, z=j % 4, co=yh)
        else:
            own, source = home & (co * 4 + z == j), dict(yh=co, co=j // 4, z=j % 4)

        @pl.when(jnp.logical_not(own))
        def _():
            signal(device(**source))

    return home


class Spread:
    links = ("z",)

    def __init__(self, shard):
        self.inputs = [(shard, VM)]
        self.outs = [(ALL, BF16, VM)]
        self.scratch = SPREAD_SCRATCH

    def run(self, inputs, outs, scratch, sent):
        outs[0][lax.axis_index("z")] = inputs[0][...]
        yield from shard_spread(WHOLE, outs[0], scratch, sent)


class End:
    links = ("z",)

    def __init__(self, part, x, cot, table, at):
        self.at = at
        self.inputs = [(a, VM) for a in (part, x, cot, table)]
        self.outs = [(SHARD, F32, VM), (SUMS, F32, VM)]
        self.scratch = sum_scratch(WHOLE)

    def run(self, inputs, outs, scratch, sent):
        (part, x, cot, table), (x_out, sums) = inputs, outs
        total = yield from shard_sum(WHOLE, part, scratch, sent)
        bias, scale = (table[r : r + 1, :] for r in self.at)
        branch = total + bias
        x_out[...] = x[...] + scale * branch
        df = (cot[...] * scale).astype(BF16)
        sums[...] = jnp.zeros_like(sums)
        sums[2:3, :] = jnp.sum(cot[...] * branch, axis=0, keepdims=True)
        sums[3:4, :] = jnp.sum(df.astype(F32), axis=0, keepdims=True)


def norm_of(value):
    mean = jnp.mean(value, axis=1, keepdims=True)
    meansq = jnp.mean(value * value, axis=1, keepdims=True)
    rstd = lax.rsqrt(meansq - mean * mean + EPS)
    return (value - mean) * rstd, rstd


def norm_back(grad, value, gain):
    hat, rstd = norm_of(value)
    e = grad * gain
    return (
        rstd
        * (
            e
            - jnp.mean(e, axis=1, keepdims=True)
            - hat * jnp.mean(e * hat, axis=1, keepdims=True)
        ),
        jnp.sum(grad * hat, axis=0, keepdims=True),
        jnp.sum(grad, axis=0, keepdims=True),
    )


GAIN, SHIFT, BRANCH, SCALE = 0, 4, 8, 12
SHARD = (ROWS, WIDTH)
ALL = (4, ROWS, WIDTH)
SUMS = (8, WIDTH)


def call(mains, inputs, outs, scratch, ident, riders=(), links=("z",), pieces=None, entry=None, pace=1.0):
    mains = mains if isinstance(mains, list) else [mains]
    inputs = [(a, VM) for a in inputs]
    outs = [(s, d, VM) for s, d in outs]
    jobs = [(inputs, outs, list(scratch))] + [(r.inputs, r.outs, r.scratch) for r in riders]
    links = {link: None for link in links}
    for r in riders:
        links.update({link: None for link in r.links})
        pieces = pieces or getattr(r, "pieces", None)
    runs = [(0, main) for main in mains] + [(i + 1, r.run) for i, r in enumerate(riders)]
    n = len(jobs)
    flat_in = [(i, a, spec is VM) for i, job in enumerate(jobs) for a, spec in job[0]]
    flat_out = [(i, s, d, spec is VM) for i, job in enumerate(jobs) for s, d, spec in job[1]]
    held = [pltpu.VMEM(a.shape, a.dtype) for _, a, inside in flat_in if inside]
    made = [pltpu.VMEM(s, d) for _, s, d, inside in flat_out if inside]

    def kernel(*refs):
        refs = list(refs)
        take = lambda count: [refs.pop(0) for _ in range(count)]
        in_refs, out_refs = take(len(flat_in)), take(len(flat_out))
        own = [take(len(job[2])) for job in jobs]
        held_refs, made_refs = take(len(held)), take(len(made))
        in_sem, out_sem = take(2)
        sent, loads = Sent(), []
        job_in, job_out = [[] for _ in jobs], [[] for _ in jobs]
        for (i, _, inside), ref in zip(flat_in, in_refs):
            if inside:
                there = held_refs[len(loads)]
                loads.append(pltpu.make_async_copy(ref, there, in_sem.at[len(loads)]))
                loads[-1].start()
                ref = there
            job_in[i].append(ref)
        for (i, shape, kind, inside), ref in zip(flat_out, out_refs):
            if inside:
                number = len(sent.results)
                here = made_refs[number]
                copy = pltpu.make_async_copy(here, ref, out_sem.at[number])
                sent.results.append([here, copy, False])
                if shape == ALL and kind == BF16:
                    here[:, REAL:ROWS] = jnp.zeros((4, TAIL, WIDTH), BF16)
                ref = here
            job_out[i].append(ref)
        more = 0 if entry is None else entry()
        greet(links, more, None if pieces is None else greet_pieces(pieces))
        for c in loads:
            c.wait()
        in_turns(
            [
                (i, paced(run(job_in[i], job_out[i], own[i], sent), pace if i > 0 else 1.0))
                for i, run in runs
            ],
            lambda i: sent.flush(*job_out[i]),
        )
        sent.finish()

    results = pl.pallas_call(
        kernel,
        out_shape=[jax.ShapeDtypeStruct(s, d) for _, s, d, _ in flat_out],
        in_specs=[ANY] * len(flat_in),
        out_specs=[ANY] * len(flat_out),
        scratch_shapes=[s for job in jobs for s in job[2]]
        + held
        + made
        + sems(max(len(held), 1), max(len(made), 1)),
        compiler_params=pltpu.CompilerParams(
            collective_id=ident, has_side_effects=True, vmem_limit_bytes=60 * 2**20
        ),
    )(*[a for _, a, _ in flat_in])
    return results[: len(outs)], results[len(outs) :]


def spread_norm(value, table, at, out, rows):
    hat, _ = norm_of(value)
    gain, shift = (table[r : r + 1, :] for r in at)
    out[lax.axis_index("z"), rows] = (hat * gain + shift).astype(BF16)


def back_through_norm(total, value, dx, branch, table, at, dx_out, sums, d_out, rows):
    gain, scale = (table[r : r + 1, :] for r in at)
    dr, gain_sum, shift_sum = norm_back(total, value[rows], gain)
    dx_new = dx[rows] + dr
    dx_out[rows] = dx_new
    df = (dx_new * scale).astype(BF16)
    d_out[lax.axis_index("z"), rows] = df
    sums[0:1, :] += gain_sum
    sums[1:2, :] += shift_sum
    sums[2:3, :] += jnp.sum(dx_new * branch[rows], axis=0, keepdims=True)
    sums[3:4, :] += jnp.sum(df.astype(F32), axis=0, keepdims=True)


def batch_rows(ref, rows):
    value = ref[:, rows]
    return value.reshape(4 * value.shape[1], WIDTH)


def put_rows(ref, rows, value):
    ref[:, rows] = value.reshape(4, rows.stop - rows.start, WIDTH).astype(ref.dtype)


def back_through_hidden(d_all, u, wup, wdown, du_out, hidden, part, rows, time):
    slope = gelu_slope(batch_rows(u, rows))
    du = (dot_nt(batch_rows(d_all, rows), wdown[...]) * slope).astype(BF16)
    put_rows(du_out, rows, du)
    hidden[0:1, :] += jnp.sum(du.astype(F32), axis=0, keepdims=True)
    yield time
    put_rows(part, rows, dot_nt(batch_rows(du_out, rows), wup[...]))


LAG = 2.0
STARTS = (0.0, 7.5, 17.0, 25.0)


def chain(work, inputs, outs, extra, ident, riders):
    each = 2 * (SUMMING + len(SPREAD_SCRATCH))
    scratch = list(extra)
    for batch in BATCHES:
        scratch += 2 * sum_scratch(batch) + 2 * SPREAD_SCRATCH

    def main_of(number, batch):
        rows = slice(batch[0], batch[0] + batch[2])
        lag = number * LAG

        def main(inputs_, outs_, scratch_, sent):
            more, own = scratch_[: len(extra)], scratch_[len(extra) + number * each :][:each]
            parts = [own[:SUMMING], own[SUMMING : 2 * SUMMING]]
            rest = own[2 * SUMMING :]
            parts += [rest[: len(SPREAD_SCRATCH)], rest[len(SPREAD_SCRATCH) :]]

            def add(i, ref):
                job = shard_sum(batch, ref, parts[i], sent)
                return (yield from delayed(job, lag + STARTS[2 * i]))

            def share(i, ref):
                job = shard_spread(batch, ref, parts[2 + i], sent)
                yield from delayed(job, lag + STARTS[2 * i + 1])

            if number == 0:
                for ref, out in zip(outs_, outs):
                    if out[0] == SUMS:
                        ref[...] = jnp.zeros_like(ref)
            else:
                yield lag
            yield from work(add, share, inputs_, outs_, more, rows, lag, sent)

        return main

    return call(
        [main_of(i, b) for i, b in enumerate(BATCHES)], inputs, outs, scratch, ident, riders
    )


def hidden_forward(n_out, wup, wdown, layer, hb, u, g, part, rows, time):
    value = dot_nn(batch_rows(n_out, rows), wup[...]) + hb[layer : layer + 1, :]
    put_rows(u, rows, value)
    yield time
    put_rows(g, rows, gelu_value(batch_rows(u, rows)).astype(BF16))
    yield time + 0.5
    put_rows(part, rows, dot_nn(batch_rows(g, rows), wdown[...]))
    yield time + 1.0


def branch_forward(total, x, table, at, branch_out, x_out, rows):
    bias, scale = (table[r : r + 1, :] for r in at)
    branch = total + bias
    branch_out[rows] = branch
    value = x[rows] + scale * branch
    x_out[rows] = value
    return value


def forward_chain(part, x, table, wup, hb, board, ident, riders):
    def work(add, share, inputs, outs, more, rows, lag, sent):
        part, x, table, wup, hb = inputs
        a, m, n2, u, g, f, x_new, n1 = outs
        (part2,) = more
        total = yield from add(0, part)
        value = branch_forward(total, x, table, (BRANCH, SCALE), a, m, rows)
        spread_norm(value, table, (GAIN + 1, SHIFT + 1), n2, rows)
        yield from share(0, n2)
        yield from until(board, 1, lag + STARTS[2] - 3.0)
        yield from hidden_forward(
            n2, wup, board[0], 0, hb, u, g, part2, rows, lag + STARTS[2] - 2.0
        )
        if lag > 0:
            sent.flush(a, m, n2, u, g)
        total = yield from add(1, part2)
        value = branch_forward(total, m, table, (BRANCH + 1, SCALE + 1), f, x_new, rows)
        spread_norm(value, table, (GAIN + 2, SHIFT + 2), n1, rows)
        yield from share(1, n1)

    shard, whole = (SHARD, F32), (ALL, BF16)
    return chain(
        work,
        (part, x, table, wup, hb),
        [shard, shard, whole, (ALL, F32), whole, shard, shard, whole],
        [pltpu.VMEM(ALL, BF16)],
        ident,
        riders,
    )


def turn_chain(part, x, cot, d_all, table, wup, hb, board, late_up, late_down, ident, riders):
    def work(add, share, inputs, outs, more, rows, lag, sent):
        part, x, cot, d_all, table, wup, hb = inputs
        a, m, n2, g, end_part, du, hidden, dm, sums, d_out = outs
        u, part2 = more
        total = yield from add(0, part)
        value = branch_forward(total, x, table, (BRANCH + 2, SCALE + 2), a, m, rows)
        spread_norm(value, table, (GAIN + 3, SHIFT + 3), n2, rows)
        yield from share(0, n2)
        yield from until(board, 1, lag + STARTS[2] - 3.0)
        wdown = board[0]
        yield from hidden_forward(
            n2, wup, wdown, 1, hb, u, g, end_part, rows, lag + STARTS[2] - 2.0
        )
        yield from back_through_hidden(
            d_all, u, wup, wdown, du, hidden, part2, rows, lag + STARTS[2]
        )
        if lag > 0:
            sent.flush(a, m, n2, g, end_part, du, hidden)
            late_up.extend([n2, du])
            late_down.extend([g, d_all])
        total = yield from add(1, part2)
        back_through_norm(
            total, m, cot, a, table, (GAIN + 3, SCALE + 2), dm, sums, d_out, rows
        )
        yield from share(1, d_out)

    shard, whole, sums = (SHARD, F32), (ALL, BF16), (SUMS, F32)
    return chain(
        work,
        (part, x, cot, d_all, table, wup, hb),
        [shard, shard, whole, whole, whole, whole, sums, shard, sums, whole],
        [pltpu.VMEM(ALL, F32), pltpu.VMEM(ALL, BF16)],
        ident,
        riders,
    )


def backward_chain(
    part, x, dm, f, m, a, n2, u, g, table, wup, wdown, late_down, late_up, ident, riders
):
    def work(add, share, inputs, outs, more, rows, lag, sent):
        part, x, dm, f, m, a, n2, u, g, table, wup, wdown = inputs
        sums1, df, du, hidden, dm_out, sums, d_out = outs
        part2, dx = more
        total = yield from add(0, part)
        back_through_norm(total, x, dm, f, table, (GAIN + 2, SCALE + 1), dx, sums1, df, rows)
        yield from share(0, df)
        if lag > 0:
            late_down.extend([g, df])
        yield from back_through_hidden(
            df, u, wup, wdown, du, hidden, part2, rows, lag + STARTS[2] - 1.0
        )
        if lag > 0:
            sent.flush(sums1, df, du, hidden)
            late_up.extend([n2, du])
        total = yield from add(1, part2)
        back_through_norm(
            total, m, dx, a, table, (GAIN + 1, SCALE), dm_out, sums, d_out, rows
        )
        yield from share(1, d_out)

    shard, whole, sums = (SHARD, F32), (ALL, BF16), (SUMS, F32)
    return chain(
        work,
        (part, x, dm, f, m, a, n2, u, g, table, wup, wdown),
        [sums, whole, whole, sums, shard, sums, whole],
        [pltpu.VMEM(ALL, BF16), pltpu.VMEM(SHARD, F32)],
        ident,
        riders,
    )


def first_step(tokens, small, ident, riders):
    pieces = Pieces(tokens)

    def main(inputs, outs, scratch, sent):
        tokens, params, hidden_bias = inputs[0], inputs[1:6], inputs[6]
        x_out, n_out, table, query_bias, up_bias = outs
        landed, pack, pack_out, psend, precv, ksend, krecv = scratch[:7]
        pack[...] = jnp.zeros_like(pack)
        for i, param in enumerate(params):
            for j in range(4):
                pack[4 * i + j : 4 * i + j + 1, :] = param[j // 2, j % 2 : j % 2 + 1, :]
        for j in range(8):
            lanes = slice(j % 4 * 128, j % 4 * 128 + 128)
            pack[20 + j : 21 + j, :] = hidden_bias[j // 4 : j // 4 + 1, lanes]
        z = lax.axis_index("z")
        me = lax.axis_index("yh") * 4 + z
        arrive = pieces.run([tokens], [landed], [psend, precv], sent)
        next(arrive)
        pack_out[me] = pack[...]

        def note(j, slot):
            return remote(
                pack, pack_out.at[slot], ksend.at[j], krecv.at[slot], device(yh=j // 4, z=j % 4)
            )

        for j in range(8):

            @pl.when(me != j)
            def _():
                note(j, me).start()

        yield 8.0
        for _ in arrive:
            pass
        for q in range(8):

            @pl.when(me != q)
            def _():
                note(q, q).wait_recv()

        value = landed[...].astype(F32)
        x_out[...] = value
        for q in range(8):
            table[:, q * 128 : q * 128 + 128] = pack_out[q, 0:16, :]
        spread_norm(value, table, (GAIN, SHIFT), n_out, slice(0, ROWS))
        spread = delayed(shard_spread(WHOLE, n_out, scratch[7:], sent), 10.0)
        time = next(spread)
        query_bias[...] = jnp.zeros_like(query_bias)
        up_bias[...] = jnp.zeros_like(up_bias)
        for half in range(2):
            block = pack_out[z + 4 * half]
            for l in range(LAYERS):
                for k in range(2):
                    lo = half * 384 + k * 256
                    r = 16 + 2 * l + k
                    query_bias[l : l + 1, lo : lo + 128] = block[r : r + 1]
                for k in range(4):
                    lo = half * 512 + k * 128
                    r = 20 + 4 * l + k
                    up_bias[l : l + 1, lo : lo + 128] = block[r : r + 1]
        yield time
        yield from spread
        for j in range(8):

            @pl.when(me != j)
            def _():
                note(j, me).wait_send()

    def entry():
        yh, z = lax.axis_index("yh"), lax.axis_index("z")
        for j in range(8):

            @pl.when(yh * 4 + z != j)
            def _():
                signal(device(yh=j // 4, z=j % 4))

        return 7

    return call(
        main,
        (tokens,) + small,
        [(SHARD, F32), (ALL, BF16), ((16, WIDTH), F32), ((8, 768), F32), ((8, WIDTH), F32)],
        [
            pltpu.VMEM(SHARD, BF16),
            pltpu.VMEM((32, 128), F32),
            pltpu.VMEM((8, 32, 128), F32),
        ]
        + sems(8, 8, 8, 8)
        + SPREAD_SCRATCH,
        ident,
        riders,
        pieces="in",
        entry=entry,
    )


def last_step(part, value, dx, table, vector_sums, qkv_sums, hidden_sums, at, ident, riders):
    def main(inputs, outs, scratch, sent):
        part, value, dx, table = inputs[:4]
        sum_refs = inputs[4 : 4 + len(vector_sums)]
        qkv_refs, hidden_refs = inputs[-4:-2], inputs[-2:]
        landed, small = outs
        ring_scratch, scratch = scratch[:SUMMING], scratch[SUMMING:]
        both, psend, precv, vectors, zgot, zsend, zrecv = scratch[:7]
        owned, ygot, ysend, yrecv, sub, xgot, xsend, xrecv = scratch[7:]
        x_, yl, co, yh, z = (lax.axis_index(a) for a in AXES)
        total = yield from shard_sum(WHOLE, part, ring_scratch, sent)
        (gain,) = (table[r : r + 1, :] for r in at)
        dr, gain_sum, shift_sum = norm_back(total, value[...], gain)
        for ref, (_, norm, branch) in zip(sum_refs, vector_sums):
            for row, kind, i in ((0, GAIN, norm), (1, SHIFT, norm), (2, 12, branch), (3, 8, branch)):
                if i is not None:
                    vectors[kind + i : kind + i + 1, :] = ref[row : row + 1, :]
        vectors[at[0] : at[0] + 1, :] = gain_sum
        vectors[at[0] + SHIFT : at[0] + SHIFT + 1, :] = shift_sum

        def on_z(there, slot, h):
            cut = vectors.at[:, pl.ds((h * 4 + there) * 128, 128)]
            return remote(
                cut, zgot.at[slot, h], zsend.at[there, h], zrecv.at[slot, h], device(z=there)
            )

        def on_y(there, slot):
            to = device(yh=there // 4, yl=(there // 2) % 2, co=there % 2)
            return remote(
                sub.at[there // 4], ygot.at[slot], ysend.at[there], yrecv.at[slot], to
            )

        def on_x(there, slot):
            return remote(owned, xgot.at[slot], xsend.at[there], xrecv.at[slot], device(x=there))

        def others(me, count, do):
            for i in range(count):

                @pl.when(me != i)
                def _():
                    do(i)

        me = yh * 4 + yl * 2 + co

        def both_halves(do):
            def run(i):
                do(i, 0)
                do(i, 1)

            return run

        others(z, 4, both_halves(lambda i, h: on_z(i, z, h).start()))
        both[...] = (dx[...] + dr).astype(BF16)
        give = PiecesOut.give(both, landed, psend, precv)
        next(give)
        for h in range(2):
            zgot[z, h] = vectors[:, pl.ds(pl.multiple_of((h * 4 + z) * 128, 128), 128)]
        yield 13.0
        others(z, 4, both_halves(lambda i, h: on_z(i, i, h).wait_recv()))
        owned[:, 0:16] = zgot[0] + zgot[1] + zgot[2] + zgot[3]
        owned[:, 16:32] = jnp.zeros((2, 16, 128), F32)
        for h in range(2):
            for l in range(LAYERS):
                for k in range(3):
                    lo, r = h * 384 + k * 128, 16 + 3 * l + k
                    owned[h, r : r + 1, :] = qkv_refs[l][0:1, lo : lo + 128]
                for k in range(4):
                    lo, r = h * 512 + k * 128, 22 + 4 * l + k
                    owned[h, r : r + 1, :] = hidden_refs[l][0:1, lo : lo + 128]
        others(x_, 4, lambda i: on_x(i, x_).start())
        xgot[x_] = owned[...]
        yield 16.0
        others(x_, 4, lambda i: on_x(i, i).wait_recv())
        sub[...] = sum(xgot[i] for i in range(4))
        others(me, 8, lambda i: on_y(i, me).start())
        ygot[me] = sub[yh]
        yield 19.0
        others(me, 8, lambda i: on_y(i, i).wait_recv())
        small[...] = sum(ygot[i] for i in range(8))
        others(z, 4, both_halves(lambda i, h: on_z(i, z, h).wait_send()))
        others(me, 8, lambda i: on_y(i, me).wait_send())
        others(x_, 4, lambda i: on_x(i, x_).wait_send())
        for _ in give:
            pass

    def entry():
        x_, yl, co, yh, z = (lax.axis_index(a) for a in AXES)
        me = yh * 4 + yl * 2 + co
        for i in range(8):

            @pl.when(me != i)
            def _():
                signal(device(yh=i // 4, yl=(i // 2) % 2, co=i % 2))

        for i in range(4):

            @pl.when(x_ != i)
            def _():
                signal(device(x=i))

            @pl.when(z != i)
            def _():
                signal(device(z=i))

        return 7 + 3 + 3

    return call(
        main,
        (part, value, dx, table, *[v[0] for v in vector_sums], *qkv_sums, *hidden_sums),
        [((8, ROWS, 128), BF16), ((32, 128), F32)],
        sum_scratch(WHOLE)
        + [
            pltpu.VMEM(SHARD, BF16),
            *sems(8, 8),
            pltpu.VMEM((16, WIDTH), F32),
            pltpu.VMEM((4, 2, 16, 128), F32),
            pltpu.SemaphoreType.DMA((4, 2)),
            pltpu.SemaphoreType.DMA((4, 2)),
            pltpu.VMEM((2, 32, 128), F32),
            pltpu.VMEM((8, 32, 128), F32),
            *sems(8, 8),
            pltpu.VMEM((2, 32, 128), F32),
            pltpu.VMEM((4, 2, 32, 128), F32),
            *sems(4, 4),
        ],
        ident,
        riders,
        pieces="out",
        entry=entry,
    )


def lanes_of(head, shape):
    lane = lax.broadcasted_iota(jnp.int32, shape, 1)
    return (lane < 64, lane == 64) if head % 2 == 0 else (lane >= 64, lane == 0)


def put_head(ref, i, value, one=False):
    inside, extra = lanes_of(i, value.shape)
    ref[i, 0:OWN] = jnp.where(inside, value, jnp.where(extra & one, 1, 0).astype(BF16))
    ref[i, OWN:QROWS] = jnp.zeros((QROWS - OWN, 128), BF16)


def put_keys(ref, i, rows, value, mask):
    inside, extra = lanes_of(i, value.shape)
    ref[i, rows] = jnp.where(inside, value, jnp.where(extra, mask[rows], jnp.zeros_like(value)))


def attend_step(n_all, wqkv, wout, bias, layer, mask, ident, riders=()):
    def main(inputs, outs, scratch, sent):
        n_all, wqkv, wout, bias, mask = inputs
        part, qkv, other, att, lse = outs
        kall, vt, qpad, ot, send, recv = scratch
        to = device(co=1 - lax.axis_index("co"))
        mine, theirs = slice(0, OWN), slice(OWN, KEYS)
        yield 0.1
        normed = n_all[...].reshape(OWN, WIDTH)
        lse[...] = jnp.zeros_like(lse)
        copies = []
        for h in range(2):
            cols = slice(h * 384, h * 384 + 384)
            block = (dot_nn(normed, wqkv[:, cols]) + bias[layer : layer + 1, cols]).astype(BF16)
            qkv[:, cols] = block
            c = remote(
                qkv.at[:, pl.ds(h * 384 + 128, 256)],
                other.at[:, pl.ds(h * 256, 256)],
                send.at[h],
                recv.at[h],
                to,
            )
            c.start()
            copies.append(c)
            for i in (2 * h, 2 * h + 1):
                put_head(qpad, i, block[:, 0:128] * 0.125, True)
                put_keys(kall, i, mine, block[:, 128:256], mask)
            vt[h * 128 : h * 128 + 128, 0:OWN] = block[:, 256:384].T
        sent.extend(copies)
        yield 3.0
        for h in range(2):
            copies[h].wait_recv()
            for i in (2 * h, 2 * h + 1):
                put_keys(kall, i, theirs, other[:, h * 256 : h * 256 + 128], mask)
            vt[h * 128 : h * 128 + 128, OWN:KEYS] = other[:, h * 256 + 128 : h * 256 + 256].T

            for i in (2 * h, 2 * h + 1):
                rows = slice(i * 64, i * 64 + 64)
                for lo, n in CHUNKS:
                    s = dot_nt(kall[i], qpad[i, lo : lo + n])
                    top = jnp.max(s, axis=0, keepdims=True)
                    e = jnp.exp(s - top)
                    total = jnp.sum(e, axis=0, keepdims=True)
                    ot[rows, lo : lo + n] = dot_nn(vt[rows], e.astype(BF16)) * (1.0 / total)
                    lse[i, 0:1, lo : lo + n] = top + jnp.log(total)
                yield 6.0 + 2.0 * i
        sent.flush(qkv, other, lse)
        att[...] = ot[...].T[0:OWN].astype(BF16)
        part[...] = dot_nn(att[...], wout[...]).astype(BF16).reshape(ALL)

    return call(
        main,
        (n_all, wqkv, wout, bias, mask),
        [
            (ALL, BF16),
            ((OWN, 768), BF16),
            ((OWN, 512), BF16),
            ((OWN, 256), BF16),
            ((4, 8, QROWS), F32),
        ],
        [
            pltpu.VMEM((4, KEYS, 128), BF16),
            pltpu.VMEM((256, KEYS), BF16),
            pltpu.VMEM((4, QROWS, 128), BF16),
            pltpu.VMEM((256, QROWS), F32),
        ]
        + sems(2, 2),
        ident,
        riders,
        links=("core",),
        pace=1.6,
    )


def attend_back_step(d_all, wqkv, wout, qkv, other, att, lse, mask, ident, riders=()):
    def main(inputs, outs, scratch, sent):
        d_all, wqkv, wout, qkv, other, att, lse, mask = inputs
        part, dqkv, sums = outs
        kall, vall, kt, qone, qpad, dpad, delta, dqt, dk, dv, away, got, send, recv = scratch
        to = device(co=1 - lax.axis_index("co"))
        mine, theirs = slice(0, OWN), slice(OWN, KEYS)
        yield 0.1
        datt = dot_nt(d_all[...].reshape(OWN, WIDTH), wout[...]).astype(BF16)
        copies = []
        along = (datt.astype(F32) * att[...].astype(F32)).T
        delta[...] = jnp.zeros_like(delta)
        for i in range(4):
            delta[i, 0:1, 0:OWN] = jnp.sum(along[i * 64 : i * 64 + 64], axis=0, keepdims=True)
        for h in range(2):
            base, half = h * 384, h * 256
            own_keys, other_keys = qkv[:, base + 128 : base + 256], other[:, half : half + 128]
            for i in (2 * h, 2 * h + 1):
                query = qkv[:, base : base + 128] * 0.125
                put_head(qone, i, query, True)
                put_head(qpad, i, query)
                put_head(dpad, i, datt[:, h * 128 : h * 128 + 128])
                put_keys(kall, i, mine, own_keys, mask)
                put_keys(kall, i, theirs, other_keys, mask)
            vall[h, 0:OWN] = qkv[:, base + 256 : base + 384]
            vall[h, OWN:KEYS] = other[:, half + 128 : half + 256]
            kt[h * 128 : h * 128 + 128, 0:OWN] = own_keys.T
            kt[h * 128 : h * 128 + 128, OWN:KEYS] = other_keys.T
            dk[h] = jnp.zeros((KEYS, 128), F32)
            dv[h] = jnp.zeros((KEYS, 128), F32)

            for i in (2 * h, 2 * h + 1):
                rows = slice(i * 64, i * 64 + 64)
                for lo, n in CHUNKS:
                    qc, dc = qpad[i, lo : lo + n], dpad[i, lo : lo + n]
                    s = dot_nt(kall[i], qone[i, lo : lo + n])
                    p = jnp.exp(s - lse[i, 0:1, lo : lo + n])
                    dp = dot_nt(vall[h], dc)
                    ds = (p * (dp - delta[i, 0:1, lo : lo + n])).astype(BF16)
                    dv[h] += dot_nn(p.astype(BF16), dc)
                    dk[h] += dot_nn(ds, qc)
                    dqt[rows, lo : lo + n] = dot_nn(kt[rows], ds)
                yield 5.0 + 2.5 * i
            away[h, :, 0:128] = dk[h, OWN:KEYS].astype(BF16)
            away[h, :, 128:256] = dv[h, OWN:KEYS].astype(BF16)
            c = remote(away.at[h], got.at[h], send.at[h], recv.at[h], to)
            c.start()
            copies.append(c)
        sent.extend(copies)
        dq = dqt[...].T[0:OWN] * 0.125
        for h in range(2):
            base = h * 384
            dqkv[:, base : base + 128] = dq[:, h * 128 : h * 128 + 128].astype(BF16)
            copies[h].wait_recv()
            dqkv[:, base + 128 : base + 256] = (
                dk[h, 0:OWN] + got[h, :, 0:128].astype(F32)
            ).astype(BF16)
            dqkv[:, base + 256 : base + 384] = (
                dv[h, 0:OWN] + got[h, :, 128:256].astype(F32)
            ).astype(BF16)
        part[...] = dot_nt(dqkv[...], wqkv[...]).astype(BF16).reshape(ALL)
        sums[...] = jnp.zeros_like(sums)
        sums[0:1, :] = jnp.sum(dqkv[...].astype(F32), axis=0, keepdims=True)

    return call(
        main,
        (d_all, wqkv, wout, qkv, other, att, lse, mask),
        [(ALL, BF16), ((OWN, 768), BF16), ((8, 768), F32)],
        [
            pltpu.VMEM((4, KEYS, 128), BF16),
            pltpu.VMEM((2, KEYS, 128), BF16),
            pltpu.VMEM((256, KEYS), BF16),
            pltpu.VMEM((4, QROWS, 128), BF16),
            pltpu.VMEM((4, QROWS, 128), BF16),
            pltpu.VMEM((4, QROWS, 128), BF16),
            pltpu.VMEM((4, 8, QROWS), F32),
            pltpu.VMEM((256, QROWS), F32),
            pltpu.VMEM((2, KEYS, 128), F32),
            pltpu.VMEM((2, KEYS, 128), F32),
            pltpu.VMEM((2, OWN, 256), BF16),
            pltpu.VMEM((2, OWN, 256), BF16),
        ]
        + sems(2, 2),
        ident,
        riders,
        links=("core",),
        pace=1.6,
    )


def on_device(
    tokens,
    cotangent,
    attend_weight,
    output_weight,
    up_weight,
    down_weight,
    norm_gain,
    norm_shift,
    attend_bias,
    branch_bias,
    layer_scale,
    hidden_bias,
):
    co, yh, z = (lax.axis_index(a) for a in ("co", "yh", "z"))
    attend_weight = attend_weight.reshape(LAYERS, 256, 384)
    first = jnp.pad(tokens, ((0, 15), (0, 0)))
    cot_pieces = jnp.pad(cotangent.astype(BF16), ((0, 15), (0, 0)))
    def attend_of(l, start=0.0):
        return GatherWeight(attend_weight, l, 0, start=start)

    def output_of(l, start=0.0):
        return GatherWeight(output_weight, l, 1, start=start)

    def up_of(l):
        return GatherWeight(up_weight, l, 0)

    def down_of(l, board):
        return GatherWeight(down_weight, l, 1, VM, board)

    weights = [[None] * 4 for _ in range(LAYERS)]
    ident = iter(range(40))
    small = (norm_gain, norm_shift, branch_bias, layer_scale, attend_bias, hidden_bias)
    (x, n_all, table, query_bias, up_bias), (weights[0][0], weights[0][1]) = first_step(
        first, small, next(ident), [attend_of(0), output_of(0)]
    )
    row = jnp.arange(OWN)
    block, inside = row // ROWS, row % ROWS

    def hidden_keys(half):
        real = (inside < REAL) | ((inside == REAL) & (block == 3) & (half == 1))
        return jnp.where(real, 0.0, -1e30).astype(BF16)

    mask = jnp.concatenate([hidden_keys(co), hidden_keys(1 - co)])
    mask = jnp.broadcast_to(mask[:, None], (KEYS, 128))

    last = jnp.where((co == 1) & (z == 3), REAL + 1, REAL)
    real_row = jnp.arange(ROWS)[:, None] < last

    saved = []
    for l in range(LAYERS):
        wqkv, wout = weights[l][:2]
        riders = [up_of(l)]
        if l == 1:
            riders.append(Spread((cot * table[SCALE + 3]).astype(BF16)))
        n1 = n_all
        (part, qkv, other, att, lse), got = attend_step(
            n1, wqkv, wout, query_bias, l, mask, next(ident), riders
        )
        weights[l][2] = got[0]
        if l == 1:
            d_all = d_last = got[1]
        saved.append([x, n1, qkv, other, att, lse])
        board = []
        if l == 0:
            riders = [
                down_of(0, board), Pieces(cot_pieces, 12.0), attend_of(1, 14.0), output_of(1, 14.5)
            ]
            (a, m, n2, u, g, f, x, n_all), got = forward_chain(
                part, x, table, weights[0][2], up_bias, board, next(ident), riders
            )
            weights[0][3], weights[1][:2] = got[0], got[2:]
            cot = jnp.where(real_row, got[1].astype(F32), 0.0)
            saved[0] += [a, m, n2, u, g, f]
        else:
            late_up, late_down = [], []
            like = n_all
            riders = [
                down_of(1, board),
                ReduceWeight(like, like, 0, late_up, 17.0),
                ReduceWeight(like, like, 1, late_down, 18.5),
            ]
            (a, m, n2, g, end_part, du, hidden, dm, sums, d_all), got = turn_chain(
                part,
                x,
                cot,
                d_all,
                table,
                weights[1][2],
                up_bias,
                board,
                late_up,
                late_down,
                next(ident),
                riders,
            )
            weights[1][3], up_block, down_block = got

    hidden_sums, qkv_sums, grads = [None, hidden], [None] * LAYERS, [[None] * 4, [None] * 4]

    def summing(block):
        return SumBlock(block.shape, block)

    vector_sums = [(sums, 3, 2)]
    x1, n1, qkv, other, att, lse = saved[1]
    da = d_all
    riders = [
        End(end_part, m, cot, table, (BRANCH + 3, SCALE + 3)),
        summing(up_block),
        summing(down_block),
    ]
    (part, dqkv, qkv_sum), got = attend_back_step(
        d_all, *weights[1][:2], qkv, other, att, lse, mask, next(ident), riders
    )
    x_end, sums, grads[1][2], grads[1][3] = got
    vector_sums.append((sums, None, 3))
    qkv_sums[1] = qkv_sum
    x, n1_0, qkv, other, att_0, lse, a, m, n2, u, g0, f = saved[0]
    late_down, late_up = [], []
    riders = [
        ReduceWeight(n1, dqkv, 0, start=1.0),
        ReduceWeight(att, da, 1, start=4.0),
        ReduceWeight(like, like, 1, late_down, 15.5),
        ReduceWeight(like, like, 0, late_up, 18.0),
    ]
    (sums1, df, du, hidden, dm, sums, d_all), got = backward_chain(
        part,
        x1,
        dm,
        f,
        m,
        a,
        n2,
        u,
        g0,
        table,
        *weights[0][2:],
        late_down,
        late_up,
        next(ident),
        riders,
    )
    attend_block, output_block, down_block, up_block = got
    vector_sums += [(sums1, 2, 1), (sums, 1, 0)]
    hidden_sums[0] = hidden
    riders = [
        PiecesOut(x_end),
        ReduceWeight(att_0, d_all, 1),
        SumBlock(attend_block.shape, attend_block, True),
        summing(output_block),
        summing(down_block),
    ]
    (part, dqkv, qkv_sum), got = attend_back_step(
        d_all, *weights[0][:2], qkv, other, att_0, lse, mask, next(ident), riders
    )
    out_pieces, output_block, grads[1][0], grads[1][1], grads[0][3] = got
    qkv_sums[0] = qkv_sum
    riders = [
        ReduceSum(n1_0, dqkv, 0),
        summing(output_block),
        summing(up_block),
    ]
    (grad_pieces, small), grads[0][:3] = last_step(
        part, x, dm, table, vector_sums, qkv_sums, hidden_sums, (GAIN,), next(ident), riders
    )

    bias_grad = small[16:22].reshape(2, 3, 128)[:, 0::2]

    def rows(landed):
        return jnp.concatenate(
            [landed[0:7, 0:REAL].reshape(7 * REAL, 128), landed[7, 0 : REAL + 1]]
        ).astype(F32)

    return (
        rows(out_pieces),
        rows(grad_pieces),
        jnp.stack([grads[l][0] for l in range(LAYERS)]).transpose(0, 2, 1, 3),
        jnp.stack([grads[l][1] for l in range(LAYERS)]),
        jnp.stack([grads[l][2] for l in range(LAYERS)]),
        jnp.stack([grads[l][3] for l in range(LAYERS)]),
        small[0:4].reshape(2, 2, 128),
        small[4:8].reshape(2, 2, 128),
        bias_grad,
        small[8:12].reshape(2, 2, 128),
        small[12:16].reshape(2, 2, 128),
        small[22:30].reshape(2, 512),
    )


def solution(mesh):
    split = Mesh(mesh.devices.reshape(4, 2, 2, 2, 4), AXES)
    images, row, col = ("x", "yl", "co"), ("yl", "co"), ("yh", "z")
    placed = (
        P(images, col),
        P(images, col),
        P(None, row, None, col),
        P(None, col, row),
        P(None, row, col),
        P(None, col, row),
        P(None, None, col),
        P(None, None, col),
        P(None, None, col),
        P(None, None, col),
        P(None, None, col),
        P(None, col),
    )
    return jax.shard_map(
        on_device, mesh=split, in_specs=placed, out_specs=placed, check_vma=False
    )
```
